32 devices in a mesh: seq: 4 (over y, x), win: 8 (over z, core).
Axes of the slice: x: 2, y: 2, z: 4, core: 2. Of those that a mesh axis runs over, the one named last changes fastest.
Arguments:
- inputs: bfloat16 [8, 1536, 1536], P('win', 'seq'), may hold values from -6 to 6
- bin_order: int32 [8, 1536], P('win'), may hold values from 0 to 1535, as said below
- first_gain: bfloat16 [1536], P('seq'), may hold values from 0.5 to 1.5
- first_shift: bfloat16 [1536], P('seq'), may hold values from -1 to 1
- query_weight: bfloat16 [1536, 512], P('seq'), may hold values from -0.15625 to 0.15625
- key_weight: bfloat16 [1536, 512], P('seq'), may hold values from -0.15625 to 0.15625
- value_weight: bfloat16 [1536, 1536], P('seq'), may hold values from -0.15625 to 0.15625
- bias_content: bfloat16 [512], P('seq'), may hold values from -0.75 to 0.75
- bias_position: bfloat16 [512], P('seq'), may hold values from -0.75 to 0.75
- relative_weight: bfloat16 [192, 512], P('seq'), may hold values from -0.875 to 0.875
- out_weight: bfloat16 [1536, 1536], P('seq'), may hold values from -2 to 2
- bias_out: bfloat16 [1536], P('seq'), may hold values from -1 to 1
- second_gain: bfloat16 [1536], P('seq'), may hold values from 0.5 to 1.5
- second_shift: bfloat16 [1536], P('seq'), may hold values from -1 to 1
- inner_weight: bfloat16 [1536, 3072], P('seq'), may hold values from -0.15625 to 0.15625
- bias_inner: bfloat16 [3072], P('seq'), may hold values from -1 to 1
- outer_weight: bfloat16 [3072, 1536], P('seq'), may hold values from -0.109375 to 0.109375
- bias_outer: bfloat16 [1536], P('seq'), may hold values from -1 to 1
- grad_output: bfloat16 [8, 1536, 1536], P('win', 'seq'), may hold values from -6 to 6
Outputs:
- layer_output: bfloat16 [8, 1536, 1536], P('win', 'seq')
- grad_inputs: float32 [8, 1536, 1536], P('win', 'seq')
- grad_first_gain: float32 [1536], P('seq')
- grad_first_shift: float32 [1536], P('seq')
- grad_query_weight: float32 [1536, 512], P('seq')
- grad_key_weight: float32 [1536, 512], P('seq')
- grad_value_weight: float32 [1536, 1536], P('seq')
- grad_bias_content: float32 [512], P('seq')
- grad_bias_position: float32 [512], P('seq')
- grad_relative_weight: float32 [192, 512], P('seq')
- grad_out_weight: float32 [1536, 1536], P('seq')
- grad_bias_out: float32 [1536], P('seq')
- grad_second_gain: float32 [1536], P('seq')
- grad_second_shift: float32 [1536], P('seq')
- grad_inner_weight: float32 [1536, 3072], P('seq')
- grad_bias_inner: float32 [3072], P('seq')
- grad_outer_weight: float32 [3072, 1536], P('seq')
- grad_bias_outer: float32 [1536], P('seq')
The draws below stay inside these ranges and needn't reach their ends.
Inputs may be any that keep to these rules, and one draw needn't show every extreme that they name: Each row of bin_order is a permutation of the bins of its window: position i takes bin (s + i) mod 1536 or (s + 1535 - i) mod 1536, with the offset s and the reversal chosen for each window.
All inputs are finite; a program needn't handle non-finite values.
Results may differ from the reference program's by a relative error of at most 0.025.
Values may be sent and summed in bfloat16 or wider, within the bound.
No kernel may reach another device: no remote copies, remote signals or barrier semaphores. Data moves between devices by JAX's collectives and lax.ppermute only.
A program may use at most 320 MiB of HBM per device.

```python
import math
import jax
import jax.numpy as jnp
from jax import lax

D = 1536
HEADS = 8
KEY = 64
VAL = 192
REL = 192
FF = 3072
SPAN = 1536
HK = 512
HV = 1536
WINDOWS = 8


def draw_bin_order(key, part):
    key = jax.random.fold_in(key, 11)
    shift_key, flip_key = jax.random.split(key)
    offsets = jax.random.randint(shift_key, (WINDOWS, 1), 0, SPAN)
    flipped = jax.random.randint(flip_key, (WINDOWS, 1), 0, 2)
    position = jnp.arange(SPAN, dtype=jnp.int32)[None, :]
    position = jnp.where(flipped == 1, SPAN - 1 - position, position)
    return ((position + offsets) % SPAN).astype(jnp.int32)


def steps_of(rng, shape, shards, least, high):
    def one(axis_at, parts):
        draws = jax.random.uniform(jax.random.fold_in(jax.random.fold_in(rng, 6), axis_at), (parts,), jnp.float32, least / len(shards), high / len(shards))
        return jnp.repeat(jnp.exp(draws), shape[axis_at] // parts).reshape((-1,) + (1,) * (len(shape) - axis_at - 1))

    loudness = one(*shards[0])
    for cut in shards[1:]:
        loudness = loudness * one(*cut)
    return loudness


def scatter_about(stream_key, extent, scale, most, cuts=(), held_as=jnp.bfloat16):
    array = jax.random.normal(stream_key, extent, jnp.float32) * scale
    if len(cuts) > 0:
        array = steps_of(stream_key, extent, cuts, -0.22, 0.18) * array
    return jnp.clip(array, min=-most, max=most).astype(held_as)


def setup_inputs(seed: int = 0) -> dict:
    key_list = jax.random.split(jax.random.key(seed), 20)
    return {
        "inputs": scatter_about(key_list[0], (WINDOWS, SPAN, D), 1.0, 6.0, ((0, 8), (1, 4))),
        "bin_order": draw_bin_order(jax.random.fold_in(key_list[19], 71), 0),
        "first_gain": jnp.clip(1.0 + 0.1 * jax.random.normal(key_list[2], (D,), jnp.float32), 0.5, 1.5).astype(jnp.bfloat16),
        "first_shift": scatter_about(key_list[3], (D,), 0.2, 1.0, ((0, 4),)),
        "query_weight": scatter_about(key_list[4], (D, HK), D ** -0.5, 0.15625, ((0, 4),)),
        "key_weight": scatter_about(key_list[5], (D, HK), D ** -0.5, 0.15625, ((0, 4),)),
        "value_weight": scatter_about(key_list[6], (D, HV), D ** -0.5, 0.15625, ((0, 4),)),
        "bias_content": scatter_about(key_list[7], (HK,), 0.125, 0.75, ((0, 4),)),
        "bias_position": scatter_about(key_list[8], (HK,), 0.125, 0.75, ((0, 4),)),
        "relative_weight": scatter_about(key_list[9], (REL, HK), (REL // 4) ** -0.5, 0.875, ((0, 4),)),
        "out_weight": scatter_about(key_list[10], (HV, D), 8 ** -0.5, 2.0, ((0, 4),)),
        "bias_out": scatter_about(key_list[11], (D,), 0.2, 1.0, ((0, 4),)),
        "second_gain": jnp.clip(1.0 + 0.1 * jax.random.normal(key_list[12], (D,), jnp.float32), 0.5, 1.5).astype(jnp.bfloat16),
        "second_shift": scatter_about(key_list[13], (D,), 0.2, 1.0, ((0, 4),)),
        "inner_weight": scatter_about(key_list[14], (D, FF), D ** -0.5, 0.15625, ((0, 4),)),
        "bias_inner": scatter_about(key_list[15], (FF,), 0.2, 1.0, ((0, 4),)),
        "outer_weight": scatter_about(key_list[16], (FF, D), FF ** -0.5, 0.109375, ((0, 4),)),
        "bias_outer": scatter_about(key_list[17], (D,), 0.2, 1.0, ((0, 4),)),
        "grad_output": scatter_about(key_list[18], (WINDOWS, SPAN, D), 1.0, 6.0, ((0, 8), (1, 4))),
    }


@jax.custom_vjp
def low(v):
    return lax.optimization_barrier(v.astype(jnp.bfloat16)).astype(jnp.float32)

@jax.custom_vjp
def low_back(v):
    return v

def low_keep(v):
    return (low(v), None)

def low_pass(kept, grad):
    return (grad,)

def back_keep(v):
    return (v, None)

def back_low(kept, grad):
    return (low(grad),)
low.defvjp(low_keep, low_pass)
low_back.defvjp(back_keep, back_low)

def gamma_profile(distance, window_len, features):
    spread = window_len / (2.0 * features)
    centres = jnp.linspace(window_len / features, window_len, features, dtype=jnp.float32)
    concentration = (centres / spread) ** 2
    decay_rate = centres / spread ** 2
    logged = (concentration - 1.0) * jnp.log(distance) - decay_rate * distance
    logged = logged + concentration * jnp.log(decay_rate) - lax.lgamma(concentration)
    return jnp.exp(logged) + 1e-08

def gamma_peaks(window_len):
    features = REL // 6
    every = jnp.arange(window_len).astype(jnp.float32)[:, None]
    return lax.optimization_barrier(jnp.max(gamma_profile(every, window_len, features), axis=0))

def relative_basis(offsets, window_len, peaks):
    features = REL // 6
    distance = jnp.abs(offsets).astype(jnp.float32)[:, None]
    half_life = 2.0 ** jnp.linspace(3.0, math.log2(window_len), features, dtype=jnp.float32)
    falloff = jnp.exp(-math.log(2.0) / half_life * distance)
    widths = 2.0 ** jnp.arange(1, features + 1).astype(jnp.float32) - 1.0
    inside = jnp.where(widths > distance, 1.0, 0.0).astype(jnp.float32)
    bumps = gamma_profile(distance, window_len, features) / peaks
    joined = jnp.concatenate([falloff, inside, bumps], axis=1)
    signs = jnp.sign(offsets).astype(jnp.float32)[:, None]
    return jnp.concatenate([joined, signs * joined], axis=1)

def relative_shift(position_grid, key_count):
    query_count, grid_width = (position_grid.shape[-2], position_grid.shape[-1])
    lead = position_grid.shape[:-2]
    flatten = position_grid.reshape(lead + (query_count * grid_width,))
    flatten = flatten[..., query_count - 1:query_count - 1 + query_count * (grid_width - 1)]
    return flatten.reshape(lead + (query_count, grid_width - 1))[..., :key_count]

def normalize(values_in, gain, offset):
    centre = values_in - lax.optimization_barrier(jnp.mean(values_in, axis=-1, keepdims=True))
    spread = lax.optimization_barrier(jnp.mean(centre * centre, axis=-1, keepdims=True))
    return centre * lax.rsqrt(spread + 1e-05) * gain + offset

def attend(q_content, q_basis, key_heads, value_heads, window_len, peaks):
    block_rows = math.gcd(512, window_len)
    count = window_len // block_rows
    content_blocks = q_content.reshape(count, block_rows, HEADS, KEY)
    basis_blocks = q_basis.reshape(HEADS, count, block_rows, REL).transpose(1, 0, 2, 3)
    starts = jnp.arange(count, dtype=jnp.int32) * block_rows

    def one_block(carried):
        content_rows, basis_query, start = carried
        offsets = jnp.arange(block_rows + window_len - 1, dtype=jnp.int32) - start - (block_rows - 1)
        basis_rows = low(relative_basis(offsets, window_len, peaks))
        position_grid = jnp.einsum('hrc,mc->hrm', basis_query, basis_rows, precision=lax.Precision.HIGHEST)
        content = jnp.einsum('rhk,shk->hrs', content_rows, key_heads, precision=lax.Precision.HIGHEST)
        scores = low_back(content + relative_shift(position_grid, window_len))
        normal = jax.nn.logsumexp(scores, axis=-1, keepdims=True)
        probs = low(jnp.exp(scores - normal))
        return jnp.einsum('hrs,shc->rhc', probs, value_heads, precision=lax.Precision.HIGHEST)
    attended = lax.map(jax.checkpoint(one_block), (content_blocks, basis_blocks, starts))
    return attended.reshape(window_len, HEADS * VAL)

def forward(window_in, window_order, params):
    first_gain, first_shift, query_weight, key_weight, value_weight, bias_content, bias_position, relative_weight, out_weight, bias_out, second_gain, second_shift, inner_weight, bias_inner, outer_weight, bias_outer = params
    highest = lax.Precision.HIGHEST
    window_len = window_in.shape[0]
    peaks = gamma_peaks(window_len)
    placed = window_in[window_order]
    normed_one = low(normalize(placed, first_gain, first_shift))
    query = low_back(jnp.dot(normed_one, query_weight, precision=highest))
    query_scale = KEY ** (-0.5)
    q_content = low(query * query_scale + bias_content).reshape(window_len, HEADS, KEY)
    q_position = low(query * query_scale + bias_position).reshape(window_len, HEADS, KEY)
    q_basis = jnp.einsum('rhk,chk->hrc', q_position, relative_weight.reshape(REL, HEADS, KEY), precision=highest)
    q_basis = low(low_back(q_basis))
    key_heads = low(low_back(jnp.dot(normed_one, key_weight, precision=highest))).reshape(window_len, HEADS, KEY)
    value_heads = low(low_back(jnp.dot(normed_one, value_weight, precision=highest))).reshape(window_len, HEADS, VAL)
    attended = attend(q_content, q_basis, key_heads, value_heads, window_len, peaks)
    mixed = low(low_back(attended))
    residual = placed + low_back(jnp.dot(mixed, out_weight, precision=highest) + bias_out)
    normed_two = low(normalize(residual, second_gain, second_shift))
    inner = low_back(jnp.dot(normed_two, inner_weight, precision=highest) + bias_inner)
    activated = low(jax.nn.gelu(inner, approximate=False))
    return residual + low_back(jnp.dot(activated, outer_weight, precision=highest) + bias_outer)

def reference(inputs, bin_order, first_gain, first_shift, query_weight, key_weight, value_weight, bias_content, bias_position, relative_weight, out_weight, bias_out, second_gain, second_shift, inner_weight, bias_inner, outer_weight, bias_outer, grad_output):
    weights = tuple((weight_arg.astype(jnp.float32) for weight_arg in (first_gain, first_shift, query_weight, key_weight, value_weight, bias_content, bias_position, relative_weight, out_weight, bias_out, second_gain, second_shift, inner_weight, bias_inner, outer_weight, bias_outer)))

    def window(totals, carried):
        window_in, window_order, window_grad = carried

        def run(values_in, *params):
            return forward(values_in, window_order, params)
        result, pull = jax.vjp(run, window_in.astype(jnp.float32), *weights)
        grads = pull(window_grad.astype(jnp.float32))
        totals = tuple((left + right for left, right in zip(totals, grads[1:])))
        return (totals, (result.astype(jnp.bfloat16), grads[0]))
    zeros = tuple((jnp.zeros(weight_arg.shape, jnp.float32) for weight_arg in weights))
    totals, (outputs, input_grads) = lax.scan(window, zeros, (inputs, bin_order, grad_output))
    return (outputs, input_grads) + totals
```

```python
import functools
import math

import jax
import jax.numpy as jnp
from jax import lax
from jax.experimental import pallas as pl
from jax.experimental.pallas import tpu as pltpu
from jax.sharding import Mesh
from jax.sharding import PartitionSpec as P

HEADS = 8
KEY = 64
VAL = 192
REL = 192
BF16 = jnp.bfloat16
F32 = jnp.float32
VMEM_LIMIT = 56 * 2**20


def gamma_profile(distance, window_len, features):
    spread = window_len / (2.0 * features)
    centres = jnp.linspace(window_len / features, window_len, features, dtype=F32)
    concentration = (centres / spread) ** 2
    decay_rate = centres / spread**2
    logged = (concentration - 1.0) * jnp.log(distance) - decay_rate * distance
    logged = logged + concentration * jnp.log(decay_rate) - lax.lgamma(concentration)
    return jnp.exp(logged) + 1e-08


def gamma_peaks(window_len):
    features = REL // 6
    every = jnp.arange(window_len).astype(F32)[:, None]
    return jnp.max(gamma_profile(every, window_len, features), axis=0)


def relative_basis(offsets, window_len, peaks):
    features = REL // 6
    distance = jnp.abs(offsets).astype(F32)[:, None]
    half_life = 2.0 ** jnp.linspace(3.0, math.log2(window_len), features, dtype=F32)
    falloff = jnp.exp(-math.log(2.0) / half_life * distance)
    widths = 2.0 ** jnp.arange(1, features + 1).astype(F32) - 1.0
    inside = jnp.where(widths > distance, 1.0, 0.0).astype(F32)
    bumps = gamma_profile(distance, window_len, features) / peaks
    joined = jnp.concatenate([falloff, inside, bumps], axis=1)
    signs = jnp.sign(offsets).astype(F32)[:, None]
    return jnp.concatenate([joined, signs * joined], axis=1)


def matmul(a, b):
    return lax.dot_general(a, b, (((1,), (0,)), ((), ())), preferred_element_type=F32)


def matmul_nt(a, b):
    return lax.dot_general(a, b, (((1,), (1,)), ((), ())), preferred_element_type=F32)


def matmul_tn(a, b):
    return lax.dot_general(a, b, (((0,), (0,)), ((), ())), preferred_element_type=F32)


def head_part(rows, head):
    lanes = lax.broadcasted_iota(jnp.int32, rows.shape, 1)
    inside = (lanes >= head * KEY) & (lanes < (head + 1) * KEY)
    return jnp.where(inside, rows, jnp.zeros_like(rows))


def attend_kernel(heads, rows, content, position, keys, values, rel, table, mixed, probs):
    length = keys.shape[0]
    start = pl.multiple_of(length - rows - pl.program_id(0) * rows, rows)
    basis = table[:, pl.ds(start, length + rows)]
    parts = []
    for head in range(heads):
        q_basis = matmul_nt(head_part(position[...], head), rel[...]).astype(BF16)
        grid = matmul(q_basis, basis)
        shifted = pltpu.roll(grid, 0, 1, stride=1, stride_axis=0)[:, rows:]
        scores = matmul_nt(head_part(content[...], head), keys[...]) + shifted
        top = jnp.max(scores, axis=1, keepdims=True)
        weights = jnp.exp(scores - top)
        total = jnp.sum(weights, axis=1, keepdims=True)
        prob = (weights * (1.0 / total)).astype(BF16)
        probs[head] = prob
        parts.append(matmul(prob, values[:, head * VAL : (head + 1) * VAL]))
    mixed[...] = jnp.concatenate(parts, axis=1).astype(BF16)


def attend(content, position, keys, values, rel, table):
    length, key_width = keys.shape
    val_width = values.shape[1]
    heads = key_width // KEY
    rows = math.gcd(256, length)
    whole = lambda array: pl.BlockSpec(array.shape, lambda i: (0, 0))
    block = lambda width: pl.BlockSpec((rows, width), lambda i: (i, 0))
    return pl.pallas_call(
        functools.partial(attend_kernel, heads, rows),
        grid=(length // rows,),
        in_specs=[
            block(key_width),
            block(key_width),
            whole(keys),
            whole(values),
            whole(rel),
            whole(table),
        ],
        out_specs=[
            block(val_width),
            pl.BlockSpec((heads, rows, length), lambda i: (0, i, 0)),
        ],
        out_shape=[
            jax.ShapeDtypeStruct((length, val_width), BF16),
            jax.ShapeDtypeStruct((heads, length, length), BF16),
        ],
        compiler_params=pltpu.CompilerParams(vmem_limit_bytes=VMEM_LIMIT),
        cost_estimate=pl.CostEstimate(
            flops=2 * heads * length * length * 512,
            bytes_accessed=2 * heads * length * length + 8 * length * val_width,
            transcendentals=heads * length * length,
        ),
    )(content, position, keys, values, rel, table)


def attend_back_kernel(
    heads,
    rows,
    content,
    position,
    keys,
    values,
    rel,
    table,
    flip,
    mixed,
    d_mixed,
    probs,
    d_query,
    d_keys,
    d_values,
    d_rel,
    d_bias,
    keys_sum,
    values_sum,
):
    length, key_width = keys.shape
    step = pl.program_id(0)

    @pl.when(step == 0)
    def _():
        keys_sum[...] = jnp.zeros_like(keys_sum)
        values_sum[...] = jnp.zeros_like(values_sum)
        d_rel[...] = jnp.zeros_like(d_rel)
        d_bias[...] = jnp.zeros_like(d_bias)

    basis = table[pl.ds(pl.multiple_of(step * rows, rows), length + rows), :]
    d_content = jnp.zeros((rows, key_width), F32)
    d_position = jnp.zeros((rows, key_width), F32)
    blocks = length // rows
    for head in range(heads):
        columns = slice(head * VAL, (head + 1) * VAL)
        d_part = d_mixed[:, columns]
        delta = jnp.sum(
            d_part.astype(F32) * mixed[:, columns].astype(F32), axis=1, keepdims=True
        )
        prob = probs[head]
        values_sum[columns, :] += matmul_tn(d_part, prob)
        d_prob = matmul_nt(d_part, values[:, columns])
        d_score = (prob.astype(F32) * (d_prob - delta)).astype(BF16)
        keys_sum[...] += matmul_tn(head_part(content[...], head), d_score)
        d_content += head_part(matmul(d_score, keys[...]), head)
        turned = [
            matmul(d_score[:, (blocks - 1 - b) * rows : (blocks - b) * rows], flip[...])
            for b in range(blocks)
        ]
        turned = jnp.concatenate(turned + [jnp.zeros((rows, rows), F32)], axis=1)
        d_grid = pltpu.roll(turned, 0, 1, stride=1, stride_axis=0).astype(BF16)
        d_basis = matmul(d_grid, basis).astype(BF16)
        d_position += head_part(matmul(d_basis, rel[...]), head)
        d_rel[...] += matmul_tn(d_basis, head_part(position[...], head))
    d_query[...] = ((d_content + d_position) * KEY ** (-0.5)).astype(BF16)
    d_bias[0:1, :] += jnp.sum(d_content, axis=0, keepdims=True)
    d_bias[1:2, :] += jnp.sum(d_position, axis=0, keepdims=True)

    @pl.when(step == blocks - 1)
    def _():
        d_keys[...] = keys_sum[...].T.astype(BF16)
        d_values[...] = values_sum[...].T.astype(BF16)


def attend_back(content, position, keys, values, rel, table, mixed, d_mixed, probs):
    length, key_width = keys.shape
    val_width = values.shape[1]
    heads = key_width // KEY
    rows = math.gcd(256, length)
    at = jnp.arange(rows)
    flip = (at[:, None] + at[None, :] == rows - 1).astype(BF16)
    whole = lambda array: pl.BlockSpec(array.shape, lambda i: (0, 0))
    block = lambda width: pl.BlockSpec((rows, width), lambda i: (i, 0))
    return pl.pallas_call(
        functools.partial(attend_back_kernel, heads, rows),
        grid=(length // rows,),
        in_specs=[
            block(key_width),
            block(key_width),
            whole(keys),
            whole(values),
            whole(rel),
            whole(table),
            whole(flip),
            block(val_width),
            block(val_width),
            pl.BlockSpec((heads, rows, length), lambda i: (0, i, 0)),
        ],
        out_specs=[
            block(key_width),
            pl.BlockSpec((length, key_width), lambda i: (0, 0)),
            pl.BlockSpec((length, val_width), lambda i: (0, 0)),
            pl.BlockSpec((REL, key_width), lambda i: (0, 0)),
            pl.BlockSpec((8, key_width), lambda i: (0, 0)),
        ],
        out_shape=[
            jax.ShapeDtypeStruct((length, key_width), BF16),
            jax.ShapeDtypeStruct((length, key_width), BF16),
            jax.ShapeDtypeStruct((length, val_width), BF16),
            jax.ShapeDtypeStruct((REL, key_width), F32),
            jax.ShapeDtypeStruct((8, key_width), F32),
        ],
        scratch_shapes=[
            pltpu.VMEM((key_width, length), F32),
            pltpu.VMEM((val_width, length), F32),
        ],
        compiler_params=pltpu.CompilerParams(vmem_limit_bytes=VMEM_LIMIT),
        cost_estimate=pl.CostEstimate(
            flops=2 * heads * length * length * 1100,
            bytes_accessed=2 * heads * length * length + 16 * length * val_width,
            transcendentals=0,
        ),
    )(content, position, keys, values, rel, table, flip, mixed, d_mixed, probs)


def norm_parts(rows):
    centre = rows - jnp.mean(rows, axis=-1, keepdims=True)
    spread = jnp.mean(centre * centre, axis=-1, keepdims=True)
    scale = lax.rsqrt(spread + 1e-05)
    return centre * scale, scale


def norm_back(unit, scale, gain, grad):
    scaled = grad * gain
    mean_one = jnp.mean(scaled, axis=-1, keepdims=True)
    mean_two = jnp.mean(scaled * unit, axis=-1, keepdims=True)
    return (scaled - mean_one - unit * mean_two) * scale


def shards(
    seq_count,
    inputs,
    bin_order,
    first_gain,
    first_shift,
    query_weight,
    key_weight,
    value_weight,
    bias_content,
    bias_position,
    relative_weight,
    out_weight,
    bias_out,
    second_gain,
    second_shift,
    inner_weight,
    bias_inner,
    outer_weight,
    bias_outer,
    grad_output,
):
    row_count, width = inputs.shape[1:]
    length = bin_order.shape[1]
    here = lax.axis_index("seq")
    core = lax.axis_index("core")
    row_start = here * row_count
    key_width = query_weight.shape[1] // seq_count
    val_width = value_weight.shape[1] // seq_count
    ff = outer_weight.shape[0] * seq_count

    window = lax.all_gather(inputs[0], "seq", axis=0, tiled=True)

    def by_head(weight):
        return weight.reshape(weight.shape[0], seq_count, -1)

    mine = jnp.concatenate(
        [by_head(query_weight), by_head(key_weight), by_head(value_weight)], axis=2
    ).transpose(1, 0, 2)
    attention_weight = lax.all_to_all(mine, "seq", 0, 0, tiled=True).reshape(width, -1)

    vectors = (
        first_gain,
        first_shift,
        bias_out,
        second_gain,
        second_shift,
        bias_inner,
        bias_outer,
    )
    flat = jnp.concatenate([v for v in vectors] + [relative_weight.reshape(-1)])
    flat = lax.all_gather(flat, "seq", axis=0)
    whole_vectors = []
    at = 0
    for v in vectors:
        whole_vectors.append(flat[:, at : at + v.shape[0]].reshape(-1).astype(F32))
        at += v.shape[0]
    gain_one, shift_one, out_bias, gain_two, shift_two, inner_bias, outer_bias = whole_vectors
    relative_full = flat[:, at:].reshape(REL, -1)
    rel = lax.dynamic_slice_in_dim(relative_full, here * key_width, key_width, 1)

    def by_core(weight):
        half = weight.shape[0] // 2
        return lax.dynamic_slice_in_dim(weight, core * half, half, 0)

    inner_full = lax.all_gather(by_core(inner_weight), ("seq", "core"), axis=0, tiled=True)
    outer_full = lax.all_gather(by_core(outer_weight), ("seq", "core"), axis=0, tiled=True)

    peaks = gamma_peaks(length)
    offsets = jnp.arange(2 * length, dtype=jnp.int32)
    table = relative_basis(offsets - length, length, peaks).astype(BF16).T
    table_back = relative_basis(length - 1 - offsets, length, peaks).astype(BF16)

    order = bin_order[0]
    bins = jnp.arange(length, dtype=jnp.int32)
    placing = (order[:, None] == bins[None, :]).astype(BF16)
    unit, _ = norm_parts(window.astype(F32))
    hidden_one = (unit * gain_one + shift_one).astype(BF16)
    projected = matmul(hidden_one, attention_weight)
    query = projected[:, :key_width] * KEY ** (-0.5)
    in_bins = jnp.concatenate(
        [
            query + bias_content.astype(F32),
            query + bias_position.astype(F32),
            projected[:, key_width:],
        ],
        axis=1,
    ).astype(BF16)
    placed_heads = matmul(placing, in_bins).astype(BF16)
    content = placed_heads[:, :key_width]
    position = placed_heads[:, key_width : 2 * key_width]
    keys = placed_heads[:, 2 * key_width : 3 * key_width]
    values = placed_heads[:, 3 * key_width :]
    mixed, probs = attend(content, position, keys, values, rel, table)
    attended = lax.psum_scatter(
        matmul(mixed, out_weight).astype(BF16), "seq", scatter_dimension=0, tiled=True
    )

    own_order = lax.dynamic_slice_in_dim(order, row_start, row_count, 0)
    own_placing = (own_order[:, None] == bins[None, :]).astype(BF16)
    placed = matmul(own_placing, window)
    residual = placed + attended.astype(F32) + out_bias
    unit_two, scale_two = norm_parts(residual)
    hidden_two = (unit_two * gain_two + shift_two).astype(BF16)
    inner = matmul(hidden_two, inner_full) + inner_bias
    below = 0.5 * (1.0 + lax.erf(inner * (0.5**0.5)))
    slope = below + inner * jnp.exp(-0.5 * inner * inner) * (0.5 / math.pi) ** 0.5
    activated = (inner * below).astype(BF16)
    layer_output = residual + matmul(activated, outer_full) + outer_bias
    grad_rows = grad_output[0]
    grad_float = grad_rows.astype(F32)
    d_inner = (matmul_nt(grad_rows, outer_full) * slope).astype(BF16)
    d_normed_two = matmul_nt(d_inner, inner_full)
    d_residual = grad_float + norm_back(unit_two, scale_two, gain_two, d_normed_two)
    d_mixed_in = d_residual.astype(BF16)
    d_mixed_all = lax.all_gather(d_mixed_in, "seq", axis=0, tiled=True)

    d_attended = matmul_nt(d_mixed_all, out_weight).astype(BF16)
    d_query, d_keys, d_values, d_rel, d_bias = attend_back(
        content, position, keys, values, rel, table_back, mixed, d_attended, probs
    )
    d_heads = jnp.concatenate([d_query, d_keys, d_values], axis=1)
    d_bins = matmul_tn(placing, d_heads).astype(BF16)
    d_normed_one = matmul_nt(d_bins, attention_weight)
    arrived = lax.psum_scatter(
        d_normed_one.astype(BF16), "seq", scatter_dimension=0, tiled=True
    ).astype(F32)
    own_unit, own_scale = norm_parts(inputs[0].astype(F32))
    own_bins = row_start + jnp.arange(row_count, dtype=jnp.int32)
    own_returning = (order[None, :] == own_bins[:, None]).astype(BF16)
    grad_inputs = norm_back(own_unit, own_scale, gain_one, arrived) + matmul(
        own_returning, d_mixed_all
    )

    def spread_ff(grad):
        piece = lax.psum_scatter(
            grad.astype(BF16), ("seq", "core"), scatter_dimension=0, tiled=True
        )
        piece = lax.psum_scatter(piece, "wz", scatter_dimension=0, tiled=True)
        return lax.all_gather(piece, ("core", "wz"), axis=0, tiled=True).astype(F32)

    grad_inner_w = spread_ff(matmul_tn(hidden_two, d_inner))
    grad_outer_w = spread_ff(matmul_tn(activated, grad_rows))
    grad_out_w = matmul_tn(mixed, d_mixed_all).astype(BF16)
    grad_attention = matmul_tn(hidden_one, d_bins).astype(BF16)
    half = row_count // 2
    grad_attention = grad_attention.reshape(seq_count, 2, half, -1)
    grad_attention = lax.psum_scatter(grad_attention, "core", scatter_dimension=1)
    grad_out_w = lax.psum_scatter(grad_out_w, "core", scatter_dimension=0, tiled=True)
    grad_attention, grad_out_w = lax.psum((grad_attention, grad_out_w), "wz")
    grad_attention = lax.all_to_all(grad_attention, "seq", 0, 0, tiled=True)
    grad_attention = lax.all_gather(grad_attention, "core", axis=1, tiled=True)
    grad_out_w = lax.all_gather(grad_out_w, "core", axis=0, tiled=True).astype(F32)
    grad_attention = grad_attention.astype(F32).transpose(1, 0, 2)
    grad_query_w = grad_attention[:, :, :key_width].reshape(row_count, -1)
    grad_key_w = grad_attention[:, :, key_width : 2 * key_width].reshape(row_count, -1)
    grad_value_w = grad_attention[:, :, 2 * key_width :].reshape(row_count, -1)

    sums = (
        jnp.sum(d_normed_one * unit, axis=0),
        jnp.sum(d_normed_one, axis=0),
        jnp.sum(d_mixed_in.astype(F32), axis=0),
        jnp.sum(d_normed_two * unit_two, axis=0),
        jnp.sum(d_normed_two, axis=0),
        jnp.sum(d_inner.astype(F32), axis=0),
        jnp.sum(grad_float, axis=0),
    )
    rel_wide = lax.dynamic_update_slice_in_dim(
        jnp.zeros((REL, key_width * seq_count), F32), d_rel, here * key_width, 1
    )
    bias_wide = lax.dynamic_update_slice_in_dim(
        jnp.zeros((8, key_width * seq_count), F32), d_bias, here * key_width, 1
    )
    sums, rel_wide, bias_wide = lax.psum((sums, rel_wide, bias_wide), ("seq", "wz", "core"))

    def own(vector):
        part = vector.shape[0] // seq_count
        return lax.dynamic_slice_in_dim(vector, here * part, part, 0)

    g_gain_one, g_shift_one, g_out_b, g_gain_two, g_shift_two, g_inner_b, g_outer_b = map(own, sums)
    return (
        layer_output.astype(BF16)[None],
        grad_inputs[None],
        g_gain_one,
        g_shift_one,
        grad_query_w,
        grad_key_w,
        grad_value_w,
        own(bias_wide[0]),
        own(bias_wide[1]),
        own(rel_wide),
        grad_out_w,
        g_out_b,
        g_gain_two,
        g_shift_two,
        grad_inner_w,
        g_inner_b,
        grad_outer_w,
        g_outer_b,
    )


def solution(mesh):
    seq_count = mesh.shape["seq"]
    devices = mesh.devices.reshape(seq_count, -1, 2)
    split_mesh = Mesh(devices, ("seq", "wz", "core"))
    rows = P(("wz", "core"), "seq", None)
    vector = P("seq")
    matrix = P("seq", None)
    weights = (
        vector,
        vector,
        matrix,
        matrix,
        matrix,
        vector,
        vector,
        matrix,
        matrix,
        vector,
        vector,
        vector,
        matrix,
        vector,
        matrix,
        vector,
    )
    return jax.shard_map(
        functools.partial(shards, seq_count),
        mesh=split_mesh,
        in_specs=(rows, P(("wz", "core"), None)) + weights + (rows,),
        out_specs=(rows, rows) + weights,
        check_vma=False,
    )
```

```python
import functools
import math

import jax
import jax.numpy as jnp
from jax import lax
from jax.experimental import pallas as pl
from jax.experimental.pallas import tpu as pltpu
from jax.sharding import Mesh
from jax.sharding import PartitionSpec as P

HEADS = 8
KEY = 64
VAL = 192
REL = 192
BF16 = jnp.bfloat16
F32 = jnp.float32
VMEM_LIMIT = 56 * 2**20


def gamma_profile(distance, window_len, features):
    spread = window_len / (2.0 * features)
    centres = jnp.linspace(window_len / features, window_len, features, dtype=F32)
    concentration = (centres / spread) ** 2
    decay_rate = centres / spread**2
    logged = (concentration - 1.0) * jnp.log(distance) - decay_rate * distance
    logged = logged + concentration * jnp.log(decay_rate) - lax.lgamma(concentration)
    return jnp.exp(logged) + 1e-08


def gamma_peaks(window_len):
    features = REL // 6
    every = jnp.arange(window_len).astype(F32)[:, None]
    return jnp.max(gamma_profile(every, window_len, features), axis=0)


def relative_basis(offsets, window_len, peaks):
    features = REL // 6
    distance = jnp.abs(offsets).astype(F32)[:, None]
    half_life = 2.0 ** jnp.linspace(3.0, math.log2(window_len), features, dtype=F32)
    falloff = jnp.exp(-math.log(2.0) / half_life * distance)
    widths = 2.0 ** jnp.arange(1, features + 1).astype(F32) - 1.0
    inside = jnp.where(widths > distance, 1.0, 0.0).astype(F32)
    bumps = gamma_profile(distance, window_len, features) / peaks
    joined = jnp.concatenate([falloff, inside, bumps], axis=1)
    signs = jnp.sign(offsets).astype(F32)[:, None]
    return jnp.concatenate([joined, signs * joined], axis=1)


def matmul(a, b):
    return lax.dot_general(a, b, (((1,), (0,)), ((), ())), preferred_element_type=F32)


def matmul_nt(a, b):
    return lax.dot_general(a, b, (((1,), (1,)), ((), ())), preferred_element_type=F32)


def matmul_tn(a, b):
    return lax.dot_general(a, b, (((0,), (0,)), ((), ())), preferred_element_type=F32)


def head_part(rows, head):
    lanes = lax.broadcasted_iota(jnp.int32, rows.shape, 1)
    inside = (lanes >= head * KEY) & (lanes < (head + 1) * KEY)
    return jnp.where(inside, rows, jnp.zeros_like(rows))


def attend_kernel(heads, rows, content, position, keys, values, rel, table, mixed, probs):
    length = keys.shape[0]
    start = pl.multiple_of(length - rows - pl.program_id(0) * rows, rows)
    basis = table[:, pl.ds(start, length + rows)]
    parts = []
    for head in range(heads):
        q_basis = matmul_nt(head_part(position[...], head), rel[...]).astype(BF16)
        grid = matmul(q_basis, basis)
        shifted = pltpu.roll(grid, 0, 1, stride=1, stride_axis=0)[:, rows:]
        scores = matmul_nt(head_part(content[...], head), keys[...]) + shifted
        top = jnp.max(scores, axis=1, keepdims=True)
        weights = jnp.exp(scores - top)
        total = jnp.sum(weights, axis=1, keepdims=True)
        prob = (weights * (1.0 / total)).astype(BF16)
        probs[head] = prob
        parts.append(matmul(prob, values[:, head * VAL : (head + 1) * VAL]))
    mixed[...] = jnp.concatenate(parts, axis=1).astype(BF16)


def attend(content, position, keys, values, rel, table):
    length, key_width = keys.shape
    val_width = values.shape[1]
    heads = key_width // KEY
    rows = math.gcd(256, length)
    whole = lambda array: pl.BlockSpec(array.shape, lambda i: (0, 0))
    block = lambda width: pl.BlockSpec((rows, width), lambda i: (i, 0))
    return pl.pallas_call(
        functools.partial(attend_kernel, heads, rows),
        grid=(length // rows,),
        in_specs=[
            block(key_width),
            block(key_width),
            whole(keys),
            whole(values),
            whole(rel),
            whole(table),
        ],
        out_specs=[
            block(val_width),
            pl.BlockSpec((heads, rows, length), lambda i: (0, i, 0)),
        ],
        out_shape=[
            jax.ShapeDtypeStruct((length, val_width), BF16),
            jax.ShapeDtypeStruct((heads, length, length), BF16),
        ],
        compiler_params=pltpu.CompilerParams(vmem_limit_bytes=VMEM_LIMIT),
        cost_estimate=pl.CostEstimate(
            flops=2 * heads * length * length * 512,
            bytes_accessed=2 * heads * length * length + 8 * length * val_width,
            transcendentals=heads * length * length,
        ),
    )(content, position, keys, values, rel, table)


def attend_back_kernel(
    heads,
    rows,
    content,
    position,
    keys,
    values,
    rel,
    table,
    flip,
    mixed,
    d_mixed,
    probs,
    d_query,
    d_keys,
    d_values,
    d_rel,
    d_bias,
    keys_sum,
    values_sum,
):
    length, key_width = keys.shape
    step = pl.program_id(0)

    @pl.when(step == 0)
    def _():
        keys_sum[...] = jnp.zeros_like(keys_sum)
        values_sum[...] = jnp.zeros_like(values_sum)
        d_rel[...] = jnp.zeros_like(d_rel)
        d_bias[...] = jnp.zeros_like(d_bias)

    basis = table[pl.ds(pl.multiple_of(step * rows, rows), length + rows), :]
    d_content = jnp.zeros((rows, key_width), F32)
    d_position = jnp.zeros((rows, key_width), F32)
    blocks = length // rows
    for head in range(heads):
        columns = slice(head * VAL, (head + 1) * VAL)
        d_part = d_mixed[:, columns]
        delta = jnp.sum(
            d_part.astype(F32) * mixed[:, columns].astype(F32), axis=1, keepdims=True
        )
        prob = probs[head]
        values_sum[columns, :] += matmul_tn(d_part, prob)
        d_prob = matmul_nt(d_part, values[:, columns])
        d_score = (prob.astype(F32) * (d_prob - delta)).astype(BF16)
        keys_sum[...] += matmul_tn(head_part(content[...], head), d_score)
        d_content += head_part(matmul(d_score, keys[...]), head)
        turned = [
            matmul(d_score[:, (blocks - 1 - b) * rows : (blocks - b) * rows], flip[...])
            for b in range(blocks)
        ]
        turned = jnp.concatenate(turned + [jnp.zeros((rows, rows), F32)], axis=1)
        d_grid = pltpu.roll(turned, 0, 1, stride=1, stride_axis=0).astype(BF16)
        d_basis = matmul(d_grid, basis).astype(BF16)
        d_position += head_part(matmul(d_basis, rel[...]), head)
        d_rel[...] += matmul_tn(d_basis, head_part(position[...], head))
    d_query[...] = ((d_content + d_position) * KEY ** (-0.5)).astype(BF16)
    d_bias[0:1, :] += jnp.sum(d_content, axis=0, keepdims=True)
    d_bias[1:2, :] += jnp.sum(d_position, axis=0, keepdims=True)

    @pl.when(step == blocks - 1)
    def _():
        d_keys[...] = keys_sum[...].T.astype(BF16)
        d_values[...] = values_sum[...].T.astype(BF16)


def attend_back(content, position, keys, values, rel, table, mixed, d_mixed, probs):
    length, key_width = keys.shape
    val_width = values.shape[1]
    heads = key_width // KEY
    rows = math.gcd(256, length)
    at = jnp.arange(rows)
    flip = (at[:, None] + at[None, :] == rows - 1).astype(BF16)
    whole = lambda array: pl.BlockSpec(array.shape, lambda i: (0, 0))
    block = lambda width: pl.BlockSpec((rows, width), lambda i: (i, 0))
    return pl.pallas_call(
        functools.partial(attend_back_kernel, heads, rows),
        grid=(length // rows,),
        in_specs=[
            block(key_width),
            block(key_width),
            whole(keys),
            whole(values),
            whole(rel),
            whole(table),
            whole(flip),
            block(val_width),
            block(val_width),
            pl.BlockSpec((heads, rows, length), lambda i: (0, i, 0)),
        ],
        out_specs=[
            block(key_width),
            pl.BlockSpec((length, key_width), lambda i: (0, 0)),
            pl.BlockSpec((length, val_width), lambda i: (0, 0)),
            pl.BlockSpec((REL, key_width), lambda i: (0, 0)),
            pl.BlockSpec((8, key_width), lambda i: (0, 0)),
        ],
        out_shape=[
            jax.ShapeDtypeStruct((length, key_width), BF16),
            jax.ShapeDtypeStruct((length, key_width), BF16),
            jax.ShapeDtypeStruct((length, val_width), BF16),
            jax.ShapeDtypeStruct((REL, key_width), F32),
            jax.ShapeDtypeStruct((8, key_width), F32),
        ],
        scratch_shapes=[
            pltpu.VMEM((key_width, length), F32),
            pltpu.VMEM((val_width, length), F32),
        ],
        compiler_params=pltpu.CompilerParams(vmem_limit_bytes=VMEM_LIMIT),
        cost_estimate=pl.CostEstimate(
            flops=2 * heads * length * length * 1100,
            bytes_accessed=2 * heads * length * length + 16 * length * val_width,
            transcendentals=0,
        ),
    )(content, position, keys, values, rel, table, flip, mixed, d_mixed, probs)


def norm_parts(rows):
    centre = rows - jnp.mean(rows, axis=-1, keepdims=True)
    spread = jnp.mean(centre * centre, axis=-1, keepdims=True)
    scale = lax.rsqrt(spread + 1e-05)
    return centre * scale, scale


def norm_back(unit, scale, gain, grad):
    scaled = grad * gain
    mean_one = jnp.mean(scaled, axis=-1, keepdims=True)
    mean_two = jnp.mean(scaled * unit, axis=-1, keepdims=True)
    return (scaled - mean_one - unit * mean_two) * scale


def swap(array, mask, count):
    return lax.ppermute(array, "seq", [(i, i ^ mask) for i in range(count)])


def bit_orders(count):
    bits = [1 << k for k in range(count.bit_length() - 1)]
    return bits, bits[::-1]


def gather_blocks(rows, count):
    half = rows.shape[0] // 2
    sides = []
    for order, part in zip(bit_orders(count), (rows[:half], rows[half:])):
        have = {0: part}
        for bit in order:
            have.update({m ^ bit: swap(have[m], bit, count) for m in sorted(have)})
        sides.append(have)
    return [sides[k][m] for m in range(count) for k in range(2)]


def scatter_sum(blocks, count):
    half = blocks[0].shape[1] // 2
    sides = []
    for k, order in enumerate(bit_orders(count)):
        have = {m: blocks[m][:, k * half : (k + 1) * half] for m in range(count)}
        for bit in order:
            sent = {m: swap(have[m].astype(BF16), bit, count) for m in sorted(have) if m & bit}
            have = {m: have[m] + sent[m | bit].astype(F32) for m in have if not m & bit}
        sides.append(have[0])
    return jnp.concatenate(sides, axis=1)


def shards(
    seq_count,
    win_count,
    inputs,
    bin_order,
    first_gain,
    first_shift,
    query_weight,
    key_weight,
    value_weight,
    bias_content,
    bias_position,
    relative_weight,
    out_weight,
    bias_out,
    second_gain,
    second_shift,
    inner_weight,
    bias_inner,
    outer_weight,
    bias_outer,
    grad_output,
):
    row_count, width = inputs.shape[1:]
    length = bin_order.shape[1]
    here = lax.axis_index("seq")
    core = lax.axis_index("core")
    row_start = here * row_count
    key_width = query_weight.shape[1] // seq_count
    val_width = value_weight.shape[1] // seq_count
    heads_width = 2 * key_width + val_width

    others = [jnp.bitwise_xor(here, m) for m in range(seq_count)]
    along = jnp.concatenate(
        [other * row_count + jnp.arange(row_count, dtype=jnp.int32) for other in others]
    )

    def natural(rows):
        parts = rows.reshape(seq_count, row_count, -1)
        parts = [lax.dynamic_index_in_dim(parts, other, 0) for other in others]
        return jnp.concatenate(parts, axis=0).reshape(rows.shape)

    window = jnp.concatenate(gather_blocks(inputs[0], seq_count), axis=0)

    def by_head(weight):
        return weight.reshape(weight.shape[0], seq_count, -1)

    vectors = (
        first_gain,
        first_shift,
        bias_out,
        second_gain,
        second_shift,
        bias_inner,
        bias_outer,
    )
    vector_size = sum(v.shape[0] for v in vectors)
    rel_size = relative_weight.shape[0] * key_width
    extra_rows = -(-(vector_size + rel_size) // (16 * heads_width)) * 16
    extra = jnp.concatenate(
        [jnp.broadcast_to(v[None], (seq_count, v.shape[0])) for v in vectors]
        + [
            by_head(relative_weight).transpose(1, 0, 2).reshape(seq_count, rel_size),
            jnp.zeros((seq_count, extra_rows * heads_width - vector_size - rel_size), BF16),
        ],
        axis=1,
    ).reshape(seq_count, extra_rows, heads_width)
    mine = jnp.concatenate(
        [by_head(query_weight), by_head(key_weight), by_head(value_weight)], axis=2
    ).transpose(1, 0, 2)
    mine = lax.all_to_all(jnp.concatenate([mine, extra], axis=1), "seq", 0, 0, tiled=True)
    attention_weight = mine[:, :row_count].reshape(width, heads_width)
    flat = mine[:, row_count:].reshape(seq_count, -1)
    whole_vectors = []
    at = 0
    for v in vectors:
        whole_vectors.append(flat[:, at : at + v.shape[0]].reshape(-1).astype(F32))
        at += v.shape[0]
    gain_one, shift_one, out_bias, gain_two, shift_two, inner_bias, outer_bias = whole_vectors
    rel = flat[:, at : at + rel_size].reshape(REL, key_width)

    def by_core(weight):
        half = weight.shape[0] // 2
        return lax.dynamic_slice_in_dim(weight, core * half, half, 0)

    inner_full = lax.all_gather(by_core(inner_weight), ("seq", "core"), axis=0, tiled=True)
    outer_full = lax.all_gather(by_core(outer_weight), ("seq", "core"), axis=0, tiled=True)

    peaks = gamma_peaks(length)
    offsets = jnp.arange(2 * length, dtype=jnp.int32)
    table = relative_basis(offsets - length, length, peaks).astype(BF16).T
    table_back = relative_basis(length - 1 - offsets, length, peaks).astype(BF16)

    order = bin_order[0]
    placing = (order[:, None] == along[None, :]).astype(BF16)
    unit, _ = norm_parts(window.astype(F32))
    hidden_one = (unit * gain_one + shift_one).astype(BF16)
    projected = matmul(hidden_one, attention_weight)
    query = projected[:, :key_width] * KEY ** (-0.5)
    in_bins = jnp.concatenate(
        [
            query + bias_content.astype(F32),
            query + bias_position.astype(F32),
            projected[:, key_width:],
        ],
        axis=1,
    ).astype(BF16)
    placed_heads = matmul(placing, in_bins).astype(BF16)
    content = placed_heads[:, :key_width]
    position = placed_heads[:, key_width : 2 * key_width]
    keys = placed_heads[:, 2 * key_width : 3 * key_width]
    values = placed_heads[:, 3 * key_width :]
    mixed, probs = attend(content, position, keys, values, rel, table)
    mixed_along = natural(mixed).reshape(seq_count, row_count, val_width)
    attended = scatter_sum([matmul(mixed_along[m], out_weight) for m in range(seq_count)], seq_count)

    own_order = lax.dynamic_slice_in_dim(order, row_start, row_count, 0)
    own_placing = (own_order[:, None] == along[None, :]).astype(BF16)
    placed = matmul(own_placing, window)
    residual = placed + attended + out_bias
    unit_two, scale_two = norm_parts(residual)
    hidden_two = (unit_two * gain_two + shift_two).astype(BF16)
    inner = matmul(hidden_two, inner_full) + inner_bias
    below = 0.5 * (1.0 + lax.erf(inner * (0.5**0.5)))
    slope = below + inner * jnp.exp(-0.5 * inner * inner) * (0.5 / math.pi) ** 0.5
    activated = (inner * below).astype(BF16)
    grad_rows = grad_output[0]
    grad_float = grad_rows.astype(F32)
    d_inner = (matmul_nt(grad_rows, outer_full) * slope).astype(BF16)
    d_normed_two = matmul_nt(d_inner, inner_full)
    d_residual = grad_float + norm_back(unit_two, scale_two, gain_two, d_normed_two)
    d_mixed_in = d_residual.astype(BF16)
    d_mixed_all = jnp.concatenate(gather_blocks(d_mixed_in, seq_count), axis=0)
    layer_output = (residual + matmul(activated, outer_full) + outer_bias).astype(BF16)
    grad_inner_w = matmul_tn(hidden_two, d_inner).astype(BF16)
    grad_outer_w = matmul_tn(activated, grad_rows).astype(BF16)

    d_attended = natural(matmul_nt(d_mixed_all, out_weight).astype(BF16))
    d_attended, grad_inner_w, grad_outer_w, layer_output = lax.optimization_barrier(
        (d_attended, grad_inner_w, grad_outer_w, layer_output)
    )
    d_query, d_keys, d_values, d_rel, d_bias = attend_back(
        content, position, keys, values, rel, table_back, mixed, d_attended, probs
    )
    d_heads = jnp.concatenate([d_query, d_keys, d_values], axis=1)
    d_along = matmul_tn(placing, d_heads).astype(BF16)
    d_normed_one = matmul_nt(d_along, attention_weight)
    arrived = scatter_sum(
        [d_normed_one[m * row_count : (m + 1) * row_count] for m in range(seq_count)], seq_count
    )
    own_unit, own_scale = norm_parts(inputs[0].astype(F32))
    own_bins = row_start + jnp.arange(row_count, dtype=jnp.int32)
    order_parts = order.reshape(seq_count, row_count)
    along_order = jnp.concatenate(
        [lax.dynamic_index_in_dim(order_parts, other, 0, keepdims=False) for other in others]
    )
    own_returning = (along_order[None, :] == own_bins[:, None]).astype(BF16)
    grad_inputs = norm_back(own_unit, own_scale, gain_one, arrived) + matmul(
        own_returning, d_mixed_all
    )

    def spread_ff(grad):
        piece = lax.psum_scatter(grad, ("seq", "core"), scatter_dimension=0, tiled=True)
        piece = lax.psum_scatter(piece, "wz", scatter_dimension=0, tiled=True)
        return lax.all_gather(piece, ("core", "wz"), axis=0, tiled=True).astype(F32)

    grad_inner_w = spread_ff(grad_inner_w)
    grad_outer_w = spread_ff(grad_outer_w)
    grad_out_w = matmul_tn(mixed_along.reshape(length, val_width), d_mixed_all).astype(BF16)
    grad_out_w = lax.psum_scatter(grad_out_w, ("core", "wz"), scatter_dimension=0, tiled=True)
    grad_out_w = lax.all_gather(grad_out_w, ("core", "wz"), axis=0, tiled=True).astype(F32)
    grad_attention = matmul_tn(hidden_one, d_along).astype(BF16)

    sums = (
        jnp.sum(d_normed_one * unit, axis=0),
        jnp.sum(d_normed_one, axis=0),
        jnp.sum(d_mixed_in.astype(F32), axis=0),
        jnp.sum(d_normed_two * unit_two, axis=0),
        jnp.sum(d_normed_two, axis=0),
        jnp.sum(d_inner.astype(F32), axis=0),
        jnp.sum(grad_float, axis=0),
    )
    bias_wide = lax.dynamic_update_slice_in_dim(
        jnp.zeros((seq_count, 2 * key_width), F32), d_bias[:2].reshape(1, -1), here, 0
    )
    flat = [v.reshape(seq_count, -1) for v in sums] + [bias_wide, d_rel.reshape(seq_count, -1)]
    flat_size = sum(v.shape[1] for v in flat)
    unit_rows = 16 * win_count
    tail_rows = -(-(row_count + -(-flat_size // heads_width)) // unit_rows) * unit_rows - row_count
    flat.append(jnp.zeros((seq_count, tail_rows * heads_width - flat_size), F32))
    flat = jnp.concatenate(flat, axis=1).astype(BF16).reshape(seq_count, tail_rows, heads_width)
    packed = jnp.concatenate(
        [grad_attention.reshape(seq_count, row_count, heads_width), flat], axis=1
    )
    packed = lax.psum_scatter(packed, ("core", "wz"), scatter_dimension=1, tiled=True)
    packed = lax.all_to_all(packed, "seq", 0, 0, tiled=True)
    packed = lax.all_gather(packed, ("core", "wz"), axis=1, tiled=True)
    grad_attention = packed[:, :row_count].astype(F32).transpose(1, 0, 2)
    grad_query_w = grad_attention[:, :, :key_width].reshape(row_count, -1)
    grad_key_w = grad_attention[:, :, key_width : 2 * key_width].reshape(row_count, -1)
    grad_value_w = grad_attention[:, :, 2 * key_width :].reshape(row_count, -1)
    flat = packed[:, row_count:].astype(F32).reshape(seq_count, -1)
    own_sums = []
    at = 0
    for v in sums:
        size = v.shape[0] // seq_count
        own_sums.append(jnp.sum(flat[:, at : at + size], axis=0))
        at += size
    g_gain_one, g_shift_one, g_out_b, g_gain_two, g_shift_two, g_inner_b, g_outer_b = own_sums
    grad_bias = jnp.sum(flat[:, at : at + 2 * key_width], axis=0)
    at += 2 * key_width
    rel_rows = REL // seq_count
    grad_rel = flat[:, at : at + rel_rows * key_width].reshape(seq_count, rel_rows, key_width)
    grad_rel = grad_rel.transpose(1, 0, 2).reshape(rel_rows, -1)
    return (
        layer_output[None],
        grad_inputs[None],
        g_gain_one,
        g_shift_one,
        grad_query_w,
        grad_key_w,
        grad_value_w,
        grad_bias[:key_width],
        grad_bias[key_width:],
        grad_rel,
        grad_out_w,
        g_out_b,
        g_gain_two,
        g_shift_two,
        grad_inner_w,
        g_inner_b,
        grad_outer_w,
        g_outer_b,
    )


def solution(mesh):
    seq_count = mesh.shape["seq"]
    devices = mesh.devices.reshape(seq_count, -1, 2)
    split_mesh = Mesh(devices, ("seq", "wz", "core"))
    rows = P(("wz", "core"), "seq", None)
    vector = P("seq")
    matrix = P("seq", None)
    weights = (
        vector,
        vector,
        matrix,
        matrix,
        matrix,
        vector,
        vector,
        matrix,
        matrix,
        vector,
        vector,
        vector,
        matrix,
        vector,
        matrix,
        vector,
    )
    return jax.shard_map(
        functools.partial(shards, seq_count, mesh.shape["win"]),
        mesh=split_mesh,
        in_specs=(rows, P(("wz", "core"), None)) + weights + (rows,),
        out_specs=(rows, rows) + weights,
        check_vma=False,
    )
```

```python
import functools
import math

import jax
import jax.numpy as jnp
from jax import lax
from jax.experimental import pallas as pl
from jax.experimental.pallas import tpu as pltpu
from jax.sharding import Mesh
from jax.sharding import PartitionSpec as P

HEADS = 8
KEY = 64
VAL = 192
REL = 192
BF16 = jnp.bfloat16
F32 = jnp.float32
VMEM_LIMIT = 56 * 2**20


def gamma_profile(distance, window_len, features):
    spread = window_len / (2.0 * features)
    centres = jnp.linspace(window_len / features, window_len, features, dtype=F32)
    concentration = (centres / spread) ** 2
    decay_rate = centres / spread**2
    logged = (concentration - 1.0) * jnp.log(distance) - decay_rate * distance
    logged = logged + concentration * jnp.log(decay_rate) - lax.lgamma(concentration)
    return jnp.exp(logged) + 1e-08


def gamma_peaks(window_len):
    features = REL // 6
    every = jnp.arange(window_len).astype(F32)[:, None]
    return jnp.max(gamma_profile(every, window_len, features), axis=0)


def relative_basis(offsets, window_len, peaks):
    features = REL // 6
    distance = jnp.abs(offsets).astype(F32)[:, None]
    half_life = 2.0 ** jnp.linspace(3.0, math.log2(window_len), features, dtype=F32)
    falloff = jnp.exp(-math.log(2.0) / half_life * distance)
    widths = 2.0 ** jnp.arange(1, features + 1).astype(F32) - 1.0
    inside = jnp.where(widths > distance, 1.0, 0.0).astype(F32)
    bumps = gamma_profile(distance, window_len, features) / peaks
    joined = jnp.concatenate([falloff, inside, bumps], axis=1)
    signs = jnp.sign(offsets).astype(F32)[:, None]
    return jnp.concatenate([joined, signs * joined], axis=1)


def matmul(a, b):
    return lax.dot_general(a, b, (((1,), (0,)), ((), ())), preferred_element_type=F32)


def matmul_nt(a, b):
    return lax.dot_general(a, b, (((1,), (1,)), ((), ())), preferred_element_type=F32)


def matmul_tn(a, b):
    return lax.dot_general(a, b, (((0,), (0,)), ((), ())), preferred_element_type=F32)


def head_part(rows, head):
    lanes = lax.broadcasted_iota(jnp.int32, rows.shape, 1)
    inside = (lanes >= head * KEY) & (lanes < (head + 1) * KEY)
    return jnp.where(inside, rows, jnp.zeros_like(rows))


def attend_kernel(heads, rows, content, position, keys, values, rel, table, mixed, probs):
    length = keys.shape[0]
    start = pl.multiple_of(length - rows - pl.program_id(0) * rows, rows)
    basis = table[:, pl.ds(start, length + rows)]
    parts = []
    for head in range(heads):
        q_basis = matmul_nt(head_part(position[...], head), rel[...]).astype(BF16)
        grid = matmul(q_basis, basis)
        shifted = pltpu.roll(grid, 0, 1, stride=1, stride_axis=0)[:, rows:]
        scores = matmul_nt(head_part(content[...], head), keys[...]) + shifted
        top = jnp.max(scores, axis=1, keepdims=True)
        weights = jnp.exp(scores - top)
        total = jnp.sum(weights, axis=1, keepdims=True)
        prob = (weights * (1.0 / total)).astype(BF16)
        probs[head] = prob
        parts.append(matmul(prob, values[:, head * VAL : (head + 1) * VAL]))
    mixed[...] = jnp.concatenate(parts, axis=1).astype(BF16)


def attend(content, position, keys, values, rel, table):
    length, key_width = keys.shape
    val_width = values.shape[1]
    heads = key_width // KEY
    rows = math.gcd(256, length)
    whole = lambda array: pl.BlockSpec(array.shape, lambda i: (0, 0))
    block = lambda width: pl.BlockSpec((rows, width), lambda i: (i, 0))
    return pl.pallas_call(
        functools.partial(attend_kernel, heads, rows),
        grid=(length // rows,),
        in_specs=[
            block(key_width),
            block(key_width),
            whole(keys),
            whole(values),
            whole(rel),
            whole(table),
        ],
        out_specs=[
            block(val_width),
            pl.BlockSpec((heads, rows, length), lambda i: (0, i, 0)),
        ],
        out_shape=[
            jax.ShapeDtypeStruct((length, val_width), BF16),
            jax.ShapeDtypeStruct((heads, length, length), BF16),
        ],
        compiler_params=pltpu.CompilerParams(vmem_limit_bytes=VMEM_LIMIT),
        cost_estimate=pl.CostEstimate(
            flops=2 * heads * length * length * 512,
            bytes_accessed=2 * heads * length * length + 8 * length * val_width,
            transcendentals=heads * length * length,
        ),
    )(content, position, keys, values, rel, table)


def attend_back_kernel(
    heads,
    rows,
    content,
    position,
    keys,
    values,
    rel,
    table,
    flip,
    mixed,
    d_mixed,
    probs,
    d_query,
    d_keys,
    d_values,
    d_rel,
    d_bias,
    keys_sum,
    values_sum,
):
    length, key_width = keys.shape
    step = pl.program_id(0)

    @pl.when(step == 0)
    def _():
        keys_sum[...] = jnp.zeros_like(keys_sum)
        values_sum[...] = jnp.zeros_like(values_sum)
        d_rel[...] = jnp.zeros_like(d_rel)
        d_bias[...] = jnp.zeros_like(d_bias)

    basis = table[pl.ds(pl.multiple_of(step * rows, rows), length + rows), :]
    d_content = jnp.zeros((rows, key_width), F32)
    d_position = jnp.zeros((rows, key_width), F32)
    blocks = length // rows
    for head in range(heads):
        columns = slice(head * VAL, (head + 1) * VAL)
        d_part = d_mixed[:, columns]
        delta = jnp.sum(
            d_part.astype(F32) * mixed[:, columns].astype(F32), axis=1, keepdims=True
        )
        prob = probs[head]
        values_sum[columns, :] += matmul_tn(d_part, prob)
        d_prob = matmul_nt(d_part, values[:, columns])
        d_score = (prob.astype(F32) * (d_prob - delta)).astype(BF16)
        keys_sum[...] += matmul_tn(head_part(content[...], head), d_score)
        d_content += head_part(matmul(d_score, keys[...]), head)
        turned = [
            matmul(d_score[:, (blocks - 1 - b) * rows : (blocks - b) * rows], flip[...])
            for b in range(blocks)
        ]
        turned = jnp.concatenate(turned + [jnp.zeros((rows, rows), F32)], axis=1)
        d_grid = pltpu.roll(turned, 0, 1, stride=1, stride_axis=0).astype(BF16)
        d_basis = matmul(d_grid, basis).astype(BF16)
        d_position += head_part(matmul(d_basis, rel[...]), head)
        d_rel[...] += matmul_tn(d_basis, head_part(position[...], head))
    d_query[...] = ((d_content + d_position) * KEY ** (-0.5)).astype(BF16)
    d_bias[0:1, :] += jnp.sum(d_content, axis=0, keepdims=True)
    d_bias[1:2, :] += jnp.sum(d_position, axis=0, keepdims=True)

    @pl.when(step == blocks - 1)
    def _():
        d_keys[...] = keys_sum[...].T.astype(BF16)
        d_values[...] = values_sum[...].T.astype(BF16)


def attend_back(content, position, keys, values, rel, table, mixed, d_mixed, probs):
    length, key_width = keys.shape
    val_width = values.shape[1]
    heads = key_width // KEY
    rows = math.gcd(256, length)
    at = jnp.arange(rows)
    flip = (at[:, None] + at[None, :] == rows - 1).astype(BF16)
    whole = lambda array: pl.BlockSpec(array.shape, lambda i: (0, 0))
    block = lambda width: pl.BlockSpec((rows, width), lambda i: (i, 0))
    return pl.pallas_call(
        functools.partial(attend_back_kernel, heads, rows),
        grid=(length // rows,),
        in_specs=[
            block(key_width),
            block(key_width),
            whole(keys),
            whole(values),
            whole(rel),
            whole(table),
            whole(flip),
            block(val_width),
            block(val_width),
            pl.BlockSpec((heads, rows, length), lambda i: (0, i, 0)),
        ],
        out_specs=[
            block(key_width),
            pl.BlockSpec((length, key_width), lambda i: (0, 0)),
            pl.BlockSpec((length, val_width), lambda i: (0, 0)),
            pl.BlockSpec((REL, key_width), lambda i: (0, 0)),
            pl.BlockSpec((8, key_width), lambda i: (0, 0)),
        ],
        out_shape=[
            jax.ShapeDtypeStruct((length, key_width), BF16),
            jax.ShapeDtypeStruct((length, key_width), BF16),
            jax.ShapeDtypeStruct((length, val_width), BF16),
            jax.ShapeDtypeStruct((REL, key_width), F32),
            jax.ShapeDtypeStruct((8, key_width), F32),
        ],
        scratch_shapes=[
            pltpu.VMEM((key_width, length), F32),
            pltpu.VMEM((val_width, length), F32),
        ],
        compiler_params=pltpu.CompilerParams(vmem_limit_bytes=VMEM_LIMIT),
        cost_estimate=pl.CostEstimate(
            flops=2 * heads * length * length * 1100,
            bytes_accessed=2 * heads * length * length + 16 * length * val_width,
            transcendentals=0,
        ),
    )(content, position, keys, values, rel, table, flip, mixed, d_mixed, probs)


def norm_parts(rows):
    centre = rows - jnp.mean(rows, axis=-1, keepdims=True)
    spread = jnp.mean(centre * centre, axis=-1, keepdims=True)
    scale = lax.rsqrt(spread + 1e-05)
    return centre * scale, scale


def norm_back(unit, scale, gain, grad):
    scaled = grad * gain
    mean_one = jnp.mean(scaled, axis=-1, keepdims=True)
    mean_two = jnp.mean(scaled * unit, axis=-1, keepdims=True)
    return (scaled - mean_one - unit * mean_two) * scale


def swap(array, mask, count):
    return lax.ppermute(array, "seq", [(i, i ^ mask) for i in range(count)])


def bit_orders(count):
    bits = [1 << k for k in range(count.bit_length() - 1)]
    return bits, bits[::-1]


def gather_blocks(rows, count):
    half = rows.shape[0] // 2
    sides = []
    for order, part in zip(bit_orders(count), (rows[:half], rows[half:])):
        have = {0: part}
        for bit in order:
            have.update({m ^ bit: swap(have[m], bit, count) for m in sorted(have)})
        sides.append(have)
    return [sides[k][m] for m in range(count) for k in range(2)]


def scatter_sum(blocks, count):
    half = blocks[0].shape[1] // 2
    sides = []
    for k, order in enumerate(bit_orders(count)):
        have = {m: blocks[m][:, k * half : (k + 1) * half] for m in range(count)}
        for bit in order:
            sent = {m: swap(have[m].astype(BF16), bit, count) for m in sorted(have) if m & bit}
            have = {m: have[m] + sent[m | bit].astype(F32) for m in have if not m & bit}
        sides.append(have[0])
    return jnp.concatenate(sides, axis=1)


def other_core(array):
    return lax.ppermute(array, "core", [(0, 1), (1, 0)])


def gather_weight(shard, order, count, here, core):
    size = shard.shape[0]
    half = size // 2
    have = {0: lax.dynamic_slice_in_dim(shard, core * half, half, 0)}
    for bit in order:
        have.update({m ^ bit: swap(have[m], bit, count) for m in sorted(have)})
    whole = jnp.zeros((count * size,) + shard.shape[1:], shard.dtype)
    whole = lax.dynamic_update_slice_in_dim(whole, shard, here * size, 0)
    for m in sorted(have):
        if m:
            start = jnp.bitwise_xor(here, m) * size
            both = ((have[m], core), (other_core(have[m]), 1 - core))
            for part, which in both:
                whole = lax.dynamic_update_slice_in_dim(whole, part, start + which * half, 0)
    return whole


def reduce_blocks(blocks, order, count):
    have = dict(enumerate(blocks))
    for bit in order:
        sent = {m: swap(have[m].astype(BF16), bit, count) for m in sorted(have) if m & bit}
        have = {m: have[m] + sent[m | bit].astype(F32) for m in have if not m & bit}
    return have[0]


def shards(
    seq_count,
    win_count,
    inputs,
    bin_order,
    first_gain,
    first_shift,
    query_weight,
    key_weight,
    value_weight,
    bias_content,
    bias_position,
    relative_weight,
    out_weight,
    bias_out,
    second_gain,
    second_shift,
    inner_weight,
    bias_inner,
    outer_weight,
    bias_outer,
    grad_output,
):
    row_count, width = inputs.shape[1:]
    length = bin_order.shape[1]
    here = lax.axis_index("seq")
    core = lax.axis_index("core")
    row_start = here * row_count
    key_width = query_weight.shape[1] // seq_count
    val_width = value_weight.shape[1] // seq_count
    heads_width = 2 * key_width + val_width

    others = [jnp.bitwise_xor(here, m) for m in range(seq_count)]
    along = jnp.concatenate(
        [other * row_count + jnp.arange(row_count, dtype=jnp.int32) for other in others]
    )

    def natural(rows):
        parts = rows.reshape(seq_count, row_count, -1)
        parts = [lax.dynamic_index_in_dim(parts, other, 0) for other in others]
        return jnp.concatenate(parts, axis=0).reshape(rows.shape)

    window = jnp.concatenate(gather_blocks(inputs[0], seq_count), axis=0)

    def by_head(weight):
        return weight.reshape(weight.shape[0], seq_count, -1)

    vectors = (
        first_gain,
        first_shift,
        bias_out,
        second_gain,
        second_shift,
        bias_inner,
        bias_outer,
    )
    vector_size = sum(v.shape[0] for v in vectors)
    rel_size = relative_weight.shape[0] * key_width
    extra_rows = -(-(vector_size + rel_size) // (16 * heads_width)) * 16
    extra = jnp.concatenate(
        [jnp.broadcast_to(v[None], (seq_count, v.shape[0])) for v in vectors]
        + [
            by_head(relative_weight).transpose(1, 0, 2).reshape(seq_count, rel_size),
            jnp.zeros((seq_count, extra_rows * heads_width - vector_size - rel_size), BF16),
        ],
        axis=1,
    ).reshape(seq_count, extra_rows, heads_width)
    mine = jnp.concatenate(
        [by_head(query_weight), by_head(key_weight), by_head(value_weight)], axis=2
    ).transpose(1, 0, 2)
    mine = lax.all_to_all(jnp.concatenate([mine, extra], axis=1), "seq", 0, 0, tiled=True)
    attention_weight = mine[:, :row_count].reshape(width, heads_width)
    flat = mine[:, row_count:].reshape(seq_count, -1)
    whole_vectors = []
    at = 0
    for v in vectors:
        whole_vectors.append(flat[:, at : at + v.shape[0]].reshape(-1).astype(F32))
        at += v.shape[0]
    gain_one, shift_one, out_bias, gain_two, shift_two, inner_bias, outer_bias = whole_vectors
    rel = flat[:, at : at + rel_size].reshape(REL, key_width)

    up, down = bit_orders(seq_count)
    window, inner_shard, outer_shard = lax.optimization_barrier(
        (window, inner_weight, outer_weight)
    )
    inner_full = gather_weight(inner_shard, up, seq_count, here, core)
    outer_full = gather_weight(outer_shard, down, seq_count, here, core)

    peaks = gamma_peaks(length)
    offsets = jnp.arange(2 * length, dtype=jnp.int32)
    table = relative_basis(offsets - length, length, peaks).astype(BF16).T
    table_back = relative_basis(length - 1 - offsets, length, peaks).astype(BF16)

    order = bin_order[0]
    placing = (order[:, None] == along[None, :]).astype(BF16)
    unit, _ = norm_parts(window.astype(F32))
    hidden_one = (unit * gain_one + shift_one).astype(BF16)
    projected = matmul(hidden_one, attention_weight)
    query = projected[:, :key_width] * KEY ** (-0.5)
    in_bins = jnp.concatenate(
        [
            query + bias_content.astype(F32),
            query + bias_position.astype(F32),
            projected[:, key_width:],
        ],
        axis=1,
    ).astype(BF16)
    placed_heads = matmul(placing, in_bins).astype(BF16)
    content = placed_heads[:, :key_width]
    position = placed_heads[:, key_width : 2 * key_width]
    keys = placed_heads[:, 2 * key_width : 3 * key_width]
    values = placed_heads[:, 3 * key_width :]
    mixed, probs = attend(content, position, keys, values, rel, table)
    mixed_along = natural(mixed).reshape(seq_count, row_count, val_width)
    attended = scatter_sum([matmul(mixed_along[m], out_weight) for m in range(seq_count)], seq_count)

    own_order = lax.dynamic_slice_in_dim(order, row_start, row_count, 0)
    own_placing = (own_order[:, None] == along[None, :]).astype(BF16)
    placed = matmul(own_placing, window)
    residual = placed + attended + out_bias
    unit_two, scale_two = norm_parts(residual)
    hidden_two = (unit_two * gain_two + shift_two).astype(BF16)
    inner = matmul(hidden_two, inner_full) + inner_bias
    below = 0.5 * (1.0 + lax.erf(inner * (0.5**0.5)))
    slope = below + inner * jnp.exp(-0.5 * inner * inner) * (0.5 / math.pi) ** 0.5
    activated = (inner * below).astype(BF16)
    grad_rows = grad_output[0]
    grad_float = grad_rows.astype(F32)
    d_inner = (matmul_nt(grad_rows, outer_full) * slope).astype(BF16)
    d_normed_two = matmul_nt(d_inner, inner_full)
    d_residual = grad_float + norm_back(unit_two, scale_two, gain_two, d_normed_two)
    d_mixed_in = d_residual.astype(BF16)
    d_mixed_all = jnp.concatenate(gather_blocks(d_mixed_in, seq_count), axis=0)
    layer_output = (residual + matmul(activated, outer_full) + outer_bias).astype(BF16)

    ff = d_inner.shape[1]
    ff_rows = ff // seq_count
    hidden_along = jnp.concatenate(
        [lax.dynamic_slice_in_dim(hidden_two, o * row_count, row_count, 1) for o in others], axis=1
    )

    def inner_half(which):
        return matmul_tn(hidden_along, lax.dynamic_slice_in_dim(d_inner, which * ff // 2, ff // 2, 1))

    def outer_half(which):
        part = [
            lax.dynamic_slice_in_dim(activated, o * ff_rows + which * ff_rows // 2, ff_rows // 2, 1)
            for o in others
        ]
        return matmul_tn(jnp.concatenate(part, axis=1), grad_rows)

    inner_sent = other_core(inner_half(1 - core).astype(BF16))
    outer_sent = other_core(outer_half(1 - core).astype(BF16))
    grad_inner_w = inner_half(core) + inner_sent.astype(F32)
    grad_outer_w = outer_half(core) + outer_sent.astype(F32)

    d_attended = natural(matmul_nt(d_mixed_all, out_weight).astype(BF16))
    grad_out_w = matmul_tn(mixed_along.reshape(length, val_width), d_mixed_all)
    half = grad_out_w.shape[0] // 2
    out_sent = other_core(
        lax.dynamic_slice_in_dim(grad_out_w, (1 - core) * half, half, 0).astype(BF16)
    )
    grad_out_w = lax.dynamic_slice_in_dim(grad_out_w, core * half, half, 0)
    grad_out_w = grad_out_w + out_sent.astype(F32)
    d_attended, grad_inner_w, grad_outer_w, grad_out_w, layer_output = lax.optimization_barrier(
        (d_attended, grad_inner_w, grad_outer_w, grad_out_w, layer_output)
    )
    grad_inner_w = reduce_blocks(grad_inner_w.reshape(seq_count, row_count, -1), up, seq_count)
    grad_outer_w = reduce_blocks(
        grad_outer_w.reshape(seq_count, ff_rows // 2, -1), down, seq_count
    )
    d_query, d_keys, d_values, d_rel, d_bias = attend_back(
        content, position, keys, values, rel, table_back, mixed, d_attended, probs
    )
    d_heads = jnp.concatenate([d_query, d_keys, d_values], axis=1)
    d_along = matmul_tn(placing, d_heads).astype(BF16)
    d_normed_one = matmul_nt(d_along, attention_weight)
    arrived = scatter_sum(
        [d_normed_one[m * row_count : (m + 1) * row_count] for m in range(seq_count)], seq_count
    )
    own_unit, own_scale = norm_parts(inputs[0].astype(F32))
    own_bins = row_start + jnp.arange(row_count, dtype=jnp.int32)
    order_parts = order.reshape(seq_count, row_count)
    along_order = jnp.concatenate(
        [lax.dynamic_index_in_dim(order_parts, other, 0, keepdims=False) for other in others]
    )
    own_returning = (along_order[None, :] == own_bins[:, None]).astype(BF16)
    grad_inputs = norm_back(own_unit, own_scale, gain_one, arrived) + matmul(
        own_returning, d_mixed_all
    )

    pieces = (grad_inner_w, grad_outer_w, grad_out_w)
    ends = [0]
    for piece in pieces:
        ends.append(ends[-1] + piece.shape[0])
    pieces = jnp.concatenate([piece.astype(BF16) for piece in pieces], axis=0)
    pieces = lax.psum_scatter(pieces, "wz", scatter_dimension=0, tiled=True)
    pieces = lax.all_gather(pieces, ("core", "wz"), axis=0, tiled=True)
    pieces = pieces.reshape(2, ends[-1], -1).astype(F32)
    grad_inner_w, grad_outer_w, grad_out_w = [
        jnp.concatenate([pieces[0, lo:hi], pieces[1, lo:hi]], axis=axis)
        for lo, hi, axis in zip(ends, ends[1:], (1, 0, 0))
    ]
    grad_attention = matmul_tn(hidden_one, d_along).astype(BF16)

    sums = (
        jnp.sum(d_normed_one * unit, axis=0),
        jnp.sum(d_normed_one, axis=0),
        jnp.sum(d_mixed_in.astype(F32), axis=0),
        jnp.sum(d_normed_two * unit_two, axis=0),
        jnp.sum(d_normed_two, axis=0),
        jnp.sum(d_inner.astype(F32), axis=0),
        jnp.sum(grad_float, axis=0),
    )
    bias_wide = lax.dynamic_update_slice_in_dim(
        jnp.zeros((seq_count, 2 * key_width), F32), d_bias[:2].reshape(1, -1), here, 0
    )
    flat = [v.reshape(seq_count, -1) for v in sums] + [bias_wide, d_rel.reshape(seq_count, -1)]
    flat_size = sum(v.shape[1] for v in flat)
    unit_rows = 16 * win_count
    tail_rows = -(-(row_count + -(-flat_size // heads_width)) // unit_rows) * unit_rows - row_count
    flat.append(jnp.zeros((seq_count, tail_rows * heads_width - flat_size), F32))
    flat = jnp.concatenate(flat, axis=1).astype(BF16).reshape(seq_count, tail_rows, heads_width)
    packed = jnp.concatenate(
        [grad_attention.reshape(seq_count, row_count, heads_width), flat], axis=1
    )
    packed = lax.psum_scatter(packed, ("core", "wz"), scatter_dimension=1, tiled=True)
    packed = lax.all_to_all(packed, "seq", 0, 0, tiled=True)
    packed = lax.all_gather(packed, ("core", "wz"), axis=1, tiled=True)
    grad_attention = packed[:, :row_count].astype(F32).transpose(1, 0, 2)
    grad_query_w = grad_attention[:, :, :key_width].reshape(row_count, -1)
    grad_key_w = grad_attention[:, :, key_width : 2 * key_width].reshape(row_count, -1)
    grad_value_w = grad_attention[:, :, 2 * key_width :].reshape(row_count, -1)
    flat = packed[:, row_count:].astype(F32).reshape(seq_count, -1)
    own_sums = []
    at = 0
    for v in sums:
        size = v.shape[0] // seq_count
        own_sums.append(jnp.sum(flat[:, at : at + size], axis=0))
        at += size
    g_gain_one, g_shift_one, g_out_b, g_gain_two, g_shift_two, g_inner_b, g_outer_b = own_sums
    grad_bias = jnp.sum(flat[:, at : at + 2 * key_width], axis=0)
    at += 2 * key_width
    rel_rows = REL // seq_count
    grad_rel = flat[:, at : at + rel_rows * key_width].reshape(seq_count, rel_rows, key_width)
    grad_rel = grad_rel.transpose(1, 0, 2).reshape(rel_rows, -1)
    return (
        layer_output[None],
        grad_inputs[None],
        g_gain_one,
        g_shift_one,
        grad_query_w,
        grad_key_w,
        grad_value_w,
        grad_bias[:key_width],
        grad_bias[key_width:],
        grad_rel,
        grad_out_w,
        g_out_b,
        g_gain_two,
        g_shift_two,
        grad_inner_w,
        g_inner_b,
        grad_outer_w,
        g_outer_b,
    )


def solution(mesh):
    seq_count = mesh.shape["seq"]
    devices = mesh.devices.reshape(seq_count, -1, 2)
    split_mesh = Mesh(devices, ("seq", "wz", "core"))
    rows = P(("wz", "core"), "seq", None)
    vector = P("seq")
    matrix = P("seq", None)
    weights = (
        vector,
        vector,
        matrix,
        matrix,
        matrix,
        vector,
        vector,
        matrix,
        matrix,
        vector,
        vector,
        vector,
        matrix,
        vector,
        matrix,
        vector,
    )
    return jax.shard_map(
        functools.partial(shards, seq_count, mesh.shape["win"]),
        mesh=split_mesh,
        in_specs=(rows, P(("wz", "core"), None)) + weights + (rows,),
        out_specs=(rows, rows) + weights,
        check_vma=False,
    )
```

```python
import functools
import math

import jax
import jax.numpy as jnp
from jax import lax
from jax.experimental import pallas as pl
from jax.experimental.pallas import tpu as pltpu
from jax.sharding import Mesh
from jax.sharding import PartitionSpec as P

HEADS = 8
KEY = 64
VAL = 192
REL = 192
BF16 = jnp.bfloat16
F32 = jnp.float32
VMEM_LIMIT = 56 * 2**20


def gamma_profile(distance, window_len, features):
    spread = window_len / (2.0 * features)
    centres = jnp.linspace(window_len / features, window_len, features, dtype=F32)
    concentration = (centres / spread) ** 2
    decay_rate = centres / spread**2
    logged = (concentration - 1.0) * jnp.log(distance) - decay_rate * distance
    logged = logged + concentration * jnp.log(decay_rate) - lax.lgamma(concentration)
    return jnp.exp(logged) + 1e-08


def gamma_peaks(window_len):
    features = REL // 6
    every = jnp.arange(window_len).astype(F32)[:, None]
    return jnp.max(gamma_profile(every, window_len, features), axis=0)


def relative_basis(offsets, window_len, peaks):
    features = REL // 6
    distance = jnp.abs(offsets).astype(F32)[:, None]
    half_life = 2.0 ** jnp.linspace(3.0, math.log2(window_len), features, dtype=F32)
    falloff = jnp.exp(-math.log(2.0) / half_life * distance)
    widths = 2.0 ** jnp.arange(1, features + 1).astype(F32) - 1.0
    inside = jnp.where(widths > distance, 1.0, 0.0).astype(F32)
    bumps = gamma_profile(distance, window_len, features) / peaks
    joined = jnp.concatenate([falloff, inside, bumps], axis=1)
    signs = jnp.sign(offsets).astype(F32)[:, None]
    return jnp.concatenate([joined, signs * joined], axis=1)


def matmul(a, b):
    return lax.dot_general(a, b, (((1,), (0,)), ((), ())), preferred_element_type=F32)


def matmul_nt(a, b):
    return lax.dot_general(a, b, (((1,), (1,)), ((), ())), preferred_element_type=F32)


def matmul_tn(a, b):
    return lax.dot_general(a, b, (((0,), (0,)), ((), ())), preferred_element_type=F32)


def head_part(rows, head):
    lanes = lax.broadcasted_iota(jnp.int32, rows.shape, 1)
    inside = (lanes >= head * KEY) & (lanes < (head + 1) * KEY)
    return jnp.where(inside, rows, jnp.zeros_like(rows))


def attend_kernel(heads, rows, content, position, keys, values, rel, table, mixed, probs):
    length = keys.shape[0]
    start = pl.multiple_of(length - rows - pl.program_id(0) * rows, rows)
    basis = table[:, pl.ds(start, length + rows)]
    parts = []
    for head in range(heads):
        q_basis = matmul_nt(head_part(position[...], head), rel[...]).astype(BF16)
        grid = matmul(q_basis, basis)
        shifted = pltpu.roll(grid, 0, 1, stride=1, stride_axis=0)[:, rows:]
        scores = matmul_nt(head_part(content[...], head), keys[...]) + shifted
        top = jnp.max(scores, axis=1, keepdims=True)
        weights = jnp.exp(scores - top)
        total = jnp.sum(weights, axis=1, keepdims=True)
        prob = (weights * (1.0 / total)).astype(BF16)
        probs[head] = prob
        parts.append(matmul(prob, values[:, head * VAL : (head + 1) * VAL]))
    mixed[...] = jnp.concatenate(parts, axis=1).astype(BF16)


def attend(content, position, keys, values, rel, table):
    length, key_width = keys.shape
    val_width = values.shape[1]
    heads = key_width // KEY
    rows = math.gcd(256, length)
    whole = lambda array: pl.BlockSpec(array.shape, lambda i: (0, 0))
    block = lambda width: pl.BlockSpec((rows, width), lambda i: (i, 0))
    return pl.pallas_call(
        functools.partial(attend_kernel, heads, rows),
        grid=(length // rows,),
        in_specs=[
            block(key_width),
            block(key_width),
            whole(keys),
            whole(values),
            whole(rel),
            whole(table),
        ],
        out_specs=[
            block(val_width),
            pl.BlockSpec((heads, rows, length), lambda i: (0, i, 0)),
        ],
        out_shape=[
            jax.ShapeDtypeStruct((length, val_width), BF16),
            jax.ShapeDtypeStruct((heads, length, length), BF16),
        ],
        compiler_params=pltpu.CompilerParams(vmem_limit_bytes=VMEM_LIMIT),
        cost_estimate=pl.CostEstimate(
            flops=2 * heads * length * length * 512,
            bytes_accessed=2 * heads * length * length + 8 * length * val_width,
            transcendentals=heads * length * length,
        ),
    )(content, position, keys, values, rel, table)


def attend_back_kernel(
    heads,
    rows,
    content,
    position,
    keys,
    values,
    rel,
    table,
    flip,
    mixed,
    d_mixed,
    probs,
    d_query,
    d_keys,
    d_values,
    d_rel,
    d_bias,
    keys_sum,
    values_sum,
):
    length, key_width = keys.shape
    step = pl.program_id(0)

    @pl.when(step == 0)
    def _():
        keys_sum[...] = jnp.zeros_like(keys_sum)
        values_sum[...] = jnp.zeros_like(values_sum)
        d_rel[...] = jnp.zeros_like(d_rel)
        d_bias[...] = jnp.zeros_like(d_bias)

    basis = table[pl.ds(pl.multiple_of(step * rows, rows), length + rows), :]
    d_content = jnp.zeros((rows, key_width), F32)
    d_position = jnp.zeros((rows, key_width), F32)
    blocks = length // rows
    for head in range(heads):
        columns = slice(head * VAL, (head + 1) * VAL)
        d_part = d_mixed[:, columns]
        delta = jnp.sum(
            d_part.astype(F32) * mixed[:, columns].astype(F32), axis=1, keepdims=True
        )
        prob = probs[head]
        values_sum[columns, :] += matmul_tn(d_part, prob)
        d_prob = matmul_nt(d_part, values[:, columns])
        d_score = (prob.astype(F32) * (d_prob - delta)).astype(BF16)
        keys_sum[...] += matmul_tn(head_part(content[...], head), d_score)
        d_content += head_part(matmul(d_score, keys[...]), head)
        turned = [
            matmul(d_score[:, (blocks - 1 - b) * rows : (blocks - b) * rows], flip[...])
            for b in range(blocks)
        ]
        turned = jnp.concatenate(turned + [jnp.zeros((rows, rows), F32)], axis=1)
        d_grid = pltpu.roll(turned, 0, 1, stride=1, stride_axis=0).astype(BF16)
        d_basis = matmul(d_grid, basis).astype(BF16)
        d_position += head_part(matmul(d_basis, rel[...]), head)
        d_rel[...] += matmul_tn(d_basis, head_part(position[...], head))
    d_query[...] = ((d_content + d_position) * KEY ** (-0.5)).astype(BF16)
    d_bias[0:1, :] += jnp.sum(d_content, axis=0, keepdims=True)
    d_bias[1:2, :] += jnp.sum(d_position, axis=0, keepdims=True)

    @pl.when(step == blocks - 1)
    def _():
        d_keys[...] = keys_sum[...].T.astype(BF16)
        d_values[...] = values_sum[...].T.astype(BF16)


def attend_back(content, position, keys, values, rel, table, mixed, d_mixed, probs):
    length, key_width = keys.shape
    val_width = values.shape[1]
    heads = key_width // KEY
    rows = math.gcd(256, length)
    at = jnp.arange(rows)
    flip = (at[:, None] + at[None, :] == rows - 1).astype(BF16)
    whole = lambda array: pl.BlockSpec(array.shape, lambda i: (0, 0))
    block = lambda width: pl.BlockSpec((rows, width), lambda i: (i, 0))
    return pl.pallas_call(
        functools.partial(attend_back_kernel, heads, rows),
        grid=(length // rows,),
        in_specs=[
            block(key_width),
            block(key_width),
            whole(keys),
            whole(values),
            whole(rel),
            whole(table),
            whole(flip),
            block(val_width),
            block(val_width),
            pl.BlockSpec((heads, rows, length), lambda i: (0, i, 0)),
        ],
        out_specs=[
            block(key_width),
            pl.BlockSpec((length, key_width), lambda i: (0, 0)),
            pl.BlockSpec((length, val_width), lambda i: (0, 0)),
            pl.BlockSpec((REL, key_width), lambda i: (0, 0)),
            pl.BlockSpec((8, key_width), lambda i: (0, 0)),
        ],
        out_shape=[
            jax.ShapeDtypeStruct((length, key_width), BF16),
            jax.ShapeDtypeStruct((length, key_width), BF16),
            jax.ShapeDtypeStruct((length, val_width), BF16),
            jax.ShapeDtypeStruct((REL, key_width), F32),
            jax.ShapeDtypeStruct((8, key_width), F32),
        ],
        scratch_shapes=[
            pltpu.VMEM((key_width, length), F32),
            pltpu.VMEM((val_width, length), F32),
        ],
        compiler_params=pltpu.CompilerParams(vmem_limit_bytes=VMEM_LIMIT),
        cost_estimate=pl.CostEstimate(
            flops=2 * heads * length * length * 1100,
            bytes_accessed=2 * heads * length * length + 16 * length * val_width,
            transcendentals=0,
        ),
    )(content, position, keys, values, rel, table, flip, mixed, d_mixed, probs)


def norm_parts(rows):
    centre = rows - jnp.mean(rows, axis=-1, keepdims=True)
    spread = jnp.mean(centre * centre, axis=-1, keepdims=True)
    scale = lax.rsqrt(spread + 1e-05)
    return centre * scale, scale


def norm_back(unit, scale, gain, grad):
    scaled = grad * gain
    mean_one = jnp.mean(scaled, axis=-1, keepdims=True)
    mean_two = jnp.mean(scaled * unit, axis=-1, keepdims=True)
    return (scaled - mean_one - unit * mean_two) * scale


def swap(array, mask, count):
    return lax.ppermute(array, "seq", [(i, i ^ mask) for i in range(count)])


def bit_orders(count):
    bits = [1 << k for k in range(count.bit_length() - 1)]
    return bits, bits[::-1]


def pin(*arrays):
    return lax.optimization_barrier(arrays)


class Gather:
    def __init__(self, part, order, count):
        self.have, self.order, self.count, self.step = {0: part}, order, count, 0

    def advance(self):
        bit = self.order[self.step]
        self.new = [m ^ bit for m in sorted(self.have)]
        self.have.update({m: swap(self.have[m ^ bit], bit, self.count) for m in self.new})
        self.step += 1

    def newest(self):
        return [self.have[m] for m in self.new]

    def put(self, arrays):
        self.have.update(zip(self.new, arrays))


def pin_gathers(gathers, *arrays):
    news = [g.newest() for g in gathers]
    flat = [block for new in news for block in new]
    out = pin(*arrays, *flat)
    at = len(arrays)
    for g, new in zip(gathers, news):
        g.put(out[at : at + len(new)])
        at += len(new)
    return out[: len(arrays)]


class Scatter:
    def __init__(self, blocks, order, count):
        self.have, self.order, self.count, self.step = dict(enumerate(blocks)), order, count, 0

    def send(self):
        bit = self.order[self.step]
        self.sent = {
            m: swap(self.have[m].astype(BF16), bit, self.count)
            for m in sorted(self.have, reverse=True)
            if m & bit
        }

    def add(self):
        bit = self.order[self.step]
        self.have = {
            m: self.have[m].astype(F32) + self.sent[m | bit].astype(F32)
            for m in self.have
            if not m & bit
        }
        self.step += 1


def split_columns(blocks, count):
    half = blocks[0].shape[1] // 2
    return [
        Scatter([block[:, k * half : (k + 1) * half] for block in blocks], order, count)
        for k, order in enumerate(bit_orders(count))
    ]


def finish(scatters):
    for scatter in scatters:
        while scatter.step < len(scatter.order):
            scatter.send()
            scatter.add()
    return [scatter.have[0] for scatter in scatters]


def other_core(array):
    return lax.ppermute(array, "core", [(0, 1), (1, 0)])


def place_weight(gather, shard, start, here, core):
    size = shard.shape[0]
    half = size // 2
    whole = lax.dynamic_update_slice_in_dim(start, shard, here * size, 0)
    for m, part in sorted(gather.have.items()):
        if m:
            at = jnp.bitwise_xor(here, m) * size
            for rows, which in ((part, core), (other_core(part), 1 - core)):
                whole = lax.dynamic_update_slice_in_dim(whole, rows, at + which * half, 0)
    return whole


def shards(
    seq_count,
    win_count,
    inputs,
    bin_order,
    first_gain,
    first_shift,
    query_weight,
    key_weight,
    value_weight,
    bias_content,
    bias_position,
    relative_weight,
    out_weight,
    bias_out,
    second_gain,
    second_shift,
    inner_weight,
    bias_inner,
    outer_weight,
    bias_outer,
    grad_output,
):
    row_count, width = inputs.shape[1:]
    length = bin_order.shape[1]
    here = lax.axis_index("seq")
    core = lax.axis_index("core")
    row_start = here * row_count
    key_width = query_weight.shape[1] // seq_count
    val_width = value_weight.shape[1] // seq_count
    heads_width = 2 * key_width + val_width

    others = [jnp.bitwise_xor(here, m) for m in range(seq_count)]
    along = jnp.concatenate(
        [other * row_count + jnp.arange(row_count, dtype=jnp.int32) for other in others]
    )

    def natural(rows):
        parts = rows.reshape(seq_count, row_count, -1)
        parts = [lax.dynamic_index_in_dim(parts, other, 0) for other in others]
        return jnp.concatenate(parts, axis=0).reshape(rows.shape)

    up, down = bit_orders(seq_count)

    def halves(rows):
        half = rows.shape[0] // 2
        return [Gather(rows[:half], up, seq_count), Gather(rows[half:], down, seq_count)]

    def joined(gathers):
        return jnp.concatenate([g.have[m] for m in range(seq_count) for g in gathers], axis=0)

    offsets = jnp.arange(2 * length, dtype=jnp.int32)
    window_gathers = halves(inputs[0])
    for g in window_gathers:
        g.advance()
    (offsets,) = pin_gathers(window_gathers, offsets)
    for step in range(1, len(up)):
        for g in window_gathers:
            g.advance()
    window = joined(window_gathers)

    def by_head(weight):
        return weight.reshape(weight.shape[0], seq_count, -1)

    vectors = (
        first_gain,
        first_shift,
        bias_out,
        second_gain,
        second_shift,
        bias_inner,
        bias_outer,
    )
    vector_size = sum(v.shape[0] for v in vectors)
    rel_size = relative_weight.shape[0] * key_width
    extra_rows = -(-(vector_size + rel_size) // (16 * heads_width)) * 16
    extra = jnp.concatenate(
        [jnp.broadcast_to(v[None], (seq_count, v.shape[0])) for v in vectors]
        + [
            by_head(relative_weight).transpose(1, 0, 2).reshape(seq_count, rel_size),
            jnp.zeros((seq_count, extra_rows * heads_width - vector_size - rel_size), BF16),
        ],
        axis=1,
    ).reshape(seq_count, extra_rows, heads_width)
    mine = jnp.concatenate(
        [by_head(query_weight), by_head(key_weight), by_head(value_weight)], axis=2
    ).transpose(1, 0, 2)
    mine = lax.all_to_all(jnp.concatenate([mine, extra], axis=1), "seq", 0, 0, tiled=True)
    attention_weight = mine[:, :row_count].reshape(width, heads_width)
    flat = mine[:, row_count:].reshape(seq_count, -1)
    whole_vectors = []
    at = 0
    for v in vectors:
        whole_vectors.append(flat[:, at : at + v.shape[0]].reshape(-1).astype(F32))
        at += v.shape[0]
    gain_one, shift_one, out_bias, gain_two, shift_two, inner_bias, outer_bias = whole_vectors
    rel = flat[:, at : at + rel_size].reshape(REL, key_width)

    def own_half(weight):
        half = weight.shape[0] // 2
        return lax.dynamic_slice_in_dim(weight, core * half, half, 0)

    inner_part, outer_part = own_half(inner_weight), own_half(outer_weight)
    window, inner_part, outer_part = pin(window, inner_part, outer_part)
    weight_gathers = [
        Gather(inner_part, up, seq_count),
        Gather(outer_part, down, seq_count),
    ]
    for g in weight_gathers:
        g.advance()

    peaks = gamma_peaks(length)
    table = relative_basis(offsets - length, length, peaks).astype(BF16).T
    table_back = relative_basis(length - 1 - offsets, length, peaks).astype(BF16)

    order = bin_order[0]
    placing = (order[:, None] == along[None, :]).astype(BF16)
    unit, _ = norm_parts(window.astype(F32))
    hidden_one = (unit * gain_one + shift_one).astype(BF16)
    projected = matmul(hidden_one, attention_weight)
    query = projected[:, :key_width] * KEY ** (-0.5)
    in_bins = jnp.concatenate(
        [
            query + bias_content.astype(F32),
            query + bias_position.astype(F32),
            projected[:, key_width:],
        ],
        axis=1,
    ).astype(BF16)
    placed_heads = matmul(placing, in_bins).astype(BF16)
    (placed_heads,) = pin_gathers(weight_gathers, placed_heads)
    for step in range(1, len(up)):
        for g in weight_gathers:
            g.advance()
    content = placed_heads[:, :key_width]
    position = placed_heads[:, key_width : 2 * key_width]
    keys = placed_heads[:, 2 * key_width : 3 * key_width]
    values = placed_heads[:, 3 * key_width :]
    mixed, probs = attend(content, position, keys, values, rel, table)
    (mixed,) = pin_gathers(weight_gathers, mixed)
    mixed_along = natural(mixed).reshape(seq_count, row_count, val_width)
    attended = [matmul(mixed_along[m], out_weight) for m in range(seq_count)]
    attended = jnp.concatenate(finish(split_columns(attended, seq_count)), axis=1)
    inner_full, outer_full = [
        place_weight(g, shard, jnp.zeros((seq_count * shard.shape[0], shard.shape[1]), BF16), here, core)
        for g, shard in zip(weight_gathers, (inner_weight, outer_weight))
    ]

    own_order = lax.dynamic_slice_in_dim(order, row_start, row_count, 0)
    own_placing = (own_order[:, None] == along[None, :]).astype(BF16)
    placed = matmul(own_placing, window)
    residual = placed + attended + out_bias
    unit_two, scale_two = norm_parts(residual)
    hidden_two = (unit_two * gain_two + shift_two).astype(BF16)
    inner = matmul(hidden_two, inner_full) + inner_bias
    below = 0.5 * (1.0 + lax.erf(inner * (0.5**0.5)))
    slope = below + inner * jnp.exp(-0.5 * inner * inner) * (0.5 / math.pi) ** 0.5
    activated = (inner * below).astype(BF16)
    grad_rows = grad_output[0]
    grad_float = grad_rows.astype(F32)
    d_inner = (matmul_nt(grad_rows, outer_full) * slope).astype(BF16)
    d_normed_two = matmul_nt(d_inner, inner_full)
    d_residual = grad_float + norm_back(unit_two, scale_two, gain_two, d_normed_two)
    d_mixed_in = d_residual.astype(BF16)
    d_mixed_gathers = halves(d_mixed_in)
    for step in range(len(up)):
        for g in d_mixed_gathers:
            g.advance()
    d_mixed_all = joined(d_mixed_gathers)
    layer_output = (residual + matmul(activated, outer_full) + outer_bias).astype(BF16)

    ff = d_inner.shape[1]
    ff_rows = ff // seq_count
    hidden_along = [
        lax.dynamic_slice_in_dim(hidden_two, o * row_count, row_count, 1) for o in others
    ]

    def inner_columns(which):
        return lax.dynamic_slice_in_dim(d_inner, which * (ff // 2), ff // 2, 1)

    def outer_rows(which):
        return [
            lax.dynamic_slice_in_dim(
                activated, o * ff_rows + which * (ff_rows // 2), ff_rows // 2, 1
            )
            for o in others
        ]

    inner_sent = matmul_tn(jnp.concatenate(hidden_along, axis=1), inner_columns(1 - core))
    inner_sent = other_core(inner_sent.astype(BF16)).reshape(seq_count, row_count, -1)
    outer_sent = matmul_tn(jnp.concatenate(outer_rows(1 - core), axis=1), grad_rows)
    outer_sent = other_core(outer_sent.astype(BF16)).reshape(seq_count, ff_rows // 2, -1)
    inner_kept = inner_columns(core)
    grad_inner_w = [
        (matmul_tn(rows, inner_kept) + inner_sent[m].astype(F32)).astype(BF16)
        for m, rows in enumerate(hidden_along)
    ]
    grad_outer_w = [
        (matmul_tn(rows, grad_rows) + outer_sent[m].astype(F32)).astype(BF16)
        for m, rows in enumerate(outer_rows(core))
    ]
    out = pin(d_mixed_all, *grad_inner_w, *grad_outer_w, layer_output)
    d_mixed_all, layer_output = out[0], out[-1]
    grad_inner_w, grad_outer_w = out[1 : 1 + seq_count], out[1 + seq_count : -1]
    inner_sums = split_columns(grad_inner_w, seq_count)
    outer_sums = split_columns(grad_outer_w, seq_count)

    def over_windows(piece):
        piece = lax.psum_scatter(piece.astype(BF16), "wz", scatter_dimension=0, tiled=True)
        return lax.all_gather(piece, ("core", "wz"), axis=0, tiled=True).astype(F32)

    for g in inner_sums:
        g.send()

    d_attended = natural(matmul_nt(d_mixed_all, out_weight).astype(BF16))
    grad_out_w = matmul_tn(mixed_along.reshape(length, val_width), d_mixed_all)
    half = grad_out_w.shape[0] // 2
    out_sent = other_core(
        lax.dynamic_slice_in_dim(grad_out_w, (1 - core) * half, half, 0).astype(BF16)
    )
    grad_out_w = lax.dynamic_slice_in_dim(grad_out_w, core * half, half, 0)
    grad_out_w = (grad_out_w + out_sent.astype(F32)).astype(BF16)
    d_attended, grad_out_w = pin(d_attended, grad_out_w)
    d_query, d_keys, d_values, d_rel, d_bias = attend_back(
        content, position, keys, values, rel, table_back, mixed, d_attended, probs
    )
    keys_of = [sorted(g.sent) for g in inner_sums]
    out = pin(d_query, d_keys, d_values, *[g.sent[m] for g, ks in zip(inner_sums, keys_of) for m in ks])
    d_query, d_keys, d_values = out[:3]
    at = 3
    for g, ks in zip(inner_sums, keys_of):
        g.sent = dict(zip(ks, out[at : at + len(ks)]))
        at += len(ks)
        g.add()
    grad_inner_w = jnp.concatenate(finish(inner_sums), axis=1)
    for g in outer_sums:
        g.send()
    d_heads = jnp.concatenate([d_query, d_keys, d_values], axis=1)
    d_along = matmul_tn(placing, d_heads).astype(BF16)
    d_normed_one = matmul_nt(d_along, attention_weight)
    arrived = [d_normed_one[m * row_count : (m + 1) * row_count] for m in range(seq_count)]
    arrived = jnp.concatenate(finish(split_columns(arrived, seq_count)), axis=1)
    for g in outer_sums:
        g.add()
    grad_outer_w = jnp.concatenate(finish(outer_sums), axis=1)
    own_unit, own_scale = norm_parts(inputs[0].astype(F32))
    own_bins = row_start + jnp.arange(row_count, dtype=jnp.int32)
    order_parts = order.reshape(seq_count, row_count)
    along_order = jnp.concatenate(
        [lax.dynamic_index_in_dim(order_parts, other, 0, keepdims=False) for other in others]
    )
    own_returning = (along_order[None, :] == own_bins[:, None]).astype(BF16)
    grad_inputs = norm_back(own_unit, own_scale, gain_one, arrived) + matmul(
        own_returning, d_mixed_all
    )

    grad_out_w = over_windows(grad_out_w)
    grad_inner_w = over_windows(grad_inner_w)
    grad_inner_w = jnp.concatenate([grad_inner_w[:row_count], grad_inner_w[row_count:]], axis=1)
    grad_outer_w = over_windows(grad_outer_w)
    grad_attention = matmul_tn(hidden_one, d_along).astype(BF16)

    sums = (
        jnp.sum(d_normed_one * unit, axis=0),
        jnp.sum(d_normed_one, axis=0),
        jnp.sum(d_mixed_in.astype(F32), axis=0),
        jnp.sum(d_normed_two * unit_two, axis=0),
        jnp.sum(d_normed_two, axis=0),
        jnp.sum(d_inner.astype(F32), axis=0),
        jnp.sum(grad_float, axis=0),
    )
    bias_wide = lax.dynamic_update_slice_in_dim(
        jnp.zeros((seq_count, 2 * key_width), F32), d_bias[:2].reshape(1, -1), here, 0
    )
    flat = [v.reshape(seq_count, -1) for v in sums] + [bias_wide, d_rel.reshape(seq_count, -1)]
    flat_size = sum(v.shape[1] for v in flat)
    unit_rows = 16 * win_count
    tail_rows = -(-(row_count + -(-flat_size // heads_width)) // unit_rows) * unit_rows - row_count
    flat.append(jnp.zeros((seq_count, tail_rows * heads_width - flat_size), F32))
    flat = jnp.concatenate(flat, axis=1).astype(BF16).reshape(seq_count, tail_rows, heads_width)
    packed = jnp.concatenate(
        [grad_attention.reshape(seq_count, row_count, heads_width), flat], axis=1
    )
    packed = lax.psum_scatter(packed, ("core", "wz"), scatter_dimension=1, tiled=True)
    packed = lax.all_to_all(packed, "seq", 0, 0, tiled=True)
    packed = lax.all_gather(packed, ("core", "wz"), axis=1, tiled=True)
    grad_attention = packed[:, :row_count].astype(F32).transpose(1, 0, 2)
    grad_query_w = grad_attention[:, :, :key_width].reshape(row_count, -1)
    grad_key_w = grad_attention[:, :, key_width : 2 * key_width].reshape(row_count, -1)
    grad_value_w = grad_attention[:, :, 2 * key_width :].reshape(row_count, -1)
    flat = packed[:, row_count:].astype(F32).reshape(seq_count, -1)
    own_sums = []
    at = 0
    for v in sums:
        size = v.shape[0] // seq_count
        own_sums.append(jnp.sum(flat[:, at : at + size], axis=0))
        at += size
    g_gain_one, g_shift_one, g_out_b, g_gain_two, g_shift_two, g_inner_b, g_outer_b = own_sums
    grad_bias = jnp.sum(flat[:, at : at + 2 * key_width], axis=0)
    at += 2 * key_width
    rel_rows = REL // seq_count
    grad_rel = flat[:, at : at + rel_rows * key_width].reshape(seq_count, rel_rows, key_width)
    grad_rel = grad_rel.transpose(1, 0, 2).reshape(rel_rows, -1)
    return (
        layer_output[None],
        grad_inputs[None],
        g_gain_one,
        g_shift_one,
        grad_query_w,
        grad_key_w,
        grad_value_w,
        grad_bias[:key_width],
        grad_bias[key_width:],
        grad_rel,
        grad_out_w,
        g_out_b,
        g_gain_two,
        g_shift_two,
        grad_inner_w,
        g_inner_b,
        grad_outer_w,
        g_outer_b,
    )


def solution(mesh):
    seq_count = mesh.shape["seq"]
    devices = mesh.devices.reshape(seq_count, -1, 2)
    split_mesh = Mesh(devices, ("seq", "wz", "core"))
    rows = P(("wz", "core"), "seq", None)
    vector = P("seq")
    matrix = P("seq", None)
    weights = (
        vector,
        vector,
        matrix,
        matrix,
        matrix,
        vector,
        vector,
        matrix,
        matrix,
        vector,
        vector,
        vector,
        matrix,
        vector,
        matrix,
        vector,
    )
    return jax.shard_map(
        functools.partial(shards, seq_count, mesh.shape["win"]),
        mesh=split_mesh,
        in_specs=(rows, P(("wz", "core"), None)) + weights + (rows,),
        out_specs=(rows, rows) + weights,
        check_vma=False,
    )
```

```python
import functools
import math

import jax
import jax.numpy as jnp
from jax import lax
from jax.experimental import pallas as pl
from jax.experimental.pallas import tpu as pltpu
from jax.sharding import Mesh
from jax.sharding import PartitionSpec as P

HEADS = 8
KEY = 64
VAL = 192
REL = 192
BF16 = jnp.bfloat16
F32 = jnp.float32
VMEM_LIMIT = 56 * 2**20


def gamma_profile(distance, window_len, features):
    spread = window_len / (2.0 * features)
    centres = jnp.linspace(window_len / features, window_len, features, dtype=F32)
    concentration = (centres / spread) ** 2
    decay_rate = centres / spread**2
    logged = (concentration - 1.0) * jnp.log(distance) - decay_rate * distance
    logged = logged + concentration * jnp.log(decay_rate) - lax.lgamma(concentration)
    return jnp.exp(logged) + 1e-08


def gamma_peaks(window_len):
    features = REL // 6
    every = jnp.arange(window_len).astype(F32)[:, None]
    return jnp.max(gamma_profile(every, window_len, features), axis=0)


def relative_basis(offsets, window_len, peaks):
    features = REL // 6
    distance = jnp.abs(offsets).astype(F32)[:, None]
    half_life = 2.0 ** jnp.linspace(3.0, math.log2(window_len), features, dtype=F32)
    falloff = jnp.exp(-math.log(2.0) / half_life * distance)
    widths = 2.0 ** jnp.arange(1, features + 1).astype(F32) - 1.0
    inside = jnp.where(widths > distance, 1.0, 0.0).astype(F32)
    bumps = gamma_profile(distance, window_len, features) / peaks
    joined = jnp.concatenate([falloff, inside, bumps], axis=1)
    signs = jnp.sign(offsets).astype(F32)[:, None]
    return jnp.concatenate([joined, signs * joined], axis=1)


def matmul(a, b):
    return lax.dot_general(a, b, (((1,), (0,)), ((), ())), preferred_element_type=F32)


def matmul_nt(a, b):
    return lax.dot_general(a, b, (((1,), (1,)), ((), ())), preferred_element_type=F32)


def matmul_tn(a, b):
    return lax.dot_general(a, b, (((0,), (0,)), ((), ())), preferred_element_type=F32)


def head_part(rows, head):
    lanes = lax.broadcasted_iota(jnp.int32, rows.shape, 1)
    inside = (lanes >= head * KEY) & (lanes < (head + 1) * KEY)
    return jnp.where(inside, rows, jnp.zeros_like(rows))


def head_columns(key_width):
    return [slice(k * key_width, (k + 1) * key_width) for k in range(3)]


def attend_kernel(heads, rows, placed, rel, table, mixed, probs):
    length = placed.shape[0]
    key_width = heads * KEY
    content_at, position_at, keys_at = head_columns(key_width)
    first = pl.program_id(0) * rows
    here = pl.ds(pl.multiple_of(first, rows), rows)
    basis = table[:, pl.ds(pl.multiple_of(length - rows - first, rows), length + rows)]
    content, position, keys = placed[here, content_at], placed[here, position_at], placed[:, keys_at]
    parts = []
    for head in range(heads):
        q_basis = matmul_nt(head_part(position, head), rel[...]).astype(BF16)
        grid = matmul(q_basis, basis)
        shifted = pltpu.roll(grid, 0, 1, stride=1, stride_axis=0)[:, rows:]
        scores = matmul_nt(head_part(content, head), keys) + shifted
        top = jnp.max(scores, axis=1, keepdims=True)
        weights = jnp.exp(scores - top)
        total = jnp.sum(weights, axis=1, keepdims=True)
        prob = (weights * (1.0 / total)).astype(BF16)
        probs[head] = prob
        values_at = 3 * key_width + head * VAL
        parts.append(matmul(prob, placed[:, values_at : values_at + VAL]))
    mixed[...] = jnp.concatenate(parts, axis=1).astype(BF16)


def attend(placed, rel, table):
    length = placed.shape[0]
    heads = rel.shape[1] // KEY
    rows = math.gcd(256, length)
    whole = lambda array: pl.BlockSpec(array.shape, lambda i: (0, 0))
    return pl.pallas_call(
        functools.partial(attend_kernel, heads, rows),
        grid=(length // rows,),
        in_specs=[whole(placed), whole(rel), whole(table)],
        out_specs=[
            pl.BlockSpec((rows, heads * VAL), lambda i: (i, 0)),
            pl.BlockSpec((heads, rows, length), lambda i: (0, i, 0)),
        ],
        out_shape=[
            jax.ShapeDtypeStruct((length, heads * VAL), BF16),
            jax.ShapeDtypeStruct((heads, length, length), BF16),
        ],
        compiler_params=pltpu.CompilerParams(vmem_limit_bytes=VMEM_LIMIT),
        cost_estimate=pl.CostEstimate(
            flops=2 * heads * length * length * 1024,
            bytes_accessed=2 * heads * length * length + 8 * length * heads * VAL,
            transcendentals=heads * length * length,
        ),
    )(placed, rel, table)


def attend_back_kernel(
    heads,
    rows,
    placed,
    rel,
    table,
    flip,
    mixed,
    d_mixed,
    probs,
    d_heads,
    d_rel,
    d_bias,
    keys_sum,
    values_sum,
):
    length = placed.shape[0]
    key_width = heads * KEY
    content_at, position_at, keys_at = head_columns(key_width)
    step = pl.program_id(0)

    @pl.when(step == 0)
    def _():
        keys_sum[...] = jnp.zeros_like(keys_sum)
        values_sum[...] = jnp.zeros_like(values_sum)
        d_rel[...] = jnp.zeros_like(d_rel)
        d_bias[...] = jnp.zeros_like(d_bias)

    first = pl.multiple_of(step * rows, rows)
    here = pl.ds(first, rows)
    basis = table[pl.ds(first, length + rows), :]
    content, position, keys = placed[here, content_at], placed[here, position_at], placed[:, keys_at]
    d_content = jnp.zeros((rows, key_width), F32)
    d_position = jnp.zeros((rows, key_width), F32)
    blocks = length // rows
    for head in range(heads):
        columns = slice(head * VAL, (head + 1) * VAL)
        values_at = 3 * key_width + head * VAL
        d_part = d_mixed[:, columns]
        delta = jnp.sum(
            d_part.astype(F32) * mixed[:, columns].astype(F32), axis=1, keepdims=True
        )
        prob = probs[head]
        values_sum[columns, :] += matmul_tn(d_part, prob)
        d_prob = matmul_nt(d_part, placed[:, values_at : values_at + VAL])
        d_score = (prob.astype(F32) * (d_prob - delta)).astype(BF16)
        keys_sum[...] += matmul_tn(head_part(content, head), d_score)
        d_content += head_part(matmul(d_score, keys), head)
        turned = [
            matmul(d_score[:, (blocks - 1 - b) * rows : (blocks - b) * rows], flip[...])
            for b in range(blocks)
        ]
        turned = jnp.concatenate(turned + [jnp.zeros((rows, rows), F32)], axis=1)
        d_grid = pltpu.roll(turned, 0, 1, stride=1, stride_axis=0).astype(BF16)
        d_basis = matmul(d_grid, basis).astype(BF16)
        d_position += head_part(matmul(d_basis, rel[...]), head)
        d_rel[...] += matmul_tn(d_basis, head_part(position, head))
    d_heads[here, :key_width] = ((d_content + d_position) * KEY ** (-0.5)).astype(BF16)
    d_bias[0:1, :] += jnp.sum(d_content, axis=0, keepdims=True)
    d_bias[1:2, :] += jnp.sum(d_position, axis=0, keepdims=True)

    @pl.when(step == blocks - 1)
    def _():
        d_heads[:, key_width : 2 * key_width] = keys_sum[...].T.astype(BF16)
        d_heads[:, 2 * key_width :] = values_sum[...].T.astype(BF16)


def attend_back(placed, rel, table, mixed, d_mixed, probs):
    length = placed.shape[0]
    key_width = rel.shape[1]
    heads = key_width // KEY
    val_width = heads * VAL
    rows = math.gcd(256, length)
    at = jnp.arange(rows)
    flip = (at[:, None] + at[None, :] == rows - 1).astype(BF16)
    whole = lambda shape: pl.BlockSpec(shape, lambda i: (0, 0))
    block = lambda width: pl.BlockSpec((rows, width), lambda i: (i, 0))
    out_shapes = [
        jax.ShapeDtypeStruct((length, 2 * key_width + val_width), BF16),
        jax.ShapeDtypeStruct((REL, key_width), F32),
        jax.ShapeDtypeStruct((8, key_width), F32),
    ]
    return pl.pallas_call(
        functools.partial(attend_back_kernel, heads, rows),
        grid=(length // rows,),
        in_specs=[
            whole(placed.shape),
            whole(rel.shape),
            whole(table.shape),
            whole(flip.shape),
            block(val_width),
            block(val_width),
            pl.BlockSpec((heads, rows, length), lambda i: (0, i, 0)),
        ],
        out_specs=[whole(out.shape) for out in out_shapes],
        out_shape=out_shapes,
        scratch_shapes=[
            pltpu.VMEM((key_width, length), F32),
            pltpu.VMEM((val_width, length), F32),
        ],
        compiler_params=pltpu.CompilerParams(vmem_limit_bytes=VMEM_LIMIT),
        cost_estimate=pl.CostEstimate(
            flops=2 * heads * length * length * 1536,
            bytes_accessed=2 * heads * length * length + 16 * length * val_width,
            transcendentals=0,
        ),
    )(placed, rel, table, flip, mixed, d_mixed, probs)


def norm_parts(rows):
    centre = rows - jnp.mean(rows, axis=-1, keepdims=True)
    spread = jnp.mean(centre * centre, axis=-1, keepdims=True)
    scale = lax.rsqrt(spread + 1e-05)
    return centre * scale, scale


def norm_back(unit, scale, gain, grad):
    scaled = grad * gain
    mean_one = jnp.mean(scaled, axis=-1, keepdims=True)
    mean_two = jnp.mean(scaled * unit, axis=-1, keepdims=True)
    return (scaled - mean_one - unit * mean_two) * scale


def swap(array, mask, count):
    return lax.ppermute(array, "seq", [(i, i ^ mask) for i in range(count)])


def bit_orders(count):
    bits = [1 << k for k in range(count.bit_length() - 1)]
    return bits, bits[::-1]


def pin(*arrays):
    return lax.optimization_barrier(arrays)


class Exchange:
    def __init__(self):
        self.new = {}


def pin_all(exchanges, *arrays):
    keys = [sorted(e.new) for e in exchanges]
    out = pin(*arrays, *[e.new[k] for e, ks in zip(exchanges, keys) for k in ks])
    at = len(arrays)
    for e, ks in zip(exchanges, keys):
        e.new = dict(zip(ks, out[at : at + len(ks)]))
        at += len(ks)
    return out[: len(arrays)]


class Gather(Exchange):
    def __init__(self, part, order, count):
        super().__init__()
        self.have, self.order, self.count, self.step = {0: part}, order, count, 0

    def take(self):
        self.have.update(self.new)
        self.new = {}

    def send(self):
        self.take()
        bit = self.order[self.step]
        self.new = {m ^ bit: swap(self.have[m], bit, self.count) for m in sorted(self.have)}
        self.step += 1


class Scatter(Exchange):
    def __init__(self, blocks, order, count):
        super().__init__()
        self.have, self.order, self.count, self.step = dict(enumerate(blocks)), order, count, 0

    def take(self):
        if self.new:
            bit = self.order[self.step - 1]
            self.have = {
                m: self.have[m].astype(F32) + self.new[m | bit].astype(F32)
                for m in self.have
                if not m & bit
            }
            self.new = {}

    def send(self):
        self.take()
        bit = self.order[self.step]
        self.new = {
            m: swap(self.have[m].astype(BF16), bit, self.count)
            for m in sorted(self.have, reverse=True)
            if m & bit
        }
        self.step += 1

    def rest(self):
        while self.step < len(self.order):
            self.send()
        self.take()
        return self.have[0]


class LineSum(Exchange):
    def __init__(self, piece, count):
        super().__init__()
        self.total, self.count, self.step = piece, count, 0
        self.inward = count // 2 - 1
        self.steps = 2 * self.inward + 1 if count > 1 else 0

    def take(self):
        if self.new:
            at, came = self.step - 1, self.new[0]
            if at <= self.inward:
                self.total = self.total.astype(F32) + came.astype(F32)
            else:
                index = lax.axis_index("wz")
                far = 2 * self.inward - at
                is_target = (index == far) | (index == self.count - 1 - far)
                self.total = jnp.where(is_target, came, self.total)
            self.new = {}

    def send(self):
        self.take()
        last = self.count - 1
        if self.step < self.inward:
            k = self.step
            pairs = [(k, k + 1), (last - k, last - k - 1)]
        elif self.step == self.inward:
            k = self.inward
            pairs = [(k, k + 1), (k + 1, k)]
        else:
            k = 2 * self.inward - self.step
            pairs = [(k + 1, k), (last - k - 1, last - k)]
        self.total = self.total.astype(BF16)
        self.new = {0: lax.ppermute(self.total, "wz", pairs)}
        self.step += 1

    def rest(self):
        while self.step < self.steps:
            self.send()
        self.take()
        return self.total.astype(BF16)


class OtherCore(Exchange):
    def __init__(self, array):
        super().__init__()
        self.new = {0: other_core(array)}


def split_columns(blocks, count):
    half = blocks[0].shape[1] // 2
    return [
        Scatter([block[:, k * half : (k + 1) * half] for block in blocks], order, count)
        for k, order in enumerate(bit_orders(count))
    ]


def other_core(array):
    return lax.ppermute(array, "core", [(0, 1), (1, 0)])


def place_weight(gather, shard, start, here, core):
    size = shard.shape[0]
    half = size // 2
    whole = lax.dynamic_update_slice_in_dim(start, shard, here * size, 0)
    for m, part in sorted(gather.have.items()):
        if m:
            at = jnp.bitwise_xor(here, m) * size
            for rows, which in ((part, core), (other_core(part), 1 - core)):
                whole = lax.dynamic_update_slice_in_dim(whole, rows, at + which * half, 0)
    return whole


def shards(
    seq_count,
    wz_count,
    inputs,
    bin_order,
    first_gain,
    first_shift,
    query_weight,
    key_weight,
    value_weight,
    bias_content,
    bias_position,
    relative_weight,
    out_weight,
    bias_out,
    second_gain,
    second_shift,
    inner_weight,
    bias_inner,
    outer_weight,
    bias_outer,
    grad_output,
):
    row_count, width = inputs.shape[1:]
    length = bin_order.shape[1]
    here = lax.axis_index("seq")
    core = lax.axis_index("core")
    row_start = here * row_count
    key_width = query_weight.shape[1] // seq_count
    val_width = value_weight.shape[1] // seq_count
    heads_width = 2 * key_width + val_width

    others = [jnp.bitwise_xor(here, m) for m in range(seq_count)]
    along = jnp.concatenate(
        [other * row_count + jnp.arange(row_count, dtype=jnp.int32) for other in others]
    )

    def natural(rows):
        parts = rows.reshape(seq_count, row_count, -1)
        parts = [lax.dynamic_index_in_dim(parts, other, 0) for other in others]
        return jnp.concatenate(parts, axis=0).reshape(rows.shape)

    up, down = bit_orders(seq_count)

    def halves(rows):
        half = rows.shape[0] // 2
        return [Gather(rows[:half], up, seq_count), Gather(rows[half:], down, seq_count)]

    def joined(gathers):
        for g in gathers:
            g.take()
        return jnp.concatenate([g.have[m] for m in range(seq_count) for g in gathers], axis=0)

    offsets = jnp.arange(2 * length, dtype=jnp.int32)
    window_gathers = halves(inputs[0])
    for g in window_gathers:
        g.send()
    (offsets,) = pin_all(window_gathers, offsets)
    for step in range(1, len(up)):
        for g in window_gathers:
            g.send()
    window = joined(window_gathers)

    def by_head(weight):
        return weight.reshape(weight.shape[0], seq_count, -1)

    vectors = (
        first_gain,
        first_shift,
        bias_out,
        second_gain,
        second_shift,
        bias_inner,
        bias_outer,
    )
    vector_size = sum(v.shape[0] for v in vectors)
    rel_size = relative_weight.shape[0] * key_width
    extra_rows = -(-(vector_size + rel_size) // (16 * heads_width)) * 16
    extra = jnp.concatenate(
        [jnp.broadcast_to(v[None], (seq_count, v.shape[0])) for v in vectors]
        + [
            by_head(relative_weight).transpose(1, 0, 2).reshape(seq_count, rel_size),
            jnp.zeros((seq_count, extra_rows * heads_width - vector_size - rel_size), BF16),
        ],
        axis=1,
    ).reshape(seq_count, extra_rows, heads_width)
    mine = jnp.concatenate(
        [by_head(query_weight), by_head(key_weight), by_head(value_weight)], axis=2
    ).transpose(1, 0, 2)
    mine = lax.all_to_all(jnp.concatenate([mine, extra], axis=1), "seq", 0, 0, tiled=True)
    attention_weight = mine[:, :row_count].reshape(width, heads_width)
    flat = mine[:, row_count:].reshape(seq_count, -1)
    whole_vectors = []
    at = 0
    for v in vectors:
        whole_vectors.append(flat[:, at : at + v.shape[0]].reshape(-1).astype(F32))
        at += v.shape[0]
    gain_one, shift_one, out_bias, gain_two, shift_two, inner_bias, outer_bias = whole_vectors
    rel = flat[:, at : at + rel_size].reshape(REL, key_width)

    def own_half(weight):
        half = weight.shape[0] // 2
        return lax.dynamic_slice_in_dim(weight, core * half, half, 0)

    inner_part, outer_part = own_half(inner_weight), own_half(outer_weight)
    window, inner_part, outer_part = pin(window, inner_part, outer_part)
    weight_gathers = [
        Gather(inner_part, up, seq_count),
        Gather(outer_part, down, seq_count),
    ]
    for g in weight_gathers:
        g.send()

    peaks = gamma_peaks(length)
    table = relative_basis(offsets - length, length, peaks).astype(BF16).T
    table_back = relative_basis(length - 1 - offsets, length, peaks).astype(BF16)

    order = bin_order[0]
    placing = (order[:, None] == along[None, :]).astype(BF16)
    unit, _ = norm_parts(window.astype(F32))
    hidden_one = (unit * gain_one + shift_one).astype(BF16)
    projected = matmul(hidden_one, attention_weight)
    query = projected[:, :key_width] * KEY ** (-0.5)
    in_bins = jnp.concatenate(
        [
            query + bias_content.astype(F32),
            query + bias_position.astype(F32),
            projected[:, key_width:],
        ],
        axis=1,
    ).astype(BF16)
    placed_heads = matmul(placing, in_bins).astype(BF16)
    (placed_heads,) = pin_all(weight_gathers, placed_heads)
    for step in range(1, len(up)):
        for g in weight_gathers:
            g.send()
    mixed, probs = attend(placed_heads, rel, table)
    (mixed,) = pin_all(weight_gathers, mixed)
    for g in weight_gathers:
        g.take()
    mixed_along = natural(mixed).reshape(seq_count, row_count, val_width)
    attended = [matmul(mixed_along[m], out_weight) for m in range(seq_count)]
    attended = [g.rest() for g in split_columns(attended, seq_count)]
    attended = jnp.concatenate(attended, axis=1)
    inner_full, outer_full = [
        place_weight(g, shard, jnp.zeros((seq_count * shard.shape[0], shard.shape[1]), BF16), here, core)
        for g, shard in zip(weight_gathers, (inner_weight, outer_weight))
    ]

    own_order = lax.dynamic_slice_in_dim(order, row_start, row_count, 0)
    own_placing = (own_order[:, None] == along[None, :]).astype(BF16)
    placed = matmul(own_placing, window)
    residual = placed + attended + out_bias
    unit_two, scale_two = norm_parts(residual)
    hidden_two = (unit_two * gain_two + shift_two).astype(BF16)
    inner = matmul(hidden_two, inner_full) + inner_bias
    below = 0.5 * (1.0 + lax.erf(inner * (0.5**0.5)))
    slope = below + inner * jnp.exp(-0.5 * inner * inner) * (0.5 / math.pi) ** 0.5
    activated = (inner * below).astype(BF16)
    grad_rows = grad_output[0]
    grad_float = grad_rows.astype(F32)
    d_inner = (matmul_nt(grad_rows, outer_full) * slope).astype(BF16)
    d_normed_two = matmul_nt(d_inner, inner_full)
    d_residual = grad_float + norm_back(unit_two, scale_two, gain_two, d_normed_two)
    d_mixed_in = d_residual.astype(BF16)
    ff = d_inner.shape[1]
    ff_rows = ff // seq_count
    hidden_along = jnp.concatenate(
        [lax.dynamic_slice_in_dim(hidden_two, o * row_count, row_count, 1) for o in others], axis=1
    )

    def inner_half(which):
        return matmul_tn(
            hidden_along, lax.dynamic_slice_in_dim(d_inner, which * (ff // 2), ff // 2, 1)
        )

    def outer_half(which):
        rows = [
            lax.dynamic_slice_in_dim(
                activated, o * ff_rows + which * (ff_rows // 2), ff_rows // 2, 1
            )
            for o in others
        ]
        return matmul_tn(jnp.concatenate(rows, axis=1), grad_rows)

    d_mixed_gathers = halves(d_mixed_in)
    for g in d_mixed_gathers:
        g.send()
    inner_away = inner_half(1 - core).astype(BF16)
    outer_away = outer_half(1 - core).astype(BF16)
    inner_away, outer_away = pin_all(d_mixed_gathers, inner_away, outer_away)
    for step in range(1, len(up)):
        for g in d_mixed_gathers:
            g.send()
    ff_core = [OtherCore(inner_away), OtherCore(outer_away)]
    layer_output = (residual + matmul(activated, outer_full) + outer_bias).astype(BF16)
    (layer_output,) = pin_all(ff_core, layer_output)
    grad_inner_w = (inner_half(core) + ff_core[0].new[0].astype(F32)).astype(BF16)
    grad_outer_w = (outer_half(core) + ff_core[1].new[0].astype(F32)).astype(BF16)
    grad_inner_w, grad_outer_w = pin_all(d_mixed_gathers, grad_inner_w, grad_outer_w)
    d_mixed_all = joined(d_mixed_gathers)

    def row_blocks(rows):
        return list(rows.reshape(seq_count, rows.shape[0] // seq_count, -1))

    inner_sums = split_columns(row_blocks(grad_inner_w), seq_count)
    outer_sums = split_columns(row_blocks(grad_outer_w), seq_count)
    for g in inner_sums:
        g.send()

    d_attended = natural(matmul_nt(d_mixed_all, out_weight).astype(BF16))
    grad_out_w = matmul_tn(mixed_along.reshape(length, val_width), d_mixed_all)
    half = grad_out_w.shape[0] // 2
    out_core = OtherCore(
        lax.dynamic_slice_in_dim(grad_out_w, (1 - core) * half, half, 0).astype(BF16)
    )
    grad_out_w = lax.dynamic_slice_in_dim(grad_out_w, core * half, half, 0)
    d_heads, d_rel, d_bias = attend_back(placed_heads, rel, table_back, mixed, d_attended, probs)
    (d_heads,) = pin_all(inner_sums + [out_core], d_heads)
    out_line = LineSum(grad_out_w + out_core.new[0].astype(F32), wz_count)
    out_line.send()
    inner_lines = []
    for step in range(1, len(up)):
        for g in inner_sums:
            g.send()
    for g in outer_sums:
        g.send()
    d_along = matmul_tn(placing, d_heads).astype(BF16)
    grad_attention = matmul_tn(hidden_one, d_along).astype(BF16)
    d_along, grad_attention = pin_all(inner_sums + [out_line], d_along, grad_attention)
    inner_lines = [LineSum(g.rest(), wz_count) for g in inner_sums]
    for g in inner_lines + [out_line]:
        g.send()
    d_normed_one = matmul_nt(d_along, attention_weight)

    sums = (
        jnp.sum(d_normed_one * unit, axis=0),
        jnp.sum(d_normed_one, axis=0),
        jnp.sum(d_mixed_in.astype(F32), axis=0),
        jnp.sum(d_normed_two * unit_two, axis=0),
        jnp.sum(d_normed_two, axis=0),
        jnp.sum(d_inner.astype(F32), axis=0),
        jnp.sum(grad_float, axis=0),
    )
    bias_wide = lax.dynamic_update_slice_in_dim(
        jnp.zeros((seq_count, 2 * key_width), F32), d_bias[:2].reshape(1, -1), here, 0
    )
    flat = [v.reshape(seq_count, -1) for v in sums] + [bias_wide, d_rel.reshape(seq_count, -1)]
    flat_size = sum(v.shape[1] for v in flat)
    tail_rows = -(-(row_count + -(-flat_size // heads_width)) // 32) * 32 - row_count
    flat.append(jnp.zeros((seq_count, tail_rows * heads_width - flat_size), F32))
    flat = jnp.concatenate(flat, axis=1).astype(BF16).reshape(seq_count, tail_rows, heads_width)
    packed = jnp.concatenate(
        [grad_attention.reshape(seq_count, row_count, heads_width), flat], axis=1
    )
    half = packed.shape[1] // 2
    packed_away = lax.dynamic_slice_in_dim(packed, (1 - core) * half, half, 1)
    packed = lax.dynamic_slice_in_dim(packed, core * half, half, 1)
    arrived = [block.astype(F32) for block in row_blocks(d_normed_one)]
    arrived = split_columns([block.astype(BF16) for block in arrived], seq_count)
    flat_have = [g.have[m] for g in arrived for m in range(seq_count)]
    out = pin_all(outer_sums, packed, packed_away, *flat_have)
    packed, packed_away = out[:2]
    for k, g in enumerate(arrived):
        g.have = dict(enumerate(out[2 + k * seq_count : 2 + (k + 1) * seq_count]))
    for step in range(1, len(up)):
        for g in outer_sums:
            g.send()
    packed_core = OtherCore(packed_away)
    for g in arrived:
        g.send()
    (packed,) = pin_all(outer_sums + inner_lines + [packed_core, out_line], packed)
    outer_lines = [LineSum(g.rest(), wz_count) for g in outer_sums]
    for g in outer_lines + inner_lines + [out_line]:
        g.send()
    packed = (packed.astype(F32) + packed_core.new[0].astype(F32)).astype(BF16)
    packed = lax.all_to_all(packed, "seq", 0, 0, tiled=True)
    (packed,) = pin_all(arrived + inner_lines, packed)
    for step in range(1, len(up)):
        for g in arrived:
            g.send()
    for g in inner_lines:
        g.send()
    packed_lines = [
        LineSum(packed[: seq_count // 2], wz_count),
        LineSum(packed[seq_count // 2 :], wz_count),
    ]
    for g in packed_lines:
        g.send()
    pin_all(arrived + outer_lines)
    arrived = jnp.concatenate([g.rest() for g in arrived], axis=1)
    own_unit, own_scale = norm_parts(inputs[0].astype(F32))
    own_bins = row_start + jnp.arange(row_count, dtype=jnp.int32)
    order_parts = order.reshape(seq_count, row_count)
    along_order = jnp.concatenate(
        [lax.dynamic_index_in_dim(order_parts, other, 0, keepdims=False) for other in others]
    )
    own_returning = (along_order[None, :] == own_bins[:, None]).astype(BF16)
    grad_inputs = norm_back(own_unit, own_scale, gain_one, arrived) + matmul(
        own_returning, d_mixed_all
    )

    first = core == 0

    def by_cores(piece):
        other = other_core(piece)
        return jnp.where(first, piece, other), jnp.where(first, other, piece)

    inner_parts = [by_cores(g.rest()) for g in inner_lines]
    grad_inner_w = jnp.concatenate(
        [part[k] for k in range(2) for part in inner_parts], axis=1
    ).astype(F32)
    outer_parts = [jnp.concatenate(by_cores(g.rest()), axis=0) for g in outer_lines]
    grad_outer_w = jnp.concatenate(outer_parts, axis=1).astype(F32)
    grad_out_w = jnp.concatenate(by_cores(out_line.rest()), axis=0).astype(F32)
    packed_parts = [jnp.concatenate(by_cores(g.rest()), axis=1) for g in packed_lines]
    packed = jnp.concatenate(packed_parts, axis=0)
    grad_attention = packed[:, :row_count].astype(F32).transpose(1, 0, 2)
    grad_query_w = grad_attention[:, :, :key_width].reshape(row_count, -1)
    grad_key_w = grad_attention[:, :, key_width : 2 * key_width].reshape(row_count, -1)
    grad_value_w = grad_attention[:, :, 2 * key_width :].reshape(row_count, -1)
    flat = packed[:, row_count:].astype(F32).reshape(seq_count, -1)
    own_sums = []
    at = 0
    for v in sums:
        size = v.shape[0] // seq_count
        own_sums.append(jnp.sum(flat[:, at : at + size], axis=0))
        at += size
    g_gain_one, g_shift_one, g_out_b, g_gain_two, g_shift_two, g_inner_b, g_outer_b = own_sums
    grad_bias = jnp.sum(flat[:, at : at + 2 * key_width], axis=0)
    at += 2 * key_width
    rel_rows = REL // seq_count
    grad_rel = flat[:, at : at + rel_rows * key_width].reshape(seq_count, rel_rows, key_width)
    grad_rel = grad_rel.transpose(1, 0, 2).reshape(rel_rows, -1)
    return (
        layer_output[None],
        grad_inputs[None],
        g_gain_one,
        g_shift_one,
        grad_query_w,
        grad_key_w,
        grad_value_w,
        grad_bias[:key_width],
        grad_bias[key_width:],
        grad_rel,
        grad_out_w,
        g_out_b,
        g_gain_two,
        g_shift_two,
        grad_inner_w,
        g_inner_b,
        grad_outer_w,
        g_outer_b,
    )


def solution(mesh):
    seq_count = mesh.shape["seq"]
    devices = mesh.devices.reshape(seq_count, -1, 2)
    split_mesh = Mesh(devices, ("seq", "wz", "core"))
    rows = P(("wz", "core"), "seq", None)
    vector = P("seq")
    matrix = P("seq", None)
    weights = (
        vector,
        vector,
        matrix,
        matrix,
        matrix,
        vector,
        vector,
        matrix,
        matrix,
        vector,
        vector,
        vector,
        matrix,
        vector,
        matrix,
        vector,
    )
    return jax.shard_map(
        functools.partial(shards, seq_count, mesh.shape["win"] // 2),
        mesh=split_mesh,
        in_specs=(rows, P(("wz", "core"), None)) + weights + (rows,),
        out_specs=(rows, rows) + weights,
        check_vma=False,
    )
```

```python
import functools
import math

import jax
import jax.numpy as jnp
import numpy as np
from jax import lax
from jax.experimental import pallas as pl
from jax.experimental.pallas import tpu as pltpu
from jax.sharding import Mesh
from jax.sharding import PartitionSpec as P

HEADS = 8
KEY = 64
VAL = 192
REL = 192
BF16 = jnp.bfloat16
F32 = jnp.float32
VMEM_LIMIT = 56 * 2**20
EXTRA = 32


def matmul(a, b):
    return lax.dot_general(a, b, (((1,), (0,)), ((), ())), preferred_element_type=F32)


def matmul_nt(a, b):
    return lax.dot_general(a, b, (((1,), (1,)), ((), ())), preferred_element_type=F32)


def matmul_tn(a, b):
    return lax.dot_general(a, b, (((0,), (0,)), ((), ())), preferred_element_type=F32)


def head_part(rows, head):
    lanes = lax.broadcasted_iota(jnp.int32, rows.shape, 1)
    inside = (lanes >= head * KEY) & (lanes < (head + 1) * KEY)
    return jnp.where(inside, rows, jnp.zeros_like(rows))


def head_columns(key_width):
    return [slice(k * key_width, (k + 1) * key_width) for k in range(3)]


def attend_kernel(heads, rows, placed, rel, table, mixed, probs):
    length = placed.shape[0]
    key_width = heads * KEY
    content_at, position_at, keys_at = head_columns(key_width)
    first = pl.program_id(0) * rows
    here = pl.ds(pl.multiple_of(first, rows), rows)
    basis = table[:, pl.ds(pl.multiple_of(length - rows - first, rows), length + rows)]
    content, position, keys = placed[here, content_at], placed[here, position_at], placed[:, keys_at]
    parts = []
    for head in range(heads):
        q_basis = matmul_nt(head_part(position, head), rel[...]).astype(BF16)
        grid = matmul(q_basis, basis)
        shifted = pltpu.roll(grid, 0, 1, stride=1, stride_axis=0)[:, rows:]
        scores = matmul_nt(head_part(content, head), keys) + shifted
        top = jnp.max(scores, axis=1, keepdims=True)
        weights = jnp.exp(scores - top)
        total = jnp.sum(weights, axis=1, keepdims=True)
        prob = (weights * (1.0 / total)).astype(BF16)
        probs[head] = prob
        values_at = 3 * key_width + head * VAL
        parts.append(matmul(prob, placed[:, values_at : values_at + VAL]))
    mixed[...] = jnp.concatenate(parts, axis=1).astype(BF16)


def attend(placed, rel, table):
    length = placed.shape[0]
    heads = rel.shape[1] // KEY
    rows = math.gcd(256, length)
    whole = lambda array: pl.BlockSpec(array.shape, lambda i: (0, 0))
    return pl.pallas_call(
        functools.partial(attend_kernel, heads, rows),
        grid=(length // rows,),
        in_specs=[whole(placed), whole(rel), whole(table)],
        out_specs=[
            pl.BlockSpec((rows, heads * VAL), lambda i: (i, 0)),
            pl.BlockSpec((heads, rows, length), lambda i: (0, i, 0)),
        ],
        out_shape=[
            jax.ShapeDtypeStruct((length, heads * VAL), BF16),
            jax.ShapeDtypeStruct((heads, length, length), BF16),
        ],
        compiler_params=pltpu.CompilerParams(vmem_limit_bytes=VMEM_LIMIT),
        cost_estimate=pl.CostEstimate(
            flops=2 * heads * length * length * 1024,
            bytes_accessed=2 * heads * length * length + 8 * length * heads * VAL,
            transcendentals=heads * length * length,
        ),
    )(placed, rel, table)


def attend_back_kernel(
    heads,
    rows,
    placed,
    rel,
    table,
    flip,
    mixed,
    d_mixed,
    probs,
    d_heads,
    d_rel,
    d_bias,
    keys_sum,
    values_sum,
):
    length = placed.shape[0]
    key_width = heads * KEY
    content_at, position_at, keys_at = head_columns(key_width)
    step = pl.program_id(0)

    @pl.when(step == 0)
    def _():
        keys_sum[...] = jnp.zeros_like(keys_sum)
        values_sum[...] = jnp.zeros_like(values_sum)
        d_rel[...] = jnp.zeros_like(d_rel)
        d_bias[...] = jnp.zeros_like(d_bias)

    first = pl.multiple_of(step * rows, rows)
    here = pl.ds(first, rows)
    basis = table[:, pl.ds(first, length + rows)]
    content, position, keys = placed[here, content_at], placed[here, position_at], placed[:, keys_at]
    d_content = jnp.zeros((rows, key_width), F32)
    d_position = jnp.zeros((rows, key_width), F32)
    blocks = length // rows
    for head in range(heads):
        columns = slice(head * VAL, (head + 1) * VAL)
        values_at = 3 * key_width + head * VAL
        d_part = d_mixed[:, columns]
        delta = jnp.sum(
            d_part.astype(F32) * mixed[:, columns].astype(F32), axis=1, keepdims=True
        )
        prob = probs[head]
        values_sum[columns, :] += matmul_tn(d_part, prob)
        d_prob = matmul_nt(d_part, placed[:, values_at : values_at + VAL])
        d_score = (prob.astype(F32) * (d_prob - delta)).astype(BF16)
        keys_sum[...] += matmul_tn(head_part(content, head), d_score)
        d_content += head_part(matmul(d_score, keys), head)
        turned = [
            matmul(d_score[:, (blocks - 1 - b) * rows : (blocks - b) * rows], flip[...])
            for b in range(blocks)
        ]
        turned = jnp.concatenate(turned + [jnp.zeros((rows, rows), F32)], axis=1)
        d_grid = pltpu.roll(turned, 0, 1, stride=1, stride_axis=0).astype(BF16)
        d_basis = matmul_nt(d_grid, basis).astype(BF16)
        d_position += head_part(matmul(d_basis, rel[...]), head)
        d_rel[...] += matmul_tn(d_basis, head_part(position, head))
    d_heads[here, :key_width] = ((d_content + d_position) * KEY ** (-0.5)).astype(BF16)
    d_bias[0:1, :] += jnp.sum(d_content, axis=0, keepdims=True)
    d_bias[1:2, :] += jnp.sum(d_position, axis=0, keepdims=True)

    @pl.when(step == blocks - 1)
    def _():
        d_heads[:, key_width : 2 * key_width] = keys_sum[...].T.astype(BF16)
        d_heads[:, 2 * key_width :] = values_sum[...].T.astype(BF16)


def attend_back(placed, rel, table, mixed, d_mixed, probs):
    length = placed.shape[0]
    key_width = rel.shape[1]
    heads = key_width // KEY
    val_width = heads * VAL
    rows = math.gcd(256, length)
    at = jnp.arange(rows)
    flip = (at[:, None] + at[None, :] == rows - 1).astype(BF16)
    whole = lambda shape: pl.BlockSpec(shape, lambda i: (0, 0))
    block = lambda width: pl.BlockSpec((rows, width), lambda i: (i, 0))
    out_shapes = [
        jax.ShapeDtypeStruct((length, 2 * key_width + val_width), BF16),
        jax.ShapeDtypeStruct((REL, key_width), F32),
        jax.ShapeDtypeStruct((8, key_width), F32),
    ]
    return pl.pallas_call(
        functools.partial(attend_back_kernel, heads, rows),
        grid=(length // rows,),
        in_specs=[
            whole(placed.shape),
            whole(rel.shape),
            whole(table.shape),
            whole(flip.shape),
            block(val_width),
            block(val_width),
            pl.BlockSpec((heads, rows, length), lambda i: (0, i, 0)),
        ],
        out_specs=[whole(out.shape) for out in out_shapes],
        out_shape=out_shapes,
        scratch_shapes=[
            pltpu.VMEM((key_width, length), F32),
            pltpu.VMEM((val_width, length), F32),
        ],
        compiler_params=pltpu.CompilerParams(vmem_limit_bytes=VMEM_LIMIT),
        cost_estimate=pl.CostEstimate(
            flops=2 * heads * length * length * 1536,
            bytes_accessed=2 * heads * length * length + 16 * length * val_width,
            transcendentals=0,
        ),
    )(placed, rel, table, flip, mixed, d_mixed, probs)


def norm_back(unit, scale, gain, grad):
    scaled = grad * gain
    mean_one = jnp.mean(scaled, axis=-1, keepdims=True)
    mean_two = jnp.mean(scaled * unit, axis=-1, keepdims=True)
    return (scaled - mean_one - unit * mean_two) * scale


def whole_spec(array):
    zeros = (0,) * len(array.shape)
    return pl.BlockSpec(array.shape, lambda *_: zeros)


def scalar_spec():
    return pl.BlockSpec(memory_space=pltpu.SMEM)


def params(**more):
    return pltpu.CompilerParams(vmem_limit_bytes=VMEM_LIMIT, **more)


def shape(dims, dtype):
    return jax.ShapeDtypeStruct(tuple(dims), dtype)


def basis_constants(window_len):
    features = REL // 6
    f = np.arange(features, dtype=np.float64)
    half_life = 2.0 ** (3.0 + f * (math.log2(window_len) - 3.0) / (features - 1))
    spread = window_len / (2.0 * features)
    first = window_len / features
    centres = first + f * (window_len - first) / (features - 1)
    concentration = (centres / spread) ** 2
    rate = centres / spread**2
    offset = concentration * np.log(rate) - np.array([math.lgamma(c) for c in concentration])
    columns = [math.log(2.0) / half_life, 2.0 ** (f + 1) - 1.0, concentration - 1.0, rate, offset]
    columns += [np.zeros(features)] * 3
    return np.stack(columns, axis=1).astype(np.float32)


def table_kernel(length, constants, forth, back):
    features = REL // 6
    decay, inside_below, power, rate, offset = [constants[:, k : k + 1] for k in range(5)]

    def gamma(distance):
        logged = power * jnp.log(jnp.maximum(distance, 1.0)) - rate * distance + offset
        return jnp.where(distance == 0.0, 0.0, jnp.exp(logged)) + 1e-08

    every = lax.broadcasted_iota(jnp.int32, (1, length), 1).astype(F32)
    peak = jnp.max(gamma(every), axis=1, keepdims=True)
    lanes = lax.broadcasted_iota(jnp.int32, (1, 2 * length), 1).astype(F32)
    for table, signed in ((forth, lanes - length), (back, length - 1 - lanes)):
        distance = jnp.abs(signed)
        sign = jnp.where(signed > 0, 1.0, jnp.where(signed < 0, -1.0, 0.0))
        parts = (
            jnp.exp(-decay * distance),
            jnp.where(inside_below > distance, 1.0, 0.0),
            gamma(distance) / peak,
        )
        for k, part in enumerate(parts):
            table[k * features : (k + 1) * features, :] = part.astype(BF16)
            table[(3 + k) * features : (4 + k) * features, :] = (sign * part).astype(BF16)


def basis_tables(constants, length):
    out = shape((REL, 2 * length), BF16)
    return pl.pallas_call(
        functools.partial(table_kernel, length),
        out_shape=[out, out],
        compiler_params=params(),
    )(constants)


def norm_of(rows):
    centre = rows - jnp.mean(rows, axis=1, keepdims=True)
    scale = lax.rsqrt(jnp.mean(centre * centre, axis=1, keepdims=True) + 1e-05)
    return centre * scale, scale


def project_kernel(blocks, row_count, *refs):
    parts, (weight, vectors, bias, window, hidden, heads, block) = refs[:blocks], refs[blocks:]
    step = pl.program_id(0)
    for k in range(blocks):

        @pl.when(step == k)
        def _():
            block[...] = parts[k][...]

    window[...] = block[...]
    unit, _ = norm_of(block[...].astype(F32))
    normed = (unit * vectors[0:1, :] + vectors[1:2, :]).astype(BF16)
    hidden[...] = normed
    total = None
    for s in range(weight.shape[0]):
        columns = normed[:, s * row_count : (s + 1) * row_count]
        term = matmul(columns, weight[s, :row_count, :])
        total = term if total is None else total + term
    key_width = bias.shape[1] // 2
    query = total[:, :key_width] * KEY ** (-0.5)
    heads[:, :key_width] = (query + bias[0:1, :key_width]).astype(BF16)
    heads[:, key_width : 2 * key_width] = (query + bias[0:1, key_width:]).astype(BF16)
    heads[:, 2 * key_width :] = total[:, key_width:].astype(BF16)


def project(parts, weight, vectors, bias, row_count):
    blocks = len(parts)
    rows, width = parts[0].shape
    heads_width = weight.shape[2] + bias.shape[1] // 2
    out = lambda w: pl.BlockSpec((rows, w), lambda i: (i, 0))
    return pl.pallas_call(
        functools.partial(project_kernel, blocks, row_count),
        grid=(blocks,),
        in_specs=[whole_spec(a) for a in (*parts, weight, vectors, bias)],
        out_specs=[out(width), out(width), out(heads_width)],
        out_shape=[shape((blocks * rows, w), BF16) for w in (width, width, heads_width)],
        scratch_shapes=[pltpu.VMEM((rows, width), BF16)],
        compiler_params=params(),
        cost_estimate=pl.CostEstimate(
            flops=2 * blocks * rows * width * heads_width,
            bytes_accessed=8 * blocks * rows * width,
            transcendentals=0,
        ),
    )(*parts, weight, vectors, bias)


def feed_kernel(count, chunk, *refs):
    parts = 2 * (2 * count - 1)
    where, placed, attended_a, attended_b, grad_rows, vectors, inner_bias = refs[:7]
    weights = refs[7 : 7 + parts]
    layer_output, d_mixed, hidden, activated, d_inner, sums, inner_sums = refs[7 + parts : 14 + parts]
    inner_whole, outer_whole, residual, unit, back, outer_sum, sems = refs[14 + parts :]
    here, core = where[0], where[1]
    copies = []
    for k, whole in enumerate((inner_whole, outer_whole)):
        mine = weights[k * (2 * count - 1) : (k + 1) * (2 * count - 1)]
        size = whole.shape[0] // count
        half = size // 2
        moves = [(mine[0], here * size, size)]
        for m in range(1, count):
            start = jnp.bitwise_xor(here, m) * size
            moves.append((mine[2 * m - 1], start + core * half, half))
            moves.append((mine[2 * m], start + (1 - core) * half, half))
        started = []
        for source, start, rows in moves:
            target = whole.at[pl.ds(pl.multiple_of(start, 16), rows), :]
            copy = pltpu.make_async_copy(source, target, sems.at[k, len(started)])
            copy.start()
            started.append(copy)
        copies.append(started)
    rows, width = placed.shape
    half = width // 2
    residual[:, :half] = placed[:, :half] + attended_a[...] + vectors[2:3, :half]
    residual[:, half:] = placed[:, half:] + attended_b[...] + vectors[2:3, half:]
    normed, scale = norm_of(residual[...])
    unit[...] = normed
    hidden[...] = (normed * vectors[3:4, :] + vectors[4:5, :]).astype(BF16)
    for started in copies:
        for copy in started:
            copy.wait()
    ff = outer_whole.shape[0]
    for c in range(ff // chunk):
        at = slice(c * chunk, (c + 1) * chunk)
        inner = matmul(hidden[...], inner_whole[:, at]) + inner_bias[0:1, at]
        below = 0.5 * (1.0 + lax.erf(inner * (0.5**0.5)))
        slope = below + inner * jnp.exp(-0.5 * inner * inner) * (0.5 / math.pi) ** 0.5
        active = (inner * below).astype(BF16)
        activated[:, at] = active
        grad = (matmul_nt(grad_rows[...], outer_whole[at, :]) * slope).astype(BF16)
        d_inner[:, at] = grad
        inner_sums[:, at] = jnp.sum(grad.astype(F32), axis=0, keepdims=True)
        back_term = matmul_nt(grad, inner_whole[:, at])
        outer_term = matmul(active, outer_whole[at, :])
        if c == 0:
            back[...] = back_term
            outer_sum[...] = outer_term
        else:
            back[...] += back_term
            outer_sum[...] += outer_term
    layer_output[...] = (residual[...] + outer_sum[...] + vectors[5:6, :]).astype(BF16)
    grad, normed = back[...], unit[...]
    dy = grad_rows[...].astype(F32)
    scaled = grad * vectors[3:4, :]
    mean_one = jnp.mean(scaled, axis=1, keepdims=True)
    mean_two = jnp.mean(scaled * normed, axis=1, keepdims=True)
    mixed_in = (dy + (scaled - mean_one - normed * mean_two) * scale).astype(BF16)
    d_mixed[...] = mixed_in
    sums[...] = jnp.zeros_like(sums)
    sums[2:3, :] = jnp.sum(mixed_in.astype(F32), axis=0, keepdims=True)
    sums[3:4, :] = jnp.sum(grad * normed, axis=0, keepdims=True)
    sums[4:5, :] = jnp.sum(grad, axis=0, keepdims=True)
    sums[5:6, :] = jnp.sum(dy, axis=0, keepdims=True)


def feed_forward(where, placed, attended, grad_rows, vectors, inner_bias, inner_parts, outer_parts):
    rows, width = placed.shape
    ff = inner_bias.shape[1]
    count = (len(inner_parts) + 1) // 2
    chunk = math.gcd(512, ff)
    weights = (*inner_parts, *outer_parts)
    small = (placed, *attended, grad_rows, vectors, inner_bias)
    outs = [
        shape((rows, width), BF16),
        shape((rows, width), BF16),
        shape((rows, width), BF16),
        shape((rows, ff), BF16),
        shape((rows, ff), BF16),
        shape((8, width), F32),
        shape((1, ff), F32),
    ]
    return pl.pallas_call(
        functools.partial(feed_kernel, count, chunk),
        in_specs=[scalar_spec()]
        + [pl.BlockSpec(memory_space=pltpu.VMEM) for _ in small]
        + [pl.BlockSpec(memory_space=pl.ANY) for _ in weights],
        out_specs=[pl.BlockSpec(memory_space=pltpu.VMEM) for _ in outs],
        out_shape=outs,
        scratch_shapes=[
            pltpu.VMEM((width, ff), BF16),
            pltpu.VMEM((ff, width), BF16),
            pltpu.VMEM((rows, width), F32),
            pltpu.VMEM((rows, width), F32),
            pltpu.VMEM((rows, width), F32),
            pltpu.VMEM((rows, width), F32),
            pltpu.SemaphoreType.DMA((2, 2 * count - 1)),
        ],
        compiler_params=params(),
        cost_estimate=pl.CostEstimate(
            flops=8 * rows * width * ff,
            bytes_accessed=4 * width * ff + 40 * rows * width,
            transcendentals=2 * rows * ff,
        ),
    )(where, *small, *weights)


def columns_at(ref, index, size, scratch):
    if size % 128 == 0:
        return ref[:, pl.ds(pl.multiple_of(index * size, 128), size)]
    for k in range(ref.shape[1] // size):

        @pl.when(index == k)
        def _():
            scratch[...] = ref[:, k * size : (k + 1) * size]

    return scratch[...]


def away_kernel(
    count, where, hidden, activated, d_inner, grad_rows, inner_away, outer_away, some, more
):
    here, other = where[0], 1 - where[1]
    rows = hidden.shape[1] // count
    ff = d_inner.shape[1]
    ff_rows = ff // count
    half = pl.ds(pl.multiple_of(other * (ff // 2), 128), ff // 2)
    step = pl.program_id(0)
    shard = jnp.bitwise_xor(here, step)
    columns = columns_at(hidden, shard, rows, some)
    inner_away[0] = matmul_tn(columns, d_inner[:, half]).astype(BF16)
    columns = columns_at(activated, 2 * shard + other, ff_rows // 2, more)
    outer_away[0] = matmul_tn(columns, grad_rows[...]).astype(BF16)


def kept_kernel(
    count, where, hidden, activated, d_inner, grad_rows, inner_came, outer_came, *refs
):
    outs, (some, more) = refs[:-2], refs[-2:]
    here, core = where[0], where[1]
    rows = hidden.shape[1] // count
    ff = d_inner.shape[1]
    ff_rows = ff // count
    half = pl.ds(pl.multiple_of(core * (ff // 2), 128), ff // 2)
    step = pl.program_id(0)
    shard = jnp.bitwise_xor(here, step)
    columns = columns_at(hidden, shard, rows, some)
    inner = matmul_tn(columns, d_inner[:, half]) + inner_came[0].astype(F32)
    columns = columns_at(activated, 2 * shard + core, ff_rows // 2, more)
    outer = matmul_tn(columns, grad_rows[...]) + outer_came[0].astype(F32)
    for k, result in enumerate((inner, outer)):
        side = result.shape[1] // 2
        for m in range(count):

            @pl.when(step == m)
            def _():
                outs[2 * (k * count + m)][...] = result[:, :side].astype(BF16)
                outs[2 * (k * count + m) + 1][...] = result[:, side:].astype(BF16)


def ff_gradients(count, where, hidden, activated, d_inner, grad_rows, came=None):
    rows = hidden.shape[1] // count
    ff = d_inner.shape[1]
    wide = [(rows, ff // 2), (ff // count // 2, grad_rows.shape[1])]
    block = lambda dims: pl.BlockSpec((1,) + dims, lambda i: (i, 0, 0))
    small = (hidden, activated, d_inner, grad_rows)
    if came is None:
        kernel, extra = away_kernel, ()
        out_specs = [block(dims) for dims in wide]
        outs = [shape((count,) + dims, BF16) for dims in wide]
    else:
        kernel, extra = kept_kernel, came
        outs = [shape((d[0], d[1] // 2), BF16) for d in wide for _ in range(2 * count)]
        out_specs = [whole_spec(out) for out in outs]
    return pl.pallas_call(
        functools.partial(kernel, count),
        grid=(count,),
        in_specs=[scalar_spec()]
        + [whole_spec(a) for a in small]
        + [block(dims) for dims in wide[: len(extra)]],
        out_specs=out_specs,
        out_shape=outs,
        scratch_shapes=[
            pltpu.VMEM((hidden.shape[0], rows), BF16),
            pltpu.VMEM((hidden.shape[0], ff // count // 2), BF16),
        ],
        compiler_params=params(),
        cost_estimate=pl.CostEstimate(
            flops=2 * hidden.shape[0] * hidden.shape[1] * ff,
            bytes_accessed=8 * rows * count * ff,
            transcendentals=0,
        ),
    )(where, *small, *extra)


def mixed_back_kernel(count, parts_count, *refs):
    where, mixed, weight = refs[:3]
    parts = refs[3 : 3 + parts_count]
    d_attended, out_away, out_kept, out_sum = refs[3 + parts_count :]
    here, core = where[0], where[1]
    rows = parts[0].shape[0]
    for k, part in enumerate(parts):
        start = jnp.bitwise_xor(here, k // 2) * (2 * rows) + (k % 2) * rows
        at = pl.ds(pl.multiple_of(start, 32), rows)
        d_attended[at, :] = matmul_nt(part[...], weight[...]).astype(BF16)
        term = matmul_tn(mixed[at, :], part[...])
        if k == 0:
            out_sum[...] = term
        else:
            out_sum[...] += term
    half = out_kept.shape[0]
    out_kept[...] = out_sum[pl.ds(pl.multiple_of(core * half, 32), half), :]
    out_away[...] = out_sum[pl.ds(pl.multiple_of((1 - core) * half, 32), half), :].astype(BF16)


def mixed_back(count, where, mixed, weight, parts):
    length, val_width = mixed.shape
    width = weight.shape[1]
    vmem = pl.BlockSpec(memory_space=pltpu.VMEM)
    return pl.pallas_call(
        functools.partial(mixed_back_kernel, count, len(parts)),
        in_specs=[scalar_spec()] + [vmem] * (2 + len(parts)),
        out_specs=[vmem] * 3,
        out_shape=[
            shape((length, val_width), BF16),
            shape((val_width // 2, width), BF16),
            shape((val_width // 2, width), F32),
        ],
        scratch_shapes=[pltpu.VMEM((val_width, width), F32)],
        compiler_params=params(),
        cost_estimate=pl.CostEstimate(
            flops=4 * length * val_width * width,
            bytes_accessed=2 * length * (width + 2 * val_width),
            transcendentals=0,
        ),
    )(where, mixed, weight, *parts)


def project_back_kernel(
    count,
    where,
    order,
    d_heads,
    window,
    hidden,
    weight,
    sums,
    inner_sums,
    d_bias,
    d_rel,
    kept,
    away,
    *refs,
):
    blocks = 2 * count
    d_normed, (grads, first_sums) = refs[: 2 * count], refs[2 * count :]
    here, core = where[0], where[1]
    step = pl.program_id(0)
    rows, width = window.shape
    row_count = 2 * rows
    length = order.shape[1]
    key_width = d_rel.shape[1]
    start = jnp.bitwise_xor(here, step // 2) * row_count + (step % 2) * rows
    bins = lax.broadcasted_iota(jnp.int32, (rows, length), 0) + start
    picks = jnp.where(order[0:1, :] == bins, 1.0, 0.0).astype(BF16)
    d_along = matmul(picks, d_heads[...]).astype(BF16)
    unit, _ = norm_of(window[...].astype(F32))

    @pl.when(step == 0)
    def _():
        grads[...] = jnp.zeros_like(grads)
        first_sums[...] = jnp.zeros_like(first_sums)

    for s in range(count):
        at = slice(s * row_count, (s + 1) * row_count)
        grads[s, :row_count, :] += matmul_tn(hidden[:, at], d_along)
        normed = matmul_nt(d_along, weight[s, :row_count, :])
        first_sums[0:1, at] += jnp.sum(normed * unit[:, at], axis=0, keepdims=True)
        first_sums[1:2, at] += jnp.sum(normed, axis=0, keepdims=True)
        side, inside = divmod(s * row_count, width // 2)
        to_rows = pl.ds(pl.multiple_of((step % 2) * rows, 32), rows)
        for m in range(count):

            @pl.when(step // 2 == m)
            def _():
                d_normed[2 * m + side][to_rows, inside : inside + row_count] = normed.astype(BF16)

    @pl.when(step == blocks - 1)
    def _():
        rel_rows = d_rel.shape[0] // count
        for s in range(count):
            at = slice(s * row_count, (s + 1) * row_count)
            grads[s, row_count : row_count + 2, :row_count] = first_sums[0:2, at]
            grads[s, row_count + 2 : row_count + 6, :row_count] = sums[2:6, at]
            for j in range(2):
                part = slice((2 * s + j) * row_count, (2 * s + j + 1) * row_count)
                grads[s, row_count + 6 + j : row_count + 7 + j, :row_count] = inner_sums[0:1, part]
            for j in range(-(-rel_rows // EXTRA)):
                some = d_rel[s * rel_rows + j * EXTRA : s * rel_rows + min(rel_rows, (j + 1) * EXTRA), :]
                lane = row_count + j * key_width
                grads[s, row_count : row_count + some.shape[0], lane : lane + key_width] = some
        for s in range(count):

            @pl.when(here == s)
            def _():
                grads[s, row_count + 8 : row_count + 10, :key_width] = d_bias[0:2, :]

        half = kept.shape[1]
        kept[...] = grads[:, pl.ds(pl.multiple_of(core * half, 16), half), :].astype(BF16)
        away[...] = grads[:, pl.ds(pl.multiple_of((1 - core) * half, 16), half), :].astype(BF16)


def project_back(count, where, order, d_heads, window, hidden, weight, sums, inner_sums, d_bias, d_rel):
    length, width = window.shape
    rows = length // (2 * count)
    heads_width = d_heads.shape[1]
    packed = (count, 2 * rows + EXTRA, heads_width)
    block = pl.BlockSpec((rows, width), lambda i: (i, 0))
    outs = [shape((count, packed[1] // 2, heads_width), BF16) for _ in range(2)]
    outs += [shape((2 * rows, width // 2), BF16) for _ in range(2 * count)]
    return pl.pallas_call(
        functools.partial(project_back_kernel, count),
        grid=(2 * count,),
        in_specs=[scalar_spec(), whole_spec(order), whole_spec(d_heads), block, block]
        + [whole_spec(a) for a in (weight, sums, inner_sums, d_bias, d_rel)],
        out_specs=[whole_spec(out) for out in outs],
        out_shape=outs,
        scratch_shapes=[pltpu.VMEM(packed, F32), pltpu.VMEM((8, width), F32)],
        compiler_params=params(),
        cost_estimate=pl.CostEstimate(
            flops=2 * length * heads_width * (length + 2 * width),
            bytes_accessed=4 * length * width + 2 * length * (width + heads_width),
            transcendentals=0,
        ),
    )(where, order, d_heads, window, hidden, weight, sums, inner_sums, d_bias, d_rel)


def swap(array, mask, count):
    return lax.ppermute(array, "seq", [(i, i ^ mask) for i in range(count)])


def bit_orders(count):
    bits = [1 << k for k in range(count.bit_length() - 1)]
    return bits, bits[::-1]


def pin(*arrays):
    return lax.optimization_barrier(arrays)


class Exchange:
    def __init__(self):
        self.new = {}


def pin_all(exchanges, *arrays):
    keys = [sorted(e.new) for e in exchanges]
    out = pin(*arrays, *[e.new[k] for e, ks in zip(exchanges, keys) for k in ks])
    at = len(arrays)
    for e, ks in zip(exchanges, keys):
        e.new = dict(zip(ks, out[at : at + len(ks)]))
        at += len(ks)
    return out[: len(arrays)]


class Gather(Exchange):
    def __init__(self, part, order, count):
        super().__init__()
        self.have, self.order, self.count, self.step = {0: part}, order, count, 0

    def take(self):
        self.have.update(self.new)
        self.new = {}

    def send(self):
        self.take()
        bit = self.order[self.step]
        self.new = {m ^ bit: swap(self.have[m], bit, self.count) for m in sorted(self.have)}
        self.step += 1


class Scatter(Exchange):
    def __init__(self, blocks, order, count):
        super().__init__()
        self.have, self.order, self.count, self.step = dict(enumerate(blocks)), order, count, 0

    def take(self):
        if self.new:
            bit = self.order[self.step - 1]
            self.have = {
                m: self.have[m].astype(F32) + self.new[m | bit].astype(F32)
                for m in self.have
                if not m & bit
            }
            self.new = {}

    def send(self):
        self.take()
        bit = self.order[self.step]
        self.new = {
            m: swap(self.have[m].astype(BF16), bit, self.count)
            for m in sorted(self.have, reverse=True)
            if m & bit
        }
        self.step += 1

    def rest(self):
        while self.step < len(self.order):
            self.send()
        self.take()
        return self.have[0]


class LineSum(Exchange):
    def __init__(self, piece, count):
        super().__init__()
        self.total, self.count, self.step = piece, count, 0
        self.inward = count // 2 - 1
        self.steps = 2 * self.inward + 1 if count > 1 else 0

    def take(self):
        if self.new:
            at, came = self.step - 1, self.new[0]
            if at <= self.inward:
                self.total = self.total.astype(F32) + came.astype(F32)
            else:
                index = lax.axis_index("wz")
                far = 2 * self.inward - at
                is_target = (index == far) | (index == self.count - 1 - far)
                self.total = jnp.where(is_target, came, self.total)
            self.new = {}

    def send(self):
        self.take()
        last = self.count - 1
        if self.step < self.inward:
            k = self.step
            pairs = [(k, k + 1), (last - k, last - k - 1)]
        elif self.step == self.inward:
            k = self.inward
            pairs = [(k, k + 1), (k + 1, k)]
        else:
            k = 2 * self.inward - self.step
            pairs = [(k + 1, k), (last - k - 1, last - k)]
        self.total = self.total.astype(BF16)
        self.new = {0: lax.ppermute(self.total, "wz", pairs)}
        self.step += 1

    def rest(self):
        while self.step < self.steps:
            self.send()
        self.take()
        return self.total.astype(BF16)


class OtherCore(Exchange):
    def __init__(self, array):
        super().__init__()
        self.new = {0: other_core(array)}


def split_columns(blocks, count):
    half = blocks[0].shape[1] // 2
    return [
        Scatter([block[:, k * half : (k + 1) * half] for block in blocks], order, count)
        for k, order in enumerate(bit_orders(count))
    ]


def other_core(array):
    return lax.ppermute(array, "core", [(0, 1), (1, 0)])


def shards(
    seq_count,
    wz_count,
    inputs,
    bin_order,
    first_gain,
    first_shift,
    query_weight,
    key_weight,
    value_weight,
    bias_content,
    bias_position,
    relative_weight,
    out_weight,
    bias_out,
    second_gain,
    second_shift,
    inner_weight,
    bias_inner,
    outer_weight,
    bias_outer,
    grad_output,
):
    row_count, width = inputs.shape[1:]
    length = bin_order.shape[1]
    here = lax.axis_index("seq")
    core = lax.axis_index("core")
    where = jnp.stack([here, core]).astype(jnp.int32)
    row_start = here * row_count
    key_width = query_weight.shape[1] // seq_count
    val_width = value_weight.shape[1] // seq_count
    heads_width = 2 * key_width + val_width
    up, down = bit_orders(seq_count)

    others = [jnp.bitwise_xor(here, m) for m in range(seq_count)]
    along = jnp.concatenate(
        [other * row_count + jnp.arange(row_count, dtype=jnp.int32) for other in others]
    )

    def natural(rows):
        parts = rows.reshape(seq_count, row_count, -1)
        parts = [lax.dynamic_index_in_dim(parts, other, 0) for other in others]
        return jnp.concatenate(parts, axis=0).reshape(rows.shape)

    def halves(rows):
        half = rows.shape[0] // 2
        return [Gather(rows[:half], up, seq_count), Gather(rows[half:], down, seq_count)]

    def blocks_of(gathers):
        for g in gathers:
            g.take()
        return [g.have[m] for m in range(seq_count) for g in gathers]

    window_gathers = halves(inputs[0])
    for g in window_gathers:
        g.send()

    def by_head(weight):
        return weight.reshape(weight.shape[0], seq_count, -1)

    vectors = jnp.stack([first_gain, first_shift, bias_out, second_gain, second_shift, bias_outer])
    vectors = jnp.concatenate([vectors, bias_inner.reshape(2, row_count)], axis=0)
    vectors = jnp.pad(vectors, ((0, EXTRA - 8), (0, 0)))
    rel_rows = relative_weight.shape[0]
    rel_blocks = -(-rel_rows // EXTRA)
    rel_part = jnp.pad(by_head(relative_weight), ((0, rel_blocks * EXTRA - rel_rows), (0, 0), (0, 0)))
    rel_part = rel_part.reshape(rel_blocks, EXTRA, seq_count, key_width).transpose(2, 1, 0, 3)
    rel_part = rel_part.reshape(seq_count, EXTRA, -1)
    spare = heads_width - row_count - rel_part.shape[2]
    extra = jnp.concatenate(
        [
            jnp.broadcast_to(vectors[None], (seq_count,) + vectors.shape),
            jnp.pad(rel_part, ((0, 0), (0, 0), (0, spare))),
        ],
        axis=2,
    )
    mine = jnp.concatenate(
        [by_head(query_weight), by_head(key_weight), by_head(value_weight)], axis=2
    ).transpose(1, 0, 2)
    mine = jnp.concatenate([mine, extra], axis=1)
    (mine,) = pin_all(window_gathers, mine)
    for step in range(1, len(up)):
        for g in window_gathers:
            g.send()
    attention_weight = lax.all_to_all(mine, "seq", 0, 0, tiled=True)
    table, table_back = basis_tables(jnp.asarray(basis_constants(length)), length)
    flat = attention_weight[:, row_count:]
    vectors = flat[:, :8, :row_count].astype(F32)
    inner_bias = vectors[:, 6:8].reshape(1, -1)
    vectors = vectors.transpose(1, 0, 2).reshape(8, width)
    rel = flat[:, :, row_count : row_count + rel_blocks * key_width]
    rel = rel.reshape(seq_count, EXTRA, rel_blocks, key_width).transpose(0, 2, 1, 3)
    rel = rel.reshape(seq_count, rel_blocks * EXTRA, key_width)[:, :rel_rows].reshape(REL, key_width)

    def own_half(weight):
        half = weight.shape[0] // 2
        return lax.dynamic_slice_in_dim(weight, core * half, half, 0)

    inner_part, outer_part = own_half(inner_weight), own_half(outer_weight)
    inner_part, outer_part = pin_all(window_gathers, inner_part, outer_part)
    window_blocks = blocks_of(window_gathers)
    weight_gathers = [
        Gather(inner_part, up, seq_count),
        Gather(outer_part, down, seq_count),
    ]
    for g in weight_gathers:
        g.send()

    order = bin_order[0]
    placing = (order[:, None] == along[None, :]).astype(BF16)
    bias = jnp.concatenate([bias_content, bias_position])[None].astype(F32)
    window, hidden_one, in_bins = project(
        window_blocks, attention_weight, vectors, bias, row_count
    )
    placed_heads = matmul(placing, in_bins).astype(BF16)
    (placed_heads,) = pin_all(weight_gathers, placed_heads)
    for step in range(1, len(up)):
        for g in weight_gathers:
            g.send()
    mixed, probs = attend(placed_heads, rel, table)
    (mixed,) = pin_all(weight_gathers, mixed)
    weight_parts = []
    for g, own in zip(weight_gathers, (inner_weight, outer_weight)):
        g.take()
        parts = [own]
        for m in range(1, seq_count):
            parts += [g.have[m], other_core(g.have[m])]
        weight_parts.append(parts)
    mixed_along = natural(mixed).reshape(seq_count, row_count, val_width)
    attended = [matmul(mixed_along[m], out_weight).astype(BF16) for m in range(seq_count)]
    attended = split_columns(attended, seq_count)
    for g in attended:
        g.send()
    own_order = lax.dynamic_slice_in_dim(order, row_start, row_count, 0)
    placed = matmul((own_order[:, None] == along[None, :]).astype(BF16), window)
    (placed,) = pin_all(attended, placed)
    attended = [g.rest() for g in attended]

    grad_rows = grad_output[0]
    layer_output, d_mixed_in, hidden_two, activated, d_inner, sums, inner_sums = feed_forward(
        where, placed, attended, grad_rows, vectors, inner_bias, *weight_parts
    )

    d_mixed_gathers = halves(d_mixed_in)
    for g in d_mixed_gathers:
        g.send()
    away = ff_gradients(seq_count, where, hidden_two, activated, d_inner, grad_rows)
    away = pin_all(d_mixed_gathers, *away)
    for step in range(1, len(up)):
        for g in d_mixed_gathers:
            g.send()
    came = [other_core(part) for part in away]
    kept = ff_gradients(seq_count, where, hidden_two, activated, d_inner, grad_rows, came)
    kept = pin_all(d_mixed_gathers, *kept)
    d_mixed_blocks = blocks_of(d_mixed_gathers)
    count = seq_count
    inner_sums_of, outer_sums_of = [
        [
            Scatter([kept[2 * (k * count + m) + side] for m in range(count)], bits, count)
            for side, bits in enumerate((up, down))
        ]
        for k in range(2)
    ]
    for g in inner_sums_of:
        g.send()

    d_attended, out_away, grad_out_w = mixed_back(
        seq_count, where, mixed, out_weight, d_mixed_blocks
    )
    out_core = OtherCore(out_away)
    d_heads, d_rel, d_bias = attend_back(placed_heads, rel, table_back, mixed, d_attended, probs)
    (d_heads,) = pin_all(inner_sums_of + [out_core], d_heads)
    for step in range(1, len(up)):
        for g in inner_sums_of:
            g.send()
    for g in outer_sums_of:
        g.send()
    out_line = LineSum(grad_out_w + out_core.new[0].astype(F32), wz_count)
    out_line.send()
    results = project_back(
        seq_count,
        where,
        order[None],
        d_heads,
        window,
        hidden_one,
        attention_weight,
        sums,
        inner_sums,
        d_bias,
        d_rel,
    )
    results = pin_all(inner_sums_of + outer_sums_of, *results)
    packed, packed_core = results[0], OtherCore(results[1])
    arrived = [
        Scatter([results[2 + 2 * m + side] for m in range(count)], bits, count)
        for side, bits in enumerate((up, down))
    ]
    inner_lines = [LineSum(g.rest(), wz_count) for g in inner_sums_of]
    for step in range(1, len(up)):
        for g in outer_sums_of:
            g.send()
    for g in inner_lines + [out_line]:
        g.send()
    (packed,) = pin_all([packed_core], packed)
    packed = (packed.astype(F32) + packed_core.new[0].astype(F32)).astype(BF16)
    packed = lax.all_to_all(packed, "seq", 0, 0, tiled=True)
    for g in arrived:
        g.send()
    (packed,) = pin_all(outer_sums_of + inner_lines, packed)
    outer_lines = [LineSum(g.rest(), wz_count) for g in outer_sums_of]
    packed_lines = [
        LineSum(packed[: seq_count // 2], wz_count),
        LineSum(packed[seq_count // 2 :], wz_count),
    ]
    for g in packed_lines + inner_lines + outer_lines + [out_line]:
        g.send()
    pin_all(arrived + inner_lines + packed_lines)
    for step in range(1, len(up)):
        for g in arrived:
            g.send()
    for g in packed_lines + inner_lines + outer_lines:
        g.send()

    own_unit, own_scale = norm_of(inputs[0].astype(F32))
    own_bins = row_start + jnp.arange(row_count, dtype=jnp.int32)
    order_parts = order.reshape(2 * seq_count, row_count // 2)
    returned = None
    for k, block in enumerate(d_mixed_blocks):
        at = lax.dynamic_index_in_dim(order_parts, 2 * others[k // 2] + k % 2, 0)
        term = matmul((at == own_bins[:, None]).astype(BF16), block)
        returned = term if returned is None else returned + term
    (returned,) = pin_all(arrived, returned)
    arrived = jnp.concatenate([g.rest() for g in arrived], axis=1)
    grad_inputs = norm_back(own_unit, own_scale, vectors[0:1], arrived) + returned

    first = core == 0

    def by_cores(piece):
        other = other_core(piece)
        return jnp.where(first, piece, other), jnp.where(first, other, piece)

    inner_parts = [by_cores(g.rest()) for g in inner_lines]
    grad_inner_w = jnp.concatenate(
        [part[k] for k in range(2) for part in inner_parts], axis=1
    ).astype(F32)
    outer_parts = [jnp.concatenate(by_cores(g.rest()), axis=0) for g in outer_lines]
    grad_outer_w = jnp.concatenate(outer_parts, axis=1).astype(F32)
    grad_out_w = jnp.concatenate(by_cores(out_line.rest()), axis=0).astype(F32)
    packed_parts = [jnp.concatenate(by_cores(g.rest()), axis=1) for g in packed_lines]
    packed = jnp.concatenate(packed_parts, axis=0)
    grad_attention = packed[:, :row_count].astype(F32).transpose(1, 0, 2)
    grad_query_w = grad_attention[:, :, :key_width].reshape(row_count, -1)
    grad_key_w = grad_attention[:, :, key_width : 2 * key_width].reshape(row_count, -1)
    grad_value_w = grad_attention[:, :, 2 * key_width :].reshape(row_count, -1)
    flat = packed[:, row_count:].astype(F32)
    small = jnp.sum(flat[:, :16, :row_count], axis=0)
    g_gain_one, g_shift_one, g_out_b, g_gain_two, g_shift_two, g_outer_b = small[:6]
    g_inner_b = small[6:8].reshape(-1)
    grad_rel = flat[:, :, row_count : row_count + rel_blocks * key_width]
    grad_rel = grad_rel.reshape(seq_count, EXTRA, rel_blocks, key_width).transpose(2, 1, 0, 3)
    grad_rel = grad_rel.reshape(rel_blocks * EXTRA, -1)[:rel_rows]
    return (
        layer_output[None],
        grad_inputs[None],
        g_gain_one,
        g_shift_one,
        grad_query_w,
        grad_key_w,
        grad_value_w,
        small[8, :key_width],
        small[9, :key_width],
        grad_rel,
        grad_out_w,
        g_out_b,
        g_gain_two,
        g_shift_two,
        grad_inner_w,
        g_inner_b,
        grad_outer_w,
        g_outer_b,
    )


def solution(mesh):
    seq_count = mesh.shape["seq"]
    devices = mesh.devices.reshape(seq_count, -1, 2)
    split_mesh = Mesh(devices, ("seq", "wz", "core"))
    rows = P(("wz", "core"), "seq", None)
    vector = P("seq")
    matrix = P("seq", None)
    weights = (
        vector,
        vector,
        matrix,
        matrix,
        matrix,
        vector,
        vector,
        matrix,
        matrix,
        vector,
        vector,
        vector,
        matrix,
        vector,
        matrix,
        vector,
    )
    return jax.shard_map(
        functools.partial(shards, seq_count, mesh.shape["win"] // 2),
        mesh=split_mesh,
        in_specs=(rows, P(("wz", "core"), None)) + weights + (rows,),
        out_specs=(rows, rows) + weights,
        check_vma=False,
    )
```

```python
import functools
import math

import jax
import jax.numpy as jnp
import numpy as np
from jax import lax
from jax.experimental import pallas as pl
from jax.experimental.pallas import tpu as pltpu
from jax.sharding import Mesh
from jax.sharding import PartitionSpec as P

HEADS = 8
KEY = 64
VAL = 192
REL = 192
BF16 = jnp.bfloat16
F32 = jnp.float32
VMEM_LIMIT = 56 * 2**20
EXTRA = 32


def matmul(a, b):
    return lax.dot_general(a, b, (((1,), (0,)), ((), ())), preferred_element_type=F32)


def matmul_nt(a, b):
    return lax.dot_general(a, b, (((1,), (1,)), ((), ())), preferred_element_type=F32)


def matmul_tn(a, b):
    return lax.dot_general(a, b, (((0,), (0,)), ((), ())), preferred_element_type=F32)


def head_part(rows, head):
    lanes = lax.broadcasted_iota(jnp.int32, rows.shape, 1)
    inside = (lanes >= head * KEY) & (lanes < (head + 1) * KEY)
    return jnp.where(inside, rows, jnp.zeros_like(rows))


def head_columns(key_width):
    return [slice(k * key_width, (k + 1) * key_width) for k in range(3)]


def attend_kernel(heads, rows, placed, rel, table, mixed, probs):
    length = placed.shape[0]
    key_width = heads * KEY
    content_at, position_at, keys_at = head_columns(key_width)
    first = pl.program_id(0) * rows
    here = pl.ds(pl.multiple_of(first, rows), rows)
    basis = table[:, pl.ds(pl.multiple_of(length - rows - first, rows), length + rows)]
    content, position, keys = placed[here, content_at], placed[here, position_at], placed[:, keys_at]
    parts = []
    for head in range(heads):
        q_basis = matmul_nt(head_part(position, head), rel[...]).astype(BF16)
        grid = matmul(q_basis, basis)
        shifted = pltpu.roll(grid, 0, 1, stride=1, stride_axis=0)[:, rows:]
        scores = matmul_nt(head_part(content, head), keys) + shifted
        top = jnp.max(scores, axis=1, keepdims=True)
        weights = jnp.exp(scores - top)
        total = jnp.sum(weights, axis=1, keepdims=True)
        prob = (weights * (1.0 / total)).astype(BF16)
        probs[head] = prob
        values_at = 3 * key_width + head * VAL
        parts.append(matmul(prob, placed[:, values_at : values_at + VAL]))
    mixed[...] = jnp.concatenate(parts, axis=1).astype(BF16)


def attend(placed, rel, table):
    length = placed.shape[0]
    heads = rel.shape[1] // KEY
    rows = math.gcd(256, length)
    whole = lambda array: pl.BlockSpec(array.shape, lambda i: (0, 0))
    return pl.pallas_call(
        functools.partial(attend_kernel, heads, rows),
        grid=(length // rows,),
        in_specs=[whole(placed), whole(rel), whole(table)],
        out_specs=[
            pl.BlockSpec((rows, heads * VAL), lambda i: (i, 0)),
            pl.BlockSpec((heads, rows, length), lambda i: (0, i, 0)),
        ],
        out_shape=[
            jax.ShapeDtypeStruct((length, heads * VAL), BF16),
            jax.ShapeDtypeStruct((heads, length, length), BF16),
        ],
        compiler_params=pltpu.CompilerParams(vmem_limit_bytes=VMEM_LIMIT),
        cost_estimate=pl.CostEstimate(
            flops=2 * heads * length * length * 1024,
            bytes_accessed=2 * heads * length * length + 8 * length * heads * VAL,
            transcendentals=heads * length * length,
        ),
    )(placed, rel, table)


def attend_back_kernel(
    heads,
    rows,
    placed,
    rel,
    table,
    flip,
    mixed,
    d_mixed,
    probs,
    d_heads,
    d_rel,
    d_bias,
    keys_sum,
    values_sum,
):
    length = placed.shape[0]
    key_width = heads * KEY
    content_at, position_at, keys_at = head_columns(key_width)
    step = pl.program_id(0)

    @pl.when(step == 0)
    def _():
        keys_sum[...] = jnp.zeros_like(keys_sum)
        values_sum[...] = jnp.zeros_like(values_sum)
        d_rel[...] = jnp.zeros_like(d_rel)
        d_bias[...] = jnp.zeros_like(d_bias)

    first = pl.multiple_of(step * rows, rows)
    here = pl.ds(first, rows)
    basis = table[:, pl.ds(first, length + rows)]
    content, position, keys = placed[here, content_at], placed[here, position_at], placed[:, keys_at]
    d_content = jnp.zeros((rows, key_width), F32)
    d_position = jnp.zeros((rows, key_width), F32)
    blocks = length // rows
    for head in range(heads):
        columns = slice(head * VAL, (head + 1) * VAL)
        values_at = 3 * key_width + head * VAL
        d_part = d_mixed[:, columns]
        delta = jnp.sum(
            d_part.astype(F32) * mixed[:, columns].astype(F32), axis=1, keepdims=True
        )
        prob = probs[head]
        values_sum[columns, :] += matmul_tn(d_part, prob)
        d_prob = matmul_nt(d_part, placed[:, values_at : values_at + VAL])
        d_score = (prob.astype(F32) * (d_prob - delta)).astype(BF16)
        keys_sum[...] += matmul_tn(head_part(content, head), d_score)
        d_content += head_part(matmul(d_score, keys), head)
        turned = [
            matmul(d_score[:, (blocks - 1 - b) * rows : (blocks - b) * rows], flip[...])
            for b in range(blocks)
        ]
        turned = jnp.concatenate(turned + [jnp.zeros((rows, rows), F32)], axis=1)
        d_grid = pltpu.roll(turned, 0, 1, stride=1, stride_axis=0).astype(BF16)
        d_basis = matmul_nt(d_grid, basis).astype(BF16)
        d_position += head_part(matmul(d_basis, rel[...]), head)
        d_rel[...] += matmul_tn(d_basis, head_part(position, head))
    d_heads[here, :key_width] = ((d_content + d_position) * KEY ** (-0.5)).astype(BF16)
    d_bias[0:1, :] += jnp.sum(d_content, axis=0, keepdims=True)
    d_bias[1:2, :] += jnp.sum(d_position, axis=0, keepdims=True)

    @pl.when(step == blocks - 1)
    def _():
        d_heads[:, key_width : 2 * key_width] = keys_sum[...].T.astype(BF16)
        d_heads[:, 2 * key_width :] = values_sum[...].T.astype(BF16)


def attend_back(placed, rel, table, mixed, d_mixed, probs):
    length = placed.shape[0]
    key_width = rel.shape[1]
    heads = key_width // KEY
    val_width = heads * VAL
    rows = math.gcd(256, length)
    at = jnp.arange(rows)
    flip = (at[:, None] + at[None, :] == rows - 1).astype(BF16)
    whole = lambda shape: pl.BlockSpec(shape, lambda i: (0, 0))
    block = lambda width: pl.BlockSpec((rows, width), lambda i: (i, 0))
    out_shapes = [
        jax.ShapeDtypeStruct((length, 2 * key_width + val_width), BF16),
        jax.ShapeDtypeStruct((REL, key_width), F32),
        jax.ShapeDtypeStruct((8, key_width), F32),
    ]
    return pl.pallas_call(
        functools.partial(attend_back_kernel, heads, rows),
        grid=(length // rows,),
        in_specs=[
            whole(placed.shape),
            whole(rel.shape),
            whole(table.shape),
            whole(flip.shape),
            block(val_width),
            block(val_width),
            pl.BlockSpec((heads, rows, length), lambda i: (0, i, 0)),
        ],
        out_specs=[whole(out.shape) for out in out_shapes],
        out_shape=out_shapes,
        scratch_shapes=[
            pltpu.VMEM((key_width, length), F32),
            pltpu.VMEM((val_width, length), F32),
        ],
        compiler_params=pltpu.CompilerParams(vmem_limit_bytes=VMEM_LIMIT),
        cost_estimate=pl.CostEstimate(
            flops=2 * heads * length * length * 1536,
            bytes_accessed=2 * heads * length * length + 16 * length * val_width,
            transcendentals=0,
        ),
    )(placed, rel, table, flip, mixed, d_mixed, probs)


def norm_back(unit, scale, gain, grad):
    scaled = grad * gain
    mean_one = jnp.mean(scaled, axis=-1, keepdims=True)
    mean_two = jnp.mean(scaled * unit, axis=-1, keepdims=True)
    return (scaled - mean_one - unit * mean_two) * scale


def whole_spec(array):
    zeros = (0,) * len(array.shape)
    return pl.BlockSpec(array.shape, lambda *_: zeros)


def scalar_spec():
    return pl.BlockSpec(memory_space=pltpu.SMEM)


def params(**more):
    return pltpu.CompilerParams(vmem_limit_bytes=VMEM_LIMIT, **more)


def shape(dims, dtype):
    return jax.ShapeDtypeStruct(tuple(dims), dtype)


def basis_constants(window_len):
    features = REL // 6
    f = np.arange(features, dtype=np.float64)
    half_life = 2.0 ** (3.0 + f * (math.log2(window_len) - 3.0) / (features - 1))
    spread = window_len / (2.0 * features)
    first = window_len / features
    centres = first + f * (window_len - first) / (features - 1)
    concentration = (centres / spread) ** 2
    rate = centres / spread**2
    offset = concentration * np.log(rate) - np.array([math.lgamma(c) for c in concentration])
    columns = [math.log(2.0) / half_life, 2.0 ** (f + 1) - 1.0, concentration - 1.0, rate, offset]
    columns += [np.zeros(features)] * 3
    return np.stack(columns, axis=1).astype(np.float32)


def table_kernel(length, constants, forth, back):
    features = REL // 6
    decay, inside_below, power, rate, offset = [constants[:, k : k + 1] for k in range(5)]

    def gamma(distance):
        logged = power * jnp.log(jnp.maximum(distance, 1.0)) - rate * distance + offset
        return jnp.where(distance == 0.0, 0.0, jnp.exp(logged)) + 1e-08

    every = lax.broadcasted_iota(jnp.int32, (1, length), 1).astype(F32)
    peak = jnp.max(gamma(every), axis=1, keepdims=True)
    lanes = lax.broadcasted_iota(jnp.int32, (1, 2 * length), 1).astype(F32)
    for table, signed in ((forth, lanes - length), (back, length - 1 - lanes)):
        distance = jnp.abs(signed)
        sign = jnp.where(signed > 0, 1.0, jnp.where(signed < 0, -1.0, 0.0))
        parts = (
            jnp.exp(-decay * distance),
            jnp.where(inside_below > distance, 1.0, 0.0),
            gamma(distance) / peak,
        )
        for k, part in enumerate(parts):
            table[k * features : (k + 1) * features, :] = part.astype(BF16)
            table[(3 + k) * features : (4 + k) * features, :] = (sign * part).astype(BF16)


def basis_tables(constants, length):
    out = shape((REL, 2 * length), BF16)
    return pl.pallas_call(
        functools.partial(table_kernel, length),
        out_shape=[out, out],
        compiler_params=params(),
    )(constants)


def norm_of(rows):
    centre = rows - jnp.mean(rows, axis=1, keepdims=True)
    scale = lax.rsqrt(jnp.mean(centre * centre, axis=1, keepdims=True) + 1e-05)
    return centre * scale, scale


def project_kernel(blocks, row_count, *refs):
    parts, (weight, vectors, bias, window, hidden, heads, block) = refs[:blocks], refs[blocks:]
    step = pl.program_id(0)
    for k in range(blocks):

        @pl.when(step == k)
        def _():
            block[...] = parts[k][...]

    window[...] = block[...]
    unit, _ = norm_of(block[...].astype(F32))
    normed = (unit * vectors[0:1, :] + vectors[1:2, :]).astype(BF16)
    hidden[...] = normed
    total = None
    for s in range(weight.shape[0]):
        columns = normed[:, s * row_count : (s + 1) * row_count]
        term = matmul(columns, weight[s, :row_count, :])
        total = term if total is None else total + term
    key_width = bias.shape[1] // 2
    query = total[:, :key_width] * KEY ** (-0.5)
    heads[:, :key_width] = (query + bias[0:1, :key_width]).astype(BF16)
    heads[:, key_width : 2 * key_width] = (query + bias[0:1, key_width:]).astype(BF16)
    heads[:, 2 * key_width :] = total[:, key_width:].astype(BF16)


def project(parts, weight, vectors, bias, row_count):
    blocks = len(parts)
    rows, width = parts[0].shape
    heads_width = weight.shape[2] + bias.shape[1] // 2
    out = lambda w: pl.BlockSpec((rows, w), lambda i: (i, 0))
    return pl.pallas_call(
        functools.partial(project_kernel, blocks, row_count),
        grid=(blocks,),
        in_specs=[whole_spec(a) for a in (*parts, weight, vectors, bias)],
        out_specs=[out(width), out(width), out(heads_width)],
        out_shape=[shape((blocks * rows, w), BF16) for w in (width, width, heads_width)],
        scratch_shapes=[pltpu.VMEM((rows, width), BF16)],
        compiler_params=params(),
        cost_estimate=pl.CostEstimate(
            flops=2 * blocks * rows * width * heads_width,
            bytes_accessed=8 * blocks * rows * width,
            transcendentals=0,
        ),
    )(*parts, weight, vectors, bias)


def feed_kernel(count, chunk, *refs):
    parts = 2 * (2 * count - 1)
    where, placed, attended_a, attended_b, grad_rows, vectors, inner_bias = refs[:7]
    weights = refs[7 : 7 + parts]
    layer_output, d_mixed, hidden, activated, d_inner, sums, inner_sums = refs[7 + parts : 14 + parts]
    inner_whole, outer_whole, residual, unit, back, outer_sum, sems = refs[14 + parts :]
    here, core = where[0], where[1]
    copies = []
    for k, whole in enumerate((inner_whole, outer_whole)):
        mine = weights[k * (2 * count - 1) : (k + 1) * (2 * count - 1)]
        size = whole.shape[0] // count
        half = size // 2
        moves = [(mine[0], here * size, size)]
        for m in range(1, count):
            start = jnp.bitwise_xor(here, m) * size
            moves.append((mine[2 * m - 1], start + core * half, half))
            moves.append((mine[2 * m], start + (1 - core) * half, half))
        started = []
        for source, start, rows in moves:
            target = whole.at[pl.ds(pl.multiple_of(start, 16), rows), :]
            copy = pltpu.make_async_copy(source, target, sems.at[k, len(started)])
            copy.start()
            started.append(copy)
        copies.append(started)
    rows, width = placed.shape
    half = width // 2
    residual[:, :half] = placed[:, :half] + attended_a[...] + vectors[2:3, :half]
    residual[:, half:] = placed[:, half:] + attended_b[...] + vectors[2:3, half:]
    normed, scale = norm_of(residual[...])
    unit[...] = normed
    hidden[...] = (normed * vectors[3:4, :] + vectors[4:5, :]).astype(BF16)
    for started in copies:
        for copy in started:
            copy.wait()
    ff = outer_whole.shape[0]
    for c in range(ff // chunk):
        at = slice(c * chunk, (c + 1) * chunk)
        inner = matmul(hidden[...], inner_whole[:, at]) + inner_bias[0:1, at]
        below = 0.5 * (1.0 + lax.erf(inner * (0.5**0.5)))
        slope = below + inner * jnp.exp(-0.5 * inner * inner) * (0.5 / math.pi) ** 0.5
        active = (inner * below).astype(BF16)
        activated[:, at] = active
        grad = (matmul_nt(grad_rows[...], outer_whole[at, :]) * slope).astype(BF16)
        d_inner[:, at] = grad
        inner_sums[:, at] = jnp.sum(grad.astype(F32), axis=0, keepdims=True)
        back_term = matmul_nt(grad, inner_whole[:, at])
        outer_term = matmul(active, outer_whole[at, :])
        if c == 0:
            back[...] = back_term
            outer_sum[...] = outer_term
        else:
            back[...] += back_term
            outer_sum[...] += outer_term
    layer_output[...] = (residual[...] + outer_sum[...] + vectors[5:6, :]).astype(BF16)
    grad, normed = back[...], unit[...]
    dy = grad_rows[...].astype(F32)
    scaled = grad * vectors[3:4, :]
    mean_one = jnp.mean(scaled, axis=1, keepdims=True)
    mean_two = jnp.mean(scaled * normed, axis=1, keepdims=True)
    mixed_in = (dy + (scaled - mean_one - normed * mean_two) * scale).astype(BF16)
    d_mixed[...] = mixed_in
    sums[...] = jnp.zeros_like(sums)
    sums[2:3, :] = jnp.sum(mixed_in.astype(F32), axis=0, keepdims=True)
    sums[3:4, :] = jnp.sum(grad * normed, axis=0, keepdims=True)
    sums[4:5, :] = jnp.sum(grad, axis=0, keepdims=True)
    sums[5:6, :] = jnp.sum(dy, axis=0, keepdims=True)


def feed_forward(where, placed, attended, grad_rows, vectors, inner_bias, inner_parts, outer_parts):
    rows, width = placed.shape
    ff = inner_bias.shape[1]
    count = (len(inner_parts) + 1) // 2
    chunk = math.gcd(512, ff)
    weights = (*inner_parts, *outer_parts)
    small = (placed, *attended, grad_rows, vectors, inner_bias)
    outs = [
        shape((rows, width), BF16),
        shape((rows, width), BF16),
        shape((rows, width), BF16),
        shape((rows, ff), BF16),
        shape((rows, ff), BF16),
        shape((8, width), F32),
        shape((1, ff), F32),
    ]
    return pl.pallas_call(
        functools.partial(feed_kernel, count, chunk),
        in_specs=[scalar_spec()]
        + [pl.BlockSpec(memory_space=pltpu.VMEM) for _ in small]
        + [pl.BlockSpec(memory_space=pl.ANY) for _ in weights],
        out_specs=[pl.BlockSpec(memory_space=pltpu.VMEM) for _ in outs],
        out_shape=outs,
        scratch_shapes=[
            pltpu.VMEM((width, ff), BF16),
            pltpu.VMEM((ff, width), BF16),
            pltpu.VMEM((rows, width), F32),
            pltpu.VMEM((rows, width), F32),
            pltpu.VMEM((rows, width), F32),
            pltpu.VMEM((rows, width), F32),
            pltpu.SemaphoreType.DMA((2, 2 * count - 1)),
        ],
        compiler_params=params(),
        cost_estimate=pl.CostEstimate(
            flops=8 * rows * width * ff,
            bytes_accessed=4 * width * ff + 40 * rows * width,
            transcendentals=2 * rows * ff,
        ),
    )(where, *small, *weights)


def columns_at(ref, index, size, scratch):
    if size % 128 == 0:
        return ref[:, pl.ds(pl.multiple_of(index * size, 128), size)]
    for k in range(ref.shape[1] // size):

        @pl.when(index == k)
        def _():
            scratch[...] = ref[:, k * size : (k + 1) * size]

    return scratch[...]


def away_kernel(
    count, where, hidden, activated, d_inner, grad_rows, inner_away, outer_away, some, more
):
    here, other = where[0], 1 - where[1]
    rows = hidden.shape[1] // count
    ff = d_inner.shape[1]
    ff_rows = ff // count
    half = pl.ds(pl.multiple_of(other * (ff // 2), 128), ff // 2)
    step = pl.program_id(0)
    shard = jnp.bitwise_xor(here, step)
    columns = columns_at(hidden, shard, rows, some)
    inner_away[0] = matmul_tn(columns, d_inner[:, half]).astype(BF16)
    columns = columns_at(activated, 2 * shard + other, ff_rows // 2, more)
    outer_away[0] = matmul_tn(columns, grad_rows[...]).astype(BF16)


def kept_kernel(
    count, where, hidden, activated, d_inner, grad_rows, inner_came, outer_came, *refs
):
    outs, (some, more) = refs[:-2], refs[-2:]
    here, core = where[0], where[1]
    rows = hidden.shape[1] // count
    ff = d_inner.shape[1]
    ff_rows = ff // count
    half = pl.ds(pl.multiple_of(core * (ff // 2), 128), ff // 2)
    step = pl.program_id(0)
    shard = jnp.bitwise_xor(here, step)
    columns = columns_at(hidden, shard, rows, some)
    inner = matmul_tn(columns, d_inner[:, half]) + inner_came[0].astype(F32)
    columns = columns_at(activated, 2 * shard + core, ff_rows // 2, more)
    outer = matmul_tn(columns, grad_rows[...]) + outer_came[0].astype(F32)
    for k, result in enumerate((inner, outer)):
        side = result.shape[1] // 2
        for m in range(count):

            @pl.when(step == m)
            def _():
                outs[2 * (k * count + m)][...] = result[:, :side].astype(BF16)
                outs[2 * (k * count + m) + 1][...] = result[:, side:].astype(BF16)


def ff_gradients(count, where, hidden, activated, d_inner, grad_rows, came=None):
    rows = hidden.shape[1] // count
    ff = d_inner.shape[1]
    wide = [(rows, ff // 2), (ff // count // 2, grad_rows.shape[1])]
    block = lambda dims: pl.BlockSpec((1,) + dims, lambda i: (i, 0, 0))
    small = (hidden, activated, d_inner, grad_rows)
    if came is None:
        kernel, extra = away_kernel, ()
        out_specs = [block(dims) for dims in wide]
        outs = [shape((count,) + dims, BF16) for dims in wide]
    else:
        kernel, extra = kept_kernel, came
        outs = [shape((d[0], d[1] // 2), BF16) for d in wide for _ in range(2 * count)]
        out_specs = [whole_spec(out) for out in outs]
    return pl.pallas_call(
        functools.partial(kernel, count),
        grid=(count,),
        in_specs=[scalar_spec()]
        + [whole_spec(a) for a in small]
        + [block(dims) for dims in wide[: len(extra)]],
        out_specs=out_specs,
        out_shape=outs,
        scratch_shapes=[
            pltpu.VMEM((hidden.shape[0], rows), BF16),
            pltpu.VMEM((hidden.shape[0], ff // count // 2), BF16),
        ],
        compiler_params=params(),
        cost_estimate=pl.CostEstimate(
            flops=2 * hidden.shape[0] * hidden.shape[1] * ff,
            bytes_accessed=8 * rows * count * ff,
            transcendentals=0,
        ),
    )(where, *small, *extra)


def mixed_back_kernel(count, parts_count, *refs):
    where, mixed, weight = refs[:3]
    parts = refs[3 : 3 + parts_count]
    d_attended, out_away, out_kept, out_sum = refs[3 + parts_count :]
    here, core = where[0], where[1]
    rows = parts[0].shape[0]
    for k, part in enumerate(parts):
        start = jnp.bitwise_xor(here, k // 2) * (2 * rows) + (k % 2) * rows
        at = pl.ds(pl.multiple_of(start, 32), rows)
        d_attended[at, :] = matmul_nt(part[...], weight[...]).astype(BF16)
        term = matmul_tn(mixed[at, :], part[...])
        if k == 0:
            out_sum[...] = term
        else:
            out_sum[...] += term
    half = out_kept.shape[0]
    out_kept[...] = out_sum[pl.ds(pl.multiple_of(core * half, 32), half), :]
    out_away[...] = out_sum[pl.ds(pl.multiple_of((1 - core) * half, 32), half), :].astype(BF16)


def mixed_back(count, where, mixed, weight, parts):
    length, val_width = mixed.shape
    width = weight.shape[1]
    vmem = pl.BlockSpec(memory_space=pltpu.VMEM)
    return pl.pallas_call(
        functools.partial(mixed_back_kernel, count, len(parts)),
        in_specs=[scalar_spec()] + [vmem] * (2 + len(parts)),
        out_specs=[vmem] * 3,
        out_shape=[
            shape((length, val_width), BF16),
            shape((val_width // 2, width), BF16),
            shape((val_width // 2, width), F32),
        ],
        scratch_shapes=[pltpu.VMEM((val_width, width), F32)],
        compiler_params=params(),
        cost_estimate=pl.CostEstimate(
            flops=4 * length * val_width * width,
            bytes_accessed=2 * length * (width + 2 * val_width),
            transcendentals=0,
        ),
    )(where, mixed, weight, *parts)


def project_back_kernel(
    count,
    where,
    order,
    d_heads,
    window,
    hidden,
    weight,
    sums,
    inner_sums,
    d_bias,
    d_rel,
    kept,
    away,
    *refs,
):
    d_normed, (grads, first_sums) = refs[: 2 * count], refs[2 * count :]
    here, core = where[0], where[1]
    step = pl.program_id(0)
    rows, width = window.shape
    row_count = rows
    length = order.shape[1]
    key_width = d_rel.shape[1]
    start = jnp.bitwise_xor(here, step) * row_count
    bins = lax.broadcasted_iota(jnp.int32, (rows, length), 0) + start
    picks = jnp.where(order[0:1, :] == bins, 1.0, 0.0).astype(BF16)
    d_along = matmul(picks, d_heads[...]).astype(BF16)
    unit, _ = norm_of(window[...].astype(F32))

    @pl.when(step == 0)
    def _():
        grads[...] = jnp.zeros_like(grads)
        first_sums[...] = jnp.zeros_like(first_sums)

    for s in range(count):
        at = slice(s * row_count, (s + 1) * row_count)
        grads[s, :row_count, :] += matmul_tn(hidden[:, at], d_along)
        normed = matmul_nt(d_along, weight[s, :row_count, :])
        first_sums[0:1, at] += jnp.sum(normed * unit[:, at], axis=0, keepdims=True)
        first_sums[1:2, at] += jnp.sum(normed, axis=0, keepdims=True)
        side, inside = divmod(s * row_count, width // 2)
        for m in range(count):

            @pl.when(step == m)
            def _():
                d_normed[2 * m + side][:, inside : inside + row_count] = normed.astype(BF16)

    @pl.when(step == count - 1)
    def _():
        rel_rows = d_rel.shape[0] // count
        for s in range(count):
            at = slice(s * row_count, (s + 1) * row_count)
            grads[s, row_count : row_count + 2, :row_count] = first_sums[0:2, at]
            grads[s, row_count + 2 : row_count + 6, :row_count] = sums[2:6, at]
            for j in range(2):
                part = slice((2 * s + j) * row_count, (2 * s + j + 1) * row_count)
                grads[s, row_count + 6 + j : row_count + 7 + j, :row_count] = inner_sums[0:1, part]
            for j in range(-(-rel_rows // EXTRA)):
                some = d_rel[s * rel_rows + j * EXTRA : s * rel_rows + min(rel_rows, (j + 1) * EXTRA), :]
                lane = row_count + j * key_width
                grads[s, row_count : row_count + some.shape[0], lane : lane + key_width] = some
        for s in range(count):

            @pl.when(here == s)
            def _():
                grads[s, row_count + 8 : row_count + 10, :key_width] = d_bias[0:2, :]

        half = kept.shape[1]
        kept[...] = grads[:, pl.ds(pl.multiple_of(core * half, 16), half), :].astype(BF16)
        away[...] = grads[:, pl.ds(pl.multiple_of((1 - core) * half, 16), half), :].astype(BF16)


def project_back(count, where, order, d_heads, window, hidden, weight, sums, inner_sums, d_bias, d_rel):
    length, width = window.shape
    rows = length // count
    heads_width = d_heads.shape[1]
    packed = (count, rows + EXTRA, heads_width)
    block = pl.BlockSpec((rows, width), lambda i: (i, 0))
    outs = [shape((count, packed[1] // 2, heads_width), BF16) for _ in range(2)]
    outs += [shape((rows, width // 2), BF16) for _ in range(2 * count)]
    return pl.pallas_call(
        functools.partial(project_back_kernel, count),
        grid=(count,),
        in_specs=[scalar_spec(), whole_spec(order), whole_spec(d_heads), block, block]
        + [whole_spec(a) for a in (weight, sums, inner_sums, d_bias, d_rel)],
        out_specs=[whole_spec(out) for out in outs],
        out_shape=outs,
        scratch_shapes=[pltpu.VMEM(packed, F32), pltpu.VMEM((8, width), F32)],
        compiler_params=params(),
        cost_estimate=pl.CostEstimate(
            flops=2 * length * heads_width * (length + 2 * width),
            bytes_accessed=4 * length * width + 2 * length * (width + heads_width),
            transcendentals=0,
        ),
    )(where, order, d_heads, window, hidden, weight, sums, inner_sums, d_bias, d_rel)


def swap(array, mask, count):
    return lax.ppermute(array, "seq", [(i, i ^ mask) for i in range(count)])


def bit_orders(count):
    bits = [1 << k for k in range(count.bit_length() - 1)]
    return bits, bits[::-1]


def pin(*arrays):
    return lax.optimization_barrier(arrays)


def unpack_kernel(count, row_count, key_width, *refs):
    where, parts, (query, key, value, extra, whole) = refs[0], refs[1:5], refs[5:]
    half = parts[0].shape[1]
    group = parts[0].shape[0]
    core = where[1]
    for k in range(2):
        mine, theirs = parts[2 * k], parts[2 * k + 1]
        for c in range(2):

            @pl.when(core == c)
            def _():
                whole[k * group : (k + 1) * group, c * half : (c + 1) * half, :] = mine[...]
                whole[k * group : (k + 1) * group, (1 - c) * half : (2 - c) * half, :] = theirs[...]

    for out, at in ((query, 0), (key, key_width), (value, 2 * key_width)):
        size = out.shape[1] // count
        for s in range(count):
            rows = whole[s, :row_count, at : at + size]
            out[:, s * size : (s + 1) * size] = rows.astype(F32)
    extra[...] = whole[:, row_count:, :].astype(F32)


def unpack(where, parts, row_count, key_width, val_width):
    group, half, width = parts[0].shape
    count = 2 * group
    vmem = pl.BlockSpec(memory_space=pltpu.VMEM)
    return pl.pallas_call(
        functools.partial(unpack_kernel, count, row_count, key_width),
        in_specs=[scalar_spec()] + [vmem] * 4,
        out_specs=[vmem] * 4,
        out_shape=[
            shape((row_count, count * key_width), F32),
            shape((row_count, count * key_width), F32),
            shape((row_count, count * val_width), F32),
            shape((count, EXTRA, width), F32),
        ],
        scratch_shapes=[pltpu.VMEM((count, 2 * half, width), BF16)],
        compiler_params=params(),
    )(where, *parts)


class Exchange:
    def __init__(self):
        self.new = {}


def pin_all(exchanges, *arrays):
    keys = [sorted(e.new) for e in exchanges]
    out = pin(*arrays, *[e.new[k] for e, ks in zip(exchanges, keys) for k in ks])
    at = len(arrays)
    for e, ks in zip(exchanges, keys):
        e.new = dict(zip(ks, out[at : at + len(ks)]))
        at += len(ks)
    return out[: len(arrays)]


class Gather(Exchange):
    def __init__(self, part, order, count):
        super().__init__()
        self.have, self.order, self.count, self.last = {0: part}, order, count, [0]

    def take(self):
        self.have.update(self.new)
        self.new = {}

    def send(self):
        self.take()
        new = {}
        for m in self.last:
            used = [k for k, bit in enumerate(self.order) if m & bit]
            for bit in self.order[max(used, default=-1) + 1 :]:
                new[m | bit] = swap(self.have[m], bit, self.count)
        self.new, self.last = new, sorted(new)


class Scatter(Exchange):
    def __init__(self, blocks, order, count):
        super().__init__()
        self.have, self.order, self.count, self.step = dict(enumerate(blocks)), order, count, 0

    def take(self):
        if self.new:
            bit = self.order[self.step - 1]
            self.have = {
                m: self.have[m].astype(F32) + self.new[m | bit].astype(F32)
                for m in self.have
                if not m & bit
            }
            self.new = {}

    def send(self):
        self.take()
        bit = self.order[self.step]
        self.new = {
            m: swap(self.have[m].astype(BF16), bit, self.count)
            for m in sorted(self.have, reverse=True)
            if m & bit
        }
        self.step += 1

    def rest(self):
        while self.step < len(self.order):
            self.send()
        self.take()
        return self.have[0]


class LineSum(Exchange):
    def __init__(self, piece, count):
        super().__init__()
        self.total, self.count, self.step = piece, count, 0
        self.inward = count // 2 - 1
        self.steps = 2 * self.inward + 1 if count > 1 else 0

    def take(self):
        if self.new:
            at, came = self.step - 1, self.new[0]
            if at <= self.inward:
                self.total = self.total.astype(F32) + came.astype(F32)
            else:
                index = lax.axis_index("wz")
                far = 2 * self.inward - at
                is_target = (index == far) | (index == self.count - 1 - far)
                self.total = jnp.where(is_target, came, self.total)
            self.new = {}

    def send(self):
        self.take()
        if self.step >= self.steps:
            return
        last = self.count - 1
        if self.step < self.inward:
            k = self.step
            pairs = [(k, k + 1), (last - k, last - k - 1)]
        elif self.step == self.inward:
            k = self.inward
            pairs = [(k, k + 1), (k + 1, k)]
        else:
            k = 2 * self.inward - self.step
            pairs = [(k + 1, k), (last - k - 1, last - k)]
        self.total = self.total.astype(BF16)
        self.new = {0: lax.ppermute(self.total, "wz", pairs)}
        self.step += 1

    def rest(self):
        while self.step < self.steps:
            self.send()
        self.take()
        return self.total.astype(BF16)


class OtherCore(Exchange):
    def __init__(self, array):
        super().__init__()
        self.new = {0: other_core(array)}


def split_columns(blocks, count):
    half = blocks[0].shape[1] // 2
    return [
        Scatter([block[:, k * half : (k + 1) * half] for block in blocks], order, count)
        for k, order in enumerate(bit_orders(count))
    ]


def other_core(array):
    return lax.ppermute(array, "core", [(0, 1), (1, 0)])


def shards(
    seq_count,
    wz_count,
    inputs,
    bin_order,
    first_gain,
    first_shift,
    query_weight,
    key_weight,
    value_weight,
    bias_content,
    bias_position,
    relative_weight,
    out_weight,
    bias_out,
    second_gain,
    second_shift,
    inner_weight,
    bias_inner,
    outer_weight,
    bias_outer,
    grad_output,
):
    row_count, width = inputs.shape[1:]
    length = bin_order.shape[1]
    here = lax.axis_index("seq")
    core = lax.axis_index("core")
    where = jnp.stack([here, core]).astype(jnp.int32)
    row_start = here * row_count
    key_width = query_weight.shape[1] // seq_count
    val_width = value_weight.shape[1] // seq_count
    heads_width = 2 * key_width + val_width
    up, down = bit_orders(seq_count)

    others = [jnp.bitwise_xor(here, m) for m in range(seq_count)]
    along = jnp.concatenate(
        [other * row_count + jnp.arange(row_count, dtype=jnp.int32) for other in others]
    )

    def natural(rows):
        parts = rows.reshape(seq_count, row_count, -1)
        parts = [lax.dynamic_index_in_dim(parts, other, 0) for other in others]
        return jnp.concatenate(parts, axis=0).reshape(rows.shape)

    def halves(rows):
        half = rows.shape[0] // 2
        return [Gather(rows[:half], up, seq_count), Gather(rows[half:], down, seq_count)]

    def blocks_of(gathers):
        for g in gathers:
            g.take()
        return [g.have[m] for m in range(seq_count) for g in gathers]

    window_gathers = halves(inputs[0])
    for g in window_gathers:
        g.send()

    def by_head(weight):
        return weight.reshape(weight.shape[0], seq_count, -1)

    vectors = jnp.stack([first_gain, first_shift, bias_out, second_gain, second_shift, bias_outer])
    vectors = jnp.concatenate([vectors, bias_inner.reshape(2, row_count)], axis=0)
    vectors = jnp.pad(vectors, ((0, EXTRA - 8), (0, 0)))
    rel_rows = relative_weight.shape[0]
    rel_blocks = -(-rel_rows // EXTRA)
    rel_part = jnp.pad(by_head(relative_weight), ((0, rel_blocks * EXTRA - rel_rows), (0, 0), (0, 0)))
    rel_part = rel_part.reshape(rel_blocks, EXTRA, seq_count, key_width).transpose(2, 1, 0, 3)
    rel_part = rel_part.reshape(seq_count, EXTRA, -1)
    spare = heads_width - row_count - rel_part.shape[2]
    extra = jnp.concatenate(
        [
            jnp.broadcast_to(vectors[None], (seq_count,) + vectors.shape),
            jnp.pad(rel_part, ((0, 0), (0, 0), (0, spare))),
        ],
        axis=2,
    )
    mine = jnp.concatenate(
        [by_head(query_weight), by_head(key_weight), by_head(value_weight)], axis=2
    ).transpose(1, 0, 2)
    mine = jnp.concatenate([mine, extra], axis=1)
    (mine,) = pin_all(window_gathers, mine)
    for step in range(1, len(up)):
        for g in window_gathers:
            g.send()
    half = mine.shape[1] // 2
    mine = lax.dynamic_slice_in_dim(mine, core * half, half, 1)
    mine = lax.all_to_all(mine, "seq", 0, 0, tiled=True)
    first = core == 0
    theirs = other_core(mine)
    attention_weight = jnp.concatenate(
        [jnp.where(first, mine, theirs), jnp.where(first, theirs, mine)], axis=1
    )
    table, table_back = basis_tables(jnp.asarray(basis_constants(length)), length)
    flat = attention_weight[:, row_count:]
    vectors = flat[:, :8, :row_count].astype(F32)
    inner_bias = vectors[:, 6:8].reshape(1, -1)
    vectors = vectors.transpose(1, 0, 2).reshape(8, width)
    rel = flat[:, :, row_count : row_count + rel_blocks * key_width]
    rel = rel.reshape(seq_count, EXTRA, rel_blocks, key_width).transpose(0, 2, 1, 3)
    rel = rel.reshape(seq_count, rel_blocks * EXTRA, key_width)[:, :rel_rows].reshape(REL, key_width)

    def own_half(weight):
        half = weight.shape[0] // 2
        return lax.dynamic_slice_in_dim(weight, core * half, half, 0)

    inner_part, outer_part = own_half(inner_weight), own_half(outer_weight)
    inner_part, outer_part = pin_all(window_gathers, inner_part, outer_part)
    window_blocks = blocks_of(window_gathers)
    weight_gathers = [
        Gather(inner_part, up, seq_count),
        Gather(outer_part, down, seq_count),
    ]
    for g in weight_gathers:
        g.send()

    order = bin_order[0]
    placing = (order[:, None] == along[None, :]).astype(BF16)
    bias = jnp.concatenate([bias_content, bias_position])[None].astype(F32)
    window, hidden_one, in_bins = project(
        window_blocks, attention_weight, vectors, bias, row_count
    )
    placed_heads = matmul(placing, in_bins).astype(BF16)
    mixed, probs = attend(placed_heads, rel, table)
    (mixed,) = pin_all(weight_gathers, mixed)
    for step in range(1, len(up)):
        for g in weight_gathers:
            g.send()
    weight_parts = []
    for g, own in zip(weight_gathers, (inner_weight, outer_weight)):
        g.take()
        parts = [own]
        for m in range(1, seq_count):
            parts += [g.have[m], other_core(g.have[m])]
        weight_parts.append(parts)
    mixed_along = natural(mixed).reshape(seq_count, row_count, val_width)
    attended = [matmul(mixed_along[m], out_weight).astype(BF16) for m in range(seq_count)]
    attended = split_columns(attended, seq_count)
    for g in attended:
        g.send()
    own_order = lax.dynamic_slice_in_dim(order, row_start, row_count, 0)
    placed = matmul((own_order[:, None] == along[None, :]).astype(BF16), window)
    (placed,) = pin_all(attended, placed)
    attended = [g.rest() for g in attended]

    grad_rows = grad_output[0]
    layer_output, d_mixed_in, hidden_two, activated, d_inner, sums, inner_sums = feed_forward(
        where, placed, attended, grad_rows, vectors, inner_bias, *weight_parts
    )

    d_mixed_gathers = halves(d_mixed_in)
    for g in d_mixed_gathers:
        g.send()
    away = ff_gradients(seq_count, where, hidden_two, activated, d_inner, grad_rows)
    away = pin_all(d_mixed_gathers, *away)
    for step in range(1, len(up)):
        for g in d_mixed_gathers:
            g.send()
    came = [other_core(part) for part in away]
    kept = ff_gradients(seq_count, where, hidden_two, activated, d_inner, grad_rows, came)
    kept = pin_all(d_mixed_gathers, *kept)
    d_mixed_blocks = blocks_of(d_mixed_gathers)
    count = seq_count
    inner_sums_of, outer_sums_of = [
        [
            Scatter([kept[2 * (k * count + m) + side] for m in range(count)], bits, count)
            for side, bits in enumerate((up, down))
        ]
        for k in range(2)
    ]
    for g in inner_sums_of:
        g.send()

    d_attended, out_away, grad_out_w = mixed_back(
        seq_count, where, mixed, out_weight, d_mixed_blocks
    )
    out_core = OtherCore(out_away)
    d_heads, d_rel, d_bias = attend_back(placed_heads, rel, table_back, mixed, d_attended, probs)
    (d_heads,) = pin_all(inner_sums_of, d_heads)
    for step in range(1, len(up)):
        for g in inner_sums_of:
            g.send()
    for g in outer_sums_of:
        g.send()
    results = project_back(
        seq_count,
        where,
        order[None],
        d_heads,
        window,
        hidden_one,
        attention_weight,
        sums,
        inner_sums,
        d_bias,
        d_rel,
    )
    results = pin_all(inner_sums_of + outer_sums_of + [out_core], *results)

    def send_all(exchanges):
        for exchange in exchanges:
            exchange.send()

    inner_lines = [LineSum(g.rest(), wz_count) for g in inner_sums_of]
    send_all(inner_lines)
    for step in range(1, len(up)):
        send_all(outer_sums_of)
    packed, packed_core = results[0], OtherCore(results[1])
    arrived = [
        Scatter([results[2 + 2 * m + side] for m in range(count)], bits, count)
        for side, bits in enumerate((up, down))
    ]
    out_line = LineSum(grad_out_w + out_core.new[0].astype(F32), wz_count)

    own_bins = row_start + jnp.arange(row_count, dtype=jnp.int32)
    order_parts = order.reshape(2 * seq_count, row_count // 2)
    returned = None
    for k, block in enumerate(d_mixed_blocks):
        at = lax.dynamic_index_in_dim(order_parts, 2 * others[k // 2] + k % 2, 0)
        term = matmul((at == own_bins[:, None]).astype(BF16), block)
        returned = term if returned is None else returned + term
    returned, packed = pin_all([packed_core] + outer_sums_of + inner_lines, returned, packed)

    outer_lines = [LineSum(g.rest(), wz_count) for g in outer_sums_of]
    send_all(outer_lines + inner_lines + [out_line])
    packed = (packed.astype(F32) + packed_core.new[0].astype(F32)).astype(BF16)
    packed = lax.all_to_all(packed, "seq", 0, 0, tiled=True)
    send_all(arrived)
    (packed,) = pin_all(arrived + outer_lines + inner_lines + [out_line], packed)

    packed_lines = [
        LineSum(packed[: seq_count // 2], wz_count),
        LineSum(packed[seq_count // 2 :], wz_count),
    ]
    for step in range(1, len(up)):
        send_all(arrived)
    send_all(packed_lines + outer_lines + inner_lines + [out_line])
    pin_all(arrived + packed_lines + outer_lines + inner_lines + [out_line])

    send_all(packed_lines + outer_lines + [out_line])
    own_unit, own_scale = norm_of(inputs[0].astype(F32))
    arrived = jnp.concatenate([g.rest() for g in arrived], axis=1)
    grad_inputs = norm_back(own_unit, own_scale, vectors[0:1], arrived) + returned

    def by_cores(line):
        piece = line.rest()
        other = other_core(piece)
        return jnp.where(first, piece, other), jnp.where(first, other, piece)

    inner_parts = [by_cores(g) for g in inner_lines]
    grad_inner_w = jnp.concatenate(
        [part[k] for k in range(2) for part in inner_parts], axis=1
    ).astype(F32)
    grad_inputs, grad_inner_w = pin_all(
        packed_lines + outer_lines + [out_line], grad_inputs, grad_inner_w
    )

    send_all(packed_lines)
    outer_parts = [jnp.concatenate(by_cores(g), axis=0) for g in outer_lines]
    grad_outer_w = jnp.concatenate(outer_parts, axis=1).astype(F32)
    grad_out_w = jnp.concatenate(by_cores(out_line), axis=0).astype(F32)
    grad_outer_w, grad_out_w = pin_all(packed_lines, grad_outer_w, grad_out_w)
    packed_parts = [part for g in packed_lines for part in (g.rest(), other_core(g.rest()))]
    grad_query_w, grad_key_w, grad_value_w, flat = unpack(
        where, packed_parts, row_count, key_width, val_width
    )
    small = jnp.sum(flat[:, :16, :row_count], axis=0)
    g_gain_one, g_shift_one, g_out_b, g_gain_two, g_shift_two, g_outer_b = small[:6]
    g_inner_b = small[6:8].reshape(-1)
    grad_rel = flat[:, :, row_count : row_count + rel_blocks * key_width]
    grad_rel = grad_rel.reshape(seq_count, EXTRA, rel_blocks, key_width).transpose(2, 1, 0, 3)
    grad_rel = grad_rel.reshape(rel_blocks * EXTRA, -1)[:rel_rows]
    return (
        layer_output[None],
        grad_inputs[None],
        g_gain_one,
        g_shift_one,
        grad_query_w,
        grad_key_w,
        grad_value_w,
        small[8, :key_width],
        small[9, :key_width],
        grad_rel,
        grad_out_w,
        g_out_b,
        g_gain_two,
        g_shift_two,
        grad_inner_w,
        g_inner_b,
        grad_outer_w,
        g_outer_b,
    )


def solution(mesh):
    seq_count = mesh.shape["seq"]
    devices = mesh.devices.reshape(seq_count, -1, 2)
    split_mesh = Mesh(devices, ("seq", "wz", "core"))
    rows = P(("wz", "core"), "seq", None)
    vector = P("seq")
    matrix = P("seq", None)
    weights = (
        vector,
        vector,
        matrix,
        matrix,
        matrix,
        vector,
        vector,
        matrix,
        matrix,
        vector,
        vector,
        vector,
        matrix,
        vector,
        matrix,
        vector,
    )
    return jax.shard_map(
        functools.partial(shards, seq_count, mesh.shape["win"] // 2),
        mesh=split_mesh,
        in_specs=(rows, P(("wz", "core"), None)) + weights + (rows,),
        out_specs=(rows, rows) + weights,
        check_vma=False,
    )
```

```python
import functools
import math

import jax
import jax.numpy as jnp
import numpy as np
from jax import lax
from jax.experimental import pallas as pl
from jax.experimental.pallas import tpu as pltpu
from jax.sharding import Mesh
from jax.sharding import PartitionSpec as P

HEADS = 8
KEY = 64
VAL = 192
REL = 192
BF16 = jnp.bfloat16
F32 = jnp.float32
VMEM_LIMIT = 56 * 2**20
EXTRA = 32


def matmul(a, b):
    return lax.dot_general(a, b, (((1,), (0,)), ((), ())), preferred_element_type=F32)


def matmul_nt(a, b):
    return lax.dot_general(a, b, (((1,), (1,)), ((), ())), preferred_element_type=F32)


def matmul_tn(a, b):
    return lax.dot_general(a, b, (((0,), (0,)), ((), ())), preferred_element_type=F32)


def head_part(rows, head):
    lanes = lax.broadcasted_iota(jnp.int32, rows.shape, 1)
    inside = (lanes >= head * KEY) & (lanes < (head + 1) * KEY)
    return jnp.where(inside, rows, jnp.zeros_like(rows))


def head_columns(key_width):
    return [slice(k * key_width, (k + 1) * key_width) for k in range(3)]


def attend_kernel(heads, rows, placed, rel, table, mixed, probs):
    length = placed.shape[0]
    key_width = heads * KEY
    content_at, position_at, keys_at = head_columns(key_width)
    first = pl.program_id(0) * rows
    here = pl.ds(pl.multiple_of(first, rows), rows)
    basis = table[:, pl.ds(pl.multiple_of(length - rows - first, rows), length + rows)]
    content, position, keys = placed[here, content_at], placed[here, position_at], placed[:, keys_at]
    parts = []
    for head in range(heads):
        q_basis = matmul_nt(head_part(position, head), rel[...]).astype(BF16)
        grid = matmul(q_basis, basis)
        shifted = pltpu.roll(grid, 0, 1, stride=1, stride_axis=0)[:, rows:]
        scores = matmul_nt(head_part(content, head), keys) + shifted
        top = jnp.max(scores, axis=1, keepdims=True)
        weights = jnp.exp(scores - top)
        total = jnp.sum(weights, axis=1, keepdims=True)
        prob = (weights * (1.0 / total)).astype(BF16)
        probs[head] = prob
        values_at = 3 * key_width + head * VAL
        parts.append(matmul(prob, placed[:, values_at : values_at + VAL]))
    mixed[...] = jnp.concatenate(parts, axis=1).astype(BF16)


def attend(placed, rel, table):
    length = placed.shape[0]
    heads = rel.shape[1] // KEY
    rows = math.gcd(256, length)
    whole = lambda array: pl.BlockSpec(array.shape, lambda i: (0, 0))
    return pl.pallas_call(
        functools.partial(attend_kernel, heads, rows),
        grid=(length // rows,),
        in_specs=[whole(placed), whole(rel), whole(table)],
        out_specs=[
            pl.BlockSpec((rows, heads * VAL), lambda i: (i, 0)),
            pl.BlockSpec((heads, rows, length), lambda i: (0, i, 0)),
        ],
        out_shape=[
            jax.ShapeDtypeStruct((length, heads * VAL), BF16),
            jax.ShapeDtypeStruct((heads, length, length), BF16),
        ],
        compiler_params=pltpu.CompilerParams(vmem_limit_bytes=VMEM_LIMIT),
        cost_estimate=pl.CostEstimate(
            flops=2 * heads * length * length * 1024,
            bytes_accessed=2 * heads * length * length + 8 * length * heads * VAL,
            transcendentals=heads * length * length,
        ),
    )(placed, rel, table)


def attend_back_kernel(heads, head, rows, *refs):
    placed, rel, table, flip, mixed, d_mixed, probs = refs[:7]
    before = refs[7:-5]
    d_heads, d_rel, d_bias, keys_sum, values_sum = refs[-5:]
    length = placed.shape[0]
    key_width = heads * KEY
    content_at, position_at, keys_at = head_columns(key_width)
    step = pl.program_id(0)

    @pl.when(step == 0)
    def _():
        keys_sum[...] = jnp.zeros_like(keys_sum)
        values_sum[...] = jnp.zeros_like(values_sum)
        for k, out in enumerate((d_heads, d_rel, d_bias)):
            out[...] = before[k][...] if before else jnp.zeros_like(out)

    first = pl.multiple_of(step * rows, rows)
    here = pl.ds(first, rows)
    basis = table[:, pl.ds(first, length + rows)]
    content, position, keys = placed[here, content_at], placed[here, position_at], placed[:, keys_at]
    blocks = length // rows
    columns = slice(head * VAL, (head + 1) * VAL)
    values_at = 3 * key_width + head * VAL
    d_part = d_mixed[:, columns]
    delta = jnp.sum(d_part.astype(F32) * mixed[:, columns].astype(F32), axis=1, keepdims=True)
    prob = probs[0]
    values_sum[...] += matmul_tn(d_part, prob)
    d_prob = matmul_nt(d_part, placed[:, values_at : values_at + VAL])
    d_score = (prob.astype(F32) * (d_prob - delta)).astype(BF16)
    keys_sum[...] += matmul_tn(head_part(content, head), d_score)
    d_content = head_part(matmul(d_score, keys), head)
    turned = [
        matmul(d_score[:, (blocks - 1 - b) * rows : (blocks - b) * rows], flip[...])
        for b in range(blocks)
    ]
    turned = jnp.concatenate(turned + [jnp.zeros((rows, rows), F32)], axis=1)
    d_grid = pltpu.roll(turned, 0, 1, stride=1, stride_axis=0).astype(BF16)
    d_basis = matmul_nt(d_grid, basis).astype(BF16)
    d_position = head_part(matmul(d_basis, rel[...]), head)
    d_rel[...] += matmul_tn(d_basis, head_part(position, head))
    d_heads[here, :key_width] += ((d_content + d_position) * KEY ** (-0.5)).astype(BF16)
    d_bias[0:1, :] += jnp.sum(d_content, axis=0, keepdims=True)
    d_bias[1:2, :] += jnp.sum(d_position, axis=0, keepdims=True)

    @pl.when(step == blocks - 1)
    def _():
        d_heads[:, key_width : 2 * key_width] += keys_sum[...].T.astype(BF16)
        values_to = 2 * key_width + head * VAL
        d_heads[:, values_to : values_to + VAL] = values_sum[...].T.astype(BF16)


def attend_back(head, placed, rel, table, mixed, d_mixed, probs, before=()):
    length = placed.shape[0]
    key_width = rel.shape[1]
    heads = key_width // KEY
    val_width = heads * VAL
    rows = math.gcd(256, length)
    at = jnp.arange(rows)
    flip = (at[:, None] + at[None, :] == rows - 1).astype(BF16)
    block = lambda width: pl.BlockSpec((rows, width), lambda i: (i, 0))
    outs = [
        shape((length, 2 * key_width + val_width), BF16),
        shape((REL, key_width), F32),
        shape((8, key_width), F32),
    ]
    return pl.pallas_call(
        functools.partial(attend_back_kernel, heads, head, rows),
        grid=(length // rows,),
        in_specs=[
            whole_spec(placed),
            whole_spec(rel),
            whole_spec(table),
            whole_spec(flip),
            block(val_width),
            block(val_width),
            pl.BlockSpec((1, rows, length), lambda i: (head, i, 0)),
        ]
        + [whole_spec(array) for array in before],
        out_specs=[whole_spec(out) for out in outs],
        out_shape=outs,
        scratch_shapes=[
            pltpu.VMEM((key_width, length), F32),
            pltpu.VMEM((VAL, length), F32),
        ],
        compiler_params=pltpu.CompilerParams(vmem_limit_bytes=VMEM_LIMIT),
        cost_estimate=pl.CostEstimate(
            flops=2 * length * length * 1536,
            bytes_accessed=2 * length * length + 16 * length * val_width,
            transcendentals=0,
        ),
    )(placed, rel, table, flip, mixed, d_mixed, probs, *before)


def norm_back(unit, scale, gain, grad):
    scaled = grad * gain
    mean_one = jnp.mean(scaled, axis=-1, keepdims=True)
    mean_two = jnp.mean(scaled * unit, axis=-1, keepdims=True)
    return (scaled - mean_one - unit * mean_two) * scale


def whole_spec(array):
    zeros = (0,) * len(array.shape)
    return pl.BlockSpec(array.shape, lambda *_: zeros)


def scalar_spec():
    return pl.BlockSpec(memory_space=pltpu.SMEM)


def params(**more):
    return pltpu.CompilerParams(vmem_limit_bytes=VMEM_LIMIT, **more)


def shape(dims, dtype):
    return jax.ShapeDtypeStruct(tuple(dims), dtype)


def basis_constants(window_len):
    features = REL // 6
    f = np.arange(features, dtype=np.float64)
    half_life = 2.0 ** (3.0 + f * (math.log2(window_len) - 3.0) / (features - 1))
    spread = window_len / (2.0 * features)
    first = window_len / features
    centres = first + f * (window_len - first) / (features - 1)
    concentration = (centres / spread) ** 2
    rate = centres / spread**2
    offset = concentration * np.log(rate) - np.array([math.lgamma(c) for c in concentration])
    columns = [math.log(2.0) / half_life, 2.0 ** (f + 1) - 1.0, concentration - 1.0, rate, offset]
    columns += [np.zeros(features)] * 3
    return np.stack(columns, axis=1).astype(np.float32)


def table_kernel(length, constants, forth, back):
    features = REL // 6
    decay, inside_below, power, rate, offset = [constants[:, k : k + 1] for k in range(5)]

    def gamma(distance):
        logged = power * jnp.log(jnp.maximum(distance, 1.0)) - rate * distance + offset
        return jnp.where(distance == 0.0, 0.0, jnp.exp(logged)) + 1e-08

    every = lax.broadcasted_iota(jnp.int32, (1, length), 1).astype(F32)
    peak = jnp.max(gamma(every), axis=1, keepdims=True)
    lanes = lax.broadcasted_iota(jnp.int32, (1, 2 * length), 1).astype(F32)
    for table, signed in ((forth, lanes - length), (back, length - 1 - lanes)):
        distance = jnp.abs(signed)
        sign = jnp.where(signed > 0, 1.0, jnp.where(signed < 0, -1.0, 0.0))
        parts = (
            jnp.exp(-decay * distance),
            jnp.where(inside_below > distance, 1.0, 0.0),
            gamma(distance) / peak,
        )
        for k, part in enumerate(parts):
            table[k * features : (k + 1) * features, :] = part.astype(BF16)
            table[(3 + k) * features : (4 + k) * features, :] = (sign * part).astype(BF16)


def basis_tables(constants, length):
    out = shape((REL, 2 * length), BF16)
    return pl.pallas_call(
        functools.partial(table_kernel, length),
        out_shape=[out, out],
        compiler_params=params(),
    )(constants)


def norm_of(rows):
    centre = rows - jnp.mean(rows, axis=1, keepdims=True)
    scale = lax.rsqrt(jnp.mean(centre * centre, axis=1, keepdims=True) + 1e-05)
    return centre * scale, scale


def project_kernel(blocks, row_count, *refs):
    parts, (weight, vectors, bias, window, hidden, heads, flat, block) = refs[:blocks], refs[blocks:]
    step = pl.program_id(0)

    @pl.when(step == 0)
    def _():
        for s in range(weight.shape[0]):
            flat[s * row_count : (s + 1) * row_count, :] = weight[s, :row_count, :]

    for k in range(blocks):

        @pl.when(step == k)
        def _():
            block[...] = parts[k][...]

    window[...] = block[...]
    unit, _ = norm_of(block[...].astype(F32))
    normed = (unit * vectors[0:1, :] + vectors[1:2, :]).astype(BF16)
    hidden[...] = normed
    total = matmul(normed, flat[...])
    key_width = bias.shape[1] // 2
    query = total[:, :key_width] * KEY ** (-0.5)
    heads[:, :key_width] = (query + bias[0:1, :key_width]).astype(BF16)
    heads[:, key_width : 2 * key_width] = (query + bias[0:1, key_width:]).astype(BF16)
    heads[:, 2 * key_width :] = total[:, key_width:].astype(BF16)


def project(parts, weight, vectors, bias, row_count):
    blocks = len(parts)
    rows, width = parts[0].shape
    heads_width = weight.shape[2] + bias.shape[1] // 2
    out = lambda w: pl.BlockSpec((rows, w), lambda i: (i, 0))
    return pl.pallas_call(
        functools.partial(project_kernel, blocks, row_count),
        grid=(blocks,),
        in_specs=[whole_spec(a) for a in (*parts, weight, vectors, bias)],
        out_specs=[
            out(width),
            out(width),
            out(heads_width),
            pl.BlockSpec((width, weight.shape[2]), lambda i: (0, 0)),
        ],
        out_shape=[shape((blocks * rows, w), BF16) for w in (width, width, heads_width)]
        + [shape((width, weight.shape[2]), BF16)],
        scratch_shapes=[pltpu.VMEM((rows, width), BF16)],
        compiler_params=params(),
        cost_estimate=pl.CostEstimate(
            flops=2 * blocks * rows * width * heads_width,
            bytes_accessed=8 * blocks * rows * width,
            transcendentals=0,
        ),
    )(*parts, weight, vectors, bias)


def feed_kernel(count, chunk, *refs):
    parts = 2 * (2 * count - 1)
    where, placed, attended_a, attended_b, grad_rows, vectors, inner_bias = refs[:7]
    weights = refs[7 : 7 + parts]
    layer_output, d_mixed, hidden, activated, d_inner, sums, inner_sums = refs[7 + parts : 14 + parts]
    inner_whole, outer_whole, residual, unit, back, outer_sum, sems = refs[14 + parts :]
    here, core = where[0], where[1]
    copies = []
    for k, whole in enumerate((inner_whole, outer_whole)):
        mine = weights[k * (2 * count - 1) : (k + 1) * (2 * count - 1)]
        size = whole.shape[0] // count
        half = size // 2
        moves = [(mine[0], here * size, size)]
        for m in range(1, count):
            start = jnp.bitwise_xor(here, m) * size
            moves.append((mine[2 * m - 1], start + core * half, half))
            moves.append((mine[2 * m], start + (1 - core) * half, half))
        started = []
        for source, start, rows in moves:
            target = whole.at[pl.ds(pl.multiple_of(start, 16), rows), :]
            copy = pltpu.make_async_copy(source, target, sems.at[k, len(started)])
            copy.start()
            started.append(copy)
        copies.append(started)
    rows, width = placed.shape
    half = width // 2
    residual[:, :half] = placed[:, :half] + attended_a[...] + vectors[2:3, :half]
    residual[:, half:] = placed[:, half:] + attended_b[...] + vectors[2:3, half:]
    normed, scale = norm_of(residual[...])
    unit[...] = normed
    hidden[...] = (normed * vectors[3:4, :] + vectors[4:5, :]).astype(BF16)
    for started in copies:
        for copy in started:
            copy.wait()
    ff = outer_whole.shape[0]
    for c in range(ff // chunk):
        at = slice(c * chunk, (c + 1) * chunk)
        inner = matmul(hidden[...], inner_whole[:, at]) + inner_bias[0:1, at]
        below = 0.5 * (1.0 + lax.erf(inner * (0.5**0.5)))
        slope = below + inner * jnp.exp(-0.5 * inner * inner) * (0.5 / math.pi) ** 0.5
        active = (inner * below).astype(BF16)
        activated[:, at] = active
        grad = (matmul_nt(grad_rows[...], outer_whole[at, :]) * slope).astype(BF16)
        d_inner[:, at] = grad
        inner_sums[:, at] = jnp.sum(grad.astype(F32), axis=0, keepdims=True)
        back_term = matmul_nt(grad, inner_whole[:, at])
        outer_term = matmul(active, outer_whole[at, :])
        if c == 0:
            back[...] = back_term
            outer_sum[...] = outer_term
        else:
            back[...] += back_term
            outer_sum[...] += outer_term
    layer_output[...] = (residual[...] + outer_sum[...] + vectors[5:6, :]).astype(BF16)
    grad, normed = back[...], unit[...]
    dy = grad_rows[...].astype(F32)
    scaled = grad * vectors[3:4, :]
    mean_one = jnp.mean(scaled, axis=1, keepdims=True)
    mean_two = jnp.mean(scaled * normed, axis=1, keepdims=True)
    mixed_in = (dy + (scaled - mean_one - normed * mean_two) * scale).astype(BF16)
    d_mixed[...] = mixed_in
    sums[...] = jnp.zeros_like(sums)
    sums[2:3, :] = jnp.sum(mixed_in.astype(F32), axis=0, keepdims=True)
    sums[3:4, :] = jnp.sum(grad * normed, axis=0, keepdims=True)
    sums[4:5, :] = jnp.sum(grad, axis=0, keepdims=True)
    sums[5:6, :] = jnp.sum(dy, axis=0, keepdims=True)


def feed_forward(where, placed, attended, grad_rows, vectors, inner_bias, inner_parts, outer_parts):
    rows, width = placed.shape
    ff = inner_bias.shape[1]
    count = (len(inner_parts) + 1) // 2
    chunk = math.gcd(512, ff)
    weights = (*inner_parts, *outer_parts)
    small = (placed, *attended, grad_rows, vectors, inner_bias)
    outs = [
        shape((rows, width), BF16),
        shape((rows, width), BF16),
        shape((rows, width), BF16),
        shape((rows, ff), BF16),
        shape((rows, ff), BF16),
        shape((8, width), F32),
        shape((1, ff), F32),
    ]
    return pl.pallas_call(
        functools.partial(feed_kernel, count, chunk),
        in_specs=[scalar_spec()]
        + [pl.BlockSpec(memory_space=pltpu.VMEM) for _ in small]
        + [pl.BlockSpec(memory_space=pl.ANY) for _ in weights],
        out_specs=[pl.BlockSpec(memory_space=pltpu.VMEM) for _ in outs],
        out_shape=outs,
        scratch_shapes=[
            pltpu.VMEM((width, ff), BF16),
            pltpu.VMEM((ff, width), BF16),
            pltpu.VMEM((rows, width), F32),
            pltpu.VMEM((rows, width), F32),
            pltpu.VMEM((rows, width), F32),
            pltpu.VMEM((rows, width), F32),
            pltpu.SemaphoreType.DMA((2, 2 * count - 1)),
        ],
        compiler_params=params(),
        cost_estimate=pl.CostEstimate(
            flops=8 * rows * width * ff,
            bytes_accessed=4 * width * ff + 40 * rows * width,
            transcendentals=2 * rows * ff,
        ),
    )(where, *small, *weights)


def columns_at(ref, index, size, scratch):
    if size % 128 == 0:
        return ref[:, pl.ds(pl.multiple_of(index * size, 128), size)]
    for k in range(ref.shape[1] // size):

        @pl.when(index == k)
        def _():
            scratch[...] = ref[:, k * size : (k + 1) * size]

    return scratch[...]


def away_kernel(
    count, where, hidden, activated, d_inner, grad_rows, inner_away, outer_away, some, more
):
    here, other = where[0], 1 - where[1]
    rows = hidden.shape[1] // count
    ff = d_inner.shape[1]
    ff_rows = ff // count
    half = pl.ds(pl.multiple_of(other * (ff // 2), 128), ff // 2)
    step = pl.program_id(0)
    shard = jnp.bitwise_xor(here, step)
    columns = columns_at(hidden, shard, rows, some)
    inner_away[0] = matmul_tn(columns, d_inner[:, half]).astype(BF16)
    columns = columns_at(activated, 2 * shard + other, ff_rows // 2, more)
    outer_away[0] = matmul_tn(columns, grad_rows[...]).astype(BF16)


def kept_kernel(
    count, where, hidden, activated, d_inner, grad_rows, inner_came, outer_came, *refs
):
    outs, (some, more) = refs[:-2], refs[-2:]
    here, core = where[0], where[1]
    rows = hidden.shape[1] // count
    ff = d_inner.shape[1]
    ff_rows = ff // count
    half = pl.ds(pl.multiple_of(core * (ff // 2), 128), ff // 2)
    step = pl.program_id(0)
    shard = jnp.bitwise_xor(here, step)
    columns = columns_at(hidden, shard, rows, some)
    inner = matmul_tn(columns, d_inner[:, half]) + inner_came[0].astype(F32)
    columns = columns_at(activated, 2 * shard + core, ff_rows // 2, more)
    outer = matmul_tn(columns, grad_rows[...]) + outer_came[0].astype(F32)
    for k, result in enumerate((inner, outer)):
        side = result.shape[1] // 2
        for m in range(count):

            @pl.when(step == m)
            def _():
                outs[2 * (k * count + m)][...] = result[:, :side].astype(BF16)
                outs[2 * (k * count + m) + 1][...] = result[:, side:].astype(BF16)


def ff_gradients(count, where, hidden, activated, d_inner, grad_rows, came=None):
    rows = hidden.shape[1] // count
    ff = d_inner.shape[1]
    wide = [(rows, ff // 2), (ff // count // 2, grad_rows.shape[1])]
    block = lambda dims: pl.BlockSpec((1,) + dims, lambda i: (i, 0, 0))
    small = (hidden, activated, d_inner, grad_rows)
    if came is None:
        kernel, extra = away_kernel, ()
        out_specs = [block(dims) for dims in wide]
        outs = [shape((count,) + dims, BF16) for dims in wide]
    else:
        kernel, extra = kept_kernel, came
        outs = [shape((d[0], d[1] // 2), BF16) for d in wide for _ in range(2 * count)]
        out_specs = [whole_spec(out) for out in outs]
    return pl.pallas_call(
        functools.partial(kernel, count),
        grid=(count,),
        in_specs=[scalar_spec()]
        + [whole_spec(a) for a in small]
        + [block(dims) for dims in wide[: len(extra)]],
        out_specs=out_specs,
        out_shape=outs,
        scratch_shapes=[
            pltpu.VMEM((hidden.shape[0], rows), BF16),
            pltpu.VMEM((hidden.shape[0], ff // count // 2), BF16),
        ],
        compiler_params=params(),
        cost_estimate=pl.CostEstimate(
            flops=2 * hidden.shape[0] * hidden.shape[1] * ff,
            bytes_accessed=8 * rows * count * ff,
            transcendentals=0,
        ),
    )(where, *small, *extra)


def mixed_back_kernel(count, parts_count, *refs):
    where, mixed, weight = refs[:3]
    parts = refs[3 : 3 + parts_count]
    d_attended, out_away, out_kept, out_sum = refs[3 + parts_count :]
    here, core = where[0], where[1]
    rows = parts[0].shape[0]
    for k, part in enumerate(parts):
        start = jnp.bitwise_xor(here, k // 2) * (2 * rows) + (k % 2) * rows
        at = pl.ds(pl.multiple_of(start, 32), rows)
        d_attended[at, :] = matmul_nt(part[...], weight[...]).astype(BF16)
        term = matmul_tn(mixed[at, :], part[...])
        if k == 0:
            out_sum[...] = term
        else:
            out_sum[...] += term
    half = out_kept.shape[0]
    out_kept[...] = out_sum[pl.ds(pl.multiple_of(core * half, 32), half), :]
    out_away[...] = out_sum[pl.ds(pl.multiple_of((1 - core) * half, 32), half), :].astype(BF16)


def mixed_back(count, where, mixed, weight, parts):
    length, val_width = mixed.shape
    width = weight.shape[1]
    vmem = pl.BlockSpec(memory_space=pltpu.VMEM)
    return pl.pallas_call(
        functools.partial(mixed_back_kernel, count, len(parts)),
        in_specs=[scalar_spec()] + [vmem] * (2 + len(parts)),
        out_specs=[vmem] * 3,
        out_shape=[
            shape((length, val_width), BF16),
            shape((val_width // 2, width), BF16),
            shape((val_width // 2, width), F32),
        ],
        scratch_shapes=[pltpu.VMEM((val_width, width), F32)],
        compiler_params=params(),
        cost_estimate=pl.CostEstimate(
            flops=4 * length * val_width * width,
            bytes_accessed=2 * length * (width + 2 * val_width),
            transcendentals=0,
        ),
    )(where, mixed, weight, *parts)


def rows_back_kernel(count, where, order, d_heads, window, weight, d_along, *refs):
    d_normed, first_sums = refs[:-1], refs[-1]
    here = where[0]
    step = pl.program_id(0)
    rows, width = window.shape
    length = order.shape[1]
    bins = lax.broadcasted_iota(jnp.int32, (rows, length), 0) + jnp.bitwise_xor(here, step) * rows
    picks = jnp.where(order[0:1, :] == bins, 1.0, 0.0).astype(BF16)
    along = matmul(picks, d_heads[...]).astype(BF16)
    d_along[...] = along
    unit, _ = norm_of(window[...].astype(F32))
    normed = matmul_nt(along, weight[...])

    @pl.when(step == 0)
    def _():
        first_sums[...] = jnp.zeros_like(first_sums)

    first_sums[0:1, :] += jnp.sum(normed * unit, axis=0, keepdims=True)
    first_sums[1:2, :] += jnp.sum(normed, axis=0, keepdims=True)
    half = width // 2
    for m in range(count):

        @pl.when(step == m)
        def _():
            d_normed[2 * m][...] = normed[:, :half].astype(BF16)
            d_normed[2 * m + 1][...] = normed[:, half:].astype(BF16)


def rows_back(count, where, order, d_heads, window, weight):
    length, width = window.shape
    rows = length // count
    heads_width = d_heads.shape[1]
    outs = [shape((length, heads_width), BF16)]
    outs += [shape((rows, width // 2), BF16) for _ in range(2 * count)]
    outs += [shape((8, width), F32)]
    return pl.pallas_call(
        functools.partial(rows_back_kernel, count),
        grid=(count,),
        in_specs=[
            scalar_spec(),
            whole_spec(order),
            whole_spec(d_heads),
            pl.BlockSpec((rows, width), lambda i: (i, 0)),
            whole_spec(weight),
        ],
        out_specs=[pl.BlockSpec((rows, heads_width), lambda i: (i, 0))]
        + [whole_spec(out) for out in outs[1:]],
        out_shape=outs,
        compiler_params=params(),
        cost_estimate=pl.CostEstimate(
            flops=2 * length * heads_width * (length + width),
            bytes_accessed=4 * length * (width + heads_width),
            transcendentals=0,
        ),
    )(where, order, d_heads, window, weight)


def pack_kernel(
    count, where, hidden, d_along, first_sums, sums, inner_sums, d_bias, d_rel, kept, away, grads
):
    here, core = where[0], where[1]
    step = pl.program_id(0)
    row_count = hidden.shape[1] // count
    key_width = d_rel.shape[1]
    terms = matmul_tn(hidden[...], d_along[...])

    @pl.when(step == 0)
    def _():
        for s in range(count):
            grads[s, :row_count, :] = terms[s * row_count : (s + 1) * row_count, :]

    @pl.when(step > 0)
    def _():
        for s in range(count):
            grads[s, :row_count, :] += terms[s * row_count : (s + 1) * row_count, :]

    @pl.when(step == pl.num_programs(0) - 1)
    def _():
        rel_rows = d_rel.shape[0] // count
        for s in range(count):
            at = slice(s * row_count, (s + 1) * row_count)
            grads[s, row_count:, :] = jnp.zeros((EXTRA, grads.shape[2]), F32)
            grads[s, row_count : row_count + 2, :row_count] = first_sums[0:2, at]
            grads[s, row_count + 2 : row_count + 6, :row_count] = sums[2:6, at]
            for j in range(2):
                part = slice((2 * s + j) * row_count, (2 * s + j + 1) * row_count)
                grads[s, row_count + 6 + j : row_count + 7 + j, :row_count] = inner_sums[0:1, part]
            for j in range(-(-rel_rows // EXTRA)):
                some = d_rel[s * rel_rows + j * EXTRA : s * rel_rows + min(rel_rows, (j + 1) * EXTRA), :]
                lane = row_count + j * key_width
                grads[s, row_count : row_count + some.shape[0], lane : lane + key_width] = some
        for s in range(count):

            @pl.when(here == s)
            def _():
                grads[s, row_count + 8 : row_count + 10, :key_width] = d_bias[0:2, :]

        half = kept.shape[1]
        kept[...] = grads[:, pl.ds(pl.multiple_of(core * half, 16), half), :].astype(BF16)
        away[...] = grads[:, pl.ds(pl.multiple_of((1 - core) * half, 16), half), :].astype(BF16)


def pack(count, where, hidden, d_along, *small):
    length, width = hidden.shape
    heads_width = d_along.shape[1]
    rows = math.gcd(768, length)
    packed = (count, width // count + EXTRA, heads_width)
    outs = [shape((count, packed[1] // 2, heads_width), BF16) for _ in range(2)]
    return pl.pallas_call(
        functools.partial(pack_kernel, count),
        grid=(length // rows,),
        in_specs=[
            scalar_spec(),
            pl.BlockSpec((rows, width), lambda i: (i, 0)),
            pl.BlockSpec((rows, heads_width), lambda i: (i, 0)),
        ]
        + [whole_spec(a) for a in small],
        out_specs=[whole_spec(out) for out in outs],
        out_shape=outs,
        scratch_shapes=[pltpu.VMEM(packed, F32)],
        compiler_params=params(),
        cost_estimate=pl.CostEstimate(
            flops=2 * length * heads_width * width,
            bytes_accessed=2 * length * (width + heads_width) + 8 * width * heads_width,
            transcendentals=0,
        ),
    )(where, hidden, d_along, *small)


def swap(array, mask, count):
    return lax.ppermute(array, "seq", [(i, i ^ mask) for i in range(count)])


def bit_orders(count):
    bits = [1 << k for k in range(count.bit_length() - 1)]
    return bits, bits[::-1]


def pin(*arrays):
    return lax.optimization_barrier(arrays)


def unpack_kernel(count, row_count, key_width, *refs):
    where, parts, (query, key, value, extra, whole) = refs[0], refs[1:5], refs[5:]
    half = parts[0].shape[1]
    group = parts[0].shape[0]
    core = where[1]
    for k in range(2):
        mine, theirs = parts[2 * k], parts[2 * k + 1]
        for c in range(2):

            @pl.when(core == c)
            def _():
                whole[k * group : (k + 1) * group, c * half : (c + 1) * half, :] = mine[...]
                whole[k * group : (k + 1) * group, (1 - c) * half : (2 - c) * half, :] = theirs[...]

    for out, at in ((query, 0), (key, key_width), (value, 2 * key_width)):
        size = out.shape[1] // count
        for s in range(count):
            rows = whole[s, :row_count, at : at + size]
            out[:, s * size : (s + 1) * size] = rows.astype(F32)
    extra[...] = whole[:, row_count:, :].astype(F32)


def unpack(where, parts, row_count, key_width, val_width):
    group, half, width = parts[0].shape
    count = 2 * group
    vmem = pl.BlockSpec(memory_space=pltpu.VMEM)
    return pl.pallas_call(
        functools.partial(unpack_kernel, count, row_count, key_width),
        in_specs=[scalar_spec()] + [vmem] * 4,
        out_specs=[vmem] * 4,
        out_shape=[
            shape((row_count, count * key_width), F32),
            shape((row_count, count * key_width), F32),
            shape((row_count, count * val_width), F32),
            shape((count, EXTRA, width), F32),
        ],
        scratch_shapes=[pltpu.VMEM((count, 2 * half, width), BF16)],
        compiler_params=params(),
    )(where, *parts)


class Exchange:
    def __init__(self):
        self.new = {}


def pin_all(exchanges, *arrays):
    keys = [sorted(e.new) for e in exchanges]
    out = pin(*arrays, *[e.new[k] for e, ks in zip(exchanges, keys) for k in ks])
    at = len(arrays)
    for e, ks in zip(exchanges, keys):
        e.new = dict(zip(ks, out[at : at + len(ks)]))
        at += len(ks)
    return out[: len(arrays)]


class Gather(Exchange):
    def __init__(self, part, order, count):
        super().__init__()
        self.have, self.order, self.count, self.last = {0: part}, order, count, [0]

    def take(self):
        self.have.update(self.new)
        self.new = {}

    def send(self):
        self.take()
        new = {}
        for m in self.last:
            used = [k for k, bit in enumerate(self.order) if m & bit]
            for bit in self.order[max(used, default=-1) + 1 :]:
                new[m | bit] = swap(self.have[m], bit, self.count)
        self.new, self.last = new, sorted(new)


class Scatter(Exchange):
    def __init__(self, blocks, order, count):
        super().__init__()
        self.have, self.order, self.count, self.step = dict(enumerate(blocks)), order, count, 0

    def take(self):
        if self.new:
            bit = self.order[self.step - 1]
            self.have = {
                m: self.have[m].astype(F32) + self.new[m | bit].astype(F32)
                for m in self.have
                if not m & bit
            }
            self.new = {}

    def send(self):
        self.take()
        bit = self.order[self.step]
        self.new = {
            m: swap(self.have[m].astype(BF16), bit, self.count)
            for m in sorted(self.have, reverse=True)
            if m & bit
        }
        self.step += 1

    def rest(self):
        while self.step < len(self.order):
            self.send()
        self.take()
        return self.have[0]


class LineSum(Exchange):
    def __init__(self, piece, count):
        super().__init__()
        self.total, self.count, self.step = piece, count, 0
        self.inward = count // 2 - 1
        self.steps = 2 * self.inward + 1 if count > 1 else 0

    def take(self):
        if self.new:
            at, came = self.step - 1, self.new[0]
            if at <= self.inward:
                self.total = self.total.astype(F32) + came.astype(F32)
            else:
                index = lax.axis_index("wz")
                far = 2 * self.inward - at
                is_target = (index == far) | (index == self.count - 1 - far)
                self.total = jnp.where(is_target, came, self.total)
            self.new = {}

    def send(self):
        self.take()
        if self.step >= self.steps:
            return
        last = self.count - 1
        if self.step < self.inward:
            k = self.step
            pairs = [(k, k + 1), (last - k, last - k - 1)]
        elif self.step == self.inward:
            k = self.inward
            pairs = [(k, k + 1), (k + 1, k)]
        else:
            k = 2 * self.inward - self.step
            pairs = [(k + 1, k), (last - k - 1, last - k)]
        self.total = self.total.astype(BF16)
        self.new = {0: lax.ppermute(self.total, "wz", pairs)}
        self.step += 1

    def rest(self):
        while self.step < self.steps:
            self.send()
        self.take()
        return self.total.astype(BF16)


class OtherCore(Exchange):
    def __init__(self, array):
        super().__init__()
        self.new = {0: other_core(array)}


def split_columns(blocks, count):
    half = blocks[0].shape[1] // 2
    return [
        Scatter([block[:, k * half : (k + 1) * half] for block in blocks], order, count)
        for k, order in enumerate(bit_orders(count))
    ]


def other_core(array):
    return lax.ppermute(array, "core", [(0, 1), (1, 0)])


def shards(
    seq_count,
    wz_count,
    inputs,
    bin_order,
    first_gain,
    first_shift,
    query_weight,
    key_weight,
    value_weight,
    bias_content,
    bias_position,
    relative_weight,
    out_weight,
    bias_out,
    second_gain,
    second_shift,
    inner_weight,
    bias_inner,
    outer_weight,
    bias_outer,
    grad_output,
):
    row_count, width = inputs.shape[1:]
    length = bin_order.shape[1]
    here = lax.axis_index("seq")
    core = lax.axis_index("core")
    where = jnp.stack([here, core]).astype(jnp.int32)
    row_start = here * row_count
    key_width = query_weight.shape[1] // seq_count
    val_width = value_weight.shape[1] // seq_count
    heads_width = 2 * key_width + val_width
    up, down = bit_orders(seq_count)

    others = [jnp.bitwise_xor(here, m) for m in range(seq_count)]
    along = jnp.concatenate(
        [other * row_count + jnp.arange(row_count, dtype=jnp.int32) for other in others]
    )

    def natural(rows):
        parts = rows.reshape(seq_count, row_count, -1)
        parts = [lax.dynamic_index_in_dim(parts, other, 0) for other in others]
        return jnp.concatenate(parts, axis=0).reshape(rows.shape)

    def halves(rows):
        half = rows.shape[0] // 2
        return [Gather(rows[:half], up, seq_count), Gather(rows[half:], down, seq_count)]

    def blocks_of(gathers):
        for g in gathers:
            g.take()
        return [g.have[m] for m in range(seq_count) for g in gathers]

    window_gathers = halves(inputs[0])
    for g in window_gathers:
        g.send()

    def by_head(weight):
        return weight.reshape(weight.shape[0], seq_count, -1)

    vectors = jnp.stack([first_gain, first_shift, bias_out, second_gain, second_shift, bias_outer])
    vectors = jnp.concatenate([vectors, bias_inner.reshape(2, row_count)], axis=0)
    vectors = jnp.pad(vectors, ((0, EXTRA - 8), (0, 0)))
    rel_rows = relative_weight.shape[0]
    rel_blocks = -(-rel_rows // EXTRA)
    rel_part = jnp.pad(by_head(relative_weight), ((0, rel_blocks * EXTRA - rel_rows), (0, 0), (0, 0)))
    rel_part = rel_part.reshape(rel_blocks, EXTRA, seq_count, key_width).transpose(2, 1, 0, 3)
    rel_part = rel_part.reshape(seq_count, EXTRA, -1)
    spare = heads_width - row_count - rel_part.shape[2]
    extra = jnp.concatenate(
        [
            jnp.broadcast_to(vectors[None], (seq_count,) + vectors.shape),
            jnp.pad(rel_part, ((0, 0), (0, 0), (0, spare))),
        ],
        axis=2,
    )
    mine = jnp.concatenate(
        [by_head(query_weight), by_head(key_weight), by_head(value_weight)], axis=2
    ).transpose(1, 0, 2)
    mine = jnp.concatenate([mine, extra], axis=1)
    half = mine.shape[1] // 2
    mine = lax.dynamic_slice_in_dim(mine, core * half, half, 1)
    mine = lax.all_to_all(mine, "seq", 0, 0, tiled=True)
    (mine,) = pin_all(window_gathers, mine)
    for step in range(1, len(up)):
        for g in window_gathers:
            g.send()
    first = core == 0
    theirs = other_core(mine)
    attention_weight = jnp.concatenate(
        [jnp.where(first, mine, theirs), jnp.where(first, theirs, mine)], axis=1
    )
    table, table_back = basis_tables(jnp.asarray(basis_constants(length)), length)
    flat = attention_weight[:, row_count:]
    vectors = flat[:, :8, :row_count].astype(F32)
    inner_bias = vectors[:, 6:8].reshape(1, -1)
    vectors = vectors.transpose(1, 0, 2).reshape(8, width)
    rel = flat[:, :, row_count : row_count + rel_blocks * key_width]
    rel = rel.reshape(seq_count, EXTRA, rel_blocks, key_width).transpose(0, 2, 1, 3)
    rel = rel.reshape(seq_count, rel_blocks * EXTRA, key_width)[:, :rel_rows].reshape(REL, key_width)

    def own_half(weight):
        half = weight.shape[0] // 2
        return lax.dynamic_slice_in_dim(weight, core * half, half, 0)

    inner_part, outer_part = own_half(inner_weight), own_half(outer_weight)
    inner_part, outer_part = pin_all(window_gathers, inner_part, outer_part)
    window_blocks = blocks_of(window_gathers)
    weight_gathers = [
        Gather(inner_part, up, seq_count),
        Gather(outer_part, down, seq_count),
    ]
    for g in weight_gathers:
        g.send()

    order = bin_order[0]
    placing = (order[:, None] == along[None, :]).astype(BF16)
    bias = jnp.concatenate([bias_content, bias_position])[None].astype(F32)
    window, hidden_one, in_bins, weight_whole = project(
        window_blocks, attention_weight, vectors, bias, row_count
    )
    placed_heads = matmul(placing, in_bins).astype(BF16)
    mixed, probs = attend(placed_heads, rel, table)
    (mixed,) = pin_all(weight_gathers, mixed)
    for step in range(1, len(up)):
        for g in weight_gathers:
            g.send()
    weight_parts = []
    for g, own in zip(weight_gathers, (inner_weight, outer_weight)):
        g.take()
        parts = [own]
        for m in range(1, seq_count):
            parts += [g.have[m], other_core(g.have[m])]
        weight_parts.append(parts)
    mixed_along = natural(mixed).reshape(seq_count, row_count, val_width)
    attended = [matmul(mixed_along[m], out_weight).astype(BF16) for m in range(seq_count)]
    attended = split_columns(attended, seq_count)
    for g in attended:
        g.send()
    own_order = lax.dynamic_slice_in_dim(order, row_start, row_count, 0)
    placed = matmul((own_order[:, None] == along[None, :]).astype(BF16), window)
    (placed,) = pin_all(attended, placed)
    attended = [g.rest() for g in attended]

    grad_rows = grad_output[0]
    layer_output, d_mixed_in, hidden_two, activated, d_inner, sums, inner_sums = feed_forward(
        where, placed, attended, grad_rows, vectors, inner_bias, *weight_parts
    )

    d_mixed_gathers = halves(d_mixed_in)
    for g in d_mixed_gathers:
        g.send()
    away = ff_gradients(seq_count, where, hidden_two, activated, d_inner, grad_rows)
    came = [other_core(part) for part in away]
    came = pin_all(d_mixed_gathers, *came)
    for step in range(1, len(up)):
        for g in d_mixed_gathers:
            g.send()
    kept = ff_gradients(seq_count, where, hidden_two, activated, d_inner, grad_rows, came)
    kept = pin_all(d_mixed_gathers, *kept)
    d_mixed_blocks = blocks_of(d_mixed_gathers)
    count = seq_count
    inner_sums_of, outer_sums_of = [
        [
            Scatter([kept[2 * (k * count + m) + side] for m in range(count)], bits, count)
            for side, bits in enumerate((up, down))
        ]
        for k in range(2)
    ]
    for g in inner_sums_of:
        g.send()

    d_attended, out_away, grad_out_w = mixed_back(
        seq_count, where, mixed, out_weight, d_mixed_blocks
    )
    out_core = OtherCore(out_away)

    def send_all(exchanges):
        for exchange in exchanges:
            exchange.send()

    back = attend_back(0, placed_heads, rel, table_back, mixed, d_attended, probs)
    back = pin_all(inner_sums_of, *back)
    for step in range(1, len(up)):
        send_all(inner_sums_of)
    send_all(outer_sums_of)
    for head in range(1, key_width // KEY):
        back = attend_back(head, placed_heads, rel, table_back, mixed, d_attended, probs, back)
    back = pin_all(inner_sums_of, *back)
    d_heads, d_rel, d_bias = back

    inner_lines = [LineSum(g.rest(), wz_count) for g in inner_sums_of]
    send_all(inner_lines)
    d_along, *d_normed, first_sums = rows_back(
        seq_count, where, order[None], d_heads, window, weight_whole
    )
    out = pin_all(outer_sums_of, d_along, *d_normed)
    d_along, d_normed = out[0], out[1:]
    for step in range(1, len(up)):
        send_all(outer_sums_of)
    results = pack(
        seq_count, where, hidden_one, d_along, first_sums, sums, inner_sums, d_bias, d_rel
    )
    out = pin_all(outer_sums_of + inner_lines + [out_core], *results, *d_mixed_blocks)
    packed, packed_core, d_mixed_blocks = out[0], OtherCore(out[1]), out[2:]
    outer_lines = [LineSum(g.rest(), wz_count) for g in outer_sums_of]
    send_all(inner_lines + outer_lines)
    out_line = LineSum(grad_out_w + out_core.new[0].astype(F32), wz_count)
    arrived = [
        Scatter([d_normed[2 * m + side] for m in range(count)], bits, count)
        for side, bits in enumerate((up, down))
    ]
    (packed,) = pin_all([packed_core], packed)
    packed = (packed.astype(F32) + packed_core.new[0].astype(F32)).astype(BF16)
    packed = lax.all_to_all(packed, "seq", 0, 0, tiled=True)
    send_all(arrived)

    own_bins = row_start + jnp.arange(row_count, dtype=jnp.int32)
    order_parts = order.reshape(2 * seq_count, row_count // 2)
    returned = None
    for k, block in enumerate(d_mixed_blocks):
        at = lax.dynamic_index_in_dim(order_parts, 2 * others[k // 2] + k % 2, 0)
        term = matmul((at == own_bins[:, None]).astype(BF16), block)
        returned = term if returned is None else returned + term
    returned, packed = pin_all(arrived + outer_lines + inner_lines, returned, packed)

    packed_lines = [
        LineSum(packed[: seq_count // 2], wz_count),
        LineSum(packed[seq_count // 2 :], wz_count),
    ]
    for step in range(1, len(up)):
        send_all(arrived)
    send_all(packed_lines + outer_lines + inner_lines)
    pin_all(arrived + packed_lines + outer_lines + inner_lines)

    send_all(packed_lines + outer_lines + [out_line])
    own_unit, own_scale = norm_of(inputs[0].astype(F32))
    arrived = jnp.concatenate([g.rest() for g in arrived], axis=1)
    grad_inputs = norm_back(own_unit, own_scale, vectors[0:1], arrived) + returned

    def by_cores(line):
        piece = line.rest()
        other = other_core(piece)
        return jnp.where(first, piece, other), jnp.where(first, other, piece)

    inner_parts = [by_cores(g) for g in inner_lines]
    grad_inner_w = jnp.concatenate(
        [part[k] for k in range(2) for part in inner_parts], axis=1
    ).astype(F32)
    grad_inputs, grad_inner_w = pin_all(
        packed_lines + outer_lines + [out_line], grad_inputs, grad_inner_w
    )

    send_all(packed_lines + [out_line])
    outer_parts = [jnp.concatenate(by_cores(g), axis=0) for g in outer_lines]
    grad_outer_w = jnp.concatenate(outer_parts, axis=1).astype(F32)
    (grad_outer_w,) = pin_all(packed_lines + [out_line], grad_outer_w)
    grad_out_w = jnp.concatenate(by_cores(out_line), axis=0).astype(F32)
    packed_parts = [part for g in packed_lines for part in (g.rest(), other_core(g.rest()))]
    grad_query_w, grad_key_w, grad_value_w, flat = unpack(
        where, packed_parts, row_count, key_width, val_width
    )
    small = jnp.sum(flat[:, :16, :row_count], axis=0)
    g_gain_one, g_shift_one, g_out_b, g_gain_two, g_shift_two, g_outer_b = small[:6]
    g_inner_b = small[6:8].reshape(-1)
    grad_rel = flat[:, :, row_count : row_count + rel_blocks * key_width]
    grad_rel = grad_rel.reshape(seq_count, EXTRA, rel_blocks, key_width).transpose(2, 1, 0, 3)
    grad_rel = grad_rel.reshape(rel_blocks * EXTRA, -1)[:rel_rows]
    return (
        layer_output[None],
        grad_inputs[None],
        g_gain_one,
        g_shift_one,
        grad_query_w,
        grad_key_w,
        grad_value_w,
        small[8, :key_width],
        small[9, :key_width],
        grad_rel,
        grad_out_w,
        g_out_b,
        g_gain_two,
        g_shift_two,
        grad_inner_w,
        g_inner_b,
        grad_outer_w,
        g_outer_b,
    )


def solution(mesh):
    seq_count = mesh.shape["seq"]
    devices = mesh.devices.reshape(seq_count, -1, 2)
    split_mesh = Mesh(devices, ("seq", "wz", "core"))
    rows = P(("wz", "core"), "seq", None)
    vector = P("seq")
    matrix = P("seq", None)
    weights = (
        vector,
        vector,
        matrix,
        matrix,
        matrix,
        vector,
        vector,
        matrix,
        matrix,
        vector,
        vector,
        vector,
        matrix,
        vector,
        matrix,
        vector,
    )
    return jax.shard_map(
        functools.partial(shards, seq_count, mesh.shape["win"] // 2),
        mesh=split_mesh,
        in_specs=(rows, P(("wz", "core"), None)) + weights + (rows,),
        out_specs=(rows, rows) + weights,
        check_vma=False,
    )
```

```python
import functools
import math

import jax
import jax.numpy as jnp
import numpy as np
from jax import lax
from jax.experimental import pallas as pl
from jax.experimental.pallas import tpu as pltpu
from jax.sharding import Mesh
from jax.sharding import PartitionSpec as P

HEADS = 8
KEY = 64
VAL = 192
REL = 192
BF16 = jnp.bfloat16
F32 = jnp.float32
VMEM_LIMIT = 56 * 2**20
EXTRA = 32


def matmul(a, b):
    return lax.dot_general(a, b, (((1,), (0,)), ((), ())), preferred_element_type=F32)


def matmul_nt(a, b):
    return lax.dot_general(a, b, (((1,), (1,)), ((), ())), preferred_element_type=F32)


def matmul_tn(a, b):
    return lax.dot_general(a, b, (((0,), (0,)), ((), ())), preferred_element_type=F32)


def head_part(rows, head):
    lanes = lax.broadcasted_iota(jnp.int32, rows.shape, 1)
    inside = (lanes >= head * KEY) & (lanes < (head + 1) * KEY)
    return jnp.where(inside, rows, jnp.zeros_like(rows))


def head_columns(key_width):
    return [slice(k * key_width, (k + 1) * key_width) for k in range(3)]


def attend_kernel(heads, rows, placed, rel, table, mixed, probs):
    length = placed.shape[0]
    key_width = heads * KEY
    content_at, position_at, keys_at = head_columns(key_width)
    first = pl.program_id(0) * rows
    here = pl.ds(pl.multiple_of(first, rows), rows)
    basis = table[:, pl.ds(pl.multiple_of(length - rows - first, rows), length + rows)]
    content, position, keys = placed[here, content_at], placed[here, position_at], placed[:, keys_at]
    parts = []
    for head in range(heads):
        q_basis = matmul_nt(head_part(position, head), rel[...]).astype(BF16)
        grid = matmul(q_basis, basis)
        shifted = pltpu.roll(grid, 0, 1, stride=1, stride_axis=0)[:, rows:]
        scores = matmul_nt(head_part(content, head), keys) + shifted
        top = jnp.max(scores, axis=1, keepdims=True)
        weights = jnp.exp(scores - top)
        total = jnp.sum(weights, axis=1, keepdims=True)
        prob = (weights * (1.0 / total)).astype(BF16)
        probs[head] = prob
        values_at = 3 * key_width + head * VAL
        parts.append(matmul(prob, placed[:, values_at : values_at + VAL]))
    mixed[...] = jnp.concatenate(parts, axis=1).astype(BF16)


def attend(placed, rel, table):
    length = placed.shape[0]
    heads = rel.shape[1] // KEY
    rows = math.gcd(256, length)
    whole = lambda array: pl.BlockSpec(array.shape, lambda i: (0, 0))
    return pl.pallas_call(
        functools.partial(attend_kernel, heads, rows),
        grid=(length // rows,),
        in_specs=[whole(placed), whole(rel), whole(table)],
        out_specs=[
            pl.BlockSpec((rows, heads * VAL), lambda i: (i, 0)),
            pl.BlockSpec((heads, rows, length), lambda i: (0, i, 0)),
        ],
        out_shape=[
            jax.ShapeDtypeStruct((length, heads * VAL), BF16),
            jax.ShapeDtypeStruct((heads, length, length), BF16),
        ],
        compiler_params=pltpu.CompilerParams(vmem_limit_bytes=VMEM_LIMIT),
        cost_estimate=pl.CostEstimate(
            flops=2 * heads * length * length * 1024,
            bytes_accessed=2 * heads * length * length + 8 * length * heads * VAL,
            transcendentals=heads * length * length,
        ),
    )(placed, rel, table)


def attend_back_kernel(heads, head, rows, *refs):
    placed, rel, table, flip, mixed, d_mixed, probs = refs[:7]
    before = refs[7:-5]
    d_heads, d_rel, d_bias, keys_sum, values_sum = refs[-5:]
    length = placed.shape[0]
    key_width = heads * KEY
    content_at, position_at, keys_at = head_columns(key_width)
    step = pl.program_id(0)

    @pl.when(step == 0)
    def _():
        keys_sum[...] = jnp.zeros_like(keys_sum)
        values_sum[...] = jnp.zeros_like(values_sum)
        for k, out in enumerate((d_heads, d_rel, d_bias)):
            out[...] = before[k][...] if before else jnp.zeros_like(out)

    first = pl.multiple_of(step * rows, rows)
    here = pl.ds(first, rows)
    basis = table[:, pl.ds(first, length + rows)]
    content, position, keys = placed[here, content_at], placed[here, position_at], placed[:, keys_at]
    blocks = length // rows
    columns = slice(head * VAL, (head + 1) * VAL)
    values_at = 3 * key_width + head * VAL
    d_part = d_mixed[:, columns]
    delta = jnp.sum(d_part.astype(F32) * mixed[:, columns].astype(F32), axis=1, keepdims=True)
    prob = probs[0]
    values_sum[...] += matmul_tn(d_part, prob)
    d_prob = matmul_nt(d_part, placed[:, values_at : values_at + VAL])
    d_score = (prob.astype(F32) * (d_prob - delta)).astype(BF16)
    keys_sum[...] += matmul_tn(head_part(content, head), d_score)
    d_content = head_part(matmul(d_score, keys), head)
    turned = [
        matmul(d_score[:, (blocks - 1 - b) * rows : (blocks - b) * rows], flip[...])
        for b in range(blocks)
    ]
    turned = jnp.concatenate(turned + [jnp.zeros((rows, rows), F32)], axis=1)
    d_grid = pltpu.roll(turned, 0, 1, stride=1, stride_axis=0).astype(BF16)
    d_basis = matmul_nt(d_grid, basis).astype(BF16)
    d_position = head_part(matmul(d_basis, rel[...]), head)
    d_rel[...] += matmul_tn(d_basis, head_part(position, head))
    d_heads[here, :key_width] += ((d_content + d_position) * KEY ** (-0.5)).astype(BF16)
    d_bias[0:1, :] += jnp.sum(d_content, axis=0, keepdims=True)
    d_bias[1:2, :] += jnp.sum(d_position, axis=0, keepdims=True)

    @pl.when(step == blocks - 1)
    def _():
        d_heads[:, key_width : 2 * key_width] += keys_sum[...].T.astype(BF16)
        values_to = 2 * key_width + head * VAL
        d_heads[:, values_to : values_to + VAL] = values_sum[...].T.astype(BF16)


def attend_back(head, placed, rel, table, mixed, d_mixed, probs, before=()):
    length = placed.shape[0]
    key_width = rel.shape[1]
    heads = key_width // KEY
    val_width = heads * VAL
    rows = math.gcd(256, length)
    at = jnp.arange(rows)
    flip = (at[:, None] + at[None, :] == rows - 1).astype(BF16)
    block = lambda width: pl.BlockSpec((rows, width), lambda i: (i, 0))
    outs = [
        shape((length, 2 * key_width + val_width), BF16),
        shape((REL, key_width), F32),
        shape((8, key_width), F32),
    ]
    return pl.pallas_call(
        functools.partial(attend_back_kernel, heads, head, rows),
        grid=(length // rows,),
        in_specs=[
            whole_spec(placed),
            whole_spec(rel),
            whole_spec(table),
            whole_spec(flip),
            block(val_width),
            block(val_width),
            pl.BlockSpec((1, rows, length), lambda i: (head, i, 0)),
        ]
        + [whole_spec(array) for array in before],
        out_specs=[whole_spec(out) for out in outs],
        out_shape=outs,
        scratch_shapes=[
            pltpu.VMEM((key_width, length), F32),
            pltpu.VMEM((VAL, length), F32),
        ],
        compiler_params=pltpu.CompilerParams(vmem_limit_bytes=VMEM_LIMIT),
        cost_estimate=pl.CostEstimate(
            flops=2 * length * length * 1536,
            bytes_accessed=2 * length * length + 16 * length * val_width,
            transcendentals=0,
        ),
    )(placed, rel, table, flip, mixed, d_mixed, probs, *before)


def norm_back(unit, scale, gain, grad):
    scaled = grad * gain
    mean_one = jnp.mean(scaled, axis=-1, keepdims=True)
    mean_two = jnp.mean(scaled * unit, axis=-1, keepdims=True)
    return (scaled - mean_one - unit * mean_two) * scale


def whole_spec(array):
    zeros = (0,) * len(array.shape)
    return pl.BlockSpec(array.shape, lambda *_: zeros)


def scalar_spec():
    return pl.BlockSpec(memory_space=pltpu.SMEM)


def params(**more):
    return pltpu.CompilerParams(vmem_limit_bytes=VMEM_LIMIT, **more)


def shape(dims, dtype):
    return jax.ShapeDtypeStruct(tuple(dims), dtype)


def basis_constants(window_len):
    features = REL // 6
    f = np.arange(features, dtype=np.float64)
    half_life = 2.0 ** (3.0 + f * (math.log2(window_len) - 3.0) / (features - 1))
    spread = window_len / (2.0 * features)
    first = window_len / features
    centres = first + f * (window_len - first) / (features - 1)
    concentration = (centres / spread) ** 2
    rate = centres / spread**2
    offset = concentration * np.log(rate) - np.array([math.lgamma(c) for c in concentration])
    columns = [math.log(2.0) / half_life, 2.0 ** (f + 1) - 1.0, concentration - 1.0, rate, offset]
    columns += [np.zeros(features)] * 3
    return np.stack(columns, axis=1).astype(np.float32)


def table_kernel(length, constants, forth, back):
    features = REL // 6
    decay, inside_below, power, rate, offset = [constants[:, k : k + 1] for k in range(5)]

    def gamma(distance):
        logged = power * jnp.log(jnp.maximum(distance, 1.0)) - rate * distance + offset
        return jnp.where(distance == 0.0, 0.0, jnp.exp(logged)) + 1e-08

    every = lax.broadcasted_iota(jnp.int32, (1, length), 1).astype(F32)
    peak = jnp.max(gamma(every), axis=1, keepdims=True)
    lanes = lax.broadcasted_iota(jnp.int32, (1, 2 * length), 1).astype(F32)
    for table, signed in ((forth, lanes - length), (back, length - 1 - lanes)):
        distance = jnp.abs(signed)
        sign = jnp.where(signed > 0, 1.0, jnp.where(signed < 0, -1.0, 0.0))
        parts = (
            jnp.exp(-decay * distance),
            jnp.where(inside_below > distance, 1.0, 0.0),
            gamma(distance) / peak,
        )
        for k, part in enumerate(parts):
            table[k * features : (k + 1) * features, :] = part.astype(BF16)
            table[(3 + k) * features : (4 + k) * features, :] = (sign * part).astype(BF16)


def basis_tables(constants, length):
    out = shape((REL, 2 * length), BF16)
    return pl.pallas_call(
        functools.partial(table_kernel, length),
        out_shape=[out, out],
        compiler_params=params(),
    )(constants)


def norm_of(rows):
    centre = rows - jnp.mean(rows, axis=1, keepdims=True)
    scale = lax.rsqrt(jnp.mean(centre * centre, axis=1, keepdims=True) + 1e-05)
    return centre * scale, scale


def project_kernel(blocks, row_count, *refs):
    parts, (weight, vectors, bias, window, hidden, heads, flat, block) = refs[:blocks], refs[blocks:]
    step = pl.program_id(0)

    @pl.when(step == 0)
    def _():
        for s in range(weight.shape[0]):
            flat[s * row_count : (s + 1) * row_count, :] = weight[s, :row_count, :]

    for k in range(blocks):

        @pl.when(step == k)
        def _():
            block[...] = parts[k][...]

    window[...] = block[...]
    unit, _ = norm_of(block[...].astype(F32))
    normed = (unit * vectors[0:1, :] + vectors[1:2, :]).astype(BF16)
    hidden[...] = normed
    total = matmul(normed, flat[...])
    key_width = bias.shape[1] // 2
    query = total[:, :key_width] * KEY ** (-0.5)
    heads[:, :key_width] = (query + bias[0:1, :key_width]).astype(BF16)
    heads[:, key_width : 2 * key_width] = (query + bias[0:1, key_width:]).astype(BF16)
    heads[:, 2 * key_width :] = total[:, key_width:].astype(BF16)


def project(parts, weight, vectors, bias, row_count):
    blocks = len(parts)
    rows, width = parts[0].shape
    heads_width = weight.shape[2] + bias.shape[1] // 2
    out = lambda w: pl.BlockSpec((rows, w), lambda i: (i, 0))
    return pl.pallas_call(
        functools.partial(project_kernel, blocks, row_count),
        grid=(blocks,),
        in_specs=[whole_spec(a) for a in (*parts, weight, vectors, bias)],
        out_specs=[
            out(width),
            out(width),
            out(heads_width),
            pl.BlockSpec((width, weight.shape[2]), lambda i: (0, 0)),
        ],
        out_shape=[shape((blocks * rows, w), BF16) for w in (width, width, heads_width)]
        + [shape((width, weight.shape[2]), BF16)],
        scratch_shapes=[pltpu.VMEM((rows, width), BF16)],
        compiler_params=params(),
        cost_estimate=pl.CostEstimate(
            flops=2 * blocks * rows * width * heads_width,
            bytes_accessed=8 * blocks * rows * width,
            transcendentals=0,
        ),
    )(*parts, weight, vectors, bias)


def feed_kernel(count, chunk, *refs):
    parts = 2 * (2 * count - 1)
    where, placed, attended_a, attended_b, grad_rows, vectors, inner_bias = refs[:7]
    weights = refs[7 : 7 + parts]
    layer_output, d_mixed, hidden, activated, d_inner, sums, inner_sums = refs[7 + parts : 14 + parts]
    inner_whole, outer_whole, residual, unit, back, outer_sum, sems = refs[14 + parts :]
    here, core = where[0], where[1]
    copies = []
    for k, whole in enumerate((inner_whole, outer_whole)):
        mine = weights[k * (2 * count - 1) : (k + 1) * (2 * count - 1)]
        size = whole.shape[0] // count
        half = size // 2
        moves = [(mine[0], here * size, size)]
        for m in range(1, count):
            start = jnp.bitwise_xor(here, m) * size
            moves.append((mine[2 * m - 1], start + core * half, half))
            moves.append((mine[2 * m], start + (1 - core) * half, half))
        started = []
        for source, start, rows in moves:
            target = whole.at[pl.ds(pl.multiple_of(start, 16), rows), :]
            copy = pltpu.make_async_copy(source, target, sems.at[k, len(started)])
            copy.start()
            started.append(copy)
        copies.append(started)
    rows, width = placed.shape
    half = width // 2
    residual[:, :half] = placed[:, :half] + attended_a[...] + vectors[2:3, :half]
    residual[:, half:] = placed[:, half:] + attended_b[...] + vectors[2:3, half:]
    normed, scale = norm_of(residual[...])
    unit[...] = normed
    hidden[...] = (normed * vectors[3:4, :] + vectors[4:5, :]).astype(BF16)
    for started in copies:
        for copy in started:
            copy.wait()
    ff = outer_whole.shape[0]
    for c in range(ff // chunk):
        at = slice(c * chunk, (c + 1) * chunk)
        inner = matmul(hidden[...], inner_whole[:, at]) + inner_bias[0:1, at]
        below = 0.5 * (1.0 + lax.erf(inner * (0.5**0.5)))
        slope = below + inner * jnp.exp(-0.5 * inner * inner) * (0.5 / math.pi) ** 0.5
        active = (inner * below).astype(BF16)
        activated[:, at] = active
        grad = (matmul_nt(grad_rows[...], outer_whole[at, :]) * slope).astype(BF16)
        d_inner[:, at] = grad
        inner_sums[:, at] = jnp.sum(grad.astype(F32), axis=0, keepdims=True)
        back_term = matmul_nt(grad, inner_whole[:, at])
        outer_term = matmul(active, outer_whole[at, :])
        if c == 0:
            back[...] = back_term
            outer_sum[...] = outer_term
        else:
            back[...] += back_term
            outer_sum[...] += outer_term
    layer_output[...] = (residual[...] + outer_sum[...] + vectors[5:6, :]).astype(BF16)
    grad, normed = back[...], unit[...]
    dy = grad_rows[...].astype(F32)
    scaled = grad * vectors[3:4, :]
    mean_one = jnp.mean(scaled, axis=1, keepdims=True)
    mean_two = jnp.mean(scaled * normed, axis=1, keepdims=True)
    mixed_in = (dy + (scaled - mean_one - normed * mean_two) * scale).astype(BF16)
    d_mixed[...] = mixed_in
    sums[...] = jnp.zeros_like(sums)
    sums[2:3, :] = jnp.sum(mixed_in.astype(F32), axis=0, keepdims=True)
    sums[3:4, :] = jnp.sum(grad * normed, axis=0, keepdims=True)
    sums[4:5, :] = jnp.sum(grad, axis=0, keepdims=True)
    sums[5:6, :] = jnp.sum(dy, axis=0, keepdims=True)


def feed_forward(where, placed, attended, grad_rows, vectors, inner_bias, inner_parts, outer_parts):
    rows, width = placed.shape
    ff = inner_bias.shape[1]
    count = (len(inner_parts) + 1) // 2
    chunk = math.gcd(512, ff)
    weights = (*inner_parts, *outer_parts)
    small = (placed, *attended, grad_rows, vectors, inner_bias)
    outs = [
        shape((rows, width), BF16),
        shape((rows, width), BF16),
        shape((rows, width), BF16),
        shape((rows, ff), BF16),
        shape((rows, ff), BF16),
        shape((8, width), F32),
        shape((1, ff), F32),
    ]
    return pl.pallas_call(
        functools.partial(feed_kernel, count, chunk),
        in_specs=[scalar_spec()]
        + [pl.BlockSpec(memory_space=pltpu.VMEM) for _ in small]
        + [pl.BlockSpec(memory_space=pl.ANY) for _ in weights],
        out_specs=[pl.BlockSpec(memory_space=pltpu.VMEM) for _ in outs],
        out_shape=outs,
        scratch_shapes=[
            pltpu.VMEM((width, ff), BF16),
            pltpu.VMEM((ff, width), BF16),
            pltpu.VMEM((rows, width), F32),
            pltpu.VMEM((rows, width), F32),
            pltpu.VMEM((rows, width), F32),
            pltpu.VMEM((rows, width), F32),
            pltpu.SemaphoreType.DMA((2, 2 * count - 1)),
        ],
        compiler_params=params(),
        cost_estimate=pl.CostEstimate(
            flops=8 * rows * width * ff,
            bytes_accessed=4 * width * ff + 40 * rows * width,
            transcendentals=2 * rows * ff,
        ),
    )(where, *small, *weights)


def columns_at(ref, index, size, scratch):
    if size % 128 == 0:
        return ref[:, pl.ds(pl.multiple_of(index * size, 128), size)]
    for k in range(ref.shape[1] // size):

        @pl.when(index == k)
        def _():
            scratch[...] = ref[:, k * size : (k + 1) * size]

    return scratch[...]


def away_kernel(
    count, where, hidden, activated, d_inner, grad_rows, inner_away, outer_away, some, more
):
    here, other = where[0], 1 - where[1]
    rows = hidden.shape[1] // count
    ff = d_inner.shape[1]
    ff_rows = ff // count
    half = pl.ds(pl.multiple_of(other * (ff // 2), 128), ff // 2)
    step = pl.program_id(0)
    shard = jnp.bitwise_xor(here, step)
    columns = columns_at(hidden, shard, rows, some)
    inner_away[0] = matmul_tn(columns, d_inner[:, half]).astype(BF16)
    columns = columns_at(activated, 2 * shard + other, ff_rows // 2, more)
    outer_away[0] = matmul_tn(columns, grad_rows[...]).astype(BF16)


def kept_kernel(
    count, where, hidden, activated, d_inner, grad_rows, inner_came, outer_came, *refs
):
    outs, (some, more) = refs[:-2], refs[-2:]
    here, core = where[0], where[1]
    rows = hidden.shape[1] // count
    ff = d_inner.shape[1]
    ff_rows = ff // count
    half = pl.ds(pl.multiple_of(core * (ff // 2), 128), ff // 2)
    step = pl.program_id(0)
    shard = jnp.bitwise_xor(here, step)
    columns = columns_at(hidden, shard, rows, some)
    inner = matmul_tn(columns, d_inner[:, half]) + inner_came[0].astype(F32)
    columns = columns_at(activated, 2 * shard + core, ff_rows // 2, more)
    outer = matmul_tn(columns, grad_rows[...]) + outer_came[0].astype(F32)
    for k, result in enumerate((inner, outer)):
        side = result.shape[1] // 2
        for m in range(count):

            @pl.when(step == m)
            def _():
                outs[2 * (k * count + m)][...] = result[:, :side].astype(BF16)
                outs[2 * (k * count + m) + 1][...] = result[:, side:].astype(BF16)


def ff_gradients(count, where, hidden, activated, d_inner, grad_rows, came=None):
    rows = hidden.shape[1] // count
    ff = d_inner.shape[1]
    wide = [(rows, ff // 2), (ff // count // 2, grad_rows.shape[1])]
    block = lambda dims: pl.BlockSpec((1,) + dims, lambda i: (i, 0, 0))
    small = (hidden, activated, d_inner, grad_rows)
    if came is None:
        kernel, extra = away_kernel, ()
        out_specs = [block(dims) for dims in wide]
        outs = [shape((count,) + dims, BF16) for dims in wide]
    else:
        kernel, extra = kept_kernel, came
        outs = [shape((d[0], d[1] // 2), BF16) for d in wide for _ in range(2 * count)]
        out_specs = [whole_spec(out) for out in outs]
    return pl.pallas_call(
        functools.partial(kernel, count),
        grid=(count,),
        in_specs=[scalar_spec()]
        + [whole_spec(a) for a in small]
        + [block(dims) for dims in wide[: len(extra)]],
        out_specs=out_specs,
        out_shape=outs,
        scratch_shapes=[
            pltpu.VMEM((hidden.shape[0], rows), BF16),
            pltpu.VMEM((hidden.shape[0], ff // count // 2), BF16),
        ],
        compiler_params=params(),
        cost_estimate=pl.CostEstimate(
            flops=2 * hidden.shape[0] * hidden.shape[1] * ff,
            bytes_accessed=8 * rows * count * ff,
            transcendentals=0,
        ),
    )(where, *small, *extra)


def mixed_back_kernel(count, parts_count, *refs):
    where, mixed, weight = refs[:3]
    parts = refs[3 : 3 + parts_count]
    d_attended, out_away, out_kept, out_sum = refs[3 + parts_count :]
    here, core = where[0], where[1]
    rows = parts[0].shape[0]
    for k, part in enumerate(parts):
        start = jnp.bitwise_xor(here, k // 2) * (2 * rows) + (k % 2) * rows
        at = pl.ds(pl.multiple_of(start, 32), rows)
        d_attended[at, :] = matmul_nt(part[...], weight[...]).astype(BF16)
        term = matmul_tn(mixed[at, :], part[...])
        if k == 0:
            out_sum[...] = term
        else:
            out_sum[...] += term
    half = out_kept.shape[0]
    out_kept[...] = out_sum[pl.ds(pl.multiple_of(core * half, 32), half), :]
    out_away[...] = out_sum[pl.ds(pl.multiple_of((1 - core) * half, 32), half), :].astype(BF16)


def mixed_back(count, where, mixed, weight, parts):
    length, val_width = mixed.shape
    width = weight.shape[1]
    vmem = pl.BlockSpec(memory_space=pltpu.VMEM)
    return pl.pallas_call(
        functools.partial(mixed_back_kernel, count, len(parts)),
        in_specs=[scalar_spec()] + [vmem] * (2 + len(parts)),
        out_specs=[vmem] * 3,
        out_shape=[
            shape((length, val_width), BF16),
            shape((val_width // 2, width), BF16),
            shape((val_width // 2, width), F32),
        ],
        scratch_shapes=[pltpu.VMEM((val_width, width), F32)],
        compiler_params=params(),
        cost_estimate=pl.CostEstimate(
            flops=4 * length * val_width * width,
            bytes_accessed=2 * length * (width + 2 * val_width),
            transcendentals=0,
        ),
    )(where, mixed, weight, *parts)


def rows_back_kernel(count, where, order, d_heads, window, weight, d_along, *refs):
    d_normed, first_sums = refs[:-1], refs[-1]
    here = where[0]
    step = pl.program_id(0)
    rows, width = window.shape
    length = order.shape[1]
    bins = lax.broadcasted_iota(jnp.int32, (rows, length), 0) + jnp.bitwise_xor(here, step) * rows
    picks = jnp.where(order[0:1, :] == bins, 1.0, 0.0).astype(BF16)
    along = matmul(picks, d_heads[...]).astype(BF16)
    d_along[...] = along
    unit, _ = norm_of(window[...].astype(F32))
    normed = matmul_nt(along, weight[...])

    @pl.when(step == 0)
    def _():
        first_sums[...] = jnp.zeros_like(first_sums)

    first_sums[0:1, :] += jnp.sum(normed * unit, axis=0, keepdims=True)
    first_sums[1:2, :] += jnp.sum(normed, axis=0, keepdims=True)
    half = width // 2
    for m in range(count):

        @pl.when(step == m)
        def _():
            d_normed[2 * m][...] = normed[:, :half].astype(BF16)
            d_normed[2 * m + 1][...] = normed[:, half:].astype(BF16)


def rows_back(count, where, order, d_heads, window, weight):
    length, width = window.shape
    rows = length // count
    heads_width = d_heads.shape[1]
    outs = [shape((length, heads_width), BF16)]
    outs += [shape((rows, width // 2), BF16) for _ in range(2 * count)]
    outs += [shape((8, width), F32)]
    return pl.pallas_call(
        functools.partial(rows_back_kernel, count),
        grid=(count,),
        in_specs=[
            scalar_spec(),
            whole_spec(order),
            whole_spec(d_heads),
            pl.BlockSpec((rows, width), lambda i: (i, 0)),
            whole_spec(weight),
        ],
        out_specs=[pl.BlockSpec((rows, heads_width), lambda i: (i, 0))]
        + [whole_spec(out) for out in outs[1:]],
        out_shape=outs,
        compiler_params=params(),
        cost_estimate=pl.CostEstimate(
            flops=2 * length * heads_width * (length + width),
            bytes_accessed=4 * length * (width + heads_width),
            transcendentals=0,
        ),
    )(where, order, d_heads, window, weight)


def pack_kernel(
    count, where, hidden, d_along, first_sums, sums, inner_sums, d_bias, d_rel, kept, away, grads
):
    here, core = where[0], where[1]
    step = pl.program_id(0)
    row_count = hidden.shape[1] // count
    key_width = d_rel.shape[1]
    terms = matmul_tn(hidden[...], d_along[...])

    @pl.when(step == 0)
    def _():
        for s in range(count):
            grads[s, :row_count, :] = terms[s * row_count : (s + 1) * row_count, :]

    @pl.when(step > 0)
    def _():
        for s in range(count):
            grads[s, :row_count, :] += terms[s * row_count : (s + 1) * row_count, :]

    @pl.when(step == pl.num_programs(0) - 1)
    def _():
        rel_rows = d_rel.shape[0] // count
        for s in range(count):
            at = slice(s * row_count, (s + 1) * row_count)
            grads[s, row_count:, :] = jnp.zeros((EXTRA, grads.shape[2]), F32)
            grads[s, row_count : row_count + 2, :row_count] = first_sums[0:2, at]
            grads[s, row_count + 2 : row_count + 6, :row_count] = sums[2:6, at]
            for j in range(2):
                part = slice((2 * s + j) * row_count, (2 * s + j + 1) * row_count)
                grads[s, row_count + 6 + j : row_count + 7 + j, :row_count] = inner_sums[0:1, part]
            for j in range(-(-rel_rows // EXTRA)):
                some = d_rel[s * rel_rows + j * EXTRA : s * rel_rows + min(rel_rows, (j + 1) * EXTRA), :]
                lane = row_count + j * key_width
                grads[s, row_count : row_count + some.shape[0], lane : lane + key_width] = some
        for s in range(count):

            @pl.when(here == s)
            def _():
                grads[s, row_count + 8 : row_count + 10, :key_width] = d_bias[0:2, :]

        half = kept.shape[1]
        kept[...] = grads[:, pl.ds(pl.multiple_of(core * half, 16), half), :].astype(BF16)
        away[...] = grads[:, pl.ds(pl.multiple_of((1 - core) * half, 16), half), :].astype(BF16)


def pack(count, where, hidden, d_along, *small):
    length, width = hidden.shape
    heads_width = d_along.shape[1]
    rows = math.gcd(768, length)
    packed = (count, width // count + EXTRA, heads_width)
    outs = [shape((count, packed[1] // 2, heads_width), BF16) for _ in range(2)]
    return pl.pallas_call(
        functools.partial(pack_kernel, count),
        grid=(length // rows,),
        in_specs=[
            scalar_spec(),
            pl.BlockSpec((rows, width), lambda i: (i, 0)),
            pl.BlockSpec((rows, heads_width), lambda i: (i, 0)),
        ]
        + [whole_spec(a) for a in small],
        out_specs=[whole_spec(out) for out in outs],
        out_shape=outs,
        scratch_shapes=[pltpu.VMEM(packed, F32)],
        compiler_params=params(),
        cost_estimate=pl.CostEstimate(
            flops=2 * length * heads_width * width,
            bytes_accessed=2 * length * (width + heads_width) + 8 * width * heads_width,
            transcendentals=0,
        ),
    )(where, hidden, d_along, *small)


def swap(array, mask, count):
    return lax.ppermute(array, "seq", [(i, i ^ mask) for i in range(count)])


def bit_orders(count):
    bits = [1 << k for k in range(count.bit_length() - 1)]
    return bits, bits[::-1]


def pin(*arrays):
    return lax.optimization_barrier(arrays)


def returned_kernel(count, where, order, *refs):
    parts, returned = refs[:-1], refs[-1]
    here = where[0]
    rows = parts[0].shape[0]
    bins = lax.broadcasted_iota(jnp.int32, (returned.shape[0], rows), 0)
    bins = bins + here * returned.shape[0]
    for k, part in enumerate(parts):
        shard = jnp.bitwise_xor(here, k // 2)
        picks = jnp.where(order[pl.ds(2 * shard + k % 2, 1), :] == bins, 1.0, 0.0).astype(BF16)
        term = matmul(picks, part[...])
        if k == 0:
            returned[...] = term
        else:
            returned[...] += term


def returned_rows(count, where, order, parts):
    rows, width = parts[0].shape
    vmem = pl.BlockSpec(memory_space=pltpu.VMEM)
    return pl.pallas_call(
        functools.partial(returned_kernel, count),
        in_specs=[scalar_spec()] + [vmem] * (1 + len(parts)),
        out_specs=vmem,
        out_shape=shape((2 * rows, width), F32),
        compiler_params=params(),
        cost_estimate=pl.CostEstimate(
            flops=4 * rows * rows * len(parts) * width,
            bytes_accessed=2 * rows * width * len(parts) + 8 * rows * width,
            transcendentals=0,
        ),
    )(where, order, *parts)


def unpack_kernel(count, row_count, key_width, *refs):
    where, mine, theirs, query, key, value, extra, whole = refs
    half = mine.shape[1]
    core = where[1]
    for c in range(2):

        @pl.when(core == c)
        def _():
            whole[:, c * half : (c + 1) * half, :] = mine[...]
            whole[:, (1 - c) * half : (2 - c) * half, :] = theirs[...]

    for out, at in ((query, 0), (key, key_width), (value, 2 * key_width)):
        size = out.shape[1] // count
        for s in range(count):
            rows = whole[s, :row_count, at : at + size]
            out[:, s * size : (s + 1) * size] = rows.astype(F32)
    extra[...] = whole[:, row_count:, :].astype(F32)


def unpack(where, parts, row_count, key_width, val_width):
    count, half, width = parts[0].shape
    vmem = pl.BlockSpec(memory_space=pltpu.VMEM)
    return pl.pallas_call(
        functools.partial(unpack_kernel, count, row_count, key_width),
        in_specs=[scalar_spec()] + [vmem] * 2,
        out_specs=[vmem] * 4,
        out_shape=[
            shape((row_count, count * key_width), F32),
            shape((row_count, count * key_width), F32),
            shape((row_count, count * val_width), F32),
            shape((count, EXTRA, width), F32),
        ],
        scratch_shapes=[pltpu.VMEM((count, 2 * half, width), BF16)],
        compiler_params=params(),
    )(where, *parts)


class Exchange:
    def __init__(self):
        self.new = {}


def pin_all(exchanges, *arrays):
    keys = [sorted(e.new) for e in exchanges]
    out = pin(*arrays, *[e.new[k] for e, ks in zip(exchanges, keys) for k in ks])
    at = len(arrays)
    for e, ks in zip(exchanges, keys):
        e.new = dict(zip(ks, out[at : at + len(ks)]))
        at += len(ks)
    return out[: len(arrays)]


def pin_after(exchanges, *arrays):
    pin_all(exchanges, *arrays)


class Gather(Exchange):
    def __init__(self, part, order, count):
        super().__init__()
        self.have, self.order, self.count, self.last = {0: part}, order, count, [0]

    def take(self):
        self.have.update(self.new)
        self.new = {}

    def send(self):
        self.take()
        new = {}
        for m in self.last:
            used = [k for k, bit in enumerate(self.order) if m & bit]
            for bit in self.order[max(used, default=-1) + 1 :]:
                new[m | bit] = swap(self.have[m], bit, self.count)
        self.new, self.last = new, sorted(new)


class Scatter(Exchange):
    def __init__(self, blocks, order, count):
        super().__init__()
        self.have, self.order, self.count, self.step = dict(enumerate(blocks)), order, count, 0

    def take(self):
        if self.new:
            bit = self.order[self.step - 1]
            self.have = {
                m: self.have[m].astype(F32) + self.new[m | bit].astype(F32)
                for m in self.have
                if not m & bit
            }
            self.new = {}

    def send(self):
        self.take()
        bit = self.order[self.step]
        self.new = {
            m: swap(self.have[m].astype(BF16), bit, self.count)
            for m in sorted(self.have, reverse=True)
            if m & bit
        }
        self.step += 1

    def rest(self):
        while self.step < len(self.order):
            self.send()
        self.take()
        return self.have[0]


class CubeSum(Exchange):
    def __init__(self, piece, count):
        super().__init__()
        self.total, self.step = piece, 0
        self.count, self.bits = count, count.bit_length() - 1

    def swap(self, array, bit):
        return lax.ppermute(array, "wz", [(i, i ^ bit) for i in range(self.count)])

    def mine(self, bit):
        return jnp.where(lax.axis_index("wz") & bit, 1, 0)

    def take(self):
        if self.new:
            came, at = self.new[0], self.step - 1
            if at < self.bits:
                half = came.shape[0]
                kept = lax.dynamic_slice_in_dim(self.total, self.mine(1 << at) * half, half, 0)
                self.total = (kept.astype(F32) + came.astype(F32)).astype(BF16)
            else:
                upper = self.mine(1 << (2 * self.bits - 1 - at)) == 1
                self.total = jnp.concatenate(
                    [jnp.where(upper, came, self.total), jnp.where(upper, self.total, came)], axis=0
                )
            self.new = {}

    def send(self):
        self.take()
        if self.step >= 2 * self.bits:
            return
        if self.step < self.bits:
            bit = 1 << self.step
            half = self.total.shape[0] // 2
            away = lax.dynamic_slice_in_dim(self.total, (1 - self.mine(bit)) * half, half, 0)
            self.new = {0: self.swap(away.astype(BF16), bit)}
        else:
            self.new = {0: self.swap(self.total, 1 << (2 * self.bits - 1 - self.step))}
        self.step += 1

    def rest(self):
        while self.step < 2 * self.bits:
            self.send()
        self.take()
        return self.total.astype(BF16)


class OtherCore(Exchange):
    def __init__(self, array):
        super().__init__()
        self.new = {0: other_core(array)}


def split_columns(blocks, count):
    half = blocks[0].shape[1] // 2
    return [
        Scatter([block[:, k * half : (k + 1) * half] for block in blocks], order, count)
        for k, order in enumerate(bit_orders(count))
    ]


def other_core(array):
    return lax.ppermute(array, "core", [(0, 1), (1, 0)])


def shards(
    seq_count,
    wz_count,
    inputs,
    bin_order,
    first_gain,
    first_shift,
    query_weight,
    key_weight,
    value_weight,
    bias_content,
    bias_position,
    relative_weight,
    out_weight,
    bias_out,
    second_gain,
    second_shift,
    inner_weight,
    bias_inner,
    outer_weight,
    bias_outer,
    grad_output,
):
    row_count, width = inputs.shape[1:]
    length = bin_order.shape[1]
    here = lax.axis_index("seq")
    core = lax.axis_index("core")
    where = jnp.stack([here, core]).astype(jnp.int32)
    row_start = here * row_count
    key_width = query_weight.shape[1] // seq_count
    val_width = value_weight.shape[1] // seq_count
    heads_width = 2 * key_width + val_width
    up, down = bit_orders(seq_count)

    others = [jnp.bitwise_xor(here, m) for m in range(seq_count)]
    along = jnp.concatenate(
        [other * row_count + jnp.arange(row_count, dtype=jnp.int32) for other in others]
    )

    def natural(rows):
        parts = rows.reshape(seq_count, row_count, -1)
        parts = [lax.dynamic_index_in_dim(parts, other, 0) for other in others]
        return jnp.concatenate(parts, axis=0).reshape(rows.shape)

    def halves(rows):
        half = rows.shape[0] // 2
        return [Gather(rows[:half], up, seq_count), Gather(rows[half:], down, seq_count)]

    def blocks_of(gathers):
        for g in gathers:
            g.take()
        return [g.have[m] for m in range(seq_count) for g in gathers]

    window_gathers = halves(inputs[0])
    for g in window_gathers:
        g.send()

    def by_head(weight):
        return weight.reshape(weight.shape[0], seq_count, -1)

    vectors = jnp.stack([first_gain, first_shift, bias_out, second_gain, second_shift, bias_outer])
    vectors = jnp.concatenate([vectors, bias_inner.reshape(2, row_count)], axis=0)
    vectors = jnp.pad(vectors, ((0, EXTRA - 8), (0, 0)))
    rel_rows = relative_weight.shape[0]
    rel_blocks = -(-rel_rows // EXTRA)
    rel_part = jnp.pad(by_head(relative_weight), ((0, rel_blocks * EXTRA - rel_rows), (0, 0), (0, 0)))
    rel_part = rel_part.reshape(rel_blocks, EXTRA, seq_count, key_width).transpose(2, 1, 0, 3)
    rel_part = rel_part.reshape(seq_count, EXTRA, -1)
    spare = heads_width - row_count - rel_part.shape[2]
    extra = jnp.concatenate(
        [
            jnp.broadcast_to(vectors[None], (seq_count,) + vectors.shape),
            jnp.pad(rel_part, ((0, 0), (0, 0), (0, spare))),
        ],
        axis=2,
    )
    mine = jnp.concatenate(
        [by_head(query_weight), by_head(key_weight), by_head(value_weight)], axis=2
    ).transpose(1, 0, 2)
    mine = jnp.concatenate([mine, extra], axis=1)
    half = mine.shape[1] // 2
    mine = lax.dynamic_slice_in_dim(mine, core * half, half, 1)
    (mine,) = pin_all(window_gathers, mine)
    for step in range(1, len(up)):
        for g in window_gathers:
            g.send()
    mine = lax.all_to_all(mine, "seq", 0, 0, tiled=True)
    (mine,) = pin_all(window_gathers, mine)
    first = core == 0
    theirs = other_core(mine)
    attention_weight = jnp.concatenate(
        [jnp.where(first, mine, theirs), jnp.where(first, theirs, mine)], axis=1
    )
    table, table_back = basis_tables(jnp.asarray(basis_constants(length)), length)
    flat = attention_weight[:, row_count:]
    vectors = flat[:, :8, :row_count].astype(F32)
    inner_bias = vectors[:, 6:8].reshape(1, -1)
    vectors = vectors.transpose(1, 0, 2).reshape(8, width)
    rel = flat[:, :, row_count : row_count + rel_blocks * key_width]
    rel = rel.reshape(seq_count, EXTRA, rel_blocks, key_width).transpose(0, 2, 1, 3)
    rel = rel.reshape(seq_count, rel_blocks * EXTRA, key_width)[:, :rel_rows].reshape(REL, key_width)

    def own_half(weight):
        half = weight.shape[0] // 2
        return lax.dynamic_slice_in_dim(weight, core * half, half, 0)

    inner_part, outer_part = own_half(inner_weight), own_half(outer_weight)
    inner_part, outer_part = pin_all(window_gathers, inner_part, outer_part)
    window_blocks = blocks_of(window_gathers)
    weight_gathers = [
        Gather(inner_part, up, seq_count),
        Gather(outer_part, down, seq_count),
    ]
    for g in weight_gathers:
        g.send()

    order = bin_order[0]
    placing = (order[:, None] == along[None, :]).astype(BF16)
    bias = jnp.concatenate([bias_content, bias_position])[None].astype(F32)
    window, hidden_one, in_bins, weight_whole = project(
        window_blocks, attention_weight, vectors, bias, row_count
    )
    placed_heads = matmul(placing, in_bins).astype(BF16)
    mixed, probs = attend(placed_heads, rel, table)
    (mixed,) = pin_all(weight_gathers, mixed)
    for step in range(1, len(up)):
        for g in weight_gathers:
            g.send()
    weight_parts = []
    for g, own in zip(weight_gathers, (inner_weight, outer_weight)):
        g.take()
        parts = [own]
        for m in range(1, seq_count):
            parts += [g.have[m], other_core(g.have[m])]
        weight_parts.append(parts)
    mixed_along = natural(mixed).reshape(seq_count, row_count, val_width)
    attended = [matmul(mixed_along[m], out_weight).astype(BF16) for m in range(seq_count)]
    attended = split_columns(attended, seq_count)
    for g in attended:
        g.send()
    own_order = lax.dynamic_slice_in_dim(order, row_start, row_count, 0)
    placed = matmul((own_order[:, None] == along[None, :]).astype(BF16), window)
    (placed,) = pin_all(attended, placed)
    attended = [g.rest() for g in attended]

    grad_rows = grad_output[0]
    layer_output, d_mixed_in, hidden_two, activated, d_inner, sums, inner_sums = feed_forward(
        where, placed, attended, grad_rows, vectors, inner_bias, *weight_parts
    )

    d_mixed_gathers = halves(d_mixed_in)
    for g in d_mixed_gathers:
        g.send()
    away = ff_gradients(seq_count, where, hidden_two, activated, d_inner, grad_rows)
    pin_after(d_mixed_gathers, *away)
    for step in range(1, len(up)):
        for g in d_mixed_gathers:
            g.send()
    came = [other_core(part) for part in away]
    kept = ff_gradients(seq_count, where, hidden_two, activated, d_inner, grad_rows, came)
    kept = pin_all(d_mixed_gathers, *kept)
    d_mixed_blocks = blocks_of(d_mixed_gathers)
    count = seq_count
    inner_sums_of, outer_sums_of = [
        [
            Scatter([kept[2 * (k * count + m) + side] for m in range(count)], bits, count)
            for side, bits in enumerate((up, down))
        ]
        for k in range(2)
    ]
    for g in inner_sums_of:
        g.send()

    d_attended, out_away, grad_out_w = mixed_back(
        seq_count, where, mixed, out_weight, d_mixed_blocks
    )
    out_core = OtherCore(out_away)

    def send_all(exchanges):
        for exchange in exchanges:
            exchange.send()

    back = attend_back(0, placed_heads, rel, table_back, mixed, d_attended, probs)
    back = pin_all(inner_sums_of, *back)
    for step in range(1, len(up)):
        send_all(inner_sums_of)
    send_all(outer_sums_of)
    for head in range(1, key_width // KEY):
        back = attend_back(head, placed_heads, rel, table_back, mixed, d_attended, probs, back)
    back = pin_all(inner_sums_of, *back)
    d_heads, d_rel, d_bias = back

    def joined_sum(scatters):
        return CubeSum(jnp.concatenate([g.rest() for g in scatters], axis=1), wz_count)

    inner_cube = joined_sum(inner_sums_of)
    inner_cube.send()
    d_along, *d_normed, first_sums = rows_back(
        seq_count, where, order[None], d_heads, window, weight_whole
    )
    out = pin_all(outer_sums_of + [inner_cube], d_along, *d_normed)
    d_along, d_normed = out[0], out[1:]
    for step in range(1, len(up)):
        send_all(outer_sums_of)
    inner_cube.send()
    arrived = [
        Scatter([d_normed[2 * m + side] for m in range(count)], bits, count)
        for side, bits in enumerate((up, down))
    ]
    results = pack(
        seq_count, where, hidden_one, d_along, first_sums, sums, inner_sums, d_bias, d_rel
    )
    results = pin_all(outer_sums_of + [inner_cube, out_core], *results)
    packed_core = OtherCore(results[1])
    outer_cube = joined_sum(outer_sums_of)
    outer_cube.send()
    inner_cube.send()
    (packed,) = pin_all([packed_core], results[0])
    packed = (packed.astype(F32) + packed_core.new[0].astype(F32)).astype(BF16)
    packed_shape = packed.shape
    packed = lax.all_to_all(packed, "seq", 0, 0, tiled=True)
    send_all(arrived)
    out_cube = CubeSum(grad_out_w + out_core.new[0].astype(F32), wz_count)
    (packed,) = pin_all([inner_cube, outer_cube], packed)
    packed_cube = CubeSum(packed.reshape(-1, packed_shape[2]), wz_count)
    cubes = [packed_cube, outer_cube, inner_cube]
    send_all(cubes)
    d_mixed_blocks = pin_all(arrived, *d_mixed_blocks)
    returned = returned_rows(
        seq_count, where, order.reshape(2 * seq_count, row_count // 2), d_mixed_blocks
    )
    for step in range(1, len(up)):
        send_all(arrived)
    (returned,) = pin_all(cubes, returned)

    def both_halves(cube, axis):
        piece = cube.rest()
        other = other_core(piece)
        parts = [jnp.where(first, piece, other), jnp.where(first, other, piece)]
        return jnp.concatenate(parts, axis=axis).astype(F32)

    cubes = [packed_cube, outer_cube, out_cube]
    send_all(cubes)
    grad_inner_w = both_halves(inner_cube, 1)
    (grad_inner_w,) = pin_all(cubes + arrived, grad_inner_w)
    send_all(cubes)
    own_unit, own_scale = norm_of(inputs[0].astype(F32))
    arrived = jnp.concatenate([g.rest() for g in arrived], axis=1)
    grad_inputs = norm_back(own_unit, own_scale, vectors[0:1], arrived) + returned
    (grad_inputs,) = pin_all(cubes, grad_inputs)
    send_all([packed_cube, out_cube])
    grad_outer_w = both_halves(outer_cube, 0)
    (grad_outer_w,) = pin_all([packed_cube, out_cube], grad_outer_w)
    grad_out_w = both_halves(out_cube, 0)
    packed = packed_cube.rest().reshape(packed_shape)
    grad_query_w, grad_key_w, grad_value_w, flat = unpack(
        where, (packed, other_core(packed)), row_count, key_width, val_width
    )
    small = jnp.sum(flat[:, :16, :row_count], axis=0)
    g_gain_one, g_shift_one, g_out_b, g_gain_two, g_shift_two, g_outer_b = small[:6]
    g_inner_b = small[6:8].reshape(-1)
    grad_rel = flat[:, :, row_count : row_count + rel_blocks * key_width]
    grad_rel = grad_rel.reshape(seq_count, EXTRA, rel_blocks, key_width).transpose(2, 1, 0, 3)
    grad_rel = grad_rel.reshape(rel_blocks * EXTRA, -1)[:rel_rows]
    return (
        layer_output[None],
        grad_inputs[None],
        g_gain_one,
        g_shift_one,
        grad_query_w,
        grad_key_w,
        grad_value_w,
        small[8, :key_width],
        small[9, :key_width],
        grad_rel,
        grad_out_w,
        g_out_b,
        g_gain_two,
        g_shift_two,
        grad_inner_w,
        g_inner_b,
        grad_outer_w,
        g_outer_b,
    )


def solution(mesh):
    seq_count = mesh.shape["seq"]
    devices = mesh.devices.reshape(seq_count, -1, 2)
    split_mesh = Mesh(devices, ("seq", "wz", "core"))
    rows = P(("wz", "core"), "seq", None)
    vector = P("seq")
    matrix = P("seq", None)
    weights = (
        vector,
        vector,
        matrix,
        matrix,
        matrix,
        vector,
        vector,
        matrix,
        matrix,
        vector,
        vector,
        vector,
        matrix,
        vector,
        matrix,
        vector,
    )
    return jax.shard_map(
        functools.partial(shards, seq_count, mesh.shape["win"] // 2),
        mesh=split_mesh,
        in_specs=(rows, P(("wz", "core"), None)) + weights + (rows,),
        out_specs=(rows, rows) + weights,
        check_vma=False,
    )
```

```python
import functools
import math

import jax
import jax.numpy as jnp
import numpy as np
from jax import lax
from jax.experimental import pallas as pl
from jax.experimental.pallas import tpu as pltpu
from jax.sharding import Mesh
from jax.sharding import PartitionSpec as P

HEADS = 8
KEY = 64
VAL = 192
REL = 192
BF16 = jnp.bfloat16
F32 = jnp.float32
VMEM_LIMIT = 56 * 2**20
EXTRA = 32


def matmul(a, b):
    return lax.dot_general(a, b, (((1,), (0,)), ((), ())), preferred_element_type=F32)


def matmul_nt(a, b):
    return lax.dot_general(a, b, (((1,), (1,)), ((), ())), preferred_element_type=F32)


def matmul_tn(a, b):
    return lax.dot_general(a, b, (((0,), (0,)), ((), ())), preferred_element_type=F32)


def head_part(rows, head):
    lanes = lax.broadcasted_iota(jnp.int32, rows.shape, 1)
    inside = (lanes >= head * KEY) & (lanes < (head + 1) * KEY)
    return jnp.where(inside, rows, jnp.zeros_like(rows))


def head_columns(key_width):
    return [slice(k * key_width, (k + 1) * key_width) for k in range(3)]


def attend_kernel(heads, rows, placed, rel, table, mixed, probs):
    length = placed.shape[0]
    key_width = heads * KEY
    content_at, position_at, keys_at = head_columns(key_width)
    first = pl.program_id(0) * rows
    here = pl.ds(pl.multiple_of(first, rows), rows)
    basis = table[:, pl.ds(pl.multiple_of(length - rows - first, rows), length + rows)]
    content, position, keys = placed[here, content_at], placed[here, position_at], placed[:, keys_at]
    parts = []
    for head in range(heads):
        q_basis = matmul_nt(head_part(position, head), rel[...]).astype(BF16)
        grid = matmul(q_basis, basis)
        shifted = pltpu.roll(grid, 0, 1, stride=1, stride_axis=0)[:, rows:]
        scores = matmul_nt(head_part(content, head), keys) + shifted
        top = jnp.max(scores, axis=1, keepdims=True)
        weights = jnp.exp(scores - top)
        total = jnp.sum(weights, axis=1, keepdims=True)
        prob = (weights * (1.0 / total)).astype(BF16)
        probs[head] = prob
        values_at = 3 * key_width + head * VAL
        parts.append(matmul(prob, placed[:, values_at : values_at + VAL]))
    mixed[...] = jnp.concatenate(parts, axis=1).astype(BF16)


def attend(placed, rel, table):
    length = placed.shape[0]
    heads = rel.shape[1] // KEY
    rows = math.gcd(256, length)
    whole = lambda array: pl.BlockSpec(array.shape, lambda i: (0, 0))
    return pl.pallas_call(
        functools.partial(attend_kernel, heads, rows),
        grid=(length // rows,),
        in_specs=[whole(placed), whole(rel), whole(table)],
        out_specs=[
            pl.BlockSpec((rows, heads * VAL), lambda i: (i, 0)),
            pl.BlockSpec((heads, rows, length), lambda i: (0, i, 0)),
        ],
        out_shape=[
            jax.ShapeDtypeStruct((length, heads * VAL), BF16),
            jax.ShapeDtypeStruct((heads, length, length), BF16),
        ],
        compiler_params=pltpu.CompilerParams(vmem_limit_bytes=VMEM_LIMIT),
        cost_estimate=pl.CostEstimate(
            flops=2 * heads * length * length * 1024,
            bytes_accessed=2 * heads * length * length + 8 * length * heads * VAL,
            transcendentals=heads * length * length,
        ),
    )(placed, rel, table)


def attend_back_kernel(heads, head, rows, *refs):
    placed, rel, table, flip, mixed, d_mixed, probs = refs[:7]
    before = refs[7:-5]
    d_heads, d_rel, d_bias, keys_sum, values_sum = refs[-5:]
    length = placed.shape[0]
    key_width = heads * KEY
    content_at, position_at, keys_at = head_columns(key_width)
    step = pl.program_id(0)

    @pl.when(step == 0)
    def _():
        keys_sum[...] = jnp.zeros_like(keys_sum)
        values_sum[...] = jnp.zeros_like(values_sum)
        for k, out in enumerate((d_heads, d_rel, d_bias)):
            out[...] = before[k][...] if before else jnp.zeros_like(out)

    first = pl.multiple_of(step * rows, rows)
    here = pl.ds(first, rows)
    basis = table[:, pl.ds(first, length + rows)]
    content, position, keys = placed[here, content_at], placed[here, position_at], placed[:, keys_at]
    blocks = length // rows
    columns = slice(head * VAL, (head + 1) * VAL)
    values_at = 3 * key_width + head * VAL
    d_part = d_mixed[:, columns]
    delta = jnp.sum(d_part.astype(F32) * mixed[:, columns].astype(F32), axis=1, keepdims=True)
    prob = probs[0]
    values_sum[...] += matmul_tn(d_part, prob)
    d_prob = matmul_nt(d_part, placed[:, values_at : values_at + VAL])
    d_score = (prob.astype(F32) * (d_prob - delta)).astype(BF16)
    keys_sum[...] += matmul_tn(head_part(content, head), d_score)
    d_content = head_part(matmul(d_score, keys), head)
    turned = [
        matmul(d_score[:, (blocks - 1 - b) * rows : (blocks - b) * rows], flip[...])
        for b in range(blocks)
    ]
    turned = jnp.concatenate(turned + [jnp.zeros((rows, rows), F32)], axis=1)
    d_grid = pltpu.roll(turned, 0, 1, stride=1, stride_axis=0).astype(BF16)
    d_basis = matmul_nt(d_grid, basis).astype(BF16)
    d_position = head_part(matmul(d_basis, rel[...]), head)
    d_rel[...] += matmul_tn(d_basis, head_part(position, head))
    d_heads[here, :key_width] += ((d_content + d_position) * KEY ** (-0.5)).astype(BF16)
    d_bias[0:1, :] += jnp.sum(d_content, axis=0, keepdims=True)
    d_bias[1:2, :] += jnp.sum(d_position, axis=0, keepdims=True)

    @pl.when(step == blocks - 1)
    def _():
        d_heads[:, key_width : 2 * key_width] += keys_sum[...].T.astype(BF16)
        values_to = 2 * key_width + head * VAL
        d_heads[:, values_to : values_to + VAL] = values_sum[...].T.astype(BF16)


def attend_back(head, placed, rel, table, mixed, d_mixed, probs, before=()):
    length = placed.shape[0]
    key_width = rel.shape[1]
    heads = key_width // KEY
    val_width = heads * VAL
    rows = math.gcd(256, length)
    at = jnp.arange(rows)
    flip = (at[:, None] + at[None, :] == rows - 1).astype(BF16)
    block = lambda width: pl.BlockSpec((rows, width), lambda i: (i, 0))
    outs = [
        shape((length, 2 * key_width + val_width), BF16),
        shape((REL, key_width), F32),
        shape((8, key_width), F32),
    ]
    return pl.pallas_call(
        functools.partial(attend_back_kernel, heads, head, rows),
        grid=(length // rows,),
        in_specs=[
            whole_spec(placed),
            whole_spec(rel),
            whole_spec(table),
            whole_spec(flip),
            block(val_width),
            block(val_width),
            pl.BlockSpec((1, rows, length), lambda i: (head, i, 0)),
        ]
        + [whole_spec(array) for array in before],
        out_specs=[whole_spec(out) for out in outs],
        out_shape=outs,
        scratch_shapes=[
            pltpu.VMEM((key_width, length), F32),
            pltpu.VMEM((VAL, length), F32),
        ],
        compiler_params=pltpu.CompilerParams(vmem_limit_bytes=VMEM_LIMIT),
        cost_estimate=pl.CostEstimate(
            flops=2 * length * length * 1536,
            bytes_accessed=2 * length * length + 16 * length * val_width,
            transcendentals=0,
        ),
    )(placed, rel, table, flip, mixed, d_mixed, probs, *before)


def norm_back(unit, scale, gain, grad):
    scaled = grad * gain
    mean_one = jnp.mean(scaled, axis=-1, keepdims=True)
    mean_two = jnp.mean(scaled * unit, axis=-1, keepdims=True)
    return (scaled - mean_one - unit * mean_two) * scale


def whole_spec(array):
    zeros = (0,) * len(array.shape)
    return pl.BlockSpec(array.shape, lambda *_: zeros)


def scalar_spec():
    return pl.BlockSpec(memory_space=pltpu.SMEM)


def params(**more):
    return pltpu.CompilerParams(vmem_limit_bytes=VMEM_LIMIT, **more)


def shape(dims, dtype):
    return jax.ShapeDtypeStruct(tuple(dims), dtype)


def basis_constants(window_len):
    features = REL // 6
    f = np.arange(features, dtype=np.float64)
    half_life = 2.0 ** (3.0 + f * (math.log2(window_len) - 3.0) / (features - 1))
    spread = window_len / (2.0 * features)
    first = window_len / features
    centres = first + f * (window_len - first) / (features - 1)
    concentration = (centres / spread) ** 2
    rate = centres / spread**2
    offset = concentration * np.log(rate) - np.array([math.lgamma(c) for c in concentration])
    columns = [math.log(2.0) / half_life, 2.0 ** (f + 1) - 1.0, concentration - 1.0, rate, offset]
    columns += [np.zeros(features)] * 3
    return np.stack(columns, axis=1).astype(np.float32)


def table_kernel(length, constants, forth, back):
    features = REL // 6
    decay, inside_below, power, rate, offset = [constants[:, k : k + 1] for k in range(5)]

    def gamma(distance):
        logged = power * jnp.log(jnp.maximum(distance, 1.0)) - rate * distance + offset
        return jnp.where(distance == 0.0, 0.0, jnp.exp(logged)) + 1e-08

    every = lax.broadcasted_iota(jnp.int32, (1, length), 1).astype(F32)
    peak = jnp.max(gamma(every), axis=1, keepdims=True)
    lanes = lax.broadcasted_iota(jnp.int32, (1, 2 * length), 1).astype(F32)
    for table, signed in ((forth, lanes - length), (back, length - 1 - lanes)):
        distance = jnp.abs(signed)
        sign = jnp.where(signed > 0, 1.0, jnp.where(signed < 0, -1.0, 0.0))
        parts = (
            jnp.exp(-decay * distance),
            jnp.where(inside_below > distance, 1.0, 0.0),
            gamma(distance) / peak,
        )
        for k, part in enumerate(parts):
            table[k * features : (k + 1) * features, :] = part.astype(BF16)
            table[(3 + k) * features : (4 + k) * features, :] = (sign * part).astype(BF16)


def basis_tables(constants, length):
    out = shape((REL, 2 * length), BF16)
    return pl.pallas_call(
        functools.partial(table_kernel, length),
        out_shape=[out, out],
        compiler_params=params(),
    )(constants)


def norm_of(rows):
    centre = rows - jnp.mean(rows, axis=1, keepdims=True)
    scale = lax.rsqrt(jnp.mean(centre * centre, axis=1, keepdims=True) + 1e-05)
    return centre * scale, scale


def project_kernel(blocks, row_count, *refs):
    parts, (weight, vectors, bias, window, hidden, heads, flat, block) = refs[:blocks], refs[blocks:]
    step = pl.program_id(0)

    @pl.when(step == 0)
    def _():
        for s in range(weight.shape[0]):
            flat[s * row_count : (s + 1) * row_count, :] = weight[s, :row_count, :]

    for k in range(blocks):

        @pl.when(step == k)
        def _():
            block[...] = parts[k][...]

    window[...] = block[...]
    unit, _ = norm_of(block[...].astype(F32))
    normed = (unit * vectors[0:1, :] + vectors[1:2, :]).astype(BF16)
    hidden[...] = normed
    total = matmul(normed, flat[...])
    key_width = bias.shape[1] // 2
    query = total[:, :key_width] * KEY ** (-0.5)
    heads[:, :key_width] = (query + bias[0:1, :key_width]).astype(BF16)
    heads[:, key_width : 2 * key_width] = (query + bias[0:1, key_width:]).astype(BF16)
    heads[:, 2 * key_width :] = total[:, key_width:].astype(BF16)


def project(parts, weight, vectors, bias, row_count):
    blocks = len(parts)
    rows, width = parts[0].shape
    heads_width = weight.shape[2] + bias.shape[1] // 2
    out = lambda w: pl.BlockSpec((rows, w), lambda i: (i, 0))
    return pl.pallas_call(
        functools.partial(project_kernel, blocks, row_count),
        grid=(blocks,),
        in_specs=[whole_spec(a) for a in (*parts, weight, vectors, bias)],
        out_specs=[
            out(width),
            out(width),
            out(heads_width),
            pl.BlockSpec((width, weight.shape[2]), lambda i: (0, 0)),
        ],
        out_shape=[shape((blocks * rows, w), BF16) for w in (width, width, heads_width)]
        + [shape((width, weight.shape[2]), BF16)],
        scratch_shapes=[pltpu.VMEM((rows, width), BF16)],
        compiler_params=params(),
        cost_estimate=pl.CostEstimate(
            flops=2 * blocks * rows * width * heads_width,
            bytes_accessed=8 * blocks * rows * width,
            transcendentals=0,
        ),
    )(*parts, weight, vectors, bias)


def feed_kernel(count, chunk, *refs):
    parts = 2 * (2 * count - 1)
    where, placed, attended_a, attended_b, grad_rows, vectors, inner_bias = refs[:7]
    weights = refs[7 : 7 + parts]
    layer_output, d_mixed, hidden, activated, d_inner, sums, inner_sums = refs[7 + parts : 14 + parts]
    inner_whole, outer_whole, residual, unit, back, outer_sum, sems = refs[14 + parts :]
    here, core = where[0], where[1]
    copies = []
    for k, whole in enumerate((inner_whole, outer_whole)):
        mine = weights[k * (2 * count - 1) : (k + 1) * (2 * count - 1)]
        size = whole.shape[0] // count
        half = size // 2
        moves = [(mine[0], here * size, size)]
        for m in range(1, count):
            start = jnp.bitwise_xor(here, m) * size
            moves.append((mine[2 * m - 1], start + core * half, half))
            moves.append((mine[2 * m], start + (1 - core) * half, half))
        started = []
        for source, start, rows in moves:
            target = whole.at[pl.ds(pl.multiple_of(start, 16), rows), :]
            copy = pltpu.make_async_copy(source, target, sems.at[k, len(started)])
            copy.start()
            started.append(copy)
        copies.append(started)
    rows, width = placed.shape
    half = width // 2
    residual[:, :half] = placed[:, :half] + attended_a[...] + vectors[2:3, :half]
    residual[:, half:] = placed[:, half:] + attended_b[...] + vectors[2:3, half:]
    normed, scale = norm_of(residual[...])
    unit[...] = normed
    hidden[...] = (normed * vectors[3:4, :] + vectors[4:5, :]).astype(BF16)
    for started in copies:
        for copy in started:
            copy.wait()
    ff = outer_whole.shape[0]
    for c in range(ff // chunk):
        at = slice(c * chunk, (c + 1) * chunk)
        inner = matmul(hidden[...], inner_whole[:, at]) + inner_bias[0:1, at]
        below = 0.5 * (1.0 + lax.erf(inner * (0.5**0.5)))
        slope = below + inner * jnp.exp(-0.5 * inner * inner) * (0.5 / math.pi) ** 0.5
        active = (inner * below).astype(BF16)
        activated[:, at] = active
        grad = (matmul_nt(grad_rows[...], outer_whole[at, :]) * slope).astype(BF16)
        d_inner[:, at] = grad
        inner_sums[:, at] = jnp.sum(grad.astype(F32), axis=0, keepdims=True)
        back_term = matmul_nt(grad, inner_whole[:, at])
        outer_term = matmul(active, outer_whole[at, :])
        if c == 0:
            back[...] = back_term
            outer_sum[...] = outer_term
        else:
            back[...] += back_term
            outer_sum[...] += outer_term
    layer_output[...] = (residual[...] + outer_sum[...] + vectors[5:6, :]).astype(BF16)
    grad, normed = back[...], unit[...]
    dy = grad_rows[...].astype(F32)
    scaled = grad * vectors[3:4, :]
    mean_one = jnp.mean(scaled, axis=1, keepdims=True)
    mean_two = jnp.mean(scaled * normed, axis=1, keepdims=True)
    mixed_in = (dy + (scaled - mean_one - normed * mean_two) * scale).astype(BF16)
    d_mixed[...] = mixed_in
    sums[...] = jnp.zeros_like(sums)
    sums[2:3, :] = jnp.sum(mixed_in.astype(F32), axis=0, keepdims=True)
    sums[3:4, :] = jnp.sum(grad * normed, axis=0, keepdims=True)
    sums[4:5, :] = jnp.sum(grad, axis=0, keepdims=True)
    sums[5:6, :] = jnp.sum(dy, axis=0, keepdims=True)


def feed_forward(where, placed, attended, grad_rows, vectors, inner_bias, inner_parts, outer_parts):
    rows, width = placed.shape
    ff = inner_bias.shape[1]
    count = (len(inner_parts) + 1) // 2
    chunk = math.gcd(512, ff)
    weights = (*inner_parts, *outer_parts)
    small = (placed, *attended, grad_rows, vectors, inner_bias)
    outs = [
        shape((rows, width), BF16),
        shape((rows, width), BF16),
        shape((rows, width), BF16),
        shape((rows, ff), BF16),
        shape((rows, ff), BF16),
        shape((8, width), F32),
        shape((1, ff), F32),
    ]
    return pl.pallas_call(
        functools.partial(feed_kernel, count, chunk),
        in_specs=[scalar_spec()]
        + [pl.BlockSpec(memory_space=pltpu.VMEM) for _ in small]
        + [pl.BlockSpec(memory_space=pl.ANY) for _ in weights],
        out_specs=[pl.BlockSpec(memory_space=pltpu.VMEM) for _ in outs],
        out_shape=outs,
        scratch_shapes=[
            pltpu.VMEM((width, ff), BF16),
            pltpu.VMEM((ff, width), BF16),
            pltpu.VMEM((rows, width), F32),
            pltpu.VMEM((rows, width), F32),
            pltpu.VMEM((rows, width), F32),
            pltpu.VMEM((rows, width), F32),
            pltpu.SemaphoreType.DMA((2, 2 * count - 1)),
        ],
        compiler_params=params(),
        cost_estimate=pl.CostEstimate(
            flops=8 * rows * width * ff,
            bytes_accessed=4 * width * ff + 40 * rows * width,
            transcendentals=2 * rows * ff,
        ),
    )(where, *small, *weights)


def columns_at(ref, index, size, scratch):
    if size % 128 == 0:
        return ref[:, pl.ds(pl.multiple_of(index * size, 128), size)]
    for k in range(ref.shape[1] // size):

        @pl.when(index == k)
        def _():
            scratch[...] = ref[:, k * size : (k + 1) * size]

    return scratch[...]


def away_kernel(
    count, where, hidden, activated, d_inner, grad_rows, inner_away, outer_away, some, more
):
    here, other = where[0], 1 - where[1]
    rows = hidden.shape[1] // count
    ff = d_inner.shape[1]
    ff_rows = ff // count
    half = pl.ds(pl.multiple_of(other * (ff // 2), 128), ff // 2)
    step = pl.program_id(0)
    shard = jnp.bitwise_xor(here, step)
    columns = columns_at(hidden, shard, rows, some)
    inner_away[0] = matmul_tn(columns, d_inner[:, half]).astype(BF16)
    columns = columns_at(activated, 2 * shard + other, ff_rows // 2, more)
    outer_away[0] = matmul_tn(columns, grad_rows[...]).astype(BF16)


def kept_kernel(
    count, where, hidden, activated, d_inner, grad_rows, inner_came, outer_came, *refs
):
    outs, (some, more) = refs[:-2], refs[-2:]
    here, core = where[0], where[1]
    rows = hidden.shape[1] // count
    ff = d_inner.shape[1]
    ff_rows = ff // count
    half = pl.ds(pl.multiple_of(core * (ff // 2), 128), ff // 2)
    step = pl.program_id(0)
    shard = jnp.bitwise_xor(here, step)
    columns = columns_at(hidden, shard, rows, some)
    inner = matmul_tn(columns, d_inner[:, half]) + inner_came[0].astype(F32)
    columns = columns_at(activated, 2 * shard + core, ff_rows // 2, more)
    outer = matmul_tn(columns, grad_rows[...]) + outer_came[0].astype(F32)
    for k, result in enumerate((inner, outer)):
        side = result.shape[1] // 2
        for m in range(count):

            @pl.when(step == m)
            def _():
                outs[2 * (k * count + m)][...] = result[:, :side].astype(BF16)
                outs[2 * (k * count + m) + 1][...] = result[:, side:].astype(BF16)


def ff_gradients(count, where, hidden, activated, d_inner, grad_rows, came=None):
    rows = hidden.shape[1] // count
    ff = d_inner.shape[1]
    wide = [(rows, ff // 2), (ff // count // 2, grad_rows.shape[1])]
    block = lambda dims: pl.BlockSpec((1,) + dims, lambda i: (i, 0, 0))
    small = (hidden, activated, d_inner, grad_rows)
    if came is None:
        kernel, extra = away_kernel, ()
        out_specs = [block(dims) for dims in wide]
        outs = [shape((count,) + dims, BF16) for dims in wide]
    else:
        kernel, extra = kept_kernel, came
        outs = [shape((d[0], d[1] // 2), BF16) for d in wide for _ in range(2 * count)]
        out_specs = [whole_spec(out) for out in outs]
    return pl.pallas_call(
        functools.partial(kernel, count),
        grid=(count,),
        in_specs=[scalar_spec()]
        + [whole_spec(a) for a in small]
        + [block(dims) for dims in wide[: len(extra)]],
        out_specs=out_specs,
        out_shape=outs,
        scratch_shapes=[
            pltpu.VMEM((hidden.shape[0], rows), BF16),
            pltpu.VMEM((hidden.shape[0], ff // count // 2), BF16),
        ],
        compiler_params=params(),
        cost_estimate=pl.CostEstimate(
            flops=2 * hidden.shape[0] * hidden.shape[1] * ff,
            bytes_accessed=8 * rows * count * ff,
            transcendentals=0,
        ),
    )(where, *small, *extra)


def mixed_back_kernel(count, parts_count, *refs):
    where, mixed, weight = refs[:3]
    parts = refs[3 : 3 + parts_count]
    d_attended, out_away, out_kept, out_sum = refs[3 + parts_count :]
    here, core = where[0], where[1]
    rows = parts[0].shape[0]
    for k, part in enumerate(parts):
        start = jnp.bitwise_xor(here, k // 2) * (2 * rows) + (k % 2) * rows
        at = pl.ds(pl.multiple_of(start, 32), rows)
        d_attended[at, :] = matmul_nt(part[...], weight[...]).astype(BF16)
        term = matmul_tn(mixed[at, :], part[...])
        if k == 0:
            out_sum[...] = term
        else:
            out_sum[...] += term
    half = out_kept.shape[0]
    out_kept[...] = out_sum[pl.ds(pl.multiple_of(core * half, 32), half), :]
    out_away[...] = out_sum[pl.ds(pl.multiple_of((1 - core) * half, 32), half), :].astype(BF16)


def mixed_back(count, where, mixed, weight, parts):
    length, val_width = mixed.shape
    width = weight.shape[1]
    vmem = pl.BlockSpec(memory_space=pltpu.VMEM)
    return pl.pallas_call(
        functools.partial(mixed_back_kernel, count, len(parts)),
        in_specs=[scalar_spec()] + [vmem] * (2 + len(parts)),
        out_specs=[vmem] * 3,
        out_shape=[
            shape((length, val_width), BF16),
            shape((val_width // 2, width), BF16),
            shape((val_width // 2, width), F32),
        ],
        scratch_shapes=[pltpu.VMEM((val_width, width), F32)],
        compiler_params=params(),
        cost_estimate=pl.CostEstimate(
            flops=4 * length * val_width * width,
            bytes_accessed=2 * length * (width + 2 * val_width),
            transcendentals=0,
        ),
    )(where, mixed, weight, *parts)


def rows_back_kernel(count, where, order, d_heads, window, weight, d_along, *refs):
    d_normed, first_sums = refs[:-1], refs[-1]
    here = where[0]
    step = pl.program_id(0)
    rows, width = window.shape
    length = order.shape[1]
    bins = lax.broadcasted_iota(jnp.int32, (rows, length), 0) + jnp.bitwise_xor(here, step) * rows
    picks = jnp.where(order[0:1, :] == bins, 1.0, 0.0).astype(BF16)
    along = matmul(picks, d_heads[...]).astype(BF16)
    d_along[...] = along
    unit, _ = norm_of(window[...].astype(F32))
    normed = matmul_nt(along, weight[...])

    @pl.when(step == 0)
    def _():
        first_sums[...] = jnp.zeros_like(first_sums)

    first_sums[0:1, :] += jnp.sum(normed * unit, axis=0, keepdims=True)
    first_sums[1:2, :] += jnp.sum(normed, axis=0, keepdims=True)
    half = width // 2
    for m in range(count):

        @pl.when(step == m)
        def _():
            d_normed[2 * m][...] = normed[:, :half].astype(BF16)
            d_normed[2 * m + 1][...] = normed[:, half:].astype(BF16)


def rows_back(count, where, order, d_heads, window, weight):
    length, width = window.shape
    rows = length // count
    heads_width = d_heads.shape[1]
    outs = [shape((length, heads_width), BF16)]
    outs += [shape((rows, width // 2), BF16) for _ in range(2 * count)]
    outs += [shape((8, width), F32)]
    return pl.pallas_call(
        functools.partial(rows_back_kernel, count),
        grid=(count,),
        in_specs=[
            scalar_spec(),
            whole_spec(order),
            whole_spec(d_heads),
            pl.BlockSpec((rows, width), lambda i: (i, 0)),
            whole_spec(weight),
        ],
        out_specs=[pl.BlockSpec((rows, heads_width), lambda i: (i, 0))]
        + [whole_spec(out) for out in outs[1:]],
        out_shape=outs,
        compiler_params=params(),
        cost_estimate=pl.CostEstimate(
            flops=2 * length * heads_width * (length + width),
            bytes_accessed=4 * length * (width + heads_width),
            transcendentals=0,
        ),
    )(where, order, d_heads, window, weight)


def pack_kernel(
    count, where, hidden, d_along, first_sums, sums, inner_sums, d_bias, d_rel, kept, away, grads
):
    here, core = where[0], where[1]
    step = pl.program_id(0)
    row_count = hidden.shape[1] // count
    key_width = d_rel.shape[1]
    terms = matmul_tn(hidden[...], d_along[...])

    @pl.when(step == 0)
    def _():
        for s in range(count):
            grads[s, :row_count, :] = terms[s * row_count : (s + 1) * row_count, :]

    @pl.when(step > 0)
    def _():
        for s in range(count):
            grads[s, :row_count, :] += terms[s * row_count : (s + 1) * row_count, :]

    @pl.when(step == pl.num_programs(0) - 1)
    def _():
        rel_rows = d_rel.shape[0] // count
        for s in range(count):
            at = slice(s * row_count, (s + 1) * row_count)
            grads[s, row_count:, :] = jnp.zeros((EXTRA, grads.shape[2]), F32)
            grads[s, row_count : row_count + 2, :row_count] = first_sums[0:2, at]
            grads[s, row_count + 2 : row_count + 6, :row_count] = sums[2:6, at]
            for j in range(2):
                part = slice((2 * s + j) * row_count, (2 * s + j + 1) * row_count)
                grads[s, row_count + 6 + j : row_count + 7 + j, :row_count] = inner_sums[0:1, part]
            for j in range(-(-rel_rows // EXTRA)):
                some = d_rel[s * rel_rows + j * EXTRA : s * rel_rows + min(rel_rows, (j + 1) * EXTRA), :]
                lane = row_count + j * key_width
                grads[s, row_count : row_count + some.shape[0], lane : lane + key_width] = some
        for s in range(count):

            @pl.when(here == s)
            def _():
                grads[s, row_count + 8 : row_count + 10, :key_width] = d_bias[0:2, :]

        half = kept.shape[1]
        kept[...] = grads[:, pl.ds(pl.multiple_of(core * half, 16), half), :].astype(BF16)
        away[...] = grads[:, pl.ds(pl.multiple_of((1 - core) * half, 16), half), :].astype(BF16)


def pack(count, where, hidden, d_along, *small):
    length, width = hidden.shape
    heads_width = d_along.shape[1]
    rows = math.gcd(768, length)
    packed = (count, width // count + EXTRA, heads_width)
    outs = [shape((count, packed[1] // 2, heads_width), BF16) for _ in range(2)]
    return pl.pallas_call(
        functools.partial(pack_kernel, count),
        grid=(length // rows,),
        in_specs=[
            scalar_spec(),
            pl.BlockSpec((rows, width), lambda i: (i, 0)),
            pl.BlockSpec((rows, heads_width), lambda i: (i, 0)),
        ]
        + [whole_spec(a) for a in small],
        out_specs=[whole_spec(out) for out in outs],
        out_shape=outs,
        scratch_shapes=[pltpu.VMEM(packed, F32)],
        compiler_params=params(),
        cost_estimate=pl.CostEstimate(
            flops=2 * length * heads_width * width,
            bytes_accessed=2 * length * (width + heads_width) + 8 * width * heads_width,
            transcendentals=0,
        ),
    )(where, hidden, d_along, *small)


def swap(array, mask, count):
    return lax.ppermute(array, "seq", [(i, i ^ mask) for i in range(count)])


def bit_orders(count):
    bits = [1 << k for k in range(count.bit_length() - 1)]
    return bits, bits[::-1]


def pin(*arrays):
    return lax.optimization_barrier(arrays)


def returned_kernel(count, where, order, *refs):
    parts, returned = refs[:-1], refs[-1]
    here = where[0]
    rows = parts[0].shape[0]
    bins = lax.broadcasted_iota(jnp.int32, (returned.shape[0], rows), 0)
    bins = bins + here * returned.shape[0]
    for k, part in enumerate(parts):
        shard = jnp.bitwise_xor(here, k // 2)
        picks = jnp.where(order[pl.ds(2 * shard + k % 2, 1), :] == bins, 1.0, 0.0).astype(BF16)
        term = matmul(picks, part[...])
        if k == 0:
            returned[...] = term
        else:
            returned[...] += term


def returned_rows(count, where, order, parts):
    rows, width = parts[0].shape
    vmem = pl.BlockSpec(memory_space=pltpu.VMEM)
    return pl.pallas_call(
        functools.partial(returned_kernel, count),
        in_specs=[scalar_spec()] + [vmem] * (1 + len(parts)),
        out_specs=vmem,
        out_shape=shape((2 * rows, width), F32),
        compiler_params=params(),
        cost_estimate=pl.CostEstimate(
            flops=4 * rows * rows * len(parts) * width,
            bytes_accessed=2 * rows * width * len(parts) + 8 * rows * width,
            transcendentals=0,
        ),
    )(where, order, *parts)


def unpack_kernel(count, row_count, key_width, *refs):
    where, mine, theirs, query, key, value, extra, whole = refs
    half = mine.shape[1]
    core = where[1]
    for c in range(2):

        @pl.when(core == c)
        def _():
            whole[:, c * half : (c + 1) * half, :] = mine[...]
            whole[:, (1 - c) * half : (2 - c) * half, :] = theirs[...]

    for out, at in ((query, 0), (key, key_width), (value, 2 * key_width)):
        size = out.shape[1] // count
        for s in range(count):
            rows = whole[s, :row_count, at : at + size]
            out[:, s * size : (s + 1) * size] = rows.astype(F32)
    extra[...] = whole[:, row_count:, :].astype(F32)


def unpack(where, parts, row_count, key_width, val_width):
    count, half, width = parts[0].shape
    vmem = pl.BlockSpec(memory_space=pltpu.VMEM)
    return pl.pallas_call(
        functools.partial(unpack_kernel, count, row_count, key_width),
        in_specs=[scalar_spec()] + [vmem] * 2,
        out_specs=[vmem] * 4,
        out_shape=[
            shape((row_count, count * key_width), F32),
            shape((row_count, count * key_width), F32),
            shape((row_count, count * val_width), F32),
            shape((count, EXTRA, width), F32),
        ],
        scratch_shapes=[pltpu.VMEM((count, 2 * half, width), BF16)],
        compiler_params=params(),
    )(where, *parts)


class Exchange:
    def __init__(self):
        self.new = {}


def pin_all(exchanges, *arrays):
    keys = [sorted(e.new) for e in exchanges]
    out = pin(*arrays, *[e.new[k] for e, ks in zip(exchanges, keys) for k in ks])
    at = len(arrays)
    for e, ks in zip(exchanges, keys):
        e.new = dict(zip(ks, out[at : at + len(ks)]))
        at += len(ks)
    return out[: len(arrays)]


def pin_after(exchanges, *arrays):
    pin_all(exchanges, *arrays)


class Gather(Exchange):
    def __init__(self, part, order, count):
        super().__init__()
        self.have, self.order, self.count, self.last = {0: part}, order, count, [0]

    def take(self):
        self.have.update(self.new)
        self.new = {}

    def send(self):
        self.take()
        new = {}
        for m in self.last:
            used = [k for k, bit in enumerate(self.order) if m & bit]
            for bit in self.order[max(used, default=-1) + 1 :]:
                new[m | bit] = swap(self.have[m], bit, self.count)
        self.new, self.last = new, sorted(new)


class Scatter(Exchange):
    def __init__(self, blocks, order, count):
        super().__init__()
        self.have, self.order, self.count, self.step = dict(enumerate(blocks)), order, count, 0

    def take(self):
        if self.new:
            bit = self.order[self.step - 1]
            self.have = {
                m: self.have[m].astype(F32) + self.new[m | bit].astype(F32)
                for m in self.have
                if not m & bit
            }
            self.new = {}

    def send(self):
        self.take()
        bit = self.order[self.step]
        self.new = {
            m: swap(self.have[m].astype(BF16), bit, self.count)
            for m in sorted(self.have, reverse=True)
            if m & bit
        }
        self.step += 1

    def rest(self):
        while self.step < len(self.order):
            self.send()
        self.take()
        return self.have[0]


class CubeSum(Exchange):
    def __init__(self, piece, count):
        super().__init__()
        self.total, self.step = piece, 0
        self.count, self.bits = count, count.bit_length() - 1

    def swap(self, array, bit):
        return lax.ppermute(array, "wz", [(i, i ^ bit) for i in range(self.count)])

    def mine(self, bit):
        return jnp.where(lax.axis_index("wz") & bit, 1, 0)

    def take(self):
        if self.new:
            came, at = self.new[0], self.step - 1
            if at < self.bits:
                half = came.shape[0]
                kept = lax.dynamic_slice_in_dim(self.total, self.mine(1 << at) * half, half, 0)
                self.total = (kept.astype(F32) + came.astype(F32)).astype(BF16)
            else:
                upper = self.mine(1 << (2 * self.bits - 1 - at)) == 1
                self.total = jnp.concatenate(
                    [jnp.where(upper, came, self.total), jnp.where(upper, self.total, came)], axis=0
                )
            self.new = {}

    def send(self):
        self.take()
        if self.step >= 2 * self.bits:
            return
        if self.step < self.bits:
            bit = 1 << self.step
            half = self.total.shape[0] // 2
            away = lax.dynamic_slice_in_dim(self.total, (1 - self.mine(bit)) * half, half, 0)
            self.new = {0: self.swap(away.astype(BF16), bit)}
        else:
            self.new = {0: self.swap(self.total, 1 << (2 * self.bits - 1 - self.step))}
        self.step += 1

    def rest(self):
        while self.step < 2 * self.bits:
            self.send()
        self.take()
        return self.total.astype(BF16)


class OtherCore(Exchange):
    def __init__(self, array):
        super().__init__()
        self.new = {0: other_core(array)}


def split_columns(blocks, count):
    half = blocks[0].shape[1] // 2
    return [
        Scatter([block[:, k * half : (k + 1) * half] for block in blocks], order, count)
        for k, order in enumerate(bit_orders(count))
    ]


def other_core(array):
    return lax.ppermute(array, "core", [(0, 1), (1, 0)])


def shards(
    seq_count,
    wz_count,
    inputs,
    bin_order,
    first_gain,
    first_shift,
    query_weight,
    key_weight,
    value_weight,
    bias_content,
    bias_position,
    relative_weight,
    out_weight,
    bias_out,
    second_gain,
    second_shift,
    inner_weight,
    bias_inner,
    outer_weight,
    bias_outer,
    grad_output,
):
    row_count, width = inputs.shape[1:]
    length = bin_order.shape[1]
    here = lax.axis_index("seq")
    core = lax.axis_index("core")
    where = jnp.stack([here, core]).astype(jnp.int32)
    row_start = here * row_count
    key_width = query_weight.shape[1] // seq_count
    val_width = value_weight.shape[1] // seq_count
    heads_width = 2 * key_width + val_width
    up, down = bit_orders(seq_count)

    others = [jnp.bitwise_xor(here, m) for m in range(seq_count)]
    along = jnp.concatenate(
        [other * row_count + jnp.arange(row_count, dtype=jnp.int32) for other in others]
    )

    def natural(rows):
        parts = rows.reshape(seq_count, row_count, -1)
        parts = [lax.dynamic_index_in_dim(parts, other, 0) for other in others]
        return jnp.concatenate(parts, axis=0).reshape(rows.shape)

    def halves(rows):
        half = rows.shape[0] // 2
        return [Gather(rows[:half], up, seq_count), Gather(rows[half:], down, seq_count)]

    def blocks_of(gathers):
        for g in gathers:
            g.take()
        return [g.have[m] for m in range(seq_count) for g in gathers]

    window_gathers = halves(inputs[0])
    for g in window_gathers:
        g.send()

    def by_head(weight):
        return weight.reshape(weight.shape[0], seq_count, -1)

    vectors = jnp.stack([first_gain, first_shift, bias_out, second_gain, second_shift, bias_outer])
    vectors = jnp.concatenate([vectors, bias_inner.reshape(2, row_count)], axis=0)
    vectors = jnp.pad(vectors, ((0, EXTRA - 8), (0, 0)))
    rel_rows = relative_weight.shape[0]
    rel_blocks = -(-rel_rows // EXTRA)
    rel_part = jnp.pad(by_head(relative_weight), ((0, rel_blocks * EXTRA - rel_rows), (0, 0), (0, 0)))
    rel_part = rel_part.reshape(rel_blocks, EXTRA, seq_count, key_width).transpose(2, 1, 0, 3)
    rel_part = rel_part.reshape(seq_count, EXTRA, -1)
    spare = heads_width - row_count - rel_part.shape[2]
    extra = jnp.concatenate(
        [
            jnp.broadcast_to(vectors[None], (seq_count,) + vectors.shape),
            jnp.pad(rel_part, ((0, 0), (0, 0), (0, spare))),
        ],
        axis=2,
    )
    mine = jnp.concatenate(
        [by_head(query_weight), by_head(key_weight), by_head(value_weight)], axis=2
    ).transpose(1, 0, 2)
    mine = jnp.concatenate([mine, extra], axis=1)
    half = mine.shape[1] // 2
    mine = lax.dynamic_slice_in_dim(mine, core * half, half, 1)
    (mine,) = pin_all(window_gathers, mine)
    for step in range(1, len(up)):
        for g in window_gathers:
            g.send()
    mine = lax.all_to_all(mine, "seq", 0, 0, tiled=True)
    (mine,) = pin_all(window_gathers, mine)
    first = core == 0
    theirs = other_core(mine)
    attention_weight = jnp.concatenate(
        [jnp.where(first, mine, theirs), jnp.where(first, theirs, mine)], axis=1
    )
    table, table_back = basis_tables(jnp.asarray(basis_constants(length)), length)
    flat = attention_weight[:, row_count:]
    vectors = flat[:, :8, :row_count].astype(F32)
    inner_bias = vectors[:, 6:8].reshape(1, -1)
    vectors = vectors.transpose(1, 0, 2).reshape(8, width)
    rel = flat[:, :, row_count : row_count + rel_blocks * key_width]
    rel = rel.reshape(seq_count, EXTRA, rel_blocks, key_width).transpose(0, 2, 1, 3)
    rel = rel.reshape(seq_count, rel_blocks * EXTRA, key_width)[:, :rel_rows].reshape(REL, key_width)

    def own_half(weight):
        half = weight.shape[0] // 2
        return lax.dynamic_slice_in_dim(weight, core * half, half, 0)

    inner_part, outer_part = own_half(inner_weight), own_half(outer_weight)
    inner_part, outer_part = pin_all(window_gathers, inner_part, outer_part)
    window_blocks = blocks_of(window_gathers)
    weight_gathers = [
        Gather(inner_part, up, seq_count),
        Gather(outer_part, down, seq_count),
    ]
    for g in weight_gathers:
        g.send()

    order = bin_order[0]
    placing = (order[:, None] == along[None, :]).astype(BF16)
    bias = jnp.concatenate([bias_content, bias_position])[None].astype(F32)
    window, hidden_one, in_bins, weight_whole = project(
        window_blocks, attention_weight, vectors, bias, row_count
    )
    placed_heads = matmul(placing, in_bins).astype(BF16)
    mixed, probs = attend(placed_heads, rel, table)
    (mixed,) = pin_all(weight_gathers, mixed)
    for step in range(1, len(up)):
        for g in weight_gathers:
            g.send()
    weight_parts = []
    for g, own in zip(weight_gathers, (inner_weight, outer_weight)):
        g.take()
        parts = [own]
        for m in range(1, seq_count):
            parts += [g.have[m], other_core(g.have[m])]
        weight_parts.append(parts)
    mixed_along = natural(mixed).reshape(seq_count, row_count, val_width)
    attended = [matmul(mixed_along[m], out_weight).astype(BF16) for m in range(seq_count)]
    attended = split_columns(attended, seq_count)
    for g in attended:
        g.send()
    own_order = lax.dynamic_slice_in_dim(order, row_start, row_count, 0)
    placed = matmul((own_order[:, None] == along[None, :]).astype(BF16), window)
    (placed,) = pin_all(attended, placed)
    attended = [g.rest() for g in attended]

    grad_rows = grad_output[0]
    layer_output, d_mixed_in, hidden_two, activated, d_inner, sums, inner_sums = feed_forward(
        where, placed, attended, grad_rows, vectors, inner_bias, *weight_parts
    )

    d_mixed_gathers = halves(d_mixed_in)
    for g in d_mixed_gathers:
        g.send()
    away = ff_gradients(seq_count, where, hidden_two, activated, d_inner, grad_rows)
    pin_after(d_mixed_gathers, *away)
    for step in range(1, len(up)):
        for g in d_mixed_gathers:
            g.send()
    came = [other_core(part) for part in away]
    kept = ff_gradients(seq_count, where, hidden_two, activated, d_inner, grad_rows, came)
    kept = pin_all(d_mixed_gathers, *kept)
    d_mixed_blocks = blocks_of(d_mixed_gathers)
    count = seq_count
    inner_sums_of, outer_sums_of = [
        [
            Scatter([kept[2 * (k * count + m) + side] for m in range(count)], bits, count)
            for side, bits in enumerate((up, down))
        ]
        for k in range(2)
    ]
    for g in inner_sums_of:
        g.send()

    d_attended, out_away, grad_out_w = mixed_back(
        seq_count, where, mixed, out_weight, d_mixed_blocks
    )
    out_core = OtherCore(out_away)

    def send_all(exchanges):
        for exchange in exchanges:
            exchange.send()

    def scatter_windows(piece):
        return lax.psum_scatter(piece.astype(BF16), "wz", scatter_dimension=0, tiled=True)

    def gather_windows(piece):
        return lax.all_gather(piece, ("core", "wz"), axis=0, tiled=True)

    def joined_sum(scatters):
        return jnp.concatenate([g.rest().astype(BF16) for g in scatters], axis=1)

    (d_attended,) = pin_all([out_core], d_attended)
    out_sum = scatter_windows(grad_out_w + out_core.new[0].astype(F32))
    back = attend_back(0, placed_heads, rel, table_back, mixed, d_attended, probs)
    back = pin_all(inner_sums_of, *back)
    for step in range(1, len(up)):
        send_all(inner_sums_of)
    send_all(outer_sums_of)
    for head in range(1, key_width // KEY):
        back = attend_back(head, placed_heads, rel, table_back, mixed, d_attended, probs, back)
    *back, out_sum = pin_all(inner_sums_of, *back, out_sum)
    d_heads, d_rel, d_bias = back
    inner_sum = scatter_windows(joined_sum(inner_sums_of))
    out_sum = gather_windows(out_sum)
    d_along, *d_normed, first_sums = rows_back(
        seq_count, where, order[None], d_heads, window, weight_whole
    )
    out = pin_all(outer_sums_of, d_along, *d_normed)
    d_along, d_normed = out[0], out[1:]
    for step in range(1, len(up)):
        send_all(outer_sums_of)
    arrived = [
        Scatter([d_normed[2 * m + side] for m in range(count)], bits, count)
        for side, bits in enumerate((up, down))
    ]
    results = pack(
        seq_count, where, hidden_one, d_along, first_sums, sums, inner_sums, d_bias, d_rel
    )
    *results, inner_sum = pin_all(outer_sums_of, *results, inner_sum)
    packed_core = OtherCore(results[1])
    outer_sum = scatter_windows(joined_sum(outer_sums_of))
    inner_sum = gather_windows(inner_sum)
    (packed,) = pin_all([packed_core], results[0])
    packed = (packed.astype(F32) + packed_core.new[0].astype(F32)).astype(BF16)
    packed_shape = packed.shape
    packed = lax.all_to_all(packed, "seq", 0, 0, tiled=True)
    send_all(arrived)
    (packed,) = pin(packed)
    packed_cube = CubeSum(packed.reshape(-1, packed_shape[2]), wz_count)
    packed_cube.send()
    *d_mixed_blocks, outer_sum = pin_all(arrived, *d_mixed_blocks, outer_sum)
    for step in range(1, len(up)):
        send_all(arrived)
    outer_sum = gather_windows(outer_sum)
    returned = returned_rows(
        seq_count, where, order.reshape(2 * seq_count, row_count // 2), d_mixed_blocks
    )
    (returned,) = pin_all([packed_cube] + arrived, returned)
    packed_cube.send()
    own_unit, own_scale = norm_of(inputs[0].astype(F32))
    arrived = jnp.concatenate([g.rest() for g in arrived], axis=1)
    grad_inputs = norm_back(own_unit, own_scale, vectors[0:1], arrived) + returned

    def both_halves(pieces, axis):
        half = pieces.shape[0] // 2
        return jnp.concatenate([pieces[:half], pieces[half:]], axis=axis).astype(F32)

    grad_out_w = both_halves(out_sum, 0)
    grad_inputs, grad_out_w = pin_all([packed_cube], grad_inputs, grad_out_w)
    packed_cube.send()
    grad_inner_w = both_halves(inner_sum, 1)
    (grad_inner_w,) = pin_all([packed_cube], grad_inner_w)
    grad_outer_w = both_halves(outer_sum, 0)
    packed = packed_cube.rest().reshape(packed_shape)
    grad_query_w, grad_key_w, grad_value_w, flat = unpack(
        where, (packed, other_core(packed)), row_count, key_width, val_width
    )
    small = jnp.sum(flat[:, :16, :row_count], axis=0)
    g_gain_one, g_shift_one, g_out_b, g_gain_two, g_shift_two, g_outer_b = small[:6]
    g_inner_b = small[6:8].reshape(-1)
    grad_rel = flat[:, :, row_count : row_count + rel_blocks * key_width]
    grad_rel = grad_rel.reshape(seq_count, EXTRA, rel_blocks, key_width).transpose(2, 1, 0, 3)
    grad_rel = grad_rel.reshape(rel_blocks * EXTRA, -1)[:rel_rows]
    return (
        layer_output[None],
        grad_inputs[None],
        g_gain_one,
        g_shift_one,
        grad_query_w,
        grad_key_w,
        grad_value_w,
        small[8, :key_width],
        small[9, :key_width],
        grad_rel,
        grad_out_w,
        g_out_b,
        g_gain_two,
        g_shift_two,
        grad_inner_w,
        g_inner_b,
        grad_outer_w,
        g_outer_b,
    )


def solution(mesh):
    seq_count = mesh.shape["seq"]
    devices = mesh.devices.reshape(seq_count, -1, 2)
    split_mesh = Mesh(devices, ("seq", "wz", "core"))
    rows = P(("wz", "core"), "seq", None)
    vector = P("seq")
    matrix = P("seq", None)
    weights = (
        vector,
        vector,
        matrix,
        matrix,
        matrix,
        vector,
        vector,
        matrix,
        matrix,
        vector,
        vector,
        vector,
        matrix,
        vector,
        matrix,
        vector,
    )
    return jax.shard_map(
        functools.partial(shards, seq_count, mesh.shape["win"] // 2),
        mesh=split_mesh,
        in_specs=(rows, P(("wz", "core"), None)) + weights + (rows,),
        out_specs=(rows, rows) + weights,
        check_vma=False,
    )
```

```python
import functools
import math

import jax
import jax.numpy as jnp
import numpy as np
from jax import lax
from jax.experimental import pallas as pl
from jax.experimental.pallas import tpu as pltpu
from jax.sharding import Mesh
from jax.sharding import PartitionSpec as P

HEADS = 8
KEY = 64
VAL = 192
REL = 192
BF16 = jnp.bfloat16
F32 = jnp.float32
VMEM_LIMIT = 56 * 2**20
EXTRA = 32


def matmul(a, b):
    return lax.dot_general(a, b, (((1,), (0,)), ((), ())), preferred_element_type=F32)


def matmul_nt(a, b):
    return lax.dot_general(a, b, (((1,), (1,)), ((), ())), preferred_element_type=F32)


def matmul_tn(a, b):
    return lax.dot_general(a, b, (((0,), (0,)), ((), ())), preferred_element_type=F32)


def head_part(rows, head):
    lanes = lax.broadcasted_iota(jnp.int32, rows.shape, 1)
    inside = (lanes >= head * KEY) & (lanes < (head + 1) * KEY)
    return jnp.where(inside, rows, jnp.zeros_like(rows))


def head_columns(key_width):
    return [slice(k * key_width, (k + 1) * key_width) for k in range(3)]


def attend_kernel(heads, rows, placed, rel, table, mixed, probs):
    length = placed.shape[0]
    key_width = heads * KEY
    content_at, position_at, keys_at = head_columns(key_width)
    first = pl.program_id(0) * rows
    here = pl.ds(pl.multiple_of(first, rows), rows)
    basis = table[:, pl.ds(pl.multiple_of(length - rows - first, rows), length + rows)]
    content, position, keys = placed[here, content_at], placed[here, position_at], placed[:, keys_at]
    parts = []
    for head in range(heads):
        q_basis = matmul_nt(head_part(position, head), rel[...]).astype(BF16)
        grid = matmul(q_basis, basis)
        shifted = pltpu.roll(grid, 0, 1, stride=1, stride_axis=0)[:, rows:]
        scores = matmul_nt(head_part(content, head), keys) + shifted
        top = jnp.max(scores, axis=1, keepdims=True)
        weights = jnp.exp(scores - top)
        total = jnp.sum(weights, axis=1, keepdims=True)
        prob = (weights * (1.0 / total)).astype(BF16)
        probs[head] = prob
        values_at = 3 * key_width + head * VAL
        parts.append(matmul(prob, placed[:, values_at : values_at + VAL]))
    mixed[...] = jnp.concatenate(parts, axis=1).astype(BF16)


def attend(placed, rel, table):
    length = placed.shape[0]
    heads = rel.shape[1] // KEY
    rows = math.gcd(256, length)
    whole = lambda array: pl.BlockSpec(array.shape, lambda i: (0, 0))
    return pl.pallas_call(
        functools.partial(attend_kernel, heads, rows),
        grid=(length // rows,),
        in_specs=[whole(placed), whole(rel), whole(table)],
        out_specs=[
            pl.BlockSpec((rows, heads * VAL), lambda i: (i, 0)),
            pl.BlockSpec((heads, rows, length), lambda i: (0, i, 0)),
        ],
        out_shape=[
            jax.ShapeDtypeStruct((length, heads * VAL), BF16),
            jax.ShapeDtypeStruct((heads, length, length), BF16),
        ],
        compiler_params=pltpu.CompilerParams(vmem_limit_bytes=VMEM_LIMIT),
        cost_estimate=pl.CostEstimate(
            flops=2 * heads * length * length * 1024,
            bytes_accessed=2 * heads * length * length + 8 * length * heads * VAL,
            transcendentals=heads * length * length,
        ),
    )(placed, rel, table)


def attend_back_kernel(heads, head, rows, *refs):
    placed, rel, table, flip, mixed, d_mixed, probs = refs[:7]
    before = refs[7:-5]
    d_heads, d_rel, d_bias, keys_sum, values_sum = refs[-5:]
    length = placed.shape[0]
    key_width = heads * KEY
    content_at, position_at, keys_at = head_columns(key_width)
    step = pl.program_id(0)

    @pl.when(step == 0)
    def _():
        keys_sum[...] = jnp.zeros_like(keys_sum)
        values_sum[...] = jnp.zeros_like(values_sum)
        for k, out in enumerate((d_heads, d_rel, d_bias)):
            out[...] = before[k][...] if before else jnp.zeros_like(out)

    first = pl.multiple_of(step * rows, rows)
    here = pl.ds(first, rows)
    basis = table[:, pl.ds(first, length + rows)]
    content, position, keys = placed[here, content_at], placed[here, position_at], placed[:, keys_at]
    blocks = length // rows
    columns = slice(head * VAL, (head + 1) * VAL)
    values_at = 3 * key_width + head * VAL
    d_part = d_mixed[:, columns]
    delta = jnp.sum(d_part.astype(F32) * mixed[:, columns].astype(F32), axis=1, keepdims=True)
    prob = probs[0]
    values_sum[...] += matmul_tn(d_part, prob)
    d_prob = matmul_nt(d_part, placed[:, values_at : values_at + VAL])
    d_score = (prob.astype(F32) * (d_prob - delta)).astype(BF16)
    keys_sum[...] += matmul_tn(head_part(content, head), d_score)
    d_content = head_part(matmul(d_score, keys), head)
    turned = [
        matmul(d_score[:, (blocks - 1 - b) * rows : (blocks - b) * rows], flip[...])
        for b in range(blocks)
    ]
    turned = jnp.concatenate(turned + [jnp.zeros((rows, rows), F32)], axis=1)
    d_grid = pltpu.roll(turned, 0, 1, stride=1, stride_axis=0).astype(BF16)
    d_basis = matmul_nt(d_grid, basis).astype(BF16)
    d_position = head_part(matmul(d_basis, rel[...]), head)
    d_rel[...] += matmul_tn(d_basis, head_part(position, head))
    d_heads[here, :key_width] += ((d_content + d_position) * KEY ** (-0.5)).astype(BF16)
    d_bias[0:1, :] += jnp.sum(d_content, axis=0, keepdims=True)
    d_bias[1:2, :] += jnp.sum(d_position, axis=0, keepdims=True)

    @pl.when(step == blocks - 1)
    def _():
        d_heads[:, key_width : 2 * key_width] += keys_sum[...].T.astype(BF16)
        values_to = 2 * key_width + head * VAL
        d_heads[:, values_to : values_to + VAL] = values_sum[...].T.astype(BF16)


def attend_back(head, placed, rel, table, mixed, d_mixed, probs, before=()):
    length = placed.shape[0]
    key_width = rel.shape[1]
    heads = key_width // KEY
    val_width = heads * VAL
    rows = math.gcd(256, length)
    at = jnp.arange(rows)
    flip = (at[:, None] + at[None, :] == rows - 1).astype(BF16)
    block = lambda width: pl.BlockSpec((rows, width), lambda i: (i, 0))
    outs = [
        shape((length, 2 * key_width + val_width), BF16),
        shape((REL, key_width), F32),
        shape((8, key_width), F32),
    ]
    return pl.pallas_call(
        functools.partial(attend_back_kernel, heads, head, rows),
        grid=(length // rows,),
        in_specs=[
            whole_spec(placed),
            whole_spec(rel),
            whole_spec(table),
            whole_spec(flip),
            block(val_width),
            block(val_width),
            pl.BlockSpec((1, rows, length), lambda i: (head, i, 0)),
        ]
        + [whole_spec(array) for array in before],
        out_specs=[whole_spec(out) for out in outs],
        out_shape=outs,
        scratch_shapes=[
            pltpu.VMEM((key_width, length), F32),
            pltpu.VMEM((VAL, length), F32),
        ],
        compiler_params=pltpu.CompilerParams(vmem_limit_bytes=VMEM_LIMIT),
        cost_estimate=pl.CostEstimate(
            flops=2 * length * length * 1536,
            bytes_accessed=2 * length * length + 16 * length * val_width,
            transcendentals=0,
        ),
    )(placed, rel, table, flip, mixed, d_mixed, probs, *before)


def norm_back(unit, scale, gain, grad):
    scaled = grad * gain
    mean_one = jnp.mean(scaled, axis=-1, keepdims=True)
    mean_two = jnp.mean(scaled * unit, axis=-1, keepdims=True)
    return (scaled - mean_one - unit * mean_two) * scale


def whole_spec(array):
    zeros = (0,) * len(array.shape)
    return pl.BlockSpec(array.shape, lambda *_: zeros)


def scalar_spec():
    return pl.BlockSpec(memory_space=pltpu.SMEM)


def params(**more):
    return pltpu.CompilerParams(vmem_limit_bytes=VMEM_LIMIT, **more)


def shape(dims, dtype):
    return jax.ShapeDtypeStruct(tuple(dims), dtype)


def basis_constants(window_len):
    features = REL // 6
    f = np.arange(features, dtype=np.float64)
    half_life = 2.0 ** (3.0 + f * (math.log2(window_len) - 3.0) / (features - 1))
    spread = window_len / (2.0 * features)
    first = window_len / features
    centres = first + f * (window_len - first) / (features - 1)
    concentration = (centres / spread) ** 2
    rate = centres / spread**2
    offset = concentration * np.log(rate) - np.array([math.lgamma(c) for c in concentration])
    columns = [math.log(2.0) / half_life, 2.0 ** (f + 1) - 1.0, concentration - 1.0, rate, offset]
    columns += [np.zeros(features)] * 3
    return np.stack(columns, axis=1).astype(np.float32)


def table_kernel(length, constants, forth, back):
    features = REL // 6
    decay, inside_below, power, rate, offset = [constants[:, k : k + 1] for k in range(5)]

    def gamma(distance):
        logged = power * jnp.log(jnp.maximum(distance, 1.0)) - rate * distance + offset
        return jnp.where(distance == 0.0, 0.0, jnp.exp(logged)) + 1e-08

    every = lax.broadcasted_iota(jnp.int32, (1, length), 1).astype(F32)
    peak = jnp.max(gamma(every), axis=1, keepdims=True)
    lanes = lax.broadcasted_iota(jnp.int32, (1, 2 * length), 1).astype(F32)
    for table, signed in ((forth, lanes - length), (back, length - 1 - lanes)):
        distance = jnp.abs(signed)
        sign = jnp.where(signed > 0, 1.0, jnp.where(signed < 0, -1.0, 0.0))
        parts = (
            jnp.exp(-decay * distance),
            jnp.where(inside_below > distance, 1.0, 0.0),
            gamma(distance) / peak,
        )
        for k, part in enumerate(parts):
            table[k * features : (k + 1) * features, :] = part.astype(BF16)
            table[(3 + k) * features : (4 + k) * features, :] = (sign * part).astype(BF16)


def basis_tables(constants, length):
    out = shape((REL, 2 * length), BF16)
    return pl.pallas_call(
        functools.partial(table_kernel, length),
        out_shape=[out, out],
        compiler_params=params(),
    )(constants)


def norm_of(rows):
    centre = rows - jnp.mean(rows, axis=1, keepdims=True)
    scale = lax.rsqrt(jnp.mean(centre * centre, axis=1, keepdims=True) + 1e-05)
    return centre * scale, scale


def project_kernel(blocks, row_count, *refs):
    parts, (weight, vectors, bias, window, hidden, heads, flat, block) = refs[:blocks], refs[blocks:]
    step = pl.program_id(0)

    @pl.when(step == 0)
    def _():
        for s in range(weight.shape[0]):
            flat[s * row_count : (s + 1) * row_count, :] = weight[s, :row_count, :]

    for k in range(blocks):

        @pl.when(step == k)
        def _():
            block[...] = parts[k][...]

    window[...] = block[...]
    unit, _ = norm_of(block[...].astype(F32))
    normed = (unit * vectors[0:1, :] + vectors[1:2, :]).astype(BF16)
    hidden[...] = normed
    total = matmul(normed, flat[...])
    key_width = bias.shape[1] // 2
    query = total[:, :key_width] * KEY ** (-0.5)
    heads[:, :key_width] = (query + bias[0:1, :key_width]).astype(BF16)
    heads[:, key_width : 2 * key_width] = (query + bias[0:1, key_width:]).astype(BF16)
    heads[:, 2 * key_width :] = total[:, key_width:].astype(BF16)


def project(parts, weight, vectors, bias, row_count):
    blocks = len(parts)
    rows, width = parts[0].shape
    heads_width = weight.shape[2] + bias.shape[1] // 2
    out = lambda w: pl.BlockSpec((rows, w), lambda i: (i, 0))
    return pl.pallas_call(
        functools.partial(project_kernel, blocks, row_count),
        grid=(blocks,),
        in_specs=[whole_spec(a) for a in (*parts, weight, vectors, bias)],
        out_specs=[
            out(width),
            out(width),
            out(heads_width),
            pl.BlockSpec((width, weight.shape[2]), lambda i: (0, 0)),
        ],
        out_shape=[shape((blocks * rows, w), BF16) for w in (width, width, heads_width)]
        + [shape((width, weight.shape[2]), BF16)],
        scratch_shapes=[pltpu.VMEM((rows, width), BF16)],
        compiler_params=params(),
        cost_estimate=pl.CostEstimate(
            flops=2 * blocks * rows * width * heads_width,
            bytes_accessed=8 * blocks * rows * width,
            transcendentals=0,
        ),
    )(*parts, weight, vectors, bias)


def feed_kernel(count, chunk, *refs):
    parts = 2 * (2 * count - 1)
    where, placed, attended_a, attended_b, grad_rows, vectors, inner_bias = refs[:7]
    weights = refs[7 : 7 + parts]
    layer_output, d_mixed, hidden, activated, d_inner, sums, inner_sums = refs[7 + parts : 14 + parts]
    inner_whole, outer_whole, residual, unit, back, outer_sum, sems = refs[14 + parts :]
    here, core = where[0], where[1]
    copies = []
    for k, whole in enumerate((inner_whole, outer_whole)):
        mine = weights[k * (2 * count - 1) : (k + 1) * (2 * count - 1)]
        size = whole.shape[0] // count
        half = size // 2
        moves = [(mine[0], here * size, size)]
        for m in range(1, count):
            start = jnp.bitwise_xor(here, m) * size
            moves.append((mine[2 * m - 1], start + core * half, half))
            moves.append((mine[2 * m], start + (1 - core) * half, half))
        started = []
        for source, start, rows in moves:
            target = whole.at[pl.ds(pl.multiple_of(start, 16), rows), :]
            copy = pltpu.make_async_copy(source, target, sems.at[k, len(started)])
            copy.start()
            started.append(copy)
        copies.append(started)
    rows, width = placed.shape
    half = width // 2
    residual[:, :half] = placed[:, :half] + attended_a[...] + vectors[2:3, :half]
    residual[:, half:] = placed[:, half:] + attended_b[...] + vectors[2:3, half:]
    normed, scale = norm_of(residual[...])
    unit[...] = normed
    hidden[...] = (normed * vectors[3:4, :] + vectors[4:5, :]).astype(BF16)
    for started in copies:
        for copy in started:
            copy.wait()
    ff = outer_whole.shape[0]
    for c in range(ff // chunk):
        at = slice(c * chunk, (c + 1) * chunk)
        inner = matmul(hidden[...], inner_whole[:, at]) + inner_bias[0:1, at]
        below = 0.5 * (1.0 + lax.erf(inner * (0.5**0.5)))
        slope = below + inner * jnp.exp(-0.5 * inner * inner) * (0.5 / math.pi) ** 0.5
        active = (inner * below).astype(BF16)
        activated[:, at] = active
        grad = (matmul_nt(grad_rows[...], outer_whole[at, :]) * slope).astype(BF16)
        d_inner[:, at] = grad
        inner_sums[:, at] = jnp.sum(grad.astype(F32), axis=0, keepdims=True)
        back_term = matmul_nt(grad, inner_whole[:, at])
        outer_term = matmul(active, outer_whole[at, :])
        if c == 0:
            back[...] = back_term
            outer_sum[...] = outer_term
        else:
            back[...] += back_term
            outer_sum[...] += outer_term
    layer_output[...] = (residual[...] + outer_sum[...] + vectors[5:6, :]).astype(BF16)
    grad, normed = back[...], unit[...]
    dy = grad_rows[...].astype(F32)
    scaled = grad * vectors[3:4, :]
    mean_one = jnp.mean(scaled, axis=1, keepdims=True)
    mean_two = jnp.mean(scaled * normed, axis=1, keepdims=True)
    mixed_in = (dy + (scaled - mean_one - normed * mean_two) * scale).astype(BF16)
    d_mixed[...] = mixed_in
    sums[...] = jnp.zeros_like(sums)
    sums[2:3, :] = jnp.sum(mixed_in.astype(F32), axis=0, keepdims=True)
    sums[3:4, :] = jnp.sum(grad * normed, axis=0, keepdims=True)
    sums[4:5, :] = jnp.sum(grad, axis=0, keepdims=True)
    sums[5:6, :] = jnp.sum(dy, axis=0, keepdims=True)


def feed_forward(where, placed, attended, grad_rows, vectors, inner_bias, inner_parts, outer_parts):
    rows, width = placed.shape
    ff = inner_bias.shape[1]
    count = (len(inner_parts) + 1) // 2
    chunk = math.gcd(512, ff)
    weights = (*inner_parts, *outer_parts)
    small = (placed, *attended, grad_rows, vectors, inner_bias)
    outs = [
        shape((rows, width), BF16),
        shape((rows, width), BF16),
        shape((rows, width), BF16),
        shape((rows, ff), BF16),
        shape((rows, ff), BF16),
        shape((8, width), F32),
        shape((1, ff), F32),
    ]
    return pl.pallas_call(
        functools.partial(feed_kernel, count, chunk),
        in_specs=[scalar_spec()]
        + [pl.BlockSpec(memory_space=pltpu.VMEM) for _ in small]
        + [pl.BlockSpec(memory_space=pl.ANY) for _ in weights],
        out_specs=[pl.BlockSpec(memory_space=pltpu.VMEM) for _ in outs],
        out_shape=outs,
        scratch_shapes=[
            pltpu.VMEM((width, ff), BF16),
            pltpu.VMEM((ff, width), BF16),
            pltpu.VMEM((rows, width), F32),
            pltpu.VMEM((rows, width), F32),
            pltpu.VMEM((rows, width), F32),
            pltpu.VMEM((rows, width), F32),
            pltpu.SemaphoreType.DMA((2, 2 * count - 1)),
        ],
        compiler_params=params(),
        cost_estimate=pl.CostEstimate(
            flops=8 * rows * width * ff,
            bytes_accessed=4 * width * ff + 40 * rows * width,
            transcendentals=2 * rows * ff,
        ),
    )(where, *small, *weights)


def columns_at(ref, index, size, scratch):
    if size % 128 == 0:
        return ref[:, pl.ds(pl.multiple_of(index * size, 128), size)]
    for k in range(ref.shape[1] // size):

        @pl.when(index == k)
        def _():
            scratch[...] = ref[:, k * size : (k + 1) * size]

    return scratch[...]


def half_kernel(count, split, away, where, left, right, *refs):
    here, core = where[0], where[1]
    side = 1 - core if away else core
    shard = jnp.bitwise_xor(here, pl.program_id(0))
    if split:
        some = columns_at(left, shard, left.shape[1] // count, refs[-1])
        half = right.shape[1] // 2
        other = right[:, pl.ds(pl.multiple_of(side * half, 128), half)]
    else:
        some = columns_at(left, 2 * shard + side, left.shape[1] // count // 2, refs[-1])
        other = right[...]
    result = matmul_tn(some, other)
    if away:
        refs[0][0] = result.astype(BF16)
        return
    came, outs = refs[0], refs[1:-1]
    result += came[0].astype(F32)
    width = result.shape[1] // 2
    for m in range(count):

        @pl.when(pl.program_id(0) == m)
        def _():
            outs[2 * m][...] = result[:, :width].astype(BF16)
            outs[2 * m + 1][...] = result[:, width:].astype(BF16)


def half_gradient(count, split, where, left, right, came=None):
    away = came is None
    rows = left.shape[1] // count // (1 if split else 2)
    width = right.shape[1] // (2 if split else 1)
    block = pl.BlockSpec((1, rows, width), lambda i: (i, 0, 0))
    if away:
        outs, out_specs = shape((count, rows, width), BF16), block
    else:
        outs = [shape((rows, width // 2), BF16) for _ in range(2 * count)]
        out_specs = [whole_spec(out) for out in outs]
    return pl.pallas_call(
        functools.partial(half_kernel, count, split, away),
        grid=(count,),
        in_specs=[scalar_spec(), whole_spec(left), whole_spec(right)] + ([] if away else [block]),
        out_specs=out_specs,
        out_shape=outs,
        scratch_shapes=[pltpu.VMEM((left.shape[0], rows), BF16)],
        compiler_params=params(),
        cost_estimate=pl.CostEstimate(
            flops=2 * left.shape[0] * count * rows * width,
            bytes_accessed=4 * count * rows * width + 4 * left.shape[0] * left.shape[1],
            transcendentals=0,
        ),
    )(where, left, right, *(() if away else (came,)))


def mixed_back_kernel(count, parts_count, *refs):
    where, mixed, weight = refs[:3]
    parts = refs[3 : 3 + parts_count]
    d_attended, out_away, out_kept, out_sum = refs[3 + parts_count :]
    here, core = where[0], where[1]
    rows = parts[0].shape[0]
    for k, part in enumerate(parts):
        start = jnp.bitwise_xor(here, k // 2) * (2 * rows) + (k % 2) * rows
        at = pl.ds(pl.multiple_of(start, 32), rows)
        d_attended[at, :] = matmul_nt(part[...], weight[...]).astype(BF16)
        term = matmul_tn(mixed[at, :], part[...])
        if k == 0:
            out_sum[...] = term
        else:
            out_sum[...] += term
    half = out_kept.shape[0]
    out_kept[...] = out_sum[pl.ds(pl.multiple_of(core * half, 32), half), :]
    out_away[...] = out_sum[pl.ds(pl.multiple_of((1 - core) * half, 32), half), :].astype(BF16)


def mixed_back(count, where, mixed, weight, parts):
    length, val_width = mixed.shape
    width = weight.shape[1]
    vmem = pl.BlockSpec(memory_space=pltpu.VMEM)
    return pl.pallas_call(
        functools.partial(mixed_back_kernel, count, len(parts)),
        in_specs=[scalar_spec()] + [vmem] * (2 + len(parts)),
        out_specs=[vmem] * 3,
        out_shape=[
            shape((length, val_width), BF16),
            shape((val_width // 2, width), BF16),
            shape((val_width // 2, width), F32),
        ],
        scratch_shapes=[pltpu.VMEM((val_width, width), F32)],
        compiler_params=params(),
        cost_estimate=pl.CostEstimate(
            flops=4 * length * val_width * width,
            bytes_accessed=2 * length * (width + 2 * val_width),
            transcendentals=0,
        ),
    )(where, mixed, weight, *parts)


def rows_back_kernel(count, where, order, d_heads, window, weight, d_along, *refs):
    d_normed, first_sums = refs[:-1], refs[-1]
    here = where[0]
    step = pl.program_id(0)
    rows, width = window.shape
    length = order.shape[1]
    bins = lax.broadcasted_iota(jnp.int32, (rows, length), 0) + jnp.bitwise_xor(here, step) * rows
    picks = jnp.where(order[0:1, :] == bins, 1.0, 0.0).astype(BF16)
    along = matmul(picks, d_heads[...]).astype(BF16)
    d_along[...] = along
    unit, _ = norm_of(window[...].astype(F32))
    normed = matmul_nt(along, weight[...])

    @pl.when(step == 0)
    def _():
        first_sums[...] = jnp.zeros_like(first_sums)

    first_sums[0:1, :] += jnp.sum(normed * unit, axis=0, keepdims=True)
    first_sums[1:2, :] += jnp.sum(normed, axis=0, keepdims=True)
    half = width // 2
    for m in range(count):

        @pl.when(step == m)
        def _():
            d_normed[2 * m][...] = normed[:, :half].astype(BF16)
            d_normed[2 * m + 1][...] = normed[:, half:].astype(BF16)


def rows_back(count, where, order, d_heads, window, weight):
    length, width = window.shape
    rows = length // count
    heads_width = d_heads.shape[1]
    outs = [shape((length, heads_width), BF16)]
    outs += [shape((rows, width // 2), BF16) for _ in range(2 * count)]
    outs += [shape((8, width), F32)]
    return pl.pallas_call(
        functools.partial(rows_back_kernel, count),
        grid=(count,),
        in_specs=[
            scalar_spec(),
            whole_spec(order),
            whole_spec(d_heads),
            pl.BlockSpec((rows, width), lambda i: (i, 0)),
            whole_spec(weight),
        ],
        out_specs=[pl.BlockSpec((rows, heads_width), lambda i: (i, 0))]
        + [whole_spec(out) for out in outs[1:]],
        out_shape=outs,
        compiler_params=params(),
        cost_estimate=pl.CostEstimate(
            flops=2 * length * heads_width * (length + width),
            bytes_accessed=4 * length * (width + heads_width),
            transcendentals=0,
        ),
    )(where, order, d_heads, window, weight)


def pack_kernel(
    count, where, hidden, d_along, first_sums, sums, inner_sums, d_bias, d_rel, kept, away, grads
):
    here, core = where[0], where[1]
    step = pl.program_id(0)
    row_count = hidden.shape[1] // count
    key_width = d_rel.shape[1]
    terms = matmul_tn(hidden[...], d_along[...])

    @pl.when(step == 0)
    def _():
        for s in range(count):
            grads[s, :row_count, :] = terms[s * row_count : (s + 1) * row_count, :]

    @pl.when(step > 0)
    def _():
        for s in range(count):
            grads[s, :row_count, :] += terms[s * row_count : (s + 1) * row_count, :]

    @pl.when(step == pl.num_programs(0) - 1)
    def _():
        rel_rows = d_rel.shape[0] // count
        for s in range(count):
            at = slice(s * row_count, (s + 1) * row_count)
            grads[s, row_count:, :] = jnp.zeros((EXTRA, grads.shape[2]), F32)
            grads[s, row_count : row_count + 2, :row_count] = first_sums[0:2, at]
            grads[s, row_count + 2 : row_count + 6, :row_count] = sums[2:6, at]
            for j in range(2):
                part = slice((2 * s + j) * row_count, (2 * s + j + 1) * row_count)
                grads[s, row_count + 6 + j : row_count + 7 + j, :row_count] = inner_sums[0:1, part]
            for j in range(-(-rel_rows // EXTRA)):
                some = d_rel[s * rel_rows + j * EXTRA : s * rel_rows + min(rel_rows, (j + 1) * EXTRA), :]
                lane = row_count + j * key_width
                grads[s, row_count : row_count + some.shape[0], lane : lane + key_width] = some
        for s in range(count):

            @pl.when(here == s)
            def _():
                grads[s, row_count + 8 : row_count + 10, :key_width] = d_bias[0:2, :]

        half = kept.shape[1]
        kept[...] = grads[:, pl.ds(pl.multiple_of(core * half, 16), half), :].astype(BF16)
        away[...] = grads[:, pl.ds(pl.multiple_of((1 - core) * half, 16), half), :].astype(BF16)


def pack(count, where, hidden, d_along, *small):
    length, width = hidden.shape
    heads_width = d_along.shape[1]
    rows = math.gcd(768, length)
    packed = (count, width // count + EXTRA, heads_width)
    outs = [shape((count, packed[1] // 2, heads_width), BF16) for _ in range(2)]
    return pl.pallas_call(
        functools.partial(pack_kernel, count),
        grid=(length // rows,),
        in_specs=[
            scalar_spec(),
            pl.BlockSpec((rows, width), lambda i: (i, 0)),
            pl.BlockSpec((rows, heads_width), lambda i: (i, 0)),
        ]
        + [whole_spec(a) for a in small],
        out_specs=[whole_spec(out) for out in outs],
        out_shape=outs,
        scratch_shapes=[pltpu.VMEM(packed, F32)],
        compiler_params=params(),
        cost_estimate=pl.CostEstimate(
            flops=2 * length * heads_width * width,
            bytes_accessed=2 * length * (width + heads_width) + 8 * width * heads_width,
            transcendentals=0,
        ),
    )(where, hidden, d_along, *small)


def swap(array, mask, count):
    return lax.ppermute(array, "seq", [(i, i ^ mask) for i in range(count)])


def bit_orders(count):
    bits = [1 << k for k in range(count.bit_length() - 1)]
    return bits, bits[::-1]


def pin(*arrays):
    return lax.optimization_barrier(arrays)


def returned_kernel(count, where, order, *refs):
    parts, returned = refs[:-1], refs[-1]
    here = where[0]
    rows = parts[0].shape[0]
    bins = lax.broadcasted_iota(jnp.int32, (returned.shape[0], rows), 0)
    bins = bins + here * returned.shape[0]
    for k, part in enumerate(parts):
        shard = jnp.bitwise_xor(here, k // 2)
        picks = jnp.where(order[pl.ds(2 * shard + k % 2, 1), :] == bins, 1.0, 0.0).astype(BF16)
        term = matmul(picks, part[...])
        if k == 0:
            returned[...] = term
        else:
            returned[...] += term


def returned_rows(count, where, order, parts):
    rows, width = parts[0].shape
    vmem = pl.BlockSpec(memory_space=pltpu.VMEM)
    return pl.pallas_call(
        functools.partial(returned_kernel, count),
        in_specs=[scalar_spec()] + [vmem] * (1 + len(parts)),
        out_specs=vmem,
        out_shape=shape((2 * rows, width), F32),
        compiler_params=params(),
        cost_estimate=pl.CostEstimate(
            flops=4 * rows * rows * len(parts) * width,
            bytes_accessed=2 * rows * width * len(parts) + 8 * rows * width,
            transcendentals=0,
        ),
    )(where, order, *parts)


def unpack_kernel(count, row_count, key_width, *refs):
    where, mine, theirs, query, key, value, extra, whole = refs
    half = mine.shape[1]
    core = where[1]
    for c in range(2):

        @pl.when(core == c)
        def _():
            whole[:, c * half : (c + 1) * half, :] = mine[...]
            whole[:, (1 - c) * half : (2 - c) * half, :] = theirs[...]

    for out, at in ((query, 0), (key, key_width), (value, 2 * key_width)):
        size = out.shape[1] // count
        for s in range(count):
            rows = whole[s, :row_count, at : at + size]
            out[:, s * size : (s + 1) * size] = rows.astype(F32)
    extra[...] = whole[:, row_count:, :].astype(F32)


def unpack(where, parts, row_count, key_width, val_width):
    count, half, width = parts[0].shape
    vmem = pl.BlockSpec(memory_space=pltpu.VMEM)
    return pl.pallas_call(
        functools.partial(unpack_kernel, count, row_count, key_width),
        in_specs=[scalar_spec()] + [vmem] * 2,
        out_specs=[vmem] * 4,
        out_shape=[
            shape((row_count, count * key_width), F32),
            shape((row_count, count * key_width), F32),
            shape((row_count, count * val_width), F32),
            shape((count, EXTRA, width), F32),
        ],
        scratch_shapes=[pltpu.VMEM((count, 2 * half, width), BF16)],
        compiler_params=params(),
    )(where, *parts)


class Exchange:
    def __init__(self):
        self.new = {}


def pin_all(exchanges, *arrays):
    keys = [sorted(e.new) for e in exchanges]
    out = pin(*arrays, *[e.new[k] for e, ks in zip(exchanges, keys) for k in ks])
    at = len(arrays)
    for e, ks in zip(exchanges, keys):
        e.new = dict(zip(ks, out[at : at + len(ks)]))
        at += len(ks)
    return out[: len(arrays)]


def pin_some(exchanges, *arrays):
    firsts = [max(e.new) for e in exchanges]
    out = pin(*arrays, *[e.new[k] for e, k in zip(exchanges, firsts)])
    for e, k, block in zip(exchanges, firsts, out[len(arrays) :]):
        e.new[k] = block
    return out[: len(arrays)]


class Gather(Exchange):
    def __init__(self, part, order, count):
        super().__init__()
        self.have, self.order, self.count, self.last = {0: part}, order, count, [0]

    def take(self):
        self.have.update(self.new)
        self.new = {}

    def send(self):
        self.take()
        new = {}
        for m in self.last:
            used = [k for k, bit in enumerate(self.order) if m & bit]
            for bit in self.order[max(used, default=-1) + 1 :]:
                new[m | bit] = swap(self.have[m], bit, self.count)
        self.new, self.last = new, sorted(new)


class Scatter(Exchange):
    def __init__(self, blocks, order, count):
        super().__init__()
        self.have, self.order, self.count, self.step = dict(enumerate(blocks)), order, count, 0

    def take(self):
        if self.new:
            bit = self.order[self.step - 1]
            self.have = {
                m: self.have[m].astype(F32) + self.new[m | bit].astype(F32)
                for m in self.have
                if not m & bit
            }
            self.new = {}

    def send(self):
        self.take()
        bit = self.order[self.step]
        self.new = {
            m: swap(self.have[m].astype(BF16), bit, self.count)
            for m in sorted(self.have, reverse=True)
            if m & bit
        }
        self.step += 1

    def rest(self):
        while self.step < len(self.order):
            self.send()
        self.take()
        return self.have[0]


class CubeSum(Exchange):
    def __init__(self, piece, count):
        super().__init__()
        self.total, self.step = piece, 0
        self.count, self.bits = count, count.bit_length() - 1

    def swap(self, array, bit):
        return lax.ppermute(array, "wz", [(i, i ^ bit) for i in range(self.count)])

    def mine(self, bit):
        return jnp.where(lax.axis_index("wz") & bit, 1, 0)

    def take(self):
        if self.new:
            came, at = self.new[0], self.step - 1
            if at < self.bits:
                half = came.shape[0]
                kept = lax.dynamic_slice_in_dim(self.total, self.mine(1 << at) * half, half, 0)
                self.total = (kept.astype(F32) + came.astype(F32)).astype(BF16)
            else:
                upper = self.mine(1 << (2 * self.bits - 1 - at)) == 1
                self.total = jnp.concatenate(
                    [jnp.where(upper, came, self.total), jnp.where(upper, self.total, came)], axis=0
                )
            self.new = {}

    def send(self):
        self.take()
        if self.step >= 2 * self.bits:
            return
        if self.step < self.bits:
            bit = 1 << self.step
            half = self.total.shape[0] // 2
            away = lax.dynamic_slice_in_dim(self.total, (1 - self.mine(bit)) * half, half, 0)
            self.new = {0: self.swap(away.astype(BF16), bit)}
        else:
            self.new = {0: self.swap(self.total, 1 << (2 * self.bits - 1 - self.step))}
        self.step += 1

    def rest(self):
        while self.step < 2 * self.bits:
            self.send()
        self.take()
        return self.total.astype(BF16)


class OtherCore(Exchange):
    def __init__(self, array):
        super().__init__()
        self.new = {0: other_core(array)}


def split_columns(blocks, count):
    half = blocks[0].shape[1] // 2
    return [
        Scatter([block[:, k * half : (k + 1) * half] for block in blocks], order, count)
        for k, order in enumerate(bit_orders(count))
    ]


def other_core(array):
    return lax.ppermute(array, "core", [(0, 1), (1, 0)])


def shards(
    seq_count,
    wz_count,
    inputs,
    bin_order,
    first_gain,
    first_shift,
    query_weight,
    key_weight,
    value_weight,
    bias_content,
    bias_position,
    relative_weight,
    out_weight,
    bias_out,
    second_gain,
    second_shift,
    inner_weight,
    bias_inner,
    outer_weight,
    bias_outer,
    grad_output,
):
    row_count, width = inputs.shape[1:]
    length = bin_order.shape[1]
    here = lax.axis_index("seq")
    core = lax.axis_index("core")
    where = jnp.stack([here, core]).astype(jnp.int32)
    row_start = here * row_count
    key_width = query_weight.shape[1] // seq_count
    val_width = value_weight.shape[1] // seq_count
    heads_width = 2 * key_width + val_width
    up, down = bit_orders(seq_count)

    others = [jnp.bitwise_xor(here, m) for m in range(seq_count)]
    along = jnp.concatenate(
        [other * row_count + jnp.arange(row_count, dtype=jnp.int32) for other in others]
    )

    def natural(rows):
        parts = rows.reshape(seq_count, row_count, -1)
        parts = [lax.dynamic_index_in_dim(parts, other, 0) for other in others]
        return jnp.concatenate(parts, axis=0).reshape(rows.shape)

    def halves(rows):
        half = rows.shape[0] // 2
        return [Gather(rows[:half], up, seq_count), Gather(rows[half:], down, seq_count)]

    def blocks_of(gathers):
        for g in gathers:
            g.take()
        return [g.have[m] for m in range(seq_count) for g in gathers]

    window_gathers = halves(inputs[0])
    for g in window_gathers:
        g.send()

    def by_head(weight):
        return weight.reshape(weight.shape[0], seq_count, -1)

    vectors = jnp.stack([first_gain, first_shift, bias_out, second_gain, second_shift, bias_outer])
    vectors = jnp.concatenate([vectors, bias_inner.reshape(2, row_count)], axis=0)
    vectors = jnp.pad(vectors, ((0, EXTRA - 8), (0, 0)))
    rel_rows = relative_weight.shape[0]
    rel_blocks = -(-rel_rows // EXTRA)
    rel_part = jnp.pad(by_head(relative_weight), ((0, rel_blocks * EXTRA - rel_rows), (0, 0), (0, 0)))
    rel_part = rel_part.reshape(rel_blocks, EXTRA, seq_count, key_width).transpose(2, 1, 0, 3)
    rel_part = rel_part.reshape(seq_count, EXTRA, -1)
    spare = heads_width - row_count - rel_part.shape[2]
    extra = jnp.concatenate(
        [
            jnp.broadcast_to(vectors[None], (seq_count,) + vectors.shape),
            jnp.pad(rel_part, ((0, 0), (0, 0), (0, spare))),
        ],
        axis=2,
    )
    mine = jnp.concatenate(
        [by_head(query_weight), by_head(key_weight), by_head(value_weight)], axis=2
    ).transpose(1, 0, 2)
    mine = jnp.concatenate([mine, extra], axis=1)
    half = mine.shape[1] // 2
    mine = lax.dynamic_slice_in_dim(mine, core * half, half, 1)

    def own_half(weight):
        half = weight.shape[0] // 2
        return lax.dynamic_slice_in_dim(weight, core * half, half, 0)

    inner_part, outer_part = own_half(inner_weight), own_half(outer_weight)
    mine, inner_part, outer_part = pin_all(window_gathers, mine, inner_part, outer_part)
    for step in range(1, len(up)):
        for g in window_gathers:
            g.send()
    weight_gathers = [
        Gather(inner_part, up, seq_count),
        Gather(outer_part, down, seq_count),
    ]
    for g in weight_gathers:
        g.send()
    mine = lax.all_to_all(mine, "seq", 0, 0, tiled=True)
    (mine,) = pin_all(window_gathers, mine)
    first = core == 0
    theirs = other_core(mine)
    attention_weight = jnp.concatenate(
        [jnp.where(first, mine, theirs), jnp.where(first, theirs, mine)], axis=1
    )
    table, table_back = basis_tables(jnp.asarray(basis_constants(length)), length)
    flat = attention_weight[:, row_count:]
    vectors = flat[:, :8, :row_count].astype(F32)
    inner_bias = vectors[:, 6:8].reshape(1, -1)
    vectors = vectors.transpose(1, 0, 2).reshape(8, width)
    rel = flat[:, :, row_count : row_count + rel_blocks * key_width]
    rel = rel.reshape(seq_count, EXTRA, rel_blocks, key_width).transpose(0, 2, 1, 3)
    rel = rel.reshape(seq_count, rel_blocks * EXTRA, key_width)[:, :rel_rows].reshape(REL, key_width)

    window_blocks = blocks_of(window_gathers)

    order = bin_order[0]
    placing = (order[:, None] == along[None, :]).astype(BF16)
    bias = jnp.concatenate([bias_content, bias_position])[None].astype(F32)
    window, hidden_one, in_bins, weight_whole = project(
        window_blocks, attention_weight, vectors, bias, row_count
    )
    placed_heads = matmul(placing, in_bins).astype(BF16)
    (placed_heads,) = pin_all(weight_gathers, placed_heads)
    for step in range(1, len(up)):
        for g in weight_gathers:
            g.send()
    mixed, probs = attend(placed_heads, rel, table)
    (mixed,) = pin_all(weight_gathers, mixed)
    weight_parts = []
    for g, own in zip(weight_gathers, (inner_weight, outer_weight)):
        g.take()
        parts = [own]
        for m in range(1, seq_count):
            parts += [g.have[m], other_core(g.have[m])]
        weight_parts.append(parts)
    mixed_along = natural(mixed).reshape(seq_count, row_count, val_width)
    attended = [matmul(mixed_along[m], out_weight).astype(BF16) for m in range(seq_count)]
    attended = split_columns(attended, seq_count)
    for g in attended:
        g.send()
    own_order = lax.dynamic_slice_in_dim(order, row_start, row_count, 0)
    placed = matmul((own_order[:, None] == along[None, :]).astype(BF16), window)
    (placed,) = pin_all(attended, placed)
    attended = [g.rest() for g in attended]

    grad_rows = grad_output[0]
    layer_output, d_mixed_in, hidden_two, activated, d_inner, sums, inner_sums = feed_forward(
        where, placed, attended, grad_rows, vectors, inner_bias, *weight_parts
    )

    d_mixed_gathers = halves(d_mixed_in)
    for g in d_mixed_gathers:
        g.send()
    came_inner = other_core(half_gradient(seq_count, True, where, hidden_two, d_inner))
    outer_away = half_gradient(seq_count, False, where, activated, grad_rows)
    (outer_away,) = pin_all(d_mixed_gathers, outer_away)
    for step in range(1, len(up)):
        for g in d_mixed_gathers:
            g.send()
    came_outer = other_core(outer_away)
    kept_inner = half_gradient(seq_count, True, where, hidden_two, d_inner, came_inner)
    kept_outer = half_gradient(seq_count, False, where, activated, grad_rows, came_outer)
    kept = pin_all(d_mixed_gathers, *kept_inner, *kept_outer)
    d_mixed_blocks = blocks_of(d_mixed_gathers)
    count = seq_count
    inner_sums_of, outer_sums_of = [
        [
            Scatter([kept[2 * (k * count + m) + side] for m in range(count)], bits, count)
            for side, bits in enumerate((up, down))
        ]
        for k in range(2)
    ]
    for g in inner_sums_of:
        g.send()

    d_attended, out_away, grad_out_w = mixed_back(
        seq_count, where, mixed, out_weight, d_mixed_blocks
    )
    (d_attended,) = pin_some(inner_sums_of, d_attended)
    out_core = OtherCore(out_away)

    def send_all(exchanges):
        for exchange in exchanges:
            exchange.send()

    def scatter_windows(piece):
        return lax.psum_scatter(piece.astype(BF16), "wz", scatter_dimension=0, tiled=True)

    def gather_windows(piece):
        return lax.all_gather(piece, ("core", "wz"), axis=0, tiled=True)

    def joined_sum(scatters):
        return jnp.concatenate([g.rest().astype(BF16) for g in scatters], axis=1)

    (d_attended,) = pin_all([out_core], d_attended)
    out_sum = scatter_windows(grad_out_w + out_core.new[0].astype(F32))
    back = attend_back(0, placed_heads, rel, table_back, mixed, d_attended, probs)
    *back, out_sum = pin_all(inner_sums_of, *back, out_sum)
    out_sum = gather_windows(out_sum)
    for step in range(1, len(up)):
        send_all(inner_sums_of)
    send_all(outer_sums_of)
    for head in range(1, key_width // KEY):
        back = attend_back(head, placed_heads, rel, table_back, mixed, d_attended, probs, back)
    *back, out_sum = pin_all(inner_sums_of, *back, out_sum)
    d_heads, d_rel, d_bias = back
    inner_sum = scatter_windows(joined_sum(inner_sums_of))
    d_along, *d_normed, first_sums = rows_back(
        seq_count, where, order[None], d_heads, window, weight_whole
    )
    out = pin_all(outer_sums_of, d_along, *d_normed)
    d_along, d_normed = out[0], out[1:]
    for step in range(1, len(up)):
        send_all(outer_sums_of)
    arrived = [
        Scatter([d_normed[2 * m + side] for m in range(count)], bits, count)
        for side, bits in enumerate((up, down))
    ]
    results = pack(
        seq_count, where, hidden_one, d_along, first_sums, sums, inner_sums, d_bias, d_rel
    )
    *results, inner_sum = pin_all(outer_sums_of, *results, inner_sum)
    packed_core = OtherCore(results[1])
    outer_sum = scatter_windows(joined_sum(outer_sums_of))
    inner_sum = gather_windows(inner_sum)
    (packed,) = pin_all([packed_core], results[0])
    packed = (packed.astype(F32) + packed_core.new[0].astype(F32)).astype(BF16)
    packed_shape = packed.shape
    packed = lax.all_to_all(packed, "seq", 0, 0, tiled=True)
    send_all(arrived)
    (packed,) = pin(packed)
    packed_cube = CubeSum(packed.reshape(-1, packed_shape[2]), wz_count)
    packed_cube.send()
    (outer_sum,) = pin_all([packed_cube], outer_sum)
    outer_sum = gather_windows(outer_sum)
    packed_cube.send()
    d_mixed_blocks = pin_all(arrived, *d_mixed_blocks)
    for step in range(1, len(up)):
        send_all(arrived)
    returned = returned_rows(
        seq_count, where, order.reshape(2 * seq_count, row_count // 2), d_mixed_blocks
    )
    (returned,) = pin_all([packed_cube], returned)
    packed_cube.send()
    own_unit, own_scale = norm_of(inputs[0].astype(F32))
    arrived = jnp.concatenate([g.rest() for g in arrived], axis=1)
    grad_inputs = norm_back(own_unit, own_scale, vectors[0:1], arrived) + returned

    def both_halves(pieces, axis):
        half = pieces.shape[0] // 2
        return jnp.concatenate([pieces[:half], pieces[half:]], axis=axis).astype(F32)

    grad_out_w = both_halves(out_sum, 0)
    grad_inputs, grad_out_w = pin_all([packed_cube], grad_inputs, grad_out_w)
    packed_cube.send()
    grad_inner_w = both_halves(inner_sum, 1)
    grad_outer_w = both_halves(outer_sum, 0)
    packed = packed_cube.rest().reshape(packed_shape)
    grad_query_w, grad_key_w, grad_value_w, flat = unpack(
        where, (packed, other_core(packed)), row_count, key_width, val_width
    )
    small = jnp.sum(flat[:, :16, :row_count], axis=0)
    g_gain_one, g_shift_one, g_out_b, g_gain_two, g_shift_two, g_outer_b = small[:6]
    g_inner_b = small[6:8].reshape(-1)
    grad_rel = flat[:, :, row_count : row_count + rel_blocks * key_width]
    grad_rel = grad_rel.reshape(seq_count, EXTRA, rel_blocks, key_width).transpose(2, 1, 0, 3)
    grad_rel = grad_rel.reshape(rel_blocks * EXTRA, -1)[:rel_rows]
    return (
        layer_output[None],
        grad_inputs[None],
        g_gain_one,
        g_shift_one,
        grad_query_w,
        grad_key_w,
        grad_value_w,
        small[8, :key_width],
        small[9, :key_width],
        grad_rel,
        grad_out_w,
        g_out_b,
        g_gain_two,
        g_shift_two,
        grad_inner_w,
        g_inner_b,
        grad_outer_w,
        g_outer_b,
    )


def solution(mesh):
    seq_count = mesh.shape["seq"]
    devices = mesh.devices.reshape(seq_count, -1, 2)
    split_mesh = Mesh(devices, ("seq", "wz", "core"))
    rows = P(("wz", "core"), "seq", None)
    vector = P("seq")
    matrix = P("seq", None)
    weights = (
        vector,
        vector,
        matrix,
        matrix,
        matrix,
        vector,
        vector,
        matrix,
        matrix,
        vector,
        vector,
        vector,
        matrix,
        vector,
        matrix,
        vector,
    )
    return jax.shard_map(
        functools.partial(shards, seq_count, mesh.shape["win"] // 2),
        mesh=split_mesh,
        in_specs=(rows, P(("wz", "core"), None)) + weights + (rows,),
        out_specs=(rows, rows) + weights,
        check_vma=False,
    )
```

```python
import functools
import math

import jax
import jax.numpy as jnp
import numpy as np
from jax import lax
from jax.experimental import pallas as pl
from jax.experimental.pallas import tpu as pltpu
from jax.sharding import Mesh
from jax.sharding import PartitionSpec as P

HEADS = 8
KEY = 64
VAL = 192
REL = 192
BF16 = jnp.bfloat16
F32 = jnp.float32
VMEM_LIMIT = 56 * 2**20
EXTRA = 32


def matmul(a, b):
    return lax.dot_general(a, b, (((1,), (0,)), ((), ())), preferred_element_type=F32)


def matmul_nt(a, b):
    return lax.dot_general(a, b, (((1,), (1,)), ((), ())), preferred_element_type=F32)


def matmul_tn(a, b):
    return lax.dot_general(a, b, (((0,), (0,)), ((), ())), preferred_element_type=F32)


def head_part(rows, head):
    lanes = lax.broadcasted_iota(jnp.int32, rows.shape, 1)
    inside = (lanes >= head * KEY) & (lanes < (head + 1) * KEY)
    return jnp.where(inside, rows, jnp.zeros_like(rows))


def head_columns(key_width):
    return [slice(k * key_width, (k + 1) * key_width) for k in range(3)]


def attend_kernel(heads, rows, placed, rel, table, mixed, probs):
    length = placed.shape[0]
    key_width = heads * KEY
    content_at, position_at, keys_at = head_columns(key_width)
    first = pl.program_id(0) * rows
    here = pl.ds(pl.multiple_of(first, rows), rows)
    basis = table[:, pl.ds(pl.multiple_of(length - rows - first, rows), length + rows)]
    content, position, keys = placed[here, content_at], placed[here, position_at], placed[:, keys_at]
    parts = []
    for head in range(heads):
        q_basis = matmul_nt(head_part(position, head), rel[...]).astype(BF16)
        grid = matmul(q_basis, basis)
        shifted = pltpu.roll(grid, 0, 1, stride=1, stride_axis=0)[:, rows:]
        scores = matmul_nt(head_part(content, head), keys) + shifted
        top = jnp.max(scores, axis=1, keepdims=True)
        weights = jnp.exp(scores - top)
        total = jnp.sum(weights, axis=1, keepdims=True)
        prob = (weights * (1.0 / total)).astype(BF16)
        probs[head] = prob
        values_at = 3 * key_width + head * VAL
        parts.append(matmul(prob, placed[:, values_at : values_at + VAL]))
    mixed[...] = jnp.concatenate(parts, axis=1).astype(BF16)


def attend(placed, rel, table):
    length = placed.shape[0]
    heads = rel.shape[1] // KEY
    rows = math.gcd(256, length)
    whole = lambda array: pl.BlockSpec(array.shape, lambda i: (0, 0))
    return pl.pallas_call(
        functools.partial(attend_kernel, heads, rows),
        grid=(length // rows,),
        in_specs=[whole(placed), whole(rel), whole(table)],
        out_specs=[
            pl.BlockSpec((rows, heads * VAL), lambda i: (i, 0)),
            pl.BlockSpec((heads, rows, length), lambda i: (0, i, 0)),
        ],
        out_shape=[
            jax.ShapeDtypeStruct((length, heads * VAL), BF16),
            jax.ShapeDtypeStruct((heads, length, length), BF16),
        ],
        compiler_params=pltpu.CompilerParams(vmem_limit_bytes=VMEM_LIMIT),
        cost_estimate=pl.CostEstimate(
            flops=2 * heads * length * length * 1024,
            bytes_accessed=2 * heads * length * length + 8 * length * heads * VAL,
            transcendentals=heads * length * length,
        ),
    )(placed, rel, table)


def attend_back_kernel(heads, head, rows, *refs):
    placed, rel, table, flip, mixed, d_mixed, probs = refs[:7]
    before = refs[7:-5]
    d_heads, d_rel, d_bias, keys_sum, values_sum = refs[-5:]
    length = placed.shape[0]
    key_width = heads * KEY
    content_at, position_at, keys_at = head_columns(key_width)
    step = pl.program_id(0)

    @pl.when(step == 0)
    def _():
        keys_sum[...] = jnp.zeros_like(keys_sum)
        values_sum[...] = jnp.zeros_like(values_sum)
        for k, out in enumerate((d_heads, d_rel, d_bias)):
            out[...] = before[k][...] if before else jnp.zeros_like(out)

    first = pl.multiple_of(step * rows, rows)
    here = pl.ds(first, rows)
    basis = table[:, pl.ds(first, length + rows)]
    content, position, keys = placed[here, content_at], placed[here, position_at], placed[:, keys_at]
    blocks = length // rows
    columns = slice(head * VAL, (head + 1) * VAL)
    values_at = 3 * key_width + head * VAL
    d_part = d_mixed[:, columns]
    delta = jnp.sum(d_part.astype(F32) * mixed[:, columns].astype(F32), axis=1, keepdims=True)
    prob = probs[0]
    values_sum[...] += matmul_tn(d_part, prob)
    d_prob = matmul_nt(d_part, placed[:, values_at : values_at + VAL])
    d_score = (prob.astype(F32) * (d_prob - delta)).astype(BF16)
    keys_sum[...] += matmul_tn(head_part(content, head), d_score)
    d_content = head_part(matmul(d_score, keys), head)
    turned = [
        matmul(d_score[:, (blocks - 1 - b) * rows : (blocks - b) * rows], flip[...])
        for b in range(blocks)
    ]
    turned = jnp.concatenate(turned + [jnp.zeros((rows, rows), F32)], axis=1)
    d_grid = pltpu.roll(turned, 0, 1, stride=1, stride_axis=0).astype(BF16)
    d_basis = matmul_nt(d_grid, basis).astype(BF16)
    d_position = head_part(matmul(d_basis, rel[...]), head)
    d_rel[...] += matmul_tn(d_basis, head_part(position, head))
    d_heads[here, :key_width] += ((d_content + d_position) * KEY ** (-0.5)).astype(BF16)
    d_bias[0:1, :] += jnp.sum(d_content, axis=0, keepdims=True)
    d_bias[1:2, :] += jnp.sum(d_position, axis=0, keepdims=True)

    @pl.when(step == blocks - 1)
    def _():
        d_heads[:, key_width : 2 * key_width] += keys_sum[...].T.astype(BF16)
        values_to = 2 * key_width + head * VAL
        d_heads[:, values_to : values_to + VAL] = values_sum[...].T.astype(BF16)


def attend_back(head, placed, rel, table, mixed, d_mixed, probs, before=()):
    length = placed.shape[0]
    key_width = rel.shape[1]
    heads = key_width // KEY
    val_width = heads * VAL
    rows = math.gcd(256, length)
    at = jnp.arange(rows)
    flip = (at[:, None] + at[None, :] == rows - 1).astype(BF16)
    block = lambda width: pl.BlockSpec((rows, width), lambda i: (i, 0))
    outs = [
        shape((length, 2 * key_width + val_width), BF16),
        shape((REL, key_width), F32),
        shape((8, key_width), F32),
    ]
    return pl.pallas_call(
        functools.partial(attend_back_kernel, heads, head, rows),
        grid=(length // rows,),
        in_specs=[
            whole_spec(placed),
            whole_spec(rel),
            whole_spec(table),
            whole_spec(flip),
            block(val_width),
            block(val_width),
            pl.BlockSpec((1, rows, length), lambda i: (head, i, 0)),
        ]
        + [whole_spec(array) for array in before],
        out_specs=[whole_spec(out) for out in outs],
        out_shape=outs,
        scratch_shapes=[
            pltpu.VMEM((key_width, length), F32),
            pltpu.VMEM((VAL, length), F32),
        ],
        compiler_params=pltpu.CompilerParams(vmem_limit_bytes=VMEM_LIMIT),
        cost_estimate=pl.CostEstimate(
            flops=2 * length * length * 1536,
            bytes_accessed=2 * length * length + 16 * length * val_width,
            transcendentals=0,
        ),
    )(placed, rel, table, flip, mixed, d_mixed, probs, *before)


def norm_back(unit, scale, gain, grad):
    scaled = grad * gain
    mean_one = jnp.mean(scaled, axis=-1, keepdims=True)
    mean_two = jnp.mean(scaled * unit, axis=-1, keepdims=True)
    return (scaled - mean_one - unit * mean_two) * scale


def whole_spec(array):
    zeros = (0,) * len(array.shape)
    return pl.BlockSpec(array.shape, lambda *_: zeros)


def scalar_spec():
    return pl.BlockSpec(memory_space=pltpu.SMEM)


def params(**more):
    return pltpu.CompilerParams(vmem_limit_bytes=VMEM_LIMIT, **more)


def shape(dims, dtype):
    return jax.ShapeDtypeStruct(tuple(dims), dtype)


def basis_constants(window_len):
    features = REL // 6
    f = np.arange(features, dtype=np.float64)
    half_life = 2.0 ** (3.0 + f * (math.log2(window_len) - 3.0) / (features - 1))
    spread = window_len / (2.0 * features)
    first = window_len / features
    centres = first + f * (window_len - first) / (features - 1)
    concentration = (centres / spread) ** 2
    rate = centres / spread**2
    offset = concentration * np.log(rate) - np.array([math.lgamma(c) for c in concentration])
    columns = [math.log(2.0) / half_life, 2.0 ** (f + 1) - 1.0, concentration - 1.0, rate, offset]
    columns += [np.zeros(features)] * 3
    return np.stack(columns, axis=1).astype(np.float32)


def table_kernel(length, constants, forth, back):
    features = REL // 6
    decay, inside_below, power, rate, offset = [constants[:, k : k + 1] for k in range(5)]

    def gamma(distance):
        logged = power * jnp.log(jnp.maximum(distance, 1.0)) - rate * distance + offset
        return jnp.where(distance == 0.0, 0.0, jnp.exp(logged)) + 1e-08

    every = lax.broadcasted_iota(jnp.int32, (1, length), 1).astype(F32)
    peak = jnp.max(gamma(every), axis=1, keepdims=True)
    lanes = lax.broadcasted_iota(jnp.int32, (1, 2 * length), 1).astype(F32)
    for table, signed in ((forth, lanes - length), (back, length - 1 - lanes)):
        distance = jnp.abs(signed)
        sign = jnp.where(signed > 0, 1.0, jnp.where(signed < 0, -1.0, 0.0))
        parts = (
            jnp.exp(-decay * distance),
            jnp.where(inside_below > distance, 1.0, 0.0),
            gamma(distance) / peak,
        )
        for k, part in enumerate(parts):
            table[k * features : (k + 1) * features, :] = part.astype(BF16)
            table[(3 + k) * features : (4 + k) * features, :] = (sign * part).astype(BF16)


def basis_tables(constants, length):
    out = shape((REL, 2 * length), BF16)
    return pl.pallas_call(
        functools.partial(table_kernel, length),
        out_shape=[out, out],
        compiler_params=params(),
    )(constants)


def norm_of(rows):
    centre = rows - jnp.mean(rows, axis=1, keepdims=True)
    scale = lax.rsqrt(jnp.mean(centre * centre, axis=1, keepdims=True) + 1e-05)
    return centre * scale, scale


def project_kernel(blocks, row_count, *refs):
    parts, (weight, vectors, bias, window, hidden, heads, flat, block) = refs[:blocks], refs[blocks:]
    step = pl.program_id(0)

    @pl.when(step == 0)
    def _():
        for s in range(weight.shape[0]):
            flat[s * row_count : (s + 1) * row_count, :] = weight[s, :row_count, :]

    for k in range(blocks):

        @pl.when(step == k)
        def _():
            block[...] = parts[k][...]

    window[...] = block[...]
    unit, _ = norm_of(block[...].astype(F32))
    normed = (unit * vectors[0:1, :] + vectors[1:2, :]).astype(BF16)
    hidden[...] = normed
    total = matmul(normed, flat[...])
    key_width = bias.shape[1] // 2
    query = total[:, :key_width] * KEY ** (-0.5)
    heads[:, :key_width] = (query + bias[0:1, :key_width]).astype(BF16)
    heads[:, key_width : 2 * key_width] = (query + bias[0:1, key_width:]).astype(BF16)
    heads[:, 2 * key_width :] = total[:, key_width:].astype(BF16)


def project(parts, weight, vectors, bias, row_count):
    blocks = len(parts)
    rows, width = parts[0].shape
    heads_width = weight.shape[2] + bias.shape[1] // 2
    out = lambda w: pl.BlockSpec((rows, w), lambda i: (i, 0))
    return pl.pallas_call(
        functools.partial(project_kernel, blocks, row_count),
        grid=(blocks,),
        in_specs=[whole_spec(a) for a in (*parts, weight, vectors, bias)],
        out_specs=[
            out(width),
            out(width),
            out(heads_width),
            pl.BlockSpec((width, weight.shape[2]), lambda i: (0, 0)),
        ],
        out_shape=[shape((blocks * rows, w), BF16) for w in (width, width, heads_width)]
        + [shape((width, weight.shape[2]), BF16)],
        scratch_shapes=[pltpu.VMEM((rows, width), BF16)],
        compiler_params=params(),
        cost_estimate=pl.CostEstimate(
            flops=2 * blocks * rows * width * heads_width,
            bytes_accessed=8 * blocks * rows * width,
            transcendentals=0,
        ),
    )(*parts, weight, vectors, bias)


def feed_kernel(count, chunk, *refs):
    parts = 2 * (2 * count - 1)
    where, placed, attended_a, attended_b, grad_rows, vectors, inner_bias = refs[:7]
    weights = refs[7 : 7 + parts]
    layer_output, d_mixed, hidden, activated, d_inner, sums, inner_sums = refs[7 + parts : 14 + parts]
    inner_whole, outer_whole, residual, unit, back, outer_sum, sems = refs[14 + parts :]
    here, core = where[0], where[1]
    copies = []
    for k, whole in enumerate((inner_whole, outer_whole)):
        mine = weights[k * (2 * count - 1) : (k + 1) * (2 * count - 1)]
        size = whole.shape[0] // count
        half = size // 2
        moves = [(mine[0], here * size, size)]
        for m in range(1, count):
            start = jnp.bitwise_xor(here, m) * size
            moves.append((mine[2 * m - 1], start + core * half, half))
            moves.append((mine[2 * m], start + (1 - core) * half, half))
        started = []
        for source, start, rows in moves:
            target = whole.at[pl.ds(pl.multiple_of(start, 16), rows), :]
            copy = pltpu.make_async_copy(source, target, sems.at[k, len(started)])
            copy.start()
            started.append(copy)
        copies.append(started)
    rows, width = placed.shape
    half = width // 2
    residual[:, :half] = placed[:, :half] + attended_a[...] + vectors[2:3, :half]
    residual[:, half:] = placed[:, half:] + attended_b[...] + vectors[2:3, half:]
    normed, scale = norm_of(residual[...])
    unit[...] = normed
    hidden[...] = (normed * vectors[3:4, :] + vectors[4:5, :]).astype(BF16)
    for started in copies:
        for copy in started:
            copy.wait()
    ff = outer_whole.shape[0]
    for c in range(ff // chunk):
        at = slice(c * chunk, (c + 1) * chunk)
        inner = matmul(hidden[...], inner_whole[:, at]) + inner_bias[0:1, at]
        below = 0.5 * (1.0 + lax.erf(inner * (0.5**0.5)))
        slope = below + inner * jnp.exp(-0.5 * inner * inner) * (0.5 / math.pi) ** 0.5
        active = (inner * below).astype(BF16)
        activated[:, at] = active
        grad = (matmul_nt(grad_rows[...], outer_whole[at, :]) * slope).astype(BF16)
        d_inner[:, at] = grad
        inner_sums[:, at] = jnp.sum(grad.astype(F32), axis=0, keepdims=True)
        back_term = matmul_nt(grad, inner_whole[:, at])
        outer_term = matmul(active, outer_whole[at, :])
        if c == 0:
            back[...] = back_term
            outer_sum[...] = outer_term
        else:
            back[...] += back_term
            outer_sum[...] += outer_term
    layer_output[...] = (residual[...] + outer_sum[...] + vectors[5:6, :]).astype(BF16)
    grad, normed = back[...], unit[...]
    dy = grad_rows[...].astype(F32)
    scaled = grad * vectors[3:4, :]
    mean_one = jnp.mean(scaled, axis=1, keepdims=True)
    mean_two = jnp.mean(scaled * normed, axis=1, keepdims=True)
    mixed_in = (dy + (scaled - mean_one - normed * mean_two) * scale).astype(BF16)
    d_mixed[...] = mixed_in
    sums[...] = jnp.zeros_like(sums)
    sums[2:3, :] = jnp.sum(mixed_in.astype(F32), axis=0, keepdims=True)
    sums[3:4, :] = jnp.sum(grad * normed, axis=0, keepdims=True)
    sums[4:5, :] = jnp.sum(grad, axis=0, keepdims=True)
    sums[5:6, :] = jnp.sum(dy, axis=0, keepdims=True)


def feed_forward(where, placed, attended, grad_rows, vectors, inner_bias, inner_parts, outer_parts):
    rows, width = placed.shape
    ff = inner_bias.shape[1]
    count = (len(inner_parts) + 1) // 2
    chunk = math.gcd(512, ff)
    weights = (*inner_parts, *outer_parts)
    small = (placed, *attended, grad_rows, vectors, inner_bias)
    outs = [
        shape((rows, width), BF16),
        shape((rows, width), BF16),
        shape((rows, width), BF16),
        shape((rows, ff), BF16),
        shape((rows, ff), BF16),
        shape((8, width), F32),
        shape((1, ff), F32),
    ]
    return pl.pallas_call(
        functools.partial(feed_kernel, count, chunk),
        in_specs=[scalar_spec()]
        + [pl.BlockSpec(memory_space=pltpu.VMEM) for _ in small]
        + [pl.BlockSpec(memory_space=pl.ANY) for _ in weights],
        out_specs=[pl.BlockSpec(memory_space=pltpu.VMEM) for _ in outs],
        out_shape=outs,
        scratch_shapes=[
            pltpu.VMEM((width, ff), BF16),
            pltpu.VMEM((ff, width), BF16),
            pltpu.VMEM((rows, width), F32),
            pltpu.VMEM((rows, width), F32),
            pltpu.VMEM((rows, width), F32),
            pltpu.VMEM((rows, width), F32),
            pltpu.SemaphoreType.DMA((2, 2 * count - 1)),
        ],
        compiler_params=params(),
        cost_estimate=pl.CostEstimate(
            flops=8 * rows * width * ff,
            bytes_accessed=4 * width * ff + 40 * rows * width,
            transcendentals=2 * rows * ff,
        ),
    )(where, *small, *weights)


def columns_at(ref, index, size, scratch):
    if size % 128 == 0:
        return ref[:, pl.ds(pl.multiple_of(index * size, 128), size)]
    for k in range(ref.shape[1] // size):

        @pl.when(index == k)
        def _():
            scratch[...] = ref[:, k * size : (k + 1) * size]

    return scratch[...]


def half_kernel(count, split, away, where, left, right, *refs):
    here, core = where[0], where[1]
    side = 1 - core if away else core
    shard = jnp.bitwise_xor(here, pl.program_id(0))
    if split:
        some = columns_at(left, shard, left.shape[1] // count, refs[-1])
        half = right.shape[1] // 2
        other = right[:, pl.ds(pl.multiple_of(side * half, 128), half)]
    else:
        some = columns_at(left, 2 * shard + side, left.shape[1] // count // 2, refs[-1])
        other = right[...]
    result = matmul_tn(some, other)
    if away:
        refs[0][0] = result.astype(BF16)
        return
    came, outs = refs[0], refs[1:-1]
    result += came[0].astype(F32)
    width = result.shape[1] // 2
    for m in range(count):

        @pl.when(pl.program_id(0) == m)
        def _():
            outs[2 * m][...] = result[:, :width].astype(BF16)
            outs[2 * m + 1][...] = result[:, width:].astype(BF16)


def half_gradient(count, split, where, left, right, came=None):
    away = came is None
    rows = left.shape[1] // count // (1 if split else 2)
    width = right.shape[1] // (2 if split else 1)
    block = pl.BlockSpec((1, rows, width), lambda i: (i, 0, 0))
    if away:
        outs, out_specs = shape((count, rows, width), BF16), block
    else:
        outs = [shape((rows, width // 2), BF16) for _ in range(2 * count)]
        out_specs = [whole_spec(out) for out in outs]
    return pl.pallas_call(
        functools.partial(half_kernel, count, split, away),
        grid=(count,),
        in_specs=[scalar_spec(), whole_spec(left), whole_spec(right)] + ([] if away else [block]),
        out_specs=out_specs,
        out_shape=outs,
        scratch_shapes=[pltpu.VMEM((left.shape[0], rows), BF16)],
        compiler_params=params(),
        cost_estimate=pl.CostEstimate(
            flops=2 * left.shape[0] * count * rows * width,
            bytes_accessed=4 * count * rows * width + 4 * left.shape[0] * left.shape[1],
            transcendentals=0,
        ),
    )(where, left, right, *(() if away else (came,)))


def mixed_back_kernel(count, parts_count, *refs):
    where, mixed, weight = refs[:3]
    parts = refs[3 : 3 + parts_count]
    d_attended, out_away, out_kept, out_sum = refs[3 + parts_count :]
    here, core = where[0], where[1]
    rows = parts[0].shape[0]
    for k, part in enumerate(parts):
        start = jnp.bitwise_xor(here, k // 2) * (2 * rows) + (k % 2) * rows
        at = pl.ds(pl.multiple_of(start, 32), rows)
        d_attended[at, :] = matmul_nt(part[...], weight[...]).astype(BF16)
        term = matmul_tn(mixed[at, :], part[...])
        if k == 0:
            out_sum[...] = term
        else:
            out_sum[...] += term
    half = out_kept.shape[0]
    out_kept[...] = out_sum[pl.ds(pl.multiple_of(core * half, 32), half), :]
    out_away[...] = out_sum[pl.ds(pl.multiple_of((1 - core) * half, 32), half), :].astype(BF16)


def mixed_back(count, where, mixed, weight, parts):
    length, val_width = mixed.shape
    width = weight.shape[1]
    vmem = pl.BlockSpec(memory_space=pltpu.VMEM)
    return pl.pallas_call(
        functools.partial(mixed_back_kernel, count, len(parts)),
        in_specs=[scalar_spec()] + [vmem] * (2 + len(parts)),
        out_specs=[vmem] * 3,
        out_shape=[
            shape((length, val_width), BF16),
            shape((val_width // 2, width), BF16),
            shape((val_width // 2, width), F32),
        ],
        scratch_shapes=[pltpu.VMEM((val_width, width), F32)],
        compiler_params=params(),
        cost_estimate=pl.CostEstimate(
            flops=4 * length * val_width * width,
            bytes_accessed=2 * length * (width + 2 * val_width),
            transcendentals=0,
        ),
    )(where, mixed, weight, *parts)


def rows_back_kernel(count, where, order, d_heads, window, weight, d_along, *refs):
    d_normed, first_sums = refs[:-1], refs[-1]
    here = where[0]
    step = pl.program_id(0)
    rows, width = window.shape
    length = order.shape[1]
    bins = lax.broadcasted_iota(jnp.int32, (rows, length), 0) + jnp.bitwise_xor(here, step) * rows
    picks = jnp.where(order[0:1, :] == bins, 1.0, 0.0).astype(BF16)
    along = matmul(picks, d_heads[...]).astype(BF16)
    d_along[...] = along
    unit, _ = norm_of(window[...].astype(F32))
    normed = matmul_nt(along, weight[...])

    @pl.when(step == 0)
    def _():
        first_sums[...] = jnp.zeros_like(first_sums)

    first_sums[0:1, :] += jnp.sum(normed * unit, axis=0, keepdims=True)
    first_sums[1:2, :] += jnp.sum(normed, axis=0, keepdims=True)
    half = width // 2
    for m in range(count):

        @pl.when(step == m)
        def _():
            d_normed[2 * m][...] = normed[:, :half].astype(BF16)
            d_normed[2 * m + 1][...] = normed[:, half:].astype(BF16)


def rows_back(count, where, order, d_heads, window, weight):
    length, width = window.shape
    rows = length // count
    heads_width = d_heads.shape[1]
    outs = [shape((length, heads_width), BF16)]
    outs += [shape((rows, width // 2), BF16) for _ in range(2 * count)]
    outs += [shape((8, width), F32)]
    return pl.pallas_call(
        functools.partial(rows_back_kernel, count),
        grid=(count,),
        in_specs=[
            scalar_spec(),
            whole_spec(order),
            whole_spec(d_heads),
            pl.BlockSpec((rows, width), lambda i: (i, 0)),
            whole_spec(weight),
        ],
        out_specs=[pl.BlockSpec((rows, heads_width), lambda i: (i, 0))]
        + [whole_spec(out) for out in outs[1:]],
        out_shape=outs,
        compiler_params=params(),
        cost_estimate=pl.CostEstimate(
            flops=2 * length * heads_width * (length + width),
            bytes_accessed=4 * length * (width + heads_width),
            transcendentals=0,
        ),
    )(where, order, d_heads, window, weight)


def pack_kernel(
    count, where, hidden, d_along, first_sums, sums, inner_sums, d_bias, d_rel, kept, away, grads
):
    here, core = where[0], where[1]
    step = pl.program_id(0)
    row_count = hidden.shape[1] // count
    key_width = d_rel.shape[1]
    terms = matmul_tn(hidden[...], d_along[...])

    @pl.when(step == 0)
    def _():
        for s in range(count):
            grads[s, :row_count, :] = terms[s * row_count : (s + 1) * row_count, :]

    @pl.when(step > 0)
    def _():
        for s in range(count):
            grads[s, :row_count, :] += terms[s * row_count : (s + 1) * row_count, :]

    @pl.when(step == pl.num_programs(0) - 1)
    def _():
        rel_rows = d_rel.shape[0] // count
        for s in range(count):
            at = slice(s * row_count, (s + 1) * row_count)
            grads[s, row_count:, :] = jnp.zeros((EXTRA, grads.shape[2]), F32)
            grads[s, row_count : row_count + 2, :row_count] = first_sums[0:2, at]
            grads[s, row_count + 2 : row_count + 6, :row_count] = sums[2:6, at]
            for j in range(2):
                part = slice((2 * s + j) * row_count, (2 * s + j + 1) * row_count)
                grads[s, row_count + 6 + j : row_count + 7 + j, :row_count] = inner_sums[0:1, part]
            for j in range(-(-rel_rows // EXTRA)):
                some = d_rel[s * rel_rows + j * EXTRA : s * rel_rows + min(rel_rows, (j + 1) * EXTRA), :]
                lane = row_count + j * key_width
                grads[s, row_count : row_count + some.shape[0], lane : lane + key_width] = some
        for s in range(count):

            @pl.when(here == s)
            def _():
                grads[s, row_count + 8 : row_count + 10, :key_width] = d_bias[0:2, :]

        half = kept.shape[1]
        kept[...] = grads[:, pl.ds(pl.multiple_of(core * half, 16), half), :].astype(BF16)
        away[...] = grads[:, pl.ds(pl.multiple_of((1 - core) * half, 16), half), :].astype(BF16)


def pack(count, where, hidden, d_along, *small):
    length, width = hidden.shape
    heads_width = d_along.shape[1]
    rows = math.gcd(768, length)
    packed = (count, width // count + EXTRA, heads_width)
    outs = [shape((count, packed[1] // 2, heads_width), BF16) for _ in range(2)]
    return pl.pallas_call(
        functools.partial(pack_kernel, count),
        grid=(length // rows,),
        in_specs=[
            scalar_spec(),
            pl.BlockSpec((rows, width), lambda i: (i, 0)),
            pl.BlockSpec((rows, heads_width), lambda i: (i, 0)),
        ]
        + [whole_spec(a) for a in small],
        out_specs=[whole_spec(out) for out in outs],
        out_shape=outs,
        scratch_shapes=[pltpu.VMEM(packed, F32)],
        compiler_params=params(),
        cost_estimate=pl.CostEstimate(
            flops=2 * length * heads_width * width,
            bytes_accessed=2 * length * (width + heads_width) + 8 * width * heads_width,
            transcendentals=0,
        ),
    )(where, hidden, d_along, *small)


def swap(array, mask, count):
    return lax.ppermute(array, "seq", [(i, i ^ mask) for i in range(count)])


def bit_orders(count):
    bits = [1 << k for k in range(count.bit_length() - 1)]
    return bits, bits[::-1]


def pin(*arrays):
    return lax.optimization_barrier(arrays)


def returned_kernel(count, where, order, *refs):
    parts, returned = refs[:-1], refs[-1]
    here = where[0]
    rows = parts[0].shape[0]
    bins = lax.broadcasted_iota(jnp.int32, (returned.shape[0], rows), 0)
    bins = bins + here * returned.shape[0]
    for k, part in enumerate(parts):
        shard = jnp.bitwise_xor(here, k // 2)
        picks = jnp.where(order[pl.ds(2 * shard + k % 2, 1), :] == bins, 1.0, 0.0).astype(BF16)
        term = matmul(picks, part[...])
        if k == 0:
            returned[...] = term
        else:
            returned[...] += term


def returned_rows(count, where, order, parts):
    rows, width = parts[0].shape
    vmem = pl.BlockSpec(memory_space=pltpu.VMEM)
    return pl.pallas_call(
        functools.partial(returned_kernel, count),
        in_specs=[scalar_spec()] + [vmem] * (1 + len(parts)),
        out_specs=vmem,
        out_shape=shape((2 * rows, width), F32),
        compiler_params=params(),
        cost_estimate=pl.CostEstimate(
            flops=4 * rows * rows * len(parts) * width,
            bytes_accessed=2 * rows * width * len(parts) + 8 * rows * width,
            transcendentals=0,
        ),
    )(where, order, *parts)


def unpack_kernel(count, row_count, key_width, *refs):
    where, mine, theirs, query, key, value, extra, whole = refs
    half = mine.shape[1]
    core = where[1]
    for c in range(2):

        @pl.when(core == c)
        def _():
            whole[:, c * half : (c + 1) * half, :] = mine[...]
            whole[:, (1 - c) * half : (2 - c) * half, :] = theirs[...]

    for out, at in ((query, 0), (key, key_width), (value, 2 * key_width)):
        size = out.shape[1] // count
        for s in range(count):
            rows = whole[s, :row_count, at : at + size]
            out[:, s * size : (s + 1) * size] = rows.astype(F32)
    extra[...] = whole[:, row_count:, :].astype(F32)


def unpack(where, parts, row_count, key_width, val_width):
    count, half, width = parts[0].shape
    vmem = pl.BlockSpec(memory_space=pltpu.VMEM)
    return pl.pallas_call(
        functools.partial(unpack_kernel, count, row_count, key_width),
        in_specs=[scalar_spec()] + [vmem] * 2,
        out_specs=[vmem] * 4,
        out_shape=[
            shape((row_count, count * key_width), F32),
            shape((row_count, count * key_width), F32),
            shape((row_count, count * val_width), F32),
            shape((count, EXTRA, width), F32),
        ],
        scratch_shapes=[pltpu.VMEM((count, 2 * half, width), BF16)],
        compiler_params=params(),
    )(where, *parts)


class Exchange:
    def __init__(self):
        self.new = {}


def pin_all(exchanges, *arrays):
    keys = [sorted(e.new) for e in exchanges]
    out = pin(*arrays, *[e.new[k] for e, ks in zip(exchanges, keys) for k in ks])
    at = len(arrays)
    for e, ks in zip(exchanges, keys):
        e.new = dict(zip(ks, out[at : at + len(ks)]))
        at += len(ks)
    return out[: len(arrays)]


def take_after(exchanges, array):
    pin_all(exchanges, array)


def pin_some(exchanges, *arrays):
    firsts = [max(e.new) for e in exchanges]
    out = pin(*arrays, *[e.new[k] for e, k in zip(exchanges, firsts)])
    for e, k, block in zip(exchanges, firsts, out[len(arrays) :]):
        e.new[k] = block
    return out[: len(arrays)]


class Gather(Exchange):
    def __init__(self, part, order, count):
        super().__init__()
        self.have, self.order, self.count, self.last = {0: part}, order, count, [0]

    def take(self):
        self.have.update(self.new)
        self.new = {}

    def send(self):
        self.take()
        new = {}
        for m in self.last:
            used = [k for k, bit in enumerate(self.order) if m & bit]
            for bit in self.order[max(used, default=-1) + 1 :]:
                new[m | bit] = swap(self.have[m], bit, self.count)
        self.new, self.last = new, sorted(new)


class Scatter(Exchange):
    def __init__(self, blocks, order, count):
        super().__init__()
        self.have, self.order, self.count, self.step = dict(enumerate(blocks)), order, count, 0

    def take(self):
        if self.new:
            bit = self.order[self.step - 1]
            self.have = {
                m: self.have[m].astype(F32) + self.new[m | bit].astype(F32)
                for m in self.have
                if not m & bit
            }
            self.new = {}

    def send(self):
        self.take()
        bit = self.order[self.step]
        self.new = {
            m: swap(self.have[m].astype(BF16), bit, self.count)
            for m in sorted(self.have, reverse=True)
            if m & bit
        }
        self.step += 1

    def rest(self):
        while self.step < len(self.order):
            self.send()
        self.take()
        return self.have[0]


class CubeSum(Exchange):
    def __init__(self, piece, count):
        super().__init__()
        self.total, self.step = piece, 0
        self.count, self.bits = count, count.bit_length() - 1

    def swap(self, array, bit):
        return lax.ppermute(array, "wz", [(i, i ^ bit) for i in range(self.count)])

    def mine(self, bit):
        return jnp.where(lax.axis_index("wz") & bit, 1, 0)

    def take(self):
        if self.new:
            came, at = self.new[0], self.step - 1
            if at < self.bits:
                half = came.shape[0]
                kept = lax.dynamic_slice_in_dim(self.total, self.mine(1 << at) * half, half, 0)
                self.total = (kept.astype(F32) + came.astype(F32)).astype(BF16)
            else:
                upper = self.mine(1 << (2 * self.bits - 1 - at)) == 1
                self.total = jnp.concatenate(
                    [jnp.where(upper, came, self.total), jnp.where(upper, self.total, came)], axis=0
                )
            self.new = {}

    def send(self):
        self.take()
        if self.step >= 2 * self.bits:
            return
        if self.step < self.bits:
            bit = 1 << self.step
            half = self.total.shape[0] // 2
            away = lax.dynamic_slice_in_dim(self.total, (1 - self.mine(bit)) * half, half, 0)
            self.new = {0: self.swap(away.astype(BF16), bit)}
        else:
            self.new = {0: self.swap(self.total, 1 << (2 * self.bits - 1 - self.step))}
        self.step += 1

    def rest(self):
        while self.step < 2 * self.bits:
            self.send()
        self.take()
        return self.total.astype(BF16)


class OtherCore(Exchange):
    def __init__(self, array):
        super().__init__()
        self.new = {0: other_core(array)}


def split_columns(blocks, count):
    half = blocks[0].shape[1] // 2
    return [
        Scatter([block[:, k * half : (k + 1) * half] for block in blocks], order, count)
        for k, order in enumerate(bit_orders(count))
    ]


def other_core(array):
    return lax.ppermute(array, "core", [(0, 1), (1, 0)])


def shards(
    seq_count,
    wz_count,
    inputs,
    bin_order,
    first_gain,
    first_shift,
    query_weight,
    key_weight,
    value_weight,
    bias_content,
    bias_position,
    relative_weight,
    out_weight,
    bias_out,
    second_gain,
    second_shift,
    inner_weight,
    bias_inner,
    outer_weight,
    bias_outer,
    grad_output,
):
    row_count, width = inputs.shape[1:]
    length = bin_order.shape[1]
    here = lax.axis_index("seq")
    core = lax.axis_index("core")
    where = jnp.stack([here, core]).astype(jnp.int32)
    row_start = here * row_count
    key_width = query_weight.shape[1] // seq_count
    val_width = value_weight.shape[1] // seq_count
    heads_width = 2 * key_width + val_width
    up, down = bit_orders(seq_count)

    others = [jnp.bitwise_xor(here, m) for m in range(seq_count)]
    along = jnp.concatenate(
        [other * row_count + jnp.arange(row_count, dtype=jnp.int32) for other in others]
    )

    def natural(rows):
        parts = rows.reshape(seq_count, row_count, -1)
        parts = [lax.dynamic_index_in_dim(parts, other, 0) for other in others]
        return jnp.concatenate(parts, axis=0).reshape(rows.shape)

    def halves(rows):
        half = rows.shape[0] // 2
        return [Gather(rows[:half], up, seq_count), Gather(rows[half:], down, seq_count)]

    def blocks_of(gathers):
        for g in gathers:
            g.take()
        return [g.have[m] for m in range(seq_count) for g in gathers]

    window_gathers = halves(inputs[0])
    for g in window_gathers:
        g.send()

    def by_head(weight):
        return weight.reshape(weight.shape[0], seq_count, -1)

    vectors = jnp.stack([first_gain, first_shift, bias_out, second_gain, second_shift, bias_outer])
    vectors = jnp.concatenate([vectors, bias_inner.reshape(2, row_count)], axis=0)
    vectors = jnp.pad(vectors, ((0, EXTRA - 8), (0, 0)))
    rel_rows = relative_weight.shape[0]
    rel_blocks = -(-rel_rows // EXTRA)
    rel_part = jnp.pad(by_head(relative_weight), ((0, rel_blocks * EXTRA - rel_rows), (0, 0), (0, 0)))
    rel_part = rel_part.reshape(rel_blocks, EXTRA, seq_count, key_width).transpose(2, 1, 0, 3)
    rel_part = rel_part.reshape(seq_count, EXTRA, -1)
    spare = heads_width - row_count - rel_part.shape[2]
    extra = jnp.concatenate(
        [
            jnp.broadcast_to(vectors[None], (seq_count,) + vectors.shape),
            jnp.pad(rel_part, ((0, 0), (0, 0), (0, spare))),
        ],
        axis=2,
    )
    mine = jnp.concatenate(
        [by_head(query_weight), by_head(key_weight), by_head(value_weight)], axis=2
    ).transpose(1, 0, 2)
    mine = jnp.concatenate([mine, extra], axis=1)
    half = mine.shape[1] // 2
    mine = lax.dynamic_slice_in_dim(mine, core * half, half, 1)

    def own_half(weight):
        half = weight.shape[0] // 2
        return lax.dynamic_slice_in_dim(weight, core * half, half, 0)

    inner_part, outer_part = own_half(inner_weight), own_half(outer_weight)
    mine, inner_part, outer_part = pin_all(window_gathers, mine, inner_part, outer_part)
    for step in range(1, len(up)):
        for g in window_gathers:
            g.send()
    weight_gathers = [
        Gather(inner_part, up, seq_count),
        Gather(outer_part, down, seq_count),
    ]
    for g in weight_gathers:
        g.send()
    mine = lax.all_to_all(mine, "seq", 0, 0, tiled=True)
    (mine,) = pin_all(window_gathers, mine)
    first = core == 0
    theirs = other_core(mine)
    attention_weight = jnp.concatenate(
        [jnp.where(first, mine, theirs), jnp.where(first, theirs, mine)], axis=1
    )
    table, table_back = basis_tables(jnp.asarray(basis_constants(length)), length)
    flat = attention_weight[:, row_count:]
    vectors = flat[:, :8, :row_count].astype(F32)
    inner_bias = vectors[:, 6:8].reshape(1, -1)
    vectors = vectors.transpose(1, 0, 2).reshape(8, width)
    rel = flat[:, :, row_count : row_count + rel_blocks * key_width]
    rel = rel.reshape(seq_count, EXTRA, rel_blocks, key_width).transpose(0, 2, 1, 3)
    rel = rel.reshape(seq_count, rel_blocks * EXTRA, key_width)[:, :rel_rows].reshape(REL, key_width)

    window_blocks = blocks_of(window_gathers)

    order = bin_order[0]
    placing = (order[:, None] == along[None, :]).astype(BF16)
    bias = jnp.concatenate([bias_content, bias_position])[None].astype(F32)
    window, hidden_one, in_bins, weight_whole = project(
        window_blocks, attention_weight, vectors, bias, row_count
    )
    placed_heads = matmul(placing, in_bins).astype(BF16)
    mixed, probs = attend(placed_heads, rel, table)
    (mixed,) = pin_all(weight_gathers, mixed)
    for step in range(1, len(up)):
        for g in weight_gathers:
            g.send()
    weight_parts = []
    for g, own in zip(weight_gathers, (inner_weight, outer_weight)):
        g.take()
        parts = [own]
        for m in range(1, seq_count):
            parts += [g.have[m], other_core(g.have[m])]
        weight_parts.append(parts)
    mixed_along = natural(mixed).reshape(seq_count, row_count, val_width)
    attended = [matmul(mixed_along[m], out_weight).astype(BF16) for m in range(seq_count)]
    attended = split_columns(attended, seq_count)
    for g in attended:
        g.send()
    own_order = lax.dynamic_slice_in_dim(order, row_start, row_count, 0)
    placed = matmul((own_order[:, None] == along[None, :]).astype(BF16), window)
    (placed,) = pin_all(attended, placed)
    attended = [g.rest() for g in attended]

    grad_rows = grad_output[0]
    layer_output, d_mixed_in, hidden_two, activated, d_inner, sums, inner_sums = feed_forward(
        where, placed, attended, grad_rows, vectors, inner_bias, *weight_parts
    )

    d_mixed_gathers = halves(d_mixed_in)
    for g in d_mixed_gathers:
        g.send()
    came_inner = other_core(half_gradient(seq_count, True, where, hidden_two, d_inner))
    outer_away = half_gradient(seq_count, False, where, activated, grad_rows)
    came_outer = other_core(outer_away)
    kept_inner = half_gradient(seq_count, True, where, hidden_two, d_inner, came_inner)
    kept_inner = pin_all(d_mixed_gathers, *kept_inner)
    for step in range(1, len(up)):
        for g in d_mixed_gathers:
            g.send()
    kept_outer = half_gradient(seq_count, False, where, activated, grad_rows, came_outer)
    kept = pin_all(d_mixed_gathers, *kept_inner, *kept_outer)
    d_mixed_blocks = blocks_of(d_mixed_gathers)
    count = seq_count
    inner_sums_of, outer_sums_of = [
        [
            Scatter([kept[2 * (k * count + m) + side] for m in range(count)], bits, count)
            for side, bits in enumerate((up, down))
        ]
        for k in range(2)
    ]
    for g in inner_sums_of:
        g.send()

    d_attended, out_away, grad_out_w = mixed_back(
        seq_count, where, mixed, out_weight, d_mixed_blocks
    )
    (d_attended,) = pin_some(inner_sums_of, d_attended)
    out_core = OtherCore(out_away)

    def send_all(exchanges):
        for exchange in exchanges:
            exchange.send()

    def scatter_windows(piece):
        return lax.psum_scatter(piece.astype(BF16), "wz", scatter_dimension=0, tiled=True)

    def gather_windows(piece):
        return lax.all_gather(piece, ("core", "wz"), axis=0, tiled=True)

    def joined_sum(scatters):
        return jnp.concatenate([g.rest().astype(BF16) for g in scatters], axis=1)

    (d_attended,) = pin_all([out_core], d_attended)
    out_sum = scatter_windows(grad_out_w + out_core.new[0].astype(F32))
    back = attend_back(0, placed_heads, rel, table_back, mixed, d_attended, probs)
    *back, out_sum = pin_all(inner_sums_of, *back, out_sum)
    out_sum = gather_windows(out_sum)
    for step in range(1, len(up)):
        send_all(inner_sums_of)
    send_all(outer_sums_of)
    for head in range(1, key_width // KEY):
        back = attend_back(head, placed_heads, rel, table_back, mixed, d_attended, probs, back)
    *back, out_sum = pin_all(inner_sums_of, *back, out_sum)
    d_heads, d_rel, d_bias = back
    inner_sum = scatter_windows(joined_sum(inner_sums_of))
    d_along, *d_normed, first_sums = rows_back(
        seq_count, where, order[None], d_heads, window, weight_whole
    )
    out = pin_all(outer_sums_of, d_along, *d_normed)
    d_along, d_normed = out[0], out[1:]
    for step in range(1, len(up)):
        send_all(outer_sums_of)
    arrived = [
        Scatter([d_normed[2 * m + side] for m in range(count)], bits, count)
        for side, bits in enumerate((up, down))
    ]
    results = pack(
        seq_count, where, hidden_one, d_along, first_sums, sums, inner_sums, d_bias, d_rel
    )
    *results, inner_sum = pin_all(outer_sums_of, *results, inner_sum)
    packed_core = OtherCore(results[1])
    outer_sum = scatter_windows(joined_sum(outer_sums_of))
    inner_sum = gather_windows(inner_sum)
    (packed,) = pin_all([packed_core], results[0])
    packed = (packed.astype(F32) + packed_core.new[0].astype(F32)).astype(BF16)
    packed_shape = packed.shape
    packed = lax.all_to_all(packed, "seq", 0, 0, tiled=True)
    send_all(arrived)
    take_after(arrived, packed)
    packed_cube = CubeSum(packed.reshape(-1, packed_shape[2]), wz_count)
    packed_cube.send()
    (outer_sum,) = pin_all([packed_cube], outer_sum)
    outer_sum = gather_windows(outer_sum)
    packed_cube.send()
    d_mixed_blocks = pin_all(arrived, *d_mixed_blocks)
    for step in range(1, len(up)):
        send_all(arrived)
    returned = returned_rows(
        seq_count, where, order.reshape(2 * seq_count, row_count // 2), d_mixed_blocks
    )
    (returned,) = pin_all([packed_cube], returned)
    packed_cube.send()
    own_unit, own_scale = norm_of(inputs[0].astype(F32))
    arrived = jnp.concatenate([g.rest() for g in arrived], axis=1)
    grad_inputs = norm_back(own_unit, own_scale, vectors[0:1], arrived) + returned

    def both_halves(pieces, axis):
        half = pieces.shape[0] // 2
        return jnp.concatenate([pieces[:half], pieces[half:]], axis=axis).astype(F32)

    grad_out_w = both_halves(out_sum, 0)
    grad_inputs, grad_out_w = pin_all([packed_cube], grad_inputs, grad_out_w)
    packed_cube.send()
    grad_inner_w = both_halves(inner_sum, 1)
    grad_outer_w = both_halves(outer_sum, 0)
    packed = packed_cube.rest().reshape(packed_shape)
    grad_query_w, grad_key_w, grad_value_w, flat = unpack(
        where, (packed, other_core(packed)), row_count, key_width, val_width
    )
    small = jnp.sum(flat[:, :16, :row_count], axis=0)
    g_gain_one, g_shift_one, g_out_b, g_gain_two, g_shift_two, g_outer_b = small[:6]
    g_inner_b = small[6:8].reshape(-1)
    grad_rel = flat[:, :, row_count : row_count + rel_blocks * key_width]
    grad_rel = grad_rel.reshape(seq_count, EXTRA, rel_blocks, key_width).transpose(2, 1, 0, 3)
    grad_rel = grad_rel.reshape(rel_blocks * EXTRA, -1)[:rel_rows]
    return (
        layer_output[None],
        grad_inputs[None],
        g_gain_one,
        g_shift_one,
        grad_query_w,
        grad_key_w,
        grad_value_w,
        small[8, :key_width],
        small[9, :key_width],
        grad_rel,
        grad_out_w,
        g_out_b,
        g_gain_two,
        g_shift_two,
        grad_inner_w,
        g_inner_b,
        grad_outer_w,
        g_outer_b,
    )


def solution(mesh):
    seq_count = mesh.shape["seq"]
    devices = mesh.devices.reshape(seq_count, -1, 2)
    split_mesh = Mesh(devices, ("seq", "wz", "core"))
    rows = P(("wz", "core"), "seq", None)
    vector = P("seq")
    matrix = P("seq", None)
    weights = (
        vector,
        vector,
        matrix,
        matrix,
        matrix,
        vector,
        vector,
        matrix,
        matrix,
        vector,
        vector,
        vector,
        matrix,
        vector,
        matrix,
        vector,
    )
    return jax.shard_map(
        functools.partial(shards, seq_count, mesh.shape["win"] // 2),
        mesh=split_mesh,
        in_specs=(rows, P(("wz", "core"), None)) + weights + (rows,),
        out_specs=(rows, rows) + weights,
        check_vma=False,
    )
```

```python
import functools
import math

import jax
import jax.numpy as jnp
import numpy as np
from jax import lax
from jax.experimental import pallas as pl
from jax.experimental.pallas import tpu as pltpu
from jax.sharding import Mesh
from jax.sharding import PartitionSpec as P

HEADS = 8
KEY = 64
VAL = 192
REL = 192
BF16 = jnp.bfloat16
F32 = jnp.float32
VMEM_LIMIT = 56 * 2**20
EXTRA = 32


def matmul(a, b):
    return lax.dot_general(a, b, (((1,), (0,)), ((), ())), preferred_element_type=F32)


def matmul_nt(a, b):
    return lax.dot_general(a, b, (((1,), (1,)), ((), ())), preferred_element_type=F32)


def matmul_tn(a, b):
    return lax.dot_general(a, b, (((0,), (0,)), ((), ())), preferred_element_type=F32)


def head_part(rows, head):
    lanes = lax.broadcasted_iota(jnp.int32, rows.shape, 1)
    inside = (lanes >= head * KEY) & (lanes < (head + 1) * KEY)
    return jnp.where(inside, rows, jnp.zeros_like(rows))


def head_columns(key_width):
    return [slice(k * key_width, (k + 1) * key_width) for k in range(3)]


def attend_kernel(heads, rows, placed, rel, table, mixed, probs):
    length = placed.shape[0]
    key_width = heads * KEY
    content_at, position_at, keys_at = head_columns(key_width)
    first = pl.program_id(0) * rows
    here = pl.ds(pl.multiple_of(first, rows), rows)
    basis = table[:, pl.ds(pl.multiple_of(length - rows - first, rows), length + rows)]
    content, position, keys = placed[here, content_at], placed[here, position_at], placed[:, keys_at]
    parts = []
    for head in range(heads):
        q_basis = matmul_nt(head_part(position, head), rel[...]).astype(BF16)
        grid = matmul(q_basis, basis)
        shifted = pltpu.roll(grid, 0, 1, stride=1, stride_axis=0)[:, rows:]
        scores = matmul_nt(head_part(content, head), keys) + shifted
        top = jnp.max(scores, axis=1, keepdims=True)
        weights = jnp.exp(scores - top)
        total = jnp.sum(weights, axis=1, keepdims=True)
        prob = (weights * (1.0 / total)).astype(BF16)
        probs[head] = prob
        values_at = 3 * key_width + head * VAL
        parts.append(matmul(prob, placed[:, values_at : values_at + VAL]))
    mixed[...] = jnp.concatenate(parts, axis=1).astype(BF16)


def attend(placed, rel, table):
    length = placed.shape[0]
    heads = rel.shape[1] // KEY
    rows = math.gcd(256, length)
    whole = lambda array: pl.BlockSpec(array.shape, lambda i: (0, 0))
    return pl.pallas_call(
        functools.partial(attend_kernel, heads, rows),
        grid=(length // rows,),
        in_specs=[whole(placed), whole(rel), whole(table)],
        out_specs=[
            pl.BlockSpec((rows, heads * VAL), lambda i: (i, 0)),
            pl.BlockSpec((heads, rows, length), lambda i: (0, i, 0)),
        ],
        out_shape=[
            jax.ShapeDtypeStruct((length, heads * VAL), BF16),
            jax.ShapeDtypeStruct((heads, length, length), BF16),
        ],
        compiler_params=pltpu.CompilerParams(vmem_limit_bytes=VMEM_LIMIT),
        cost_estimate=pl.CostEstimate(
            flops=2 * heads * length * length * 1024,
            bytes_accessed=2 * heads * length * length + 8 * length * heads * VAL,
            transcendentals=heads * length * length,
        ),
    )(placed, rel, table)


def attend_back_kernel(heads, head, rows, *refs):
    placed, rel, table, flip, mixed, d_mixed, probs = refs[:7]
    before = refs[7:-5]
    d_heads, d_rel, d_bias, keys_sum, values_sum = refs[-5:]
    length = placed.shape[0]
    key_width = heads * KEY
    content_at, position_at, keys_at = head_columns(key_width)
    step = pl.program_id(0)

    @pl.when(step == 0)
    def _():
        keys_sum[...] = jnp.zeros_like(keys_sum)
        values_sum[...] = jnp.zeros_like(values_sum)
        for k, out in enumerate((d_heads, d_rel, d_bias)):
            out[...] = before[k][...] if before else jnp.zeros_like(out)

    first = pl.multiple_of(step * rows, rows)
    here = pl.ds(first, rows)
    basis = table[:, pl.ds(first, length + rows)]
    content, position, keys = placed[here, content_at], placed[here, position_at], placed[:, keys_at]
    blocks = length // rows
    columns = slice(head * VAL, (head + 1) * VAL)
    values_at = 3 * key_width + head * VAL
    d_part = d_mixed[:, columns]
    delta = jnp.sum(d_part.astype(F32) * mixed[:, columns].astype(F32), axis=1, keepdims=True)
    prob = probs[0]
    values_sum[...] += matmul_tn(d_part, prob)
    d_prob = matmul_nt(d_part, placed[:, values_at : values_at + VAL])
    d_score = (prob.astype(F32) * (d_prob - delta)).astype(BF16)
    keys_sum[...] += matmul_tn(head_part(content, head), d_score)
    d_content = head_part(matmul(d_score, keys), head)
    turned = [
        matmul(d_score[:, (blocks - 1 - b) * rows : (blocks - b) * rows], flip[...])
        for b in range(blocks)
    ]
    turned = jnp.concatenate(turned + [jnp.zeros((rows, rows), F32)], axis=1)
    d_grid = pltpu.roll(turned, 0, 1, stride=1, stride_axis=0).astype(BF16)
    d_basis = matmul_nt(d_grid, basis).astype(BF16)
    d_position = head_part(matmul(d_basis, rel[...]), head)
    d_rel[...] += matmul_tn(d_basis, head_part(position, head))
    d_heads[here, :key_width] += ((d_content + d_position) * KEY ** (-0.5)).astype(BF16)
    d_bias[0:1, :] += jnp.sum(d_content, axis=0, keepdims=True)
    d_bias[1:2, :] += jnp.sum(d_position, axis=0, keepdims=True)

    @pl.when(step == blocks - 1)
    def _():
        d_heads[:, key_width : 2 * key_width] += keys_sum[...].T.astype(BF16)
        values_to = 2 * key_width + head * VAL
        d_heads[:, values_to : values_to + VAL] = values_sum[...].T.astype(BF16)


def attend_back(head, placed, rel, table, mixed, d_mixed, probs, before=()):
    length = placed.shape[0]
    key_width = rel.shape[1]
    heads = key_width // KEY
    val_width = heads * VAL
    rows = math.gcd(256, length)
    at = jnp.arange(rows)
    flip = (at[:, None] + at[None, :] == rows - 1).astype(BF16)
    block = lambda width: pl.BlockSpec((rows, width), lambda i: (i, 0))
    outs = [
        shape((length, 2 * key_width + val_width), BF16),
        shape((REL, key_width), F32),
        shape((8, key_width), F32),
    ]
    return pl.pallas_call(
        functools.partial(attend_back_kernel, heads, head, rows),
        grid=(length // rows,),
        in_specs=[
            whole_spec(placed),
            whole_spec(rel),
            whole_spec(table),
            whole_spec(flip),
            block(val_width),
            block(val_width),
            pl.BlockSpec((1, rows, length), lambda i: (head, i, 0)),
        ]
        + [whole_spec(array) for array in before],
        out_specs=[whole_spec(out) for out in outs],
        out_shape=outs,
        scratch_shapes=[
            pltpu.VMEM((key_width, length), F32),
            pltpu.VMEM((VAL, length), F32),
        ],
        compiler_params=pltpu.CompilerParams(vmem_limit_bytes=VMEM_LIMIT),
        cost_estimate=pl.CostEstimate(
            flops=2 * length * length * 1536,
            bytes_accessed=2 * length * length + 16 * length * val_width,
            transcendentals=0,
        ),
    )(placed, rel, table, flip, mixed, d_mixed, probs, *before)


def norm_back(unit, scale, gain, grad):
    scaled = grad * gain
    mean_one = jnp.mean(scaled, axis=-1, keepdims=True)
    mean_two = jnp.mean(scaled * unit, axis=-1, keepdims=True)
    return (scaled - mean_one - unit * mean_two) * scale


def whole_spec(array):
    zeros = (0,) * len(array.shape)
    return pl.BlockSpec(array.shape, lambda *_: zeros)


def scalar_spec():
    return pl.BlockSpec(memory_space=pltpu.SMEM)


def params(**more):
    return pltpu.CompilerParams(vmem_limit_bytes=VMEM_LIMIT, **more)


def shape(dims, dtype):
    return jax.ShapeDtypeStruct(tuple(dims), dtype)


def basis_constants(window_len):
    features = REL // 6
    f = np.arange(features, dtype=np.float64)
    half_life = 2.0 ** (3.0 + f * (math.log2(window_len) - 3.0) / (features - 1))
    spread = window_len / (2.0 * features)
    first = window_len / features
    centres = first + f * (window_len - first) / (features - 1)
    concentration = (centres / spread) ** 2
    rate = centres / spread**2
    offset = concentration * np.log(rate) - np.array([math.lgamma(c) for c in concentration])
    columns = [math.log(2.0) / half_life, 2.0 ** (f + 1) - 1.0, concentration - 1.0, rate, offset]
    columns += [np.zeros(features)] * 3
    return np.stack(columns, axis=1).astype(np.float32)


def table_kernel(length, constants, forth, back):
    features = REL // 6
    decay, inside_below, power, rate, offset = [constants[:, k : k + 1] for k in range(5)]

    def gamma(distance):
        logged = power * jnp.log(jnp.maximum(distance, 1.0)) - rate * distance + offset
        return jnp.where(distance == 0.0, 0.0, jnp.exp(logged)) + 1e-08

    every = lax.broadcasted_iota(jnp.int32, (1, length), 1).astype(F32)
    peak = jnp.max(gamma(every), axis=1, keepdims=True)
    lanes = lax.broadcasted_iota(jnp.int32, (1, 2 * length), 1).astype(F32)
    for table, signed in ((forth, lanes - length), (back, length - 1 - lanes)):
        distance = jnp.abs(signed)
        sign = jnp.where(signed > 0, 1.0, jnp.where(signed < 0, -1.0, 0.0))
        parts = (
            jnp.exp(-decay * distance),
            jnp.where(inside_below > distance, 1.0, 0.0),
            gamma(distance) / peak,
        )
        for k, part in enumerate(parts):
            table[k * features : (k + 1) * features, :] = part.astype(BF16)
            table[(3 + k) * features : (4 + k) * features, :] = (sign * part).astype(BF16)


def basis_tables(constants, length):
    out = shape((REL, 2 * length), BF16)
    return pl.pallas_call(
        functools.partial(table_kernel, length),
        out_shape=[out, out],
        compiler_params=params(),
    )(constants)


def norm_of(rows):
    centre = rows - jnp.mean(rows, axis=1, keepdims=True)
    scale = lax.rsqrt(jnp.mean(centre * centre, axis=1, keepdims=True) + 1e-05)
    return centre * scale, scale


def project_kernel(blocks, row_count, *refs):
    parts, (weight, vectors, bias, window, hidden, heads, flat, block) = refs[:blocks], refs[blocks:]
    step = pl.program_id(0)

    @pl.when(step == 0)
    def _():
        for s in range(weight.shape[0]):
            flat[s * row_count : (s + 1) * row_count, :] = weight[s, :row_count, :]

    for k in range(blocks):

        @pl.when(step == k)
        def _():
            block[...] = parts[k][...]

    window[...] = block[...]
    unit, _ = norm_of(block[...].astype(F32))
    normed = (unit * vectors[0:1, :] + vectors[1:2, :]).astype(BF16)
    hidden[...] = normed
    total = matmul(normed, flat[...])
    key_width = bias.shape[1] // 2
    query = total[:, :key_width] * KEY ** (-0.5)
    heads[:, :key_width] = (query + bias[0:1, :key_width]).astype(BF16)
    heads[:, key_width : 2 * key_width] = (query + bias[0:1, key_width:]).astype(BF16)
    heads[:, 2 * key_width :] = total[:, key_width:].astype(BF16)


def project(parts, weight, vectors, bias, row_count):
    blocks = len(parts)
    rows, width = parts[0].shape
    heads_width = weight.shape[2] + bias.shape[1] // 2
    out = lambda w: pl.BlockSpec((rows, w), lambda i: (i, 0))
    return pl.pallas_call(
        functools.partial(project_kernel, blocks, row_count),
        grid=(blocks,),
        in_specs=[whole_spec(a) for a in (*parts, weight, vectors, bias)],
        out_specs=[
            out(width),
            out(width),
            out(heads_width),
            pl.BlockSpec((width, weight.shape[2]), lambda i: (0, 0)),
        ],
        out_shape=[shape((blocks * rows, w), BF16) for w in (width, width, heads_width)]
        + [shape((width, weight.shape[2]), BF16)],
        scratch_shapes=[pltpu.VMEM((rows, width), BF16)],
        compiler_params=params(),
        cost_estimate=pl.CostEstimate(
            flops=2 * blocks * rows * width * heads_width,
            bytes_accessed=8 * blocks * rows * width,
            transcendentals=0,
        ),
    )(*parts, weight, vectors, bias)


def feed_kernel(count, chunk, *refs):
    parts = 2 * (2 * count - 1)
    where, placed, attended_a, attended_b, grad_rows, vectors, inner_bias = refs[:7]
    weights = refs[7 : 7 + parts]
    layer_output, d_mixed, hidden, activated, d_inner, sums, inner_sums = refs[7 + parts : 14 + parts]
    inner_whole, outer_whole, residual, unit, back, outer_sum, sems = refs[14 + parts :]
    here, core = where[0], where[1]
    copies = []
    for k, whole in enumerate((inner_whole, outer_whole)):
        mine = weights[k * (2 * count - 1) : (k + 1) * (2 * count - 1)]
        size = whole.shape[0] // count
        half = size // 2
        moves = [(mine[0], here * size, size)]
        for m in range(1, count):
            start = jnp.bitwise_xor(here, m) * size
            moves.append((mine[2 * m - 1], start + core * half, half))
            moves.append((mine[2 * m], start + (1 - core) * half, half))
        started = []
        for source, start, rows in moves:
            target = whole.at[pl.ds(pl.multiple_of(start, 16), rows), :]
            copy = pltpu.make_async_copy(source, target, sems.at[k, len(started)])
            copy.start()
            started.append(copy)
        copies.append(started)
    rows, width = placed.shape
    half = width // 2
    residual[:, :half] = placed[:, :half] + attended_a[...] + vectors[2:3, :half]
    residual[:, half:] = placed[:, half:] + attended_b[...] + vectors[2:3, half:]
    normed, scale = norm_of(residual[...])
    unit[...] = normed
    hidden[...] = (normed * vectors[3:4, :] + vectors[4:5, :]).astype(BF16)
    for started in copies:
        for copy in started:
            copy.wait()
    ff = outer_whole.shape[0]
    for c in range(ff // chunk):
        at = slice(c * chunk, (c + 1) * chunk)
        inner = matmul(hidden[...], inner_whole[:, at]) + inner_bias[0:1, at]
        below = 0.5 * (1.0 + lax.erf(inner * (0.5**0.5)))
        slope = below + inner * jnp.exp(-0.5 * inner * inner) * (0.5 / math.pi) ** 0.5
        active = (inner * below).astype(BF16)
        activated[:, at] = active
        grad = (matmul_nt(grad_rows[...], outer_whole[at, :]) * slope).astype(BF16)
        d_inner[:, at] = grad
        inner_sums[:, at] = jnp.sum(grad.astype(F32), axis=0, keepdims=True)
        back_term = matmul_nt(grad, inner_whole[:, at])
        outer_term = matmul(active, outer_whole[at, :])
        if c == 0:
            back[...] = back_term
            outer_sum[...] = outer_term
        else:
            back[...] += back_term
            outer_sum[...] += outer_term
    layer_output[...] = (residual[...] + outer_sum[...] + vectors[5:6, :]).astype(BF16)
    grad, normed = back[...], unit[...]
    dy = grad_rows[...].astype(F32)
    scaled = grad * vectors[3:4, :]
    mean_one = jnp.mean(scaled, axis=1, keepdims=True)
    mean_two = jnp.mean(scaled * normed, axis=1, keepdims=True)
    mixed_in = (dy + (scaled - mean_one - normed * mean_two) * scale).astype(BF16)
    d_mixed[...] = mixed_in
    sums[...] = jnp.zeros_like(sums)
    sums[2:3, :] = jnp.sum(mixed_in.astype(F32), axis=0, keepdims=True)
    sums[3:4, :] = jnp.sum(grad * normed, axis=0, keepdims=True)
    sums[4:5, :] = jnp.sum(grad, axis=0, keepdims=True)
    sums[5:6, :] = jnp.sum(dy, axis=0, keepdims=True)


def feed_forward(where, placed, attended, grad_rows, vectors, inner_bias, inner_parts, outer_parts):
    rows, width = placed.shape
    ff = inner_bias.shape[1]
    count = (len(inner_parts) + 1) // 2
    chunk = math.gcd(512, ff)
    weights = (*inner_parts, *outer_parts)
    small = (placed, *attended, grad_rows, vectors, inner_bias)
    outs = [
        shape((rows, width), BF16),
        shape((rows, width), BF16),
        shape((rows, width), BF16),
        shape((rows, ff), BF16),
        shape((rows, ff), BF16),
        shape((8, width), F32),
        shape((1, ff), F32),
    ]
    return pl.pallas_call(
        functools.partial(feed_kernel, count, chunk),
        in_specs=[scalar_spec()]
        + [pl.BlockSpec(memory_space=pltpu.VMEM) for _ in small]
        + [pl.BlockSpec(memory_space=pl.ANY) for _ in weights],
        out_specs=[pl.BlockSpec(memory_space=pltpu.VMEM) for _ in outs],
        out_shape=outs,
        scratch_shapes=[
            pltpu.VMEM((width, ff), BF16),
            pltpu.VMEM((ff, width), BF16),
            pltpu.VMEM((rows, width), F32),
            pltpu.VMEM((rows, width), F32),
            pltpu.VMEM((rows, width), F32),
            pltpu.VMEM((rows, width), F32),
            pltpu.SemaphoreType.DMA((2, 2 * count - 1)),
        ],
        compiler_params=params(),
        cost_estimate=pl.CostEstimate(
            flops=8 * rows * width * ff,
            bytes_accessed=4 * width * ff + 40 * rows * width,
            transcendentals=2 * rows * ff,
        ),
    )(where, *small, *weights)


def columns_at(ref, index, size, scratch):
    if size % 128 == 0:
        return ref[:, pl.ds(pl.multiple_of(index * size, 128), size)]
    for k in range(ref.shape[1] // size):

        @pl.when(index == k)
        def _():
            scratch[...] = ref[:, k * size : (k + 1) * size]

    return scratch[...]


def half_kernel(count, split, away, where, left, right, *refs):
    here, core = where[0], where[1]
    side = 1 - core if away else core
    shard = jnp.bitwise_xor(here, pl.program_id(0))
    if split:
        some = columns_at(left, shard, left.shape[1] // count, refs[-1])
        half = right.shape[1] // 2
        other = right[:, pl.ds(pl.multiple_of(side * half, 128), half)]
    else:
        some = columns_at(left, 2 * shard + side, left.shape[1] // count // 2, refs[-1])
        other = right[...]
    result = matmul_tn(some, other)
    if away:
        refs[0][0] = result.astype(BF16)
        return
    came, outs = refs[0], refs[1:-1]
    result += came[0].astype(F32)
    width = result.shape[1] // 2
    for m in range(count):

        @pl.when(pl.program_id(0) == m)
        def _():
            outs[2 * m][...] = result[:, :width].astype(BF16)
            outs[2 * m + 1][...] = result[:, width:].astype(BF16)


def half_gradient(count, split, where, left, right, came=None):
    away = came is None
    rows = left.shape[1] // count // (1 if split else 2)
    width = right.shape[1] // (2 if split else 1)
    block = pl.BlockSpec((1, rows, width), lambda i: (i, 0, 0))
    if away:
        outs, out_specs = shape((count, rows, width), BF16), block
    else:
        outs = [shape((rows, width // 2), BF16) for _ in range(2 * count)]
        out_specs = [whole_spec(out) for out in outs]
    return pl.pallas_call(
        functools.partial(half_kernel, count, split, away),
        grid=(count,),
        in_specs=[scalar_spec(), whole_spec(left), whole_spec(right)] + ([] if away else [block]),
        out_specs=out_specs,
        out_shape=outs,
        scratch_shapes=[pltpu.VMEM((left.shape[0], rows), BF16)],
        compiler_params=params(),
        cost_estimate=pl.CostEstimate(
            flops=2 * left.shape[0] * count * rows * width,
            bytes_accessed=4 * count * rows * width + 4 * left.shape[0] * left.shape[1],
            transcendentals=0,
        ),
    )(where, left, right, *(() if away else (came,)))


def mixed_back_kernel(count, parts_count, *refs):
    where, mixed, weight = refs[:3]
    parts = refs[3 : 3 + parts_count]
    d_attended, out_away, out_kept, out_sum = refs[3 + parts_count :]
    here, core = where[0], where[1]
    rows = parts[0].shape[0]
    for k, part in enumerate(parts):
        start = jnp.bitwise_xor(here, k // 2) * (2 * rows) + (k % 2) * rows
        at = pl.ds(pl.multiple_of(start, 32), rows)
        d_attended[at, :] = matmul_nt(part[...], weight[...]).astype(BF16)
        term = matmul_tn(mixed[at, :], part[...])
        if k == 0:
            out_sum[...] = term
        else:
            out_sum[...] += term
    half = out_kept.shape[0]
    out_kept[...] = out_sum[pl.ds(pl.multiple_of(core * half, 32), half), :]
    out_away[...] = out_sum[pl.ds(pl.multiple_of((1 - core) * half, 32), half), :].astype(BF16)


def mixed_back(count, where, mixed, weight, parts):
    length, val_width = mixed.shape
    width = weight.shape[1]
    vmem = pl.BlockSpec(memory_space=pltpu.VMEM)
    return pl.pallas_call(
        functools.partial(mixed_back_kernel, count, len(parts)),
        in_specs=[scalar_spec()] + [vmem] * (2 + len(parts)),
        out_specs=[vmem] * 3,
        out_shape=[
            shape((length, val_width), BF16),
            shape((val_width // 2, width), BF16),
            shape((val_width // 2, width), F32),
        ],
        scratch_shapes=[pltpu.VMEM((val_width, width), F32)],
        compiler_params=params(),
        cost_estimate=pl.CostEstimate(
            flops=4 * length * val_width * width,
            bytes_accessed=2 * length * (width + 2 * val_width),
            transcendentals=0,
        ),
    )(where, mixed, weight, *parts)


def rows_back_kernel(count, where, order, d_heads, window, weight, d_along, *refs):
    d_normed, first_sums = refs[:-1], refs[-1]
    here = where[0]
    step = pl.program_id(0)
    rows, width = window.shape
    length = order.shape[1]
    bins = lax.broadcasted_iota(jnp.int32, (rows, length), 0) + jnp.bitwise_xor(here, step) * rows
    picks = jnp.where(order[0:1, :] == bins, 1.0, 0.0).astype(BF16)
    along = matmul(picks, d_heads[...]).astype(BF16)
    d_along[...] = along
    unit, _ = norm_of(window[...].astype(F32))
    normed = matmul_nt(along, weight[...])

    @pl.when(step == 0)
    def _():
        first_sums[...] = jnp.zeros_like(first_sums)

    first_sums[0:1, :] += jnp.sum(normed * unit, axis=0, keepdims=True)
    first_sums[1:2, :] += jnp.sum(normed, axis=0, keepdims=True)
    half = width // 2
    for m in range(count):

        @pl.when(step == m)
        def _():
            d_normed[2 * m][...] = normed[:, :half].astype(BF16)
            d_normed[2 * m + 1][...] = normed[:, half:].astype(BF16)


def rows_back(count, where, order, d_heads, window, weight):
    length, width = window.shape
    rows = length // count
    heads_width = d_heads.shape[1]
    outs = [shape((length, heads_width), BF16)]
    outs += [shape((rows, width // 2), BF16) for _ in range(2 * count)]
    outs += [shape((8, width), F32)]
    return pl.pallas_call(
        functools.partial(rows_back_kernel, count),
        grid=(count,),
        in_specs=[
            scalar_spec(),
            whole_spec(order),
            whole_spec(d_heads),
            pl.BlockSpec((rows, width), lambda i: (i, 0)),
            whole_spec(weight),
        ],
        out_specs=[pl.BlockSpec((rows, heads_width), lambda i: (i, 0))]
        + [whole_spec(out) for out in outs[1:]],
        out_shape=outs,
        compiler_params=params(),
        cost_estimate=pl.CostEstimate(
            flops=2 * length * heads_width * (length + width),
            bytes_accessed=4 * length * (width + heads_width),
            transcendentals=0,
        ),
    )(where, order, d_heads, window, weight)


def pack_kernel(
    count, where, hidden, d_along, first_sums, sums, inner_sums, d_bias, d_rel, kept, away, grads
):
    here, core = where[0], where[1]
    step = pl.program_id(0)
    row_count = hidden.shape[1] // count
    key_width = d_rel.shape[1]
    terms = matmul_tn(hidden[...], d_along[...])

    @pl.when(step == 0)
    def _():
        for s in range(count):
            grads[s, :row_count, :] = terms[s * row_count : (s + 1) * row_count, :]

    @pl.when(step > 0)
    def _():
        for s in range(count):
            grads[s, :row_count, :] += terms[s * row_count : (s + 1) * row_count, :]

    @pl.when(step == pl.num_programs(0) - 1)
    def _():
        rel_rows = d_rel.shape[0] // count
        for s in range(count):
            at = slice(s * row_count, (s + 1) * row_count)
            grads[s, row_count:, :] = jnp.zeros((EXTRA, grads.shape[2]), F32)
            grads[s, row_count : row_count + 2, :row_count] = first_sums[0:2, at]
            grads[s, row_count + 2 : row_count + 6, :row_count] = sums[2:6, at]
            for j in range(2):
                part = slice((2 * s + j) * row_count, (2 * s + j + 1) * row_count)
                grads[s, row_count + 6 + j : row_count + 7 + j, :row_count] = inner_sums[0:1, part]
            for j in range(-(-rel_rows // EXTRA)):
                some = d_rel[s * rel_rows + j * EXTRA : s * rel_rows + min(rel_rows, (j + 1) * EXTRA), :]
                lane = row_count + j * key_width
                grads[s, row_count : row_count + some.shape[0], lane : lane + key_width] = some
        for s in range(count):

            @pl.when(here == s)
            def _():
                grads[s, row_count + 8 : row_count + 10, :key_width] = d_bias[0:2, :]

        half = kept.shape[1]
        kept[...] = grads[:, pl.ds(pl.multiple_of(core * half, 16), half), :].astype(BF16)
        away[...] = grads[:, pl.ds(pl.multiple_of((1 - core) * half, 16), half), :].astype(BF16)


def pack(count, where, hidden, d_along, *small):
    length, width = hidden.shape
    heads_width = d_along.shape[1]
    rows = math.gcd(768, length)
    packed = (count, width // count + EXTRA, heads_width)
    outs = [shape((count, packed[1] // 2, heads_width), BF16) for _ in range(2)]
    return pl.pallas_call(
        functools.partial(pack_kernel, count),
        grid=(length // rows,),
        in_specs=[
            scalar_spec(),
            pl.BlockSpec((rows, width), lambda i: (i, 0)),
            pl.BlockSpec((rows, heads_width), lambda i: (i, 0)),
        ]
        + [whole_spec(a) for a in small],
        out_specs=[whole_spec(out) for out in outs],
        out_shape=outs,
        scratch_shapes=[pltpu.VMEM(packed, F32)],
        compiler_params=params(),
        cost_estimate=pl.CostEstimate(
            flops=2 * length * heads_width * width,
            bytes_accessed=2 * length * (width + heads_width) + 8 * width * heads_width,
            transcendentals=0,
        ),
    )(where, hidden, d_along, *small)


def swap(array, mask, count):
    return lax.ppermute(array, "seq", [(i, i ^ mask) for i in range(count)])


def bit_orders(count):
    bits = [1 << k for k in range(count.bit_length() - 1)]
    return bits, bits[::-1]


def pin(*arrays):
    return lax.optimization_barrier(arrays)


def returned_kernel(count, where, order, *refs):
    parts, returned = refs[:-1], refs[-1]
    here = where[0]
    rows = parts[0].shape[0]
    bins = lax.broadcasted_iota(jnp.int32, (returned.shape[0], rows), 0)
    bins = bins + here * returned.shape[0]
    for k, part in enumerate(parts):
        shard = jnp.bitwise_xor(here, k // 2)
        picks = jnp.where(order[pl.ds(2 * shard + k % 2, 1), :] == bins, 1.0, 0.0).astype(BF16)
        term = matmul(picks, part[...])
        if k == 0:
            returned[...] = term
        else:
            returned[...] += term


def returned_rows(count, where, order, parts):
    rows, width = parts[0].shape
    vmem = pl.BlockSpec(memory_space=pltpu.VMEM)
    return pl.pallas_call(
        functools.partial(returned_kernel, count),
        in_specs=[scalar_spec()] + [vmem] * (1 + len(parts)),
        out_specs=vmem,
        out_shape=shape((2 * rows, width), F32),
        compiler_params=params(),
        cost_estimate=pl.CostEstimate(
            flops=4 * rows * rows * len(parts) * width,
            bytes_accessed=2 * rows * width * len(parts) + 8 * rows * width,
            transcendentals=0,
        ),
    )(where, order, *parts)


def unpack_kernel(count, row_count, key_width, *refs):
    where, mine, theirs, query, key, value, extra, whole = refs
    half = mine.shape[1]
    core = where[1]
    for c in range(2):

        @pl.when(core == c)
        def _():
            whole[:, c * half : (c + 1) * half, :] = mine[...]
            whole[:, (1 - c) * half : (2 - c) * half, :] = theirs[...]

    for out, at in ((query, 0), (key, key_width), (value, 2 * key_width)):
        size = out.shape[1] // count
        for s in range(count):
            rows = whole[s, :row_count, at : at + size]
            out[:, s * size : (s + 1) * size] = rows.astype(F32)
    extra[...] = whole[:, row_count:, :].astype(F32)


def unpack(where, parts, row_count, key_width, val_width):
    count, half, width = parts[0].shape
    vmem = pl.BlockSpec(memory_space=pltpu.VMEM)
    return pl.pallas_call(
        functools.partial(unpack_kernel, count, row_count, key_width),
        in_specs=[scalar_spec()] + [vmem] * 2,
        out_specs=[vmem] * 4,
        out_shape=[
            shape((row_count, count * key_width), F32),
            shape((row_count, count * key_width), F32),
            shape((row_count, count * val_width), F32),
            shape((count, EXTRA, width), F32),
        ],
        scratch_shapes=[pltpu.VMEM((count, 2 * half, width), BF16)],
        compiler_params=params(),
    )(where, *parts)


class Exchange:
    def __init__(self):
        self.new = {}


def pin_all(exchanges, *arrays):
    keys = [sorted(e.new) for e in exchanges]
    out = pin(*arrays, *[e.new[k] for e, ks in zip(exchanges, keys) for k in ks])
    at = len(arrays)
    for e, ks in zip(exchanges, keys):
        e.new = dict(zip(ks, out[at : at + len(ks)]))
        at += len(ks)
    return out[: len(arrays)]


def take_after(exchanges, array):
    pin_all(exchanges, array)


def pin_some(exchanges, *arrays, firsts=None):
    firsts = firsts or [max(e.new) for e in exchanges]
    out = pin(*arrays, *[e.new[k] for e, k in zip(exchanges, firsts)])
    for e, k, block in zip(exchanges, firsts, out[len(arrays) :]):
        e.new[k] = block
    return out[: len(arrays)]


class Gather(Exchange):
    def __init__(self, part, order, count):
        super().__init__()
        self.have, self.order, self.count, self.last = {0: part}, order, count, [0]

    def take(self):
        self.have.update(self.new)
        self.new = {}

    def send(self):
        self.take()
        new = {}
        for m in self.last:
            used = [k for k, bit in enumerate(self.order) if m & bit]
            for bit in self.order[max(used, default=-1) + 1 :]:
                new[m | bit] = swap(self.have[m], bit, self.count)
        self.new, self.last = new, sorted(new)


class Scatter(Exchange):
    def __init__(self, blocks, order, count):
        super().__init__()
        self.have, self.order, self.count, self.step = dict(enumerate(blocks)), order, count, 0

    def take(self):
        if self.new:
            bit = self.order[self.step - 1]
            self.have = {
                m: self.have[m].astype(F32) + self.new[m | bit].astype(F32)
                for m in self.have
                if not m & bit
            }
            self.new = {}

    def send(self):
        self.take()
        bit = self.order[self.step]
        self.new = {
            m: swap(self.have[m].astype(BF16), bit, self.count)
            for m in sorted(self.have, reverse=True)
            if m & bit
        }
        self.step += 1

    def rest(self):
        while self.step < len(self.order):
            self.send()
        self.take()
        return self.have[0]


class CubeSum(Exchange):
    def __init__(self, piece, count):
        super().__init__()
        self.total, self.step = piece, 0
        self.count, self.bits = count, count.bit_length() - 1

    def swap(self, array, bit):
        return lax.ppermute(array, "wz", [(i, i ^ bit) for i in range(self.count)])

    def mine(self, bit):
        return jnp.where(lax.axis_index("wz") & bit, 1, 0)

    def take(self):
        if self.new:
            came, at = self.new[0], self.step - 1
            if at < self.bits:
                half = came.shape[0]
                kept = lax.dynamic_slice_in_dim(self.total, self.mine(1 << at) * half, half, 0)
                self.total = (kept.astype(F32) + came.astype(F32)).astype(BF16)
            else:
                upper = self.mine(1 << (2 * self.bits - 1 - at)) == 1
                self.total = jnp.concatenate(
                    [jnp.where(upper, came, self.total), jnp.where(upper, self.total, came)], axis=0
                )
            self.new = {}

    def send(self):
        self.take()
        if self.step >= 2 * self.bits:
            return
        if self.step < self.bits:
            bit = 1 << self.step
            half = self.total.shape[0] // 2
            away = lax.dynamic_slice_in_dim(self.total, (1 - self.mine(bit)) * half, half, 0)
            self.new = {0: self.swap(away.astype(BF16), bit)}
        else:
            self.new = {0: self.swap(self.total, 1 << (2 * self.bits - 1 - self.step))}
        self.step += 1

    def rest(self):
        while self.step < 2 * self.bits:
            self.send()
        self.take()
        return self.total.astype(BF16)


class OtherCore(Exchange):
    def __init__(self, array):
        super().__init__()
        self.new = {0: other_core(array)}


def split_columns(blocks, count):
    half = blocks[0].shape[1] // 2
    return [
        Scatter([block[:, k * half : (k + 1) * half] for block in blocks], order, count)
        for k, order in enumerate(bit_orders(count))
    ]


def other_core(array):
    return lax.ppermute(array, "core", [(0, 1), (1, 0)])


def shards(
    seq_count,
    wz_count,
    inputs,
    bin_order,
    first_gain,
    first_shift,
    query_weight,
    key_weight,
    value_weight,
    bias_content,
    bias_position,
    relative_weight,
    out_weight,
    bias_out,
    second_gain,
    second_shift,
    inner_weight,
    bias_inner,
    outer_weight,
    bias_outer,
    grad_output,
):
    row_count, width = inputs.shape[1:]
    length = bin_order.shape[1]
    here = lax.axis_index("seq")
    core = lax.axis_index("core")
    where = jnp.stack([here, core]).astype(jnp.int32)
    row_start = here * row_count
    key_width = query_weight.shape[1] // seq_count
    val_width = value_weight.shape[1] // seq_count
    heads_width = 2 * key_width + val_width
    up, down = bit_orders(seq_count)

    others = [jnp.bitwise_xor(here, m) for m in range(seq_count)]
    along = jnp.concatenate(
        [other * row_count + jnp.arange(row_count, dtype=jnp.int32) for other in others]
    )

    def natural(rows):
        parts = rows.reshape(seq_count, row_count, -1)
        parts = [lax.dynamic_index_in_dim(parts, other, 0) for other in others]
        return jnp.concatenate(parts, axis=0).reshape(rows.shape)

    def halves(rows):
        half = rows.shape[0] // 2
        return [Gather(rows[:half], up, seq_count), Gather(rows[half:], down, seq_count)]

    def blocks_of(gathers):
        for g in gathers:
            g.take()
        return [g.have[m] for m in range(seq_count) for g in gathers]

    window_gathers = halves(inputs[0])
    for g in window_gathers:
        g.send()

    def by_head(weight):
        return weight.reshape(weight.shape[0], seq_count, -1)

    vectors = jnp.stack([first_gain, first_shift, bias_out, second_gain, second_shift, bias_outer])
    vectors = jnp.concatenate([vectors, bias_inner.reshape(2, row_count)], axis=0)
    vectors = jnp.pad(vectors, ((0, EXTRA - 8), (0, 0)))
    rel_rows = relative_weight.shape[0]
    rel_blocks = -(-rel_rows // EXTRA)
    rel_part = jnp.pad(by_head(relative_weight), ((0, rel_blocks * EXTRA - rel_rows), (0, 0), (0, 0)))
    rel_part = rel_part.reshape(rel_blocks, EXTRA, seq_count, key_width).transpose(2, 1, 0, 3)
    rel_part = rel_part.reshape(seq_count, EXTRA, -1)
    spare = heads_width - row_count - rel_part.shape[2]
    extra = jnp.concatenate(
        [
            jnp.broadcast_to(vectors[None], (seq_count,) + vectors.shape),
            jnp.pad(rel_part, ((0, 0), (0, 0), (0, spare))),
        ],
        axis=2,
    )
    mine = jnp.concatenate(
        [by_head(query_weight), by_head(key_weight), by_head(value_weight)], axis=2
    ).transpose(1, 0, 2)
    mine = jnp.concatenate([mine, extra], axis=1)
    half = mine.shape[1] // 2
    mine = lax.dynamic_slice_in_dim(mine, core * half, half, 1)

    def own_half(weight):
        half = weight.shape[0] // 2
        return lax.dynamic_slice_in_dim(weight, core * half, half, 0)

    inner_part, outer_part = own_half(inner_weight), own_half(outer_weight)
    mine, inner_part, outer_part = pin_all(window_gathers, mine, inner_part, outer_part)
    for step in range(1, len(up)):
        for g in window_gathers:
            g.send()
    weight_gathers = [
        Gather(inner_part, up, seq_count),
        Gather(outer_part, down, seq_count),
    ]
    for g in weight_gathers:
        g.send()
    mine = lax.all_to_all(mine, "seq", 0, 0, tiled=True)
    (mine,) = pin_all(window_gathers, mine)
    first = core == 0
    theirs = other_core(mine)
    attention_weight = jnp.concatenate(
        [jnp.where(first, mine, theirs), jnp.where(first, theirs, mine)], axis=1
    )
    table, table_back = basis_tables(jnp.asarray(basis_constants(length)), length)
    flat = attention_weight[:, row_count:]
    vectors = flat[:, :8, :row_count].astype(F32)
    inner_bias = vectors[:, 6:8].reshape(1, -1)
    vectors = vectors.transpose(1, 0, 2).reshape(8, width)
    rel = flat[:, :, row_count : row_count + rel_blocks * key_width]
    rel = rel.reshape(seq_count, EXTRA, rel_blocks, key_width).transpose(0, 2, 1, 3)
    rel = rel.reshape(seq_count, rel_blocks * EXTRA, key_width)[:, :rel_rows].reshape(REL, key_width)

    window_blocks = blocks_of(window_gathers)

    order = bin_order[0]
    placing = (order[:, None] == along[None, :]).astype(BF16)
    bias = jnp.concatenate([bias_content, bias_position])[None].astype(F32)
    window, hidden_one, in_bins, weight_whole = project(
        window_blocks, attention_weight, vectors, bias, row_count
    )
    placed_heads = matmul(placing, in_bins).astype(BF16)
    mixed, probs = attend(placed_heads, rel, table)
    (mixed,) = pin_all(weight_gathers, mixed)
    for step in range(1, len(up)):
        for g in weight_gathers:
            g.send()
    weight_parts = []
    for g, own in zip(weight_gathers, (inner_weight, outer_weight)):
        g.take()
        parts = [own]
        for m in range(1, seq_count):
            parts += [g.have[m], other_core(g.have[m])]
        weight_parts.append(parts)
    mixed_along = natural(mixed).reshape(seq_count, row_count, val_width)
    attended = [matmul(mixed_along[m], out_weight).astype(BF16) for m in range(seq_count)]
    attended = split_columns(attended, seq_count)
    for g in attended:
        g.send()
    own_order = lax.dynamic_slice_in_dim(order, row_start, row_count, 0)
    placed = matmul((own_order[:, None] == along[None, :]).astype(BF16), window)
    (placed,) = pin_all(attended, placed)
    attended = [g.rest() for g in attended]

    grad_rows = grad_output[0]
    layer_output, d_mixed_in, hidden_two, activated, d_inner, sums, inner_sums = feed_forward(
        where, placed, attended, grad_rows, vectors, inner_bias, *weight_parts
    )

    d_mixed_gathers = halves(d_mixed_in)
    for g in d_mixed_gathers:
        g.send()
    came_inner = other_core(half_gradient(seq_count, True, where, hidden_two, d_inner))
    outer_away = half_gradient(seq_count, False, where, activated, grad_rows)
    (outer_away,) = pin_some(d_mixed_gathers, outer_away, firsts=[up[0], down[0]])
    came_outer = other_core(outer_away)
    kept_inner = half_gradient(seq_count, True, where, hidden_two, d_inner, came_inner)
    kept_inner = pin_all(d_mixed_gathers, *kept_inner)
    for step in range(1, len(up)):
        for g in d_mixed_gathers:
            g.send()
    kept_outer = half_gradient(seq_count, False, where, activated, grad_rows, came_outer)
    kept = pin_all(d_mixed_gathers, *kept_inner, *kept_outer)
    d_mixed_blocks = blocks_of(d_mixed_gathers)
    count = seq_count
    inner_sums_of, outer_sums_of = [
        [
            Scatter([kept[2 * (k * count + m) + side] for m in range(count)], bits, count)
            for side, bits in enumerate((up, down))
        ]
        for k in range(2)
    ]
    for g in inner_sums_of:
        g.send()

    d_attended, out_away, grad_out_w = mixed_back(
        seq_count, where, mixed, out_weight, d_mixed_blocks
    )
    (d_attended,) = pin_some(inner_sums_of, d_attended)
    out_core = OtherCore(out_away)

    def send_all(exchanges):
        for exchange in exchanges:
            exchange.send()

    def scatter_windows(piece):
        return lax.psum_scatter(piece.astype(BF16), "wz", scatter_dimension=0, tiled=True)

    def gather_windows(piece):
        return lax.all_gather(piece, ("core", "wz"), axis=0, tiled=True)

    def joined_sum(scatters):
        return jnp.concatenate([g.rest().astype(BF16) for g in scatters], axis=1)

    (d_attended,) = pin_all([out_core], d_attended)
    out_sum = scatter_windows(grad_out_w + out_core.new[0].astype(F32))
    back = attend_back(0, placed_heads, rel, table_back, mixed, d_attended, probs)
    *back, out_sum = pin_all(inner_sums_of, *back, out_sum)
    out_sum = gather_windows(out_sum)
    for step in range(1, len(up)):
        send_all(inner_sums_of)
    send_all(outer_sums_of)
    for head in range(1, key_width // KEY):
        back = attend_back(head, placed_heads, rel, table_back, mixed, d_attended, probs, back)
    *back, out_sum = pin_all(inner_sums_of, *back, out_sum)
    d_heads, d_rel, d_bias = back
    inner_sum = scatter_windows(joined_sum(inner_sums_of))
    d_along, *d_normed, first_sums = rows_back(
        seq_count, where, order[None], d_heads, window, weight_whole
    )
    out = pin_all(outer_sums_of, d_along, inner_sum, *d_normed)
    d_along, inner_sum, d_normed = out[0], out[1], out[2:]
    inner_sum = gather_windows(inner_sum)
    for step in range(1, len(up)):
        send_all(outer_sums_of)
    arrived = [
        Scatter([d_normed[2 * m + side] for m in range(count)], bits, count)
        for side, bits in enumerate((up, down))
    ]
    results = pack(
        seq_count, where, hidden_one, d_along, first_sums, sums, inner_sums, d_bias, d_rel
    )
    results = pin_all(outer_sums_of, *results)
    packed_core = OtherCore(results[1])
    outer_sum = scatter_windows(joined_sum(outer_sums_of))
    (packed,) = pin_all([packed_core], results[0])
    packed = (packed.astype(F32) + packed_core.new[0].astype(F32)).astype(BF16)
    packed_shape = packed.shape
    packed = lax.all_to_all(packed, "seq", 0, 0, tiled=True)
    send_all(arrived)
    take_after(arrived, packed)
    packed_cube = CubeSum(packed.reshape(-1, packed_shape[2]), wz_count)
    packed_cube.send()
    take_after(arrived, packed_cube.new[0])
    packed_cube.send()
    (outer_sum,) = pin_all(arrived, outer_sum)
    outer_sum = gather_windows(outer_sum)
    for step in range(1, len(up)):
        send_all(arrived)
    take_after(arrived, packed_cube.new[0])
    d_mixed_blocks = pin(packed_cube.new[0], *d_mixed_blocks)[1:]
    packed_cube.send()
    returned = returned_rows(
        seq_count, where, order.reshape(2 * seq_count, row_count // 2), d_mixed_blocks
    )
    own_unit, own_scale = norm_of(inputs[0].astype(F32))
    arrived = jnp.concatenate([g.rest() for g in arrived], axis=1)
    grad_inputs = norm_back(own_unit, own_scale, vectors[0:1], arrived) + returned

    def both_halves(pieces, axis):
        half = pieces.shape[0] // 2
        return jnp.concatenate([pieces[:half], pieces[half:]], axis=axis).astype(F32)

    grad_out_w = both_halves(out_sum, 0)
    (grad_inputs,) = pin_all([packed_cube], grad_inputs)
    packed_cube.send()
    grad_inner_w = both_halves(inner_sum, 1)
    grad_outer_w = both_halves(outer_sum, 0)
    packed = packed_cube.rest().reshape(packed_shape)
    grad_query_w, grad_key_w, grad_value_w, flat = unpack(
        where, (packed, other_core(packed)), row_count, key_width, val_width
    )
    small = jnp.sum(flat[:, :16, :row_count], axis=0)
    g_gain_one, g_shift_one, g_out_b, g_gain_two, g_shift_two, g_outer_b = small[:6]
    g_inner_b = small[6:8].reshape(-1)
    grad_rel = flat[:, :, row_count : row_count + rel_blocks * key_width]
    grad_rel = grad_rel.reshape(seq_count, EXTRA, rel_blocks, key_width).transpose(2, 1, 0, 3)
    grad_rel = grad_rel.reshape(rel_blocks * EXTRA, -1)[:rel_rows]
    return (
        layer_output[None],
        grad_inputs[None],
        g_gain_one,
        g_shift_one,
        grad_query_w,
        grad_key_w,
        grad_value_w,
        small[8, :key_width],
        small[9, :key_width],
        grad_rel,
        grad_out_w,
        g_out_b,
        g_gain_two,
        g_shift_two,
        grad_inner_w,
        g_inner_b,
        grad_outer_w,
        g_outer_b,
    )


def solution(mesh):
    seq_count = mesh.shape["seq"]
    devices = mesh.devices.reshape(seq_count, -1, 2)
    split_mesh = Mesh(devices, ("seq", "wz", "core"))
    rows = P(("wz", "core"), "seq", None)
    vector = P("seq")
    matrix = P("seq", None)
    weights = (
        vector,
        vector,
        matrix,
        matrix,
        matrix,
        vector,
        vector,
        matrix,
        matrix,
        vector,
        vector,
        vector,
        matrix,
        vector,
        matrix,
        vector,
    )
    return jax.shard_map(
        functools.partial(shards, seq_count, mesh.shape["win"] // 2),
        mesh=split_mesh,
        in_specs=(rows, P(("wz", "core"), None)) + weights + (rows,),
        out_specs=(rows, rows) + weights,
        check_vma=False,
    )
```

```python
import functools
import math

import jax
import jax.numpy as jnp
import numpy as np
from jax import lax
from jax.experimental import pallas as pl
from jax.experimental.pallas import tpu as pltpu
from jax.sharding import Mesh
from jax.sharding import PartitionSpec as P

HEADS = 8
KEY = 64
VAL = 192
REL = 192
BF16 = jnp.bfloat16
F32 = jnp.float32
VMEM_LIMIT = 56 * 2**20
EXTRA = 32


def matmul(a, b):
    return lax.dot_general(a, b, (((1,), (0,)), ((), ())), preferred_element_type=F32)


def matmul_nt(a, b):
    return lax.dot_general(a, b, (((1,), (1,)), ((), ())), preferred_element_type=F32)


def matmul_tn(a, b):
    return lax.dot_general(a, b, (((0,), (0,)), ((), ())), preferred_element_type=F32)


def head_part(rows, head):
    lanes = lax.broadcasted_iota(jnp.int32, rows.shape, 1)
    inside = (lanes >= head * KEY) & (lanes < (head + 1) * KEY)
    return jnp.where(inside, rows, jnp.zeros_like(rows))


def head_columns(key_width):
    return [slice(k * key_width, (k + 1) * key_width) for k in range(3)]


def attend_kernel(heads, rows, placed, rel, table, mixed, probs):
    length = placed.shape[0]
    key_width = heads * KEY
    content_at, position_at, keys_at = head_columns(key_width)
    first = pl.program_id(0) * rows
    here = pl.ds(pl.multiple_of(first, rows), rows)
    basis = table[:, pl.ds(pl.multiple_of(length - rows - first, rows), length + rows)]
    content, position, keys = placed[here, content_at], placed[here, position_at], placed[:, keys_at]
    parts = []
    for head in range(heads):
        q_basis = matmul_nt(head_part(position, head), rel[...]).astype(BF16)
        grid = matmul(q_basis, basis)
        shifted = pltpu.roll(grid, 0, 1, stride=1, stride_axis=0)[:, rows:]
        scores = matmul_nt(head_part(content, head), keys) + shifted
        top = jnp.max(scores, axis=1, keepdims=True)
        weights = jnp.exp(scores - top)
        total = jnp.sum(weights, axis=1, keepdims=True)
        prob = (weights * (1.0 / total)).astype(BF16)
        probs[head] = prob
        values_at = 3 * key_width + head * VAL
        parts.append(matmul(prob, placed[:, values_at : values_at + VAL]))
    mixed[...] = jnp.concatenate(parts, axis=1).astype(BF16)


def attend(placed, rel, table):
    length = placed.shape[0]
    heads = rel.shape[1] // KEY
    rows = math.gcd(256, length)
    whole = lambda array: pl.BlockSpec(array.shape, lambda i: (0, 0))
    return pl.pallas_call(
        functools.partial(attend_kernel, heads, rows),
        grid=(length // rows,),
        in_specs=[whole(placed), whole(rel), whole(table)],
        out_specs=[
            pl.BlockSpec((rows, heads * VAL), lambda i: (i, 0)),
            pl.BlockSpec((heads, rows, length), lambda i: (0, i, 0)),
        ],
        out_shape=[
            jax.ShapeDtypeStruct((length, heads * VAL), BF16),
            jax.ShapeDtypeStruct((heads, length, length), BF16),
        ],
        compiler_params=pltpu.CompilerParams(vmem_limit_bytes=VMEM_LIMIT),
        cost_estimate=pl.CostEstimate(
            flops=2 * heads * length * length * 1024,
            bytes_accessed=2 * heads * length * length + 8 * length * heads * VAL,
            transcendentals=heads * length * length,
        ),
    )(placed, rel, table)


def attend_back_kernel(heads, head, rows, *refs):
    placed, rel, table, flip, mixed, d_mixed, probs = refs[:7]
    before = refs[7:-5]
    d_heads, d_rel, d_bias, keys_sum, values_sum = refs[-5:]
    length = placed.shape[0]
    key_width = heads * KEY
    content_at, position_at, keys_at = head_columns(key_width)
    step = pl.program_id(0)

    @pl.when(step == 0)
    def _():
        keys_sum[...] = jnp.zeros_like(keys_sum)
        values_sum[...] = jnp.zeros_like(values_sum)
        for k, out in enumerate((d_heads, d_rel, d_bias)):
            out[...] = before[k][...] if before else jnp.zeros_like(out)

    first = pl.multiple_of(step * rows, rows)
    here = pl.ds(first, rows)
    basis = table[:, pl.ds(first, length + rows)]
    content, position, keys = placed[here, content_at], placed[here, position_at], placed[:, keys_at]
    blocks = length // rows
    columns = slice(head * VAL, (head + 1) * VAL)
    values_at = 3 * key_width + head * VAL
    d_part = d_mixed[:, columns]
    delta = jnp.sum(d_part.astype(F32) * mixed[:, columns].astype(F32), axis=1, keepdims=True)
    prob = probs[0]
    values_sum[...] += matmul_tn(d_part, prob)
    d_prob = matmul_nt(d_part, placed[:, values_at : values_at + VAL])
    d_score = (prob.astype(F32) * (d_prob - delta)).astype(BF16)
    keys_sum[...] += matmul_tn(head_part(content, head), d_score)
    d_content = head_part(matmul(d_score, keys), head)
    turned = [
        matmul(d_score[:, (blocks - 1 - b) * rows : (blocks - b) * rows], flip[...])
        for b in range(blocks)
    ]
    turned = jnp.concatenate(turned + [jnp.zeros((rows, rows), F32)], axis=1)
    d_grid = pltpu.roll(turned, 0, 1, stride=1, stride_axis=0).astype(BF16)
    d_basis = matmul_nt(d_grid, basis).astype(BF16)
    d_position = head_part(matmul(d_basis, rel[...]), head)
    d_rel[...] += matmul_tn(d_basis, head_part(position, head))
    d_heads[here, :key_width] += ((d_content + d_position) * KEY ** (-0.5)).astype(BF16)
    d_bias[0:1, :] += jnp.sum(d_content, axis=0, keepdims=True)
    d_bias[1:2, :] += jnp.sum(d_position, axis=0, keepdims=True)

    @pl.when(step == blocks - 1)
    def _():
        d_heads[:, key_width : 2 * key_width] += keys_sum[...].T.astype(BF16)
        values_to = 2 * key_width + head * VAL
        d_heads[:, values_to : values_to + VAL] = values_sum[...].T.astype(BF16)


def attend_back(head, placed, rel, table, mixed, d_mixed, probs, before=()):
    length = placed.shape[0]
    key_width = rel.shape[1]
    heads = key_width // KEY
    val_width = heads * VAL
    rows = math.gcd(256, length)
    at = jnp.arange(rows)
    flip = (at[:, None] + at[None, :] == rows - 1).astype(BF16)
    block = lambda width: pl.BlockSpec((rows, width), lambda i: (i, 0))
    outs = [
        shape((length, 2 * key_width + val_width), BF16),
        shape((REL, key_width), F32),
        shape((8, key_width), F32),
    ]
    return pl.pallas_call(
        functools.partial(attend_back_kernel, heads, head, rows),
        grid=(length // rows,),
        in_specs=[
            whole_spec(placed),
            whole_spec(rel),
            whole_spec(table),
            whole_spec(flip),
            block(val_width),
            block(val_width),
            pl.BlockSpec((1, rows, length), lambda i: (head, i, 0)),
        ]
        + [whole_spec(array) for array in before],
        out_specs=[whole_spec(out) for out in outs],
        out_shape=outs,
        scratch_shapes=[
            pltpu.VMEM((key_width, length), F32),
            pltpu.VMEM((VAL, length), F32),
        ],
        compiler_params=pltpu.CompilerParams(vmem_limit_bytes=VMEM_LIMIT),
        cost_estimate=pl.CostEstimate(
            flops=2 * length * length * 1536,
            bytes_accessed=2 * length * length + 16 * length * val_width,
            transcendentals=0,
        ),
    )(placed, rel, table, flip, mixed, d_mixed, probs, *before)


def norm_back(unit, scale, gain, grad):
    scaled = grad * gain
    mean_one = jnp.mean(scaled, axis=-1, keepdims=True)
    mean_two = jnp.mean(scaled * unit, axis=-1, keepdims=True)
    return (scaled - mean_one - unit * mean_two) * scale


def whole_spec(array):
    zeros = (0,) * len(array.shape)
    return pl.BlockSpec(array.shape, lambda *_: zeros)


def scalar_spec():
    return pl.BlockSpec(memory_space=pltpu.SMEM)


def params(**more):
    return pltpu.CompilerParams(vmem_limit_bytes=VMEM_LIMIT, **more)


def shape(dims, dtype):
    return jax.ShapeDtypeStruct(tuple(dims), dtype)


def basis_constants(window_len):
    features = REL // 6
    f = np.arange(features, dtype=np.float64)
    half_life = 2.0 ** (3.0 + f * (math.log2(window_len) - 3.0) / (features - 1))
    spread = window_len / (2.0 * features)
    first = window_len / features
    centres = first + f * (window_len - first) / (features - 1)
    concentration = (centres / spread) ** 2
    rate = centres / spread**2
    offset = concentration * np.log(rate) - np.array([math.lgamma(c) for c in concentration])
    columns = [math.log(2.0) / half_life, 2.0 ** (f + 1) - 1.0, concentration - 1.0, rate, offset]
    columns += [np.zeros(features)] * 3
    return np.stack(columns, axis=1).astype(np.float32)


def table_kernel(length, constants, forth, back):
    features = REL // 6
    decay, inside_below, power, rate, offset = [constants[:, k : k + 1] for k in range(5)]

    def gamma(distance):
        logged = power * jnp.log(jnp.maximum(distance, 1.0)) - rate * distance + offset
        return jnp.where(distance == 0.0, 0.0, jnp.exp(logged)) + 1e-08

    every = lax.broadcasted_iota(jnp.int32, (1, length), 1).astype(F32)
    peak = jnp.max(gamma(every), axis=1, keepdims=True)
    lanes = lax.broadcasted_iota(jnp.int32, (1, 2 * length), 1).astype(F32)
    for table, signed in ((forth, lanes - length), (back, length - 1 - lanes)):
        distance = jnp.abs(signed)
        sign = jnp.where(signed > 0, 1.0, jnp.where(signed < 0, -1.0, 0.0))
        parts = (
            jnp.exp(-decay * distance),
            jnp.where(inside_below > distance, 1.0, 0.0),
            gamma(distance) / peak,
        )
        for k, part in enumerate(parts):
            table[k * features : (k + 1) * features, :] = part.astype(BF16)
            table[(3 + k) * features : (4 + k) * features, :] = (sign * part).astype(BF16)


def basis_tables(constants, length):
    out = shape((REL, 2 * length), BF16)
    return pl.pallas_call(
        functools.partial(table_kernel, length),
        out_shape=[out, out],
        compiler_params=params(),
    )(constants)


def norm_of(rows):
    centre = rows - jnp.mean(rows, axis=1, keepdims=True)
    scale = lax.rsqrt(jnp.mean(centre * centre, axis=1, keepdims=True) + 1e-05)
    return centre * scale, scale


def project_kernel(blocks, row_count, *refs):
    parts, (weight, vectors, bias, window, hidden, heads, flat, block) = refs[:blocks], refs[blocks:]
    step = pl.program_id(0)

    @pl.when(step == 0)
    def _():
        for s in range(weight.shape[0]):
            flat[s * row_count : (s + 1) * row_count, :] = weight[s, :row_count, :]

    for k in range(blocks):

        @pl.when(step == k)
        def _():
            block[...] = parts[k][...]

    window[...] = block[...]
    unit, _ = norm_of(block[...].astype(F32))
    normed = (unit * vectors[0:1, :] + vectors[1:2, :]).astype(BF16)
    hidden[...] = normed
    total = matmul(normed, flat[...])
    key_width = bias.shape[1] // 2
    query = total[:, :key_width] * KEY ** (-0.5)
    heads[:, :key_width] = (query + bias[0:1, :key_width]).astype(BF16)
    heads[:, key_width : 2 * key_width] = (query + bias[0:1, key_width:]).astype(BF16)
    heads[:, 2 * key_width :] = total[:, key_width:].astype(BF16)


def project(parts, weight, vectors, bias, row_count):
    blocks = len(parts)
    rows, width = parts[0].shape
    heads_width = weight.shape[2] + bias.shape[1] // 2
    out = lambda w: pl.BlockSpec((rows, w), lambda i: (i, 0))
    return pl.pallas_call(
        functools.partial(project_kernel, blocks, row_count),
        grid=(blocks,),
        in_specs=[whole_spec(a) for a in (*parts, weight, vectors, bias)],
        out_specs=[
            out(width),
            out(width),
            out(heads_width),
            pl.BlockSpec((width, weight.shape[2]), lambda i: (0, 0)),
        ],
        out_shape=[shape((blocks * rows, w), BF16) for w in (width, width, heads_width)]
        + [shape((width, weight.shape[2]), BF16)],
        scratch_shapes=[pltpu.VMEM((rows, width), BF16)],
        compiler_params=params(),
        cost_estimate=pl.CostEstimate(
            flops=2 * blocks * rows * width * heads_width,
            bytes_accessed=8 * blocks * rows * width,
            transcendentals=0,
        ),
    )(*parts, weight, vectors, bias)


def feed_kernel(count, chunk, *refs):
    each = 4 * count - 3
    parts = 2 * each
    where, placed, attended_a, attended_b, grad_rows, vectors, inner_bias = refs[:7]
    weights = refs[7 : 7 + parts]
    layer_output, d_mixed, hidden, activated, d_inner, sums, inner_sums = refs[7 + parts : 14 + parts]
    inner_whole, outer_whole, residual, unit, back, outer_sum, sems = refs[14 + parts :]
    here, core, plane = where[0], where[1], where[2]
    quarters = (2 * core + plane, 2 * core + 1 - plane, 2 - 2 * core + plane, 3 - 2 * core - plane)
    copies = []
    for k, whole in enumerate((inner_whole, outer_whole)):
        mine = weights[k * each : (k + 1) * each]
        size = whole.shape[0] // count
        quarter = size // 4
        moves = [(mine[0], here * size, size)]
        for m in range(1, count):
            start = jnp.bitwise_xor(here, m) * size
            for j, which in enumerate(quarters):
                moves.append((mine[4 * m - 3 + j], start + which * quarter, quarter))
        started = []
        for source, start, rows in moves:
            target = whole.at[pl.ds(pl.multiple_of(start, 16), rows), :]
            copy = pltpu.make_async_copy(source, target, sems.at[k, len(started)])
            copy.start()
            started.append(copy)
        copies.append(started)
    rows, width = placed.shape
    half = width // 2
    residual[:, :half] = placed[:, :half] + attended_a[...] + vectors[2:3, :half]
    residual[:, half:] = placed[:, half:] + attended_b[...] + vectors[2:3, half:]
    normed, scale = norm_of(residual[...])
    unit[...] = normed
    hidden[...] = (normed * vectors[3:4, :] + vectors[4:5, :]).astype(BF16)
    for started in copies:
        for copy in started:
            copy.wait()
    ff = outer_whole.shape[0]
    for c in range(ff // chunk):
        at = slice(c * chunk, (c + 1) * chunk)
        inner = matmul(hidden[...], inner_whole[:, at]) + inner_bias[0:1, at]
        below = 0.5 * (1.0 + lax.erf(inner * (0.5**0.5)))
        slope = below + inner * jnp.exp(-0.5 * inner * inner) * (0.5 / math.pi) ** 0.5
        active = (inner * below).astype(BF16)
        activated[:, at] = active
        grad = (matmul_nt(grad_rows[...], outer_whole[at, :]) * slope).astype(BF16)
        d_inner[:, at] = grad
        inner_sums[:, at] = jnp.sum(grad.astype(F32), axis=0, keepdims=True)
        back_term = matmul_nt(grad, inner_whole[:, at])
        outer_term = matmul(active, outer_whole[at, :])
        if c == 0:
            back[...] = back_term
            outer_sum[...] = outer_term
        else:
            back[...] += back_term
            outer_sum[...] += outer_term
    layer_output[...] = (residual[...] + outer_sum[...] + vectors[5:6, :]).astype(BF16)
    grad, normed = back[...], unit[...]
    dy = grad_rows[...].astype(F32)
    scaled = grad * vectors[3:4, :]
    mean_one = jnp.mean(scaled, axis=1, keepdims=True)
    mean_two = jnp.mean(scaled * normed, axis=1, keepdims=True)
    mixed_in = (dy + (scaled - mean_one - normed * mean_two) * scale).astype(BF16)
    d_mixed[...] = mixed_in
    sums[...] = jnp.zeros_like(sums)
    sums[2:3, :] = jnp.sum(mixed_in.astype(F32), axis=0, keepdims=True)
    sums[3:4, :] = jnp.sum(grad * normed, axis=0, keepdims=True)
    sums[4:5, :] = jnp.sum(grad, axis=0, keepdims=True)
    sums[5:6, :] = jnp.sum(dy, axis=0, keepdims=True)


def feed_forward(where, placed, attended, grad_rows, vectors, inner_bias, inner_parts, outer_parts):
    rows, width = placed.shape
    ff = inner_bias.shape[1]
    count = (len(inner_parts) + 3) // 4
    chunk = math.gcd(512, ff)
    weights = (*inner_parts, *outer_parts)
    small = (placed, *attended, grad_rows, vectors, inner_bias)
    outs = [
        shape((rows, width), BF16),
        shape((rows, width), BF16),
        shape((rows, width), BF16),
        shape((rows, ff), BF16),
        shape((rows, ff), BF16),
        shape((8, width), F32),
        shape((1, ff), F32),
    ]
    return pl.pallas_call(
        functools.partial(feed_kernel, count, chunk),
        in_specs=[scalar_spec()]
        + [pl.BlockSpec(memory_space=pltpu.VMEM) for _ in small]
        + [pl.BlockSpec(memory_space=pl.ANY) for _ in weights],
        out_specs=[pl.BlockSpec(memory_space=pltpu.VMEM) for _ in outs],
        out_shape=outs,
        scratch_shapes=[
            pltpu.VMEM((width, ff), BF16),
            pltpu.VMEM((ff, width), BF16),
            pltpu.VMEM((rows, width), F32),
            pltpu.VMEM((rows, width), F32),
            pltpu.VMEM((rows, width), F32),
            pltpu.VMEM((rows, width), F32),
            pltpu.SemaphoreType.DMA((2, 4 * count - 3)),
        ],
        compiler_params=params(),
        cost_estimate=pl.CostEstimate(
            flops=8 * rows * width * ff,
            bytes_accessed=4 * width * ff + 40 * rows * width,
            transcendentals=2 * rows * ff,
        ),
    )(where, *small, *weights)


def columns_at(ref, index, size, scratch):
    if size % 128 == 0:
        return ref[:, pl.ds(pl.multiple_of(index * size, 128), size)]
    for k in range(ref.shape[1] // size):

        @pl.when(index == k)
        def _():
            scratch[...] = ref[:, k * size : (k + 1) * size]

    return scratch[...]


def half_kernel(count, split, away, where, left, right, *refs):
    here, core = where[0], where[1]
    side = 1 - core if away else core
    shard = jnp.bitwise_xor(here, pl.program_id(0))
    if split:
        some = columns_at(left, shard, left.shape[1] // count, refs[-1])
        half = right.shape[1] // 2
        other = right[:, pl.ds(pl.multiple_of(side * half, 128), half)]
    else:
        some = columns_at(left, 2 * shard + side, left.shape[1] // count // 2, refs[-1])
        other = right[...]
    result = matmul_tn(some, other)
    if away:
        refs[0][0] = result.astype(BF16)
        return
    came, outs = refs[0], refs[1:-1]
    result += came[0].astype(F32)
    width = result.shape[1] // 2
    for m in range(count):

        @pl.when(pl.program_id(0) == m)
        def _():
            outs[2 * m][...] = result[:, :width].astype(BF16)
            outs[2 * m + 1][...] = result[:, width:].astype(BF16)


def half_gradient(count, split, where, left, right, came=None):
    away = came is None
    rows = left.shape[1] // count // (1 if split else 2)
    width = right.shape[1] // (2 if split else 1)
    block = pl.BlockSpec((1, rows, width), lambda i: (i, 0, 0))
    if away:
        outs, out_specs = shape((count, rows, width), BF16), block
    else:
        outs = [shape((rows, width // 2), BF16) for _ in range(2 * count)]
        out_specs = [whole_spec(out) for out in outs]
    return pl.pallas_call(
        functools.partial(half_kernel, count, split, away),
        grid=(count,),
        in_specs=[scalar_spec(), whole_spec(left), whole_spec(right)] + ([] if away else [block]),
        out_specs=out_specs,
        out_shape=outs,
        scratch_shapes=[pltpu.VMEM((left.shape[0], rows), BF16)],
        compiler_params=params(),
        cost_estimate=pl.CostEstimate(
            flops=2 * left.shape[0] * count * rows * width,
            bytes_accessed=4 * count * rows * width + 4 * left.shape[0] * left.shape[1],
            transcendentals=0,
        ),
    )(where, left, right, *(() if away else (came,)))


def mixed_back_kernel(count, parts_count, *refs):
    where, mixed, weight = refs[:3]
    parts = refs[3 : 3 + parts_count]
    d_attended, out_away, out_kept, out_sum = refs[3 + parts_count :]
    here, core = where[0], where[1]
    rows = parts[0].shape[0]
    for k, part in enumerate(parts):
        start = jnp.bitwise_xor(here, k // 2) * (2 * rows) + (k % 2) * rows
        at = pl.ds(pl.multiple_of(start, 32), rows)
        d_attended[at, :] = matmul_nt(part[...], weight[...]).astype(BF16)
        term = matmul_tn(mixed[at, :], part[...])
        if k == 0:
            out_sum[...] = term
        else:
            out_sum[...] += term
    half = out_kept.shape[0]
    out_kept[...] = out_sum[pl.ds(pl.multiple_of(core * half, 32), half), :]
    out_away[...] = out_sum[pl.ds(pl.multiple_of((1 - core) * half, 32), half), :].astype(BF16)


def mixed_back(count, where, mixed, weight, parts):
    length, val_width = mixed.shape
    width = weight.shape[1]
    vmem = pl.BlockSpec(memory_space=pltpu.VMEM)
    return pl.pallas_call(
        functools.partial(mixed_back_kernel, count, len(parts)),
        in_specs=[scalar_spec()] + [vmem] * (2 + len(parts)),
        out_specs=[vmem] * 3,
        out_shape=[
            shape((length, val_width), BF16),
            shape((val_width // 2, width), BF16),
            shape((val_width // 2, width), F32),
        ],
        scratch_shapes=[pltpu.VMEM((val_width, width), F32)],
        compiler_params=params(),
        cost_estimate=pl.CostEstimate(
            flops=4 * length * val_width * width,
            bytes_accessed=2 * length * (width + 2 * val_width),
            transcendentals=0,
        ),
    )(where, mixed, weight, *parts)


def rows_back_kernel(count, where, order, d_heads, window, weight, d_along, *refs):
    d_normed, first_sums = refs[:-1], refs[-1]
    here = where[0]
    step = pl.program_id(0)
    rows, width = window.shape
    length = order.shape[1]
    bins = lax.broadcasted_iota(jnp.int32, (rows, length), 0) + jnp.bitwise_xor(here, step) * rows
    picks = jnp.where(order[0:1, :] == bins, 1.0, 0.0).astype(BF16)
    along = matmul(picks, d_heads[...]).astype(BF16)
    d_along[...] = along
    unit, _ = norm_of(window[...].astype(F32))
    normed = matmul_nt(along, weight[...])

    @pl.when(step == 0)
    def _():
        first_sums[...] = jnp.zeros_like(first_sums)

    first_sums[0:1, :] += jnp.sum(normed * unit, axis=0, keepdims=True)
    first_sums[1:2, :] += jnp.sum(normed, axis=0, keepdims=True)
    half = width // 2
    for m in range(count):

        @pl.when(step == m)
        def _():
            d_normed[2 * m][...] = normed[:, :half].astype(BF16)
            d_normed[2 * m + 1][...] = normed[:, half:].astype(BF16)


def rows_back(count, where, order, d_heads, window, weight):
    length, width = window.shape
    rows = length // count
    heads_width = d_heads.shape[1]
    outs = [shape((length, heads_width), BF16)]
    outs += [shape((rows, width // 2), BF16) for _ in range(2 * count)]
    outs += [shape((8, width), F32)]
    return pl.pallas_call(
        functools.partial(rows_back_kernel, count),
        grid=(count,),
        in_specs=[
            scalar_spec(),
            whole_spec(order),
            whole_spec(d_heads),
            pl.BlockSpec((rows, width), lambda i: (i, 0)),
            whole_spec(weight),
        ],
        out_specs=[pl.BlockSpec((rows, heads_width), lambda i: (i, 0))]
        + [whole_spec(out) for out in outs[1:]],
        out_shape=outs,
        compiler_params=params(),
        cost_estimate=pl.CostEstimate(
            flops=2 * length * heads_width * (length + width),
            bytes_accessed=4 * length * (width + heads_width),
            transcendentals=0,
        ),
    )(where, order, d_heads, window, weight)


def pack_kernel(
    count, where, hidden, d_along, first_sums, sums, inner_sums, d_bias, d_rel, kept, away, grads
):
    here, core = where[0], where[1]
    step = pl.program_id(0)
    row_count = hidden.shape[1] // count
    key_width = d_rel.shape[1]
    terms = matmul_tn(hidden[...], d_along[...])

    @pl.when(step == 0)
    def _():
        for s in range(count):
            grads[s, :row_count, :] = terms[s * row_count : (s + 1) * row_count, :]

    @pl.when(step > 0)
    def _():
        for s in range(count):
            grads[s, :row_count, :] += terms[s * row_count : (s + 1) * row_count, :]

    @pl.when(step == pl.num_programs(0) - 1)
    def _():
        rel_rows = d_rel.shape[0] // count
        for s in range(count):
            at = slice(s * row_count, (s + 1) * row_count)
            grads[s, row_count:, :] = jnp.zeros((EXTRA, grads.shape[2]), F32)
            grads[s, row_count : row_count + 2, :row_count] = first_sums[0:2, at]
            grads[s, row_count + 2 : row_count + 6, :row_count] = sums[2:6, at]
            for j in range(2):
                part = slice((2 * s + j) * row_count, (2 * s + j + 1) * row_count)
                grads[s, row_count + 6 + j : row_count + 7 + j, :row_count] = inner_sums[0:1, part]
            for j in range(-(-rel_rows // EXTRA)):
                some = d_rel[s * rel_rows + j * EXTRA : s * rel_rows + min(rel_rows, (j + 1) * EXTRA), :]
                lane = row_count + j * key_width
                grads[s, row_count : row_count + some.shape[0], lane : lane + key_width] = some
        for s in range(count):

            @pl.when(here == s)
            def _():
                grads[s, row_count + 8 : row_count + 10, :key_width] = d_bias[0:2, :]

        half = kept.shape[1]
        kept[...] = grads[:, pl.ds(pl.multiple_of(core * half, 16), half), :].astype(BF16)
        away[...] = grads[:, pl.ds(pl.multiple_of((1 - core) * half, 16), half), :].astype(BF16)


def pack(count, where, hidden, d_along, *small):
    length, width = hidden.shape
    heads_width = d_along.shape[1]
    rows = math.gcd(768, length)
    packed = (count, width // count + EXTRA, heads_width)
    outs = [shape((count, packed[1] // 2, heads_width), BF16) for _ in range(2)]
    return pl.pallas_call(
        functools.partial(pack_kernel, count),
        grid=(length // rows,),
        in_specs=[
            scalar_spec(),
            pl.BlockSpec((rows, width), lambda i: (i, 0)),
            pl.BlockSpec((rows, heads_width), lambda i: (i, 0)),
        ]
        + [whole_spec(a) for a in small],
        out_specs=[whole_spec(out) for out in outs],
        out_shape=outs,
        scratch_shapes=[pltpu.VMEM(packed, F32)],
        compiler_params=params(),
        cost_estimate=pl.CostEstimate(
            flops=2 * length * heads_width * width,
            bytes_accessed=2 * length * (width + heads_width) + 8 * width * heads_width,
            transcendentals=0,
        ),
    )(where, hidden, d_along, *small)


def swap(array, mask, count):
    return lax.ppermute(array, "seq", [(i, i ^ mask) for i in range(count)])


def bit_orders(count):
    bits = [1 << k for k in range(count.bit_length() - 1)]
    return bits, bits[::-1]


def pin(*arrays):
    return lax.optimization_barrier(arrays)


def returned_kernel(count, where, order, *refs):
    parts, returned = refs[:-1], refs[-1]
    here = where[0]
    rows = parts[0].shape[0]
    bins = lax.broadcasted_iota(jnp.int32, (returned.shape[0], rows), 0)
    bins = bins + here * returned.shape[0]
    for k, part in enumerate(parts):
        shard = jnp.bitwise_xor(here, k // 2)
        picks = jnp.where(order[pl.ds(2 * shard + k % 2, 1), :] == bins, 1.0, 0.0).astype(BF16)
        term = matmul(picks, part[...])
        if k == 0:
            returned[...] = term
        else:
            returned[...] += term


def returned_rows(count, where, order, parts):
    rows, width = parts[0].shape
    vmem = pl.BlockSpec(memory_space=pltpu.VMEM)
    return pl.pallas_call(
        functools.partial(returned_kernel, count),
        in_specs=[scalar_spec()] + [vmem] * (1 + len(parts)),
        out_specs=vmem,
        out_shape=shape((2 * rows, width), F32),
        compiler_params=params(),
        cost_estimate=pl.CostEstimate(
            flops=4 * rows * rows * len(parts) * width,
            bytes_accessed=2 * rows * width * len(parts) + 8 * rows * width,
            transcendentals=0,
        ),
    )(where, order, *parts)


def unpack_kernel(count, row_count, key_width, *refs):
    where, mine, theirs, query, key, value, extra, whole = refs
    half = mine.shape[1]
    core = where[1]
    for c in range(2):

        @pl.when(core == c)
        def _():
            whole[:, c * half : (c + 1) * half, :] = mine[...]
            whole[:, (1 - c) * half : (2 - c) * half, :] = theirs[...]

    for out, at in ((query, 0), (key, key_width), (value, 2 * key_width)):
        size = out.shape[1] // count
        for s in range(count):
            rows = whole[s, :row_count, at : at + size]
            out[:, s * size : (s + 1) * size] = rows.astype(F32)
    extra[...] = whole[:, row_count:, :].astype(F32)


def unpack(where, parts, row_count, key_width, val_width):
    count, half, width = parts[0].shape
    vmem = pl.BlockSpec(memory_space=pltpu.VMEM)
    return pl.pallas_call(
        functools.partial(unpack_kernel, count, row_count, key_width),
        in_specs=[scalar_spec()] + [vmem] * 2,
        out_specs=[vmem] * 4,
        out_shape=[
            shape((row_count, count * key_width), F32),
            shape((row_count, count * key_width), F32),
            shape((row_count, count * val_width), F32),
            shape((count, EXTRA, width), F32),
        ],
        scratch_shapes=[pltpu.VMEM((count, 2 * half, width), BF16)],
        compiler_params=params(),
    )(where, *parts)


class Exchange:
    def __init__(self):
        self.new = {}


def pin_all(exchanges, *arrays):
    keys = [sorted(e.new) for e in exchanges]
    out = pin(*arrays, *[e.new[k] for e, ks in zip(exchanges, keys) for k in ks])
    at = len(arrays)
    for e, ks in zip(exchanges, keys):
        e.new = dict(zip(ks, out[at : at + len(ks)]))
        at += len(ks)
    return out[: len(arrays)]


def take_after(exchanges, array):
    pin_all(exchanges, array)


def pin_some(exchanges, *arrays, firsts=None):
    firsts = firsts or [max(e.new) for e in exchanges]
    out = pin(*arrays, *[e.new[k] for e, k in zip(exchanges, firsts)])
    for e, k, block in zip(exchanges, firsts, out[len(arrays) :]):
        e.new[k] = block
    return out[: len(arrays)]


class Gather(Exchange):
    def __init__(self, part, order, count):
        super().__init__()
        self.have, self.order, self.count, self.last = {0: part}, order, count, [0]

    def take(self):
        self.have.update(self.new)
        self.new = {}

    def send(self):
        self.take()
        new = {}
        for m in self.last:
            used = [k for k, bit in enumerate(self.order) if m & bit]
            for bit in self.order[max(used, default=-1) + 1 :]:
                new[m | bit] = swap(self.have[m], bit, self.count)
        self.new, self.last = new, sorted(new)


class Scatter(Exchange):
    def __init__(self, blocks, order, count):
        super().__init__()
        self.have, self.order, self.count, self.step = dict(enumerate(blocks)), order, count, 0

    def take(self):
        if self.new:
            bit = self.order[self.step - 1]
            self.have = {
                m: self.have[m].astype(F32) + self.new[m | bit].astype(F32)
                for m in self.have
                if not m & bit
            }
            self.new = {}

    def send(self):
        self.take()
        bit = self.order[self.step]
        self.new = {
            m: swap(self.have[m].astype(BF16), bit, self.count)
            for m in sorted(self.have, reverse=True)
            if m & bit
        }
        self.step += 1

    def rest(self):
        while self.step < len(self.order):
            self.send()
        self.take()
        return self.have[0]


class CubeSum(Exchange):
    def __init__(self, piece, count):
        super().__init__()
        self.total, self.step = piece, 0
        self.count, self.bits = count, count.bit_length() - 1

    def swap(self, array, bit):
        return lax.ppermute(array, "wz", [(i, i ^ bit) for i in range(self.count)])

    def mine(self, bit):
        return jnp.where(lax.axis_index("wz") & bit, 1, 0)

    def take(self):
        if self.new:
            came, at = self.new[0], self.step - 1
            if at < self.bits:
                half = came.shape[0]
                kept = lax.dynamic_slice_in_dim(self.total, self.mine(1 << at) * half, half, 0)
                self.total = (kept.astype(F32) + came.astype(F32)).astype(BF16)
            else:
                upper = self.mine(1 << (2 * self.bits - 1 - at)) == 1
                self.total = jnp.concatenate(
                    [jnp.where(upper, came, self.total), jnp.where(upper, self.total, came)], axis=0
                )
            self.new = {}

    def send(self):
        self.take()
        if self.step >= 2 * self.bits:
            return
        if self.step < self.bits:
            bit = 1 << self.step
            half = self.total.shape[0] // 2
            away = lax.dynamic_slice_in_dim(self.total, (1 - self.mine(bit)) * half, half, 0)
            self.new = {0: self.swap(away.astype(BF16), bit)}
        else:
            self.new = {0: self.swap(self.total, 1 << (2 * self.bits - 1 - self.step))}
        self.step += 1

    def rest(self):
        while self.step < 2 * self.bits:
            self.send()
        self.take()
        return self.total.astype(BF16)


class OtherPlane(Exchange):
    def __init__(self, blocks, count):
        super().__init__()
        pairs = [(i, i ^ 1) for i in range(count)]
        self.new = {m: lax.ppermute(block, "wz", pairs) for m, block in sorted(blocks.items())}


class OtherCore(Exchange):
    def __init__(self, array):
        super().__init__()
        self.new = {0: other_core(array)}


def split_columns(blocks, count):
    half = blocks[0].shape[1] // 2
    return [
        Scatter([block[:, k * half : (k + 1) * half] for block in blocks], order, count)
        for k, order in enumerate(bit_orders(count))
    ]


def other_core(array):
    return lax.ppermute(array, "core", [(0, 1), (1, 0)])


def shards(
    seq_count,
    wz_count,
    inputs,
    bin_order,
    first_gain,
    first_shift,
    query_weight,
    key_weight,
    value_weight,
    bias_content,
    bias_position,
    relative_weight,
    out_weight,
    bias_out,
    second_gain,
    second_shift,
    inner_weight,
    bias_inner,
    outer_weight,
    bias_outer,
    grad_output,
):
    row_count, width = inputs.shape[1:]
    length = bin_order.shape[1]
    here = lax.axis_index("seq")
    core = lax.axis_index("core")
    plane = lax.axis_index("wz") & 1
    where = jnp.stack([here, core, plane]).astype(jnp.int32)
    row_start = here * row_count
    key_width = query_weight.shape[1] // seq_count
    val_width = value_weight.shape[1] // seq_count
    heads_width = 2 * key_width + val_width
    up, down = bit_orders(seq_count)

    others = [jnp.bitwise_xor(here, m) for m in range(seq_count)]
    along = jnp.concatenate(
        [other * row_count + jnp.arange(row_count, dtype=jnp.int32) for other in others]
    )

    def natural(rows):
        parts = rows.reshape(seq_count, row_count, -1)
        parts = [lax.dynamic_index_in_dim(parts, other, 0) for other in others]
        return jnp.concatenate(parts, axis=0).reshape(rows.shape)

    def halves(rows):
        half = rows.shape[0] // 2
        return [Gather(rows[:half], up, seq_count), Gather(rows[half:], down, seq_count)]

    def blocks_of(gathers):
        for g in gathers:
            g.take()
        return [g.have[m] for m in range(seq_count) for g in gathers]

    window_gathers = halves(inputs[0])
    for g in window_gathers:
        g.send()

    def by_head(weight):
        return weight.reshape(weight.shape[0], seq_count, -1)

    vectors = jnp.stack([first_gain, first_shift, bias_out, second_gain, second_shift, bias_outer])
    vectors = jnp.concatenate([vectors, bias_inner.reshape(2, row_count)], axis=0)
    vectors = jnp.pad(vectors, ((0, EXTRA - 8), (0, 0)))
    rel_rows = relative_weight.shape[0]
    rel_blocks = -(-rel_rows // EXTRA)
    rel_part = jnp.pad(by_head(relative_weight), ((0, rel_blocks * EXTRA - rel_rows), (0, 0), (0, 0)))
    rel_part = rel_part.reshape(rel_blocks, EXTRA, seq_count, key_width).transpose(2, 1, 0, 3)
    rel_part = rel_part.reshape(seq_count, EXTRA, -1)
    spare = heads_width - row_count - rel_part.shape[2]
    extra = jnp.concatenate(
        [
            jnp.broadcast_to(vectors[None], (seq_count,) + vectors.shape),
            jnp.pad(rel_part, ((0, 0), (0, 0), (0, spare))),
        ],
        axis=2,
    )
    mine = jnp.concatenate(
        [by_head(query_weight), by_head(key_weight), by_head(value_weight)], axis=2
    ).transpose(1, 0, 2)
    mine = jnp.concatenate([mine, extra], axis=1)
    half = mine.shape[1] // 2
    mine = lax.dynamic_slice_in_dim(mine, core * half, half, 1)

    def own_quarter(weight):
        quarter = weight.shape[0] // 4
        return lax.dynamic_slice_in_dim(weight, (2 * core + plane) * quarter, quarter, 0)

    inner_part, outer_part = own_quarter(inner_weight), own_quarter(outer_weight)
    mine, inner_part, outer_part = pin_all(window_gathers, mine, inner_part, outer_part)
    for step in range(1, len(up)):
        for g in window_gathers:
            g.send()
    weight_gathers = [
        Gather(inner_part, up, seq_count),
        Gather(outer_part, down, seq_count),
    ]
    for g in weight_gathers:
        g.send()
    mine = lax.all_to_all(mine, "seq", 0, 0, tiled=True)
    (mine,) = pin_all(window_gathers, mine)
    first = core == 0
    theirs = other_core(mine)
    attention_weight = jnp.concatenate(
        [jnp.where(first, mine, theirs), jnp.where(first, theirs, mine)], axis=1
    )
    table, table_back = basis_tables(jnp.asarray(basis_constants(length)), length)
    flat = attention_weight[:, row_count:]
    vectors = flat[:, :8, :row_count].astype(F32)
    inner_bias = vectors[:, 6:8].reshape(1, -1)
    vectors = vectors.transpose(1, 0, 2).reshape(8, width)
    rel = flat[:, :, row_count : row_count + rel_blocks * key_width]
    rel = rel.reshape(seq_count, EXTRA, rel_blocks, key_width).transpose(0, 2, 1, 3)
    rel = rel.reshape(seq_count, rel_blocks * EXTRA, key_width)[:, :rel_rows].reshape(REL, key_width)

    window_blocks = blocks_of(window_gathers)

    order = bin_order[0]
    placing = (order[:, None] == along[None, :]).astype(BF16)
    bias = jnp.concatenate([bias_content, bias_position])[None].astype(F32)
    window, hidden_one, in_bins, weight_whole = project(
        window_blocks, attention_weight, vectors, bias, row_count
    )
    placed_heads = matmul(placing, in_bins).astype(BF16)
    (placed_heads,) = pin_all(weight_gathers, placed_heads)
    for g in weight_gathers:
        g.take()
    planes = [[OtherPlane({1: g.have[1]}, wz_count)] for g in weight_gathers]
    later = [{m: block for m, block in g.have.items() if m > 1} for g in weight_gathers]
    for step in range(1, len(up)):
        for g in weight_gathers:
            g.send()
    mixed, probs = attend(placed_heads, rel, table)
    (mixed,) = pin_all(weight_gathers + [p[0] for p in planes], mixed)
    for p, blocks in zip(planes, later):
        p.append(OtherPlane(blocks, wz_count))
    for g, p, blocks in zip(weight_gathers, planes, later):
        g.take()
        last = {m: block for m, block in g.have.items() if m > 1 and m not in blocks}
        p.append(OtherPlane(last, wz_count))
    mixed_along = natural(mixed).reshape(seq_count, row_count, val_width)
    attended = [matmul(mixed_along[m], out_weight).astype(BF16) for m in range(seq_count)]
    attended = split_columns(attended, seq_count)
    for g in attended:
        g.send()
    own_order = lax.dynamic_slice_in_dim(order, row_start, row_count, 0)
    placed = matmul((own_order[:, None] == along[None, :]).astype(BF16), window)
    (placed,) = pin_all(attended + [p[1] for p in planes], placed)
    attended = [g.rest() for g in attended]
    weight_parts = []
    for g, p, own in zip(weight_gathers, planes, (inner_weight, outer_weight)):
        across = {m: block for exchange in p for m, block in exchange.new.items()}
        parts = [own]
        for m in range(1, seq_count):
            pair = [g.have[m], across[m]]
            parts += pair + [other_core(block) for block in pair]
        weight_parts.append(parts)

    grad_rows = grad_output[0]
    layer_output, d_mixed_in, hidden_two, activated, d_inner, sums, inner_sums = feed_forward(
        where, placed, attended, grad_rows, vectors, inner_bias, *weight_parts
    )

    d_mixed_gathers = halves(d_mixed_in)
    for g in d_mixed_gathers:
        g.send()
    came_inner = other_core(half_gradient(seq_count, True, where, hidden_two, d_inner))
    outer_away = half_gradient(seq_count, False, where, activated, grad_rows)
    (outer_away,) = pin_some(d_mixed_gathers, outer_away, firsts=[up[0], down[0]])
    came_outer = other_core(outer_away)
    kept_inner = half_gradient(seq_count, True, where, hidden_two, d_inner, came_inner)
    kept_inner = pin_all(d_mixed_gathers, *kept_inner)
    for step in range(1, len(up)):
        for g in d_mixed_gathers:
            g.send()
    kept_outer = half_gradient(seq_count, False, where, activated, grad_rows, came_outer)
    kept = pin_all(d_mixed_gathers, *kept_inner, *kept_outer)
    d_mixed_blocks = blocks_of(d_mixed_gathers)
    count = seq_count
    inner_sums_of, outer_sums_of = [
        [
            Scatter([kept[2 * (k * count + m) + side] for m in range(count)], bits, count)
            for side, bits in enumerate((up, down))
        ]
        for k in range(2)
    ]
    for g in inner_sums_of:
        g.send()

    d_attended, out_away, grad_out_w = mixed_back(
        seq_count, where, mixed, out_weight, d_mixed_blocks
    )
    (d_attended,) = pin_some(inner_sums_of, d_attended)
    out_core = OtherCore(out_away)

    def send_all(exchanges):
        for exchange in exchanges:
            exchange.send()

    def scatter_windows(piece):
        return lax.psum_scatter(piece.astype(BF16), "wz", scatter_dimension=0, tiled=True)

    def gather_windows(piece):
        return lax.all_gather(piece, ("core", "wz"), axis=0, tiled=True)

    def joined_sum(scatters):
        return jnp.concatenate([g.rest().astype(BF16) for g in scatters], axis=1)

    (d_attended,) = pin_all([out_core], d_attended)
    out_sum = scatter_windows(grad_out_w + out_core.new[0].astype(F32))
    back = attend_back(0, placed_heads, rel, table_back, mixed, d_attended, probs)
    *back, out_sum = pin_all(inner_sums_of, *back, out_sum)
    out_sum = gather_windows(out_sum)
    for step in range(1, len(up)):
        send_all(inner_sums_of)
    send_all(outer_sums_of)
    for head in range(1, key_width // KEY):
        back = attend_back(head, placed_heads, rel, table_back, mixed, d_attended, probs, back)
    *back, out_sum = pin_all(inner_sums_of, *back, out_sum)
    d_heads, d_rel, d_bias = back
    inner_sum = scatter_windows(joined_sum(inner_sums_of))
    d_along, *d_normed, first_sums = rows_back(
        seq_count, where, order[None], d_heads, window, weight_whole
    )
    out = pin_all(outer_sums_of, d_along, inner_sum, *d_normed)
    d_along, inner_sum, d_normed = out[0], out[1], out[2:]
    inner_sum = gather_windows(inner_sum)
    for step in range(1, len(up)):
        send_all(outer_sums_of)
    arrived = [
        Scatter([d_normed[2 * m + side] for m in range(count)], bits, count)
        for side, bits in enumerate((up, down))
    ]
    results = pack(
        seq_count, where, hidden_one, d_along, first_sums, sums, inner_sums, d_bias, d_rel
    )
    results = pin_all(outer_sums_of, *results)
    packed_core = OtherCore(results[1])
    outer_sum = scatter_windows(pin(joined_sum(outer_sums_of), inner_sum)[0])
    (packed,) = pin_all([packed_core], results[0])
    packed = (packed.astype(F32) + packed_core.new[0].astype(F32)).astype(BF16)
    packed_shape = packed.shape
    packed = lax.all_to_all(packed, "seq", 0, 0, tiled=True)
    send_all(arrived)
    take_after(arrived, packed)
    packed_cube = CubeSum(packed.reshape(-1, packed_shape[2]), wz_count)
    packed_cube.send()
    take_after(arrived, packed_cube.new[0])
    packed_cube.send()
    (outer_sum,) = pin_all(arrived, outer_sum)
    outer_sum = gather_windows(outer_sum)
    for step in range(1, len(up)):
        send_all(arrived)
    take_after(arrived, packed_cube.new[0])
    d_mixed_blocks = pin(packed_cube.new[0], *d_mixed_blocks)[1:]
    packed_cube.send()
    returned = returned_rows(
        seq_count, where, order.reshape(2 * seq_count, row_count // 2), d_mixed_blocks
    )
    own_unit, own_scale = norm_of(inputs[0].astype(F32))
    arrived = jnp.concatenate([g.rest() for g in arrived], axis=1)
    grad_inputs = norm_back(own_unit, own_scale, vectors[0:1], arrived) + returned

    def both_halves(pieces, axis):
        half = pieces.shape[0] // 2
        return jnp.concatenate([pieces[:half], pieces[half:]], axis=axis).astype(F32)

    grad_out_w = both_halves(out_sum, 0)
    (grad_inputs,) = pin_all([packed_cube], grad_inputs)
    packed_cube.send()
    grad_inner_w = both_halves(inner_sum, 1)
    grad_outer_w = both_halves(outer_sum, 0)
    packed = packed_cube.rest().reshape(packed_shape)
    grad_query_w, grad_key_w, grad_value_w, flat = unpack(
        where, (packed, other_core(packed)), row_count, key_width, val_width
    )
    small = jnp.sum(flat[:, :16, :row_count], axis=0)
    g_gain_one, g_shift_one, g_out_b, g_gain_two, g_shift_two, g_outer_b = small[:6]
    g_inner_b = small[6:8].reshape(-1)
    grad_rel = flat[:, :, row_count : row_count + rel_blocks * key_width]
    grad_rel = grad_rel.reshape(seq_count, EXTRA, rel_blocks, key_width).transpose(2, 1, 0, 3)
    grad_rel = grad_rel.reshape(rel_blocks * EXTRA, -1)[:rel_rows]
    return (
        layer_output[None],
        grad_inputs[None],
        g_gain_one,
        g_shift_one,
        grad_query_w,
        grad_key_w,
        grad_value_w,
        small[8, :key_width],
        small[9, :key_width],
        grad_rel,
        grad_out_w,
        g_out_b,
        g_gain_two,
        g_shift_two,
        grad_inner_w,
        g_inner_b,
        grad_outer_w,
        g_outer_b,
    )


def solution(mesh):
    seq_count = mesh.shape["seq"]
    devices = mesh.devices.reshape(seq_count, -1, 2)
    split_mesh = Mesh(devices, ("seq", "wz", "core"))
    rows = P(("wz", "core"), "seq", None)
    vector = P("seq")
    matrix = P("seq", None)
    weights = (
        vector,
        vector,
        matrix,
        matrix,
        matrix,
        vector,
        vector,
        matrix,
        matrix,
        vector,
        vector,
        vector,
        matrix,
        vector,
        matrix,
        vector,
    )
    return jax.shard_map(
        functools.partial(shards, seq_count, mesh.shape["win"] // 2),
        mesh=split_mesh,
        in_specs=(rows, P(("wz", "core"), None)) + weights + (rows,),
        out_specs=(rows, rows) + weights,
        check_vma=False,
    )
```

```python
import functools
import math

import jax
import jax.numpy as jnp
import numpy as np
from jax import lax
from jax.experimental import pallas as pl
from jax.experimental.pallas import tpu as pltpu
from jax.sharding import Mesh
from jax.sharding import PartitionSpec as P

HEADS = 8
KEY = 64
VAL = 192
REL = 192
BF16 = jnp.bfloat16
F32 = jnp.float32
VMEM_LIMIT = 56 * 2**20
EXTRA = 32


def matmul(a, b):
    return lax.dot_general(a, b, (((1,), (0,)), ((), ())), preferred_element_type=F32)


def matmul_nt(a, b):
    return lax.dot_general(a, b, (((1,), (1,)), ((), ())), preferred_element_type=F32)


def matmul_tn(a, b):
    return lax.dot_general(a, b, (((0,), (0,)), ((), ())), preferred_element_type=F32)


def head_part(rows, head):
    lanes = lax.broadcasted_iota(jnp.int32, rows.shape, 1)
    inside = (lanes >= head * KEY) & (lanes < (head + 1) * KEY)
    return jnp.where(inside, rows, jnp.zeros_like(rows))


def head_columns(key_width):
    return [slice(k * key_width, (k + 1) * key_width) for k in range(3)]


def attend_kernel(heads, rows, placed, rel, table, mixed, probs):
    length = placed.shape[0]
    key_width = heads * KEY
    content_at, position_at, keys_at = head_columns(key_width)
    first = pl.program_id(0) * rows
    here = pl.ds(pl.multiple_of(first, rows), rows)
    basis = table[:, pl.ds(pl.multiple_of(length - rows - first, rows), length + rows)]
    content, position, keys = placed[here, content_at], placed[here, position_at], placed[:, keys_at]
    parts = []
    for head in range(heads):
        q_basis = matmul_nt(head_part(position, head), rel[...]).astype(BF16)
        grid = matmul(q_basis, basis)
        shifted = pltpu.roll(grid, 0, 1, stride=1, stride_axis=0)[:, rows:]
        scores = matmul_nt(head_part(content, head), keys) + shifted
        top = jnp.max(scores, axis=1, keepdims=True)
        weights = jnp.exp(scores - top)
        total = jnp.sum(weights, axis=1, keepdims=True)
        prob = (weights * (1.0 / total)).astype(BF16)
        probs[head] = prob
        values_at = 3 * key_width + head * VAL
        parts.append(matmul(prob, placed[:, values_at : values_at + VAL]))
    mixed[...] = jnp.concatenate(parts, axis=1).astype(BF16)


def attend(placed, rel, table):
    length = placed.shape[0]
    heads = rel.shape[1] // KEY
    rows = math.gcd(256, length)
    whole = lambda array: pl.BlockSpec(array.shape, lambda i: (0, 0))
    return pl.pallas_call(
        functools.partial(attend_kernel, heads, rows),
        grid=(length // rows,),
        in_specs=[whole(placed), whole(rel), whole(table)],
        out_specs=[
            pl.BlockSpec((rows, heads * VAL), lambda i: (i, 0)),
            pl.BlockSpec((heads, rows, length), lambda i: (0, i, 0)),
        ],
        out_shape=[
            jax.ShapeDtypeStruct((length, heads * VAL), BF16),
            jax.ShapeDtypeStruct((heads, length, length), BF16),
        ],
        compiler_params=pltpu.CompilerParams(vmem_limit_bytes=VMEM_LIMIT),
        cost_estimate=pl.CostEstimate(
            flops=2 * heads * length * length * 1024,
            bytes_accessed=2 * heads * length * length + 8 * length * heads * VAL,
            transcendentals=heads * length * length,
        ),
    )(placed, rel, table)


def attend_back_kernel(heads, head, rows, *refs):
    placed, rel, table, flip, mixed, d_mixed, probs = refs[:7]
    before = refs[7:-5]
    d_heads, d_rel, d_bias, keys_sum, values_sum = refs[-5:]
    length = placed.shape[0]
    key_width = heads * KEY
    content_at, position_at, keys_at = head_columns(key_width)
    step = pl.program_id(0)

    @pl.when(step == 0)
    def _():
        keys_sum[...] = jnp.zeros_like(keys_sum)
        values_sum[...] = jnp.zeros_like(values_sum)
        for k, out in enumerate((d_heads, d_rel, d_bias)):
            out[...] = before[k][...] if before else jnp.zeros_like(out)

    first = pl.multiple_of(step * rows, rows)
    here = pl.ds(first, rows)
    basis = table[:, pl.ds(first, length + rows)]
    content, position, keys = placed[here, content_at], placed[here, position_at], placed[:, keys_at]
    blocks = length // rows
    columns = slice(head * VAL, (head + 1) * VAL)
    values_at = 3 * key_width + head * VAL
    d_part = d_mixed[:, columns]
    delta = jnp.sum(d_part.astype(F32) * mixed[:, columns].astype(F32), axis=1, keepdims=True)
    prob = probs[0]
    values_sum[...] += matmul_tn(d_part, prob)
    d_prob = matmul_nt(d_part, placed[:, values_at : values_at + VAL])
    d_score = (prob.astype(F32) * (d_prob - delta)).astype(BF16)
    keys_sum[...] += matmul_tn(head_part(content, head), d_score)
    d_content = head_part(matmul(d_score, keys), head)
    turned = [
        matmul(d_score[:, (blocks - 1 - b) * rows : (blocks - b) * rows], flip[...])
        for b in range(blocks)
    ]
    turned = jnp.concatenate(turned + [jnp.zeros((rows, rows), F32)], axis=1)
    d_grid = pltpu.roll(turned, 0, 1, stride=1, stride_axis=0).astype(BF16)
    d_basis = matmul_nt(d_grid, basis).astype(BF16)
    d_position = head_part(matmul(d_basis, rel[...]), head)
    d_rel[...] += matmul_tn(d_basis, head_part(position, head))
    d_heads[here, :key_width] += ((d_content + d_position) * KEY ** (-0.5)).astype(BF16)
    d_bias[0:1, :] += jnp.sum(d_content, axis=0, keepdims=True)
    d_bias[1:2, :] += jnp.sum(d_position, axis=0, keepdims=True)

    @pl.when(step == blocks - 1)
    def _():
        d_heads[:, key_width : 2 * key_width] += keys_sum[...].T.astype(BF16)
        values_to = 2 * key_width + head * VAL
        d_heads[:, values_to : values_to + VAL] = values_sum[...].T.astype(BF16)


def attend_back(head, placed, rel, table, mixed, d_mixed, probs, before=()):
    length = placed.shape[0]
    key_width = rel.shape[1]
    heads = key_width // KEY
    val_width = heads * VAL
    rows = math.gcd(256, length)
    at = jnp.arange(rows)
    flip = (at[:, None] + at[None, :] == rows - 1).astype(BF16)
    block = lambda width: pl.BlockSpec((rows, width), lambda i: (i, 0))
    outs = [
        shape((length, 2 * key_width + val_width), BF16),
        shape((REL, key_width), F32),
        shape((8, key_width), F32),
    ]
    return pl.pallas_call(
        functools.partial(attend_back_kernel, heads, head, rows),
        grid=(length // rows,),
        in_specs=[
            whole_spec(placed),
            whole_spec(rel),
            whole_spec(table),
            whole_spec(flip),
            block(val_width),
            block(val_width),
            pl.BlockSpec((1, rows, length), lambda i: (head, i, 0)),
        ]
        + [whole_spec(array) for array in before],
        out_specs=[whole_spec(out) for out in outs],
        out_shape=outs,
        scratch_shapes=[
            pltpu.VMEM((key_width, length), F32),
            pltpu.VMEM((VAL, length), F32),
        ],
        compiler_params=pltpu.CompilerParams(vmem_limit_bytes=VMEM_LIMIT),
        cost_estimate=pl.CostEstimate(
            flops=2 * length * length * 1536,
            bytes_accessed=2 * length * length + 16 * length * val_width,
            transcendentals=0,
        ),
    )(placed, rel, table, flip, mixed, d_mixed, probs, *before)


def norm_back(unit, scale, gain, grad):
    scaled = grad * gain
    mean_one = jnp.mean(scaled, axis=-1, keepdims=True)
    mean_two = jnp.mean(scaled * unit, axis=-1, keepdims=True)
    return (scaled - mean_one - unit * mean_two) * scale


def whole_spec(array):
    zeros = (0,) * len(array.shape)
    return pl.BlockSpec(array.shape, lambda *_: zeros)


def scalar_spec():
    return pl.BlockSpec(memory_space=pltpu.SMEM)


def params(**more):
    return pltpu.CompilerParams(vmem_limit_bytes=VMEM_LIMIT, **more)


def shape(dims, dtype):
    return jax.ShapeDtypeStruct(tuple(dims), dtype)


def basis_constants(window_len):
    features = REL // 6
    f = np.arange(features, dtype=np.float64)
    half_life = 2.0 ** (3.0 + f * (math.log2(window_len) - 3.0) / (features - 1))
    spread = window_len / (2.0 * features)
    first = window_len / features
    centres = first + f * (window_len - first) / (features - 1)
    concentration = (centres / spread) ** 2
    rate = centres / spread**2
    offset = concentration * np.log(rate) - np.array([math.lgamma(c) for c in concentration])
    columns = [math.log(2.0) / half_life, 2.0 ** (f + 1) - 1.0, concentration - 1.0, rate, offset]
    columns += [np.zeros(features)] * 3
    return np.stack(columns, axis=1).astype(np.float32)


def table_kernel(length, constants, forth, back):
    features = REL // 6
    decay, inside_below, power, rate, offset = [constants[:, k : k + 1] for k in range(5)]

    def gamma(distance):
        logged = power * jnp.log(jnp.maximum(distance, 1.0)) - rate * distance + offset
        return jnp.where(distance == 0.0, 0.0, jnp.exp(logged)) + 1e-08

    every = lax.broadcasted_iota(jnp.int32, (1, length), 1).astype(F32)
    peak = jnp.max(gamma(every), axis=1, keepdims=True)
    lanes = lax.broadcasted_iota(jnp.int32, (1, 2 * length), 1).astype(F32)
    for table, signed in ((forth, lanes - length), (back, length - 1 - lanes)):
        distance = jnp.abs(signed)
        sign = jnp.where(signed > 0, 1.0, jnp.where(signed < 0, -1.0, 0.0))
        parts = (
            jnp.exp(-decay * distance),
            jnp.where(inside_below > distance, 1.0, 0.0),
            gamma(distance) / peak,
        )
        for k, part in enumerate(parts):
            table[k * features : (k + 1) * features, :] = part.astype(BF16)
            table[(3 + k) * features : (4 + k) * features, :] = (sign * part).astype(BF16)


def basis_tables(constants, length):
    out = shape((REL, 2 * length), BF16)
    return pl.pallas_call(
        functools.partial(table_kernel, length),
        out_shape=[out, out],
        compiler_params=params(),
    )(constants)


def norm_of(rows):
    centre = rows - jnp.mean(rows, axis=1, keepdims=True)
    scale = lax.rsqrt(jnp.mean(centre * centre, axis=1, keepdims=True) + 1e-05)
    return centre * scale, scale


def project_kernel(blocks, row_count, *refs):
    parts, (weight, vectors, bias, window, hidden, heads, flat, block) = refs[:blocks], refs[blocks:]
    step = pl.program_id(0)

    @pl.when(step == 0)
    def _():
        for s in range(weight.shape[0]):
            flat[s * row_count : (s + 1) * row_count, :] = weight[s, :row_count, :]

    for k in range(blocks):

        @pl.when(step == k)
        def _():
            block[...] = parts[k][...]

    window[...] = block[...]
    unit, _ = norm_of(block[...].astype(F32))
    normed = (unit * vectors[0:1, :] + vectors[1:2, :]).astype(BF16)
    hidden[...] = normed
    total = matmul(normed, flat[...])
    key_width = bias.shape[1] // 2
    query = total[:, :key_width] * KEY ** (-0.5)
    heads[:, :key_width] = (query + bias[0:1, :key_width]).astype(BF16)
    heads[:, key_width : 2 * key_width] = (query + bias[0:1, key_width:]).astype(BF16)
    heads[:, 2 * key_width :] = total[:, key_width:].astype(BF16)


def project(parts, weight, vectors, bias, row_count):
    blocks = len(parts)
    rows, width = parts[0].shape
    heads_width = weight.shape[2] + bias.shape[1] // 2
    out = lambda w: pl.BlockSpec((rows, w), lambda i: (i, 0))
    return pl.pallas_call(
        functools.partial(project_kernel, blocks, row_count),
        grid=(blocks,),
        in_specs=[whole_spec(a) for a in (*parts, weight, vectors, bias)],
        out_specs=[
            out(width),
            out(width),
            out(heads_width),
            pl.BlockSpec((width, weight.shape[2]), lambda i: (0, 0)),
        ],
        out_shape=[shape((blocks * rows, w), BF16) for w in (width, width, heads_width)]
        + [shape((width, weight.shape[2]), BF16)],
        scratch_shapes=[pltpu.VMEM((rows, width), BF16)],
        compiler_params=params(),
        cost_estimate=pl.CostEstimate(
            flops=2 * blocks * rows * width * heads_width,
            bytes_accessed=8 * blocks * rows * width,
            transcendentals=0,
        ),
    )(*parts, weight, vectors, bias)


def feed_kernel(count, chunk, *refs):
    each = 4 * count - 3
    parts = 2 * each
    where, placed, attended_a, attended_b, grad_rows, vectors, inner_bias = refs[:7]
    weights = refs[7 : 7 + parts]
    layer_output, d_mixed, hidden, activated, d_inner, sums, inner_sums = refs[7 + parts : 14 + parts]
    inner_whole, outer_whole, residual, unit, back, outer_sum, sems = refs[14 + parts :]
    here, core, plane = where[0], where[1], where[2]
    quarters = (2 * core + plane, 2 * core + 1 - plane, 2 - 2 * core + plane, 3 - 2 * core - plane)
    copies = []
    for k, whole in enumerate((inner_whole, outer_whole)):
        mine = weights[k * each : (k + 1) * each]
        size = whole.shape[0] // count
        quarter = size // 4
        moves = [(mine[0], here * size, size)]
        for m in range(1, count):
            start = jnp.bitwise_xor(here, m) * size
            for j, which in enumerate(quarters):
                moves.append((mine[4 * m - 3 + j], start + which * quarter, quarter))
        started = []
        for source, start, rows in moves:
            target = whole.at[pl.ds(pl.multiple_of(start, 16), rows), :]
            copy = pltpu.make_async_copy(source, target, sems.at[k, len(started)])
            copy.start()
            started.append(copy)
        copies.append(started)
    rows, width = placed.shape
    half = width // 2
    residual[:, :half] = placed[:, :half] + attended_a[...] + vectors[2:3, :half]
    residual[:, half:] = placed[:, half:] + attended_b[...] + vectors[2:3, half:]
    normed, scale = norm_of(residual[...])
    unit[...] = normed
    hidden[...] = (normed * vectors[3:4, :] + vectors[4:5, :]).astype(BF16)
    for started in copies:
        for copy in started:
            copy.wait()
    ff = outer_whole.shape[0]
    for c in range(ff // chunk):
        at = slice(c * chunk, (c + 1) * chunk)
        inner = matmul(hidden[...], inner_whole[:, at]) + inner_bias[0:1, at]
        below = 0.5 * (1.0 + lax.erf(inner * (0.5**0.5)))
        slope = below + inner * jnp.exp(-0.5 * inner * inner) * (0.5 / math.pi) ** 0.5
        active = (inner * below).astype(BF16)
        activated[:, at] = active
        grad = (matmul_nt(grad_rows[...], outer_whole[at, :]) * slope).astype(BF16)
        d_inner[:, at] = grad
        inner_sums[:, at] = jnp.sum(grad.astype(F32), axis=0, keepdims=True)
        back_term = matmul_nt(grad, inner_whole[:, at])
        outer_term = matmul(active, outer_whole[at, :])
        if c == 0:
            back[...] = back_term
            outer_sum[...] = outer_term
        else:
            back[...] += back_term
            outer_sum[...] += outer_term
    layer_output[...] = (residual[...] + outer_sum[...] + vectors[5:6, :]).astype(BF16)
    grad, normed = back[...], unit[...]
    dy = grad_rows[...].astype(F32)
    scaled = grad * vectors[3:4, :]
    mean_one = jnp.mean(scaled, axis=1, keepdims=True)
    mean_two = jnp.mean(scaled * normed, axis=1, keepdims=True)
    mixed_in = (dy + (scaled - mean_one - normed * mean_two) * scale).astype(BF16)
    d_mixed[...] = mixed_in
    sums[...] = jnp.zeros_like(sums)
    sums[2:3, :] = jnp.sum(mixed_in.astype(F32), axis=0, keepdims=True)
    sums[3:4, :] = jnp.sum(grad * normed, axis=0, keepdims=True)
    sums[4:5, :] = jnp.sum(grad, axis=0, keepdims=True)
    sums[5:6, :] = jnp.sum(dy, axis=0, keepdims=True)


def feed_forward(where, placed, attended, grad_rows, vectors, inner_bias, inner_parts, outer_parts):
    rows, width = placed.shape
    ff = inner_bias.shape[1]
    count = (len(inner_parts) + 3) // 4
    chunk = math.gcd(512, ff)
    weights = (*inner_parts, *outer_parts)
    small = (placed, *attended, grad_rows, vectors, inner_bias)
    outs = [
        shape((rows, width), BF16),
        shape((rows, width), BF16),
        shape((rows, width), BF16),
        shape((rows, ff), BF16),
        shape((rows, ff), BF16),
        shape((8, width), F32),
        shape((1, ff), F32),
    ]
    return pl.pallas_call(
        functools.partial(feed_kernel, count, chunk),
        in_specs=[scalar_spec()]
        + [pl.BlockSpec(memory_space=pltpu.VMEM) for _ in small]
        + [pl.BlockSpec(memory_space=pl.ANY) for _ in weights],
        out_specs=[pl.BlockSpec(memory_space=pltpu.VMEM) for _ in outs],
        out_shape=outs,
        scratch_shapes=[
            pltpu.VMEM((width, ff), BF16),
            pltpu.VMEM((ff, width), BF16),
            pltpu.VMEM((rows, width), F32),
            pltpu.VMEM((rows, width), F32),
            pltpu.VMEM((rows, width), F32),
            pltpu.VMEM((rows, width), F32),
            pltpu.SemaphoreType.DMA((2, 4 * count - 3)),
        ],
        compiler_params=params(),
        cost_estimate=pl.CostEstimate(
            flops=8 * rows * width * ff,
            bytes_accessed=4 * width * ff + 40 * rows * width,
            transcendentals=2 * rows * ff,
        ),
    )(where, *small, *weights)


def columns_at(ref, index, size, scratch):
    if size % 128 == 0:
        return ref[:, pl.ds(pl.multiple_of(index * size, 128), size)]
    for k in range(ref.shape[1] // size):

        @pl.when(index == k)
        def _():
            scratch[...] = ref[:, k * size : (k + 1) * size]

    return scratch[...]


def half_kernel(count, split, away, where, left, right, *refs):
    here, core = where[0], where[1]
    side = 1 - core if away else core
    shard = jnp.bitwise_xor(here, pl.program_id(0))
    if split:
        some = columns_at(left, shard, left.shape[1] // count, refs[-1])
        half = right.shape[1] // 2
        other = right[:, pl.ds(pl.multiple_of(side * half, 128), half)]
    else:
        some = columns_at(left, 2 * shard + side, left.shape[1] // count // 2, refs[-1])
        other = right[...]
    result = matmul_tn(some, other)
    if away:
        refs[0][0] = result.astype(BF16)
        return
    came, outs = refs[0], refs[1:-1]
    result += came[0].astype(F32)
    width = result.shape[1] // 2
    for m in range(count):

        @pl.when(pl.program_id(0) == m)
        def _():
            outs[2 * m][...] = result[:, :width].astype(BF16)
            outs[2 * m + 1][...] = result[:, width:].astype(BF16)


def half_gradient(count, split, where, left, right, came=None):
    away = came is None
    rows = left.shape[1] // count // (1 if split else 2)
    width = right.shape[1] // (2 if split else 1)
    block = pl.BlockSpec((1, rows, width), lambda i: (i, 0, 0))
    if away:
        outs, out_specs = shape((count, rows, width), BF16), block
    else:
        outs = [shape((rows, width // 2), BF16) for _ in range(2 * count)]
        out_specs = [whole_spec(out) for out in outs]
    return pl.pallas_call(
        functools.partial(half_kernel, count, split, away),
        grid=(count,),
        in_specs=[scalar_spec(), whole_spec(left), whole_spec(right)] + ([] if away else [block]),
        out_specs=out_specs,
        out_shape=outs,
        scratch_shapes=[pltpu.VMEM((left.shape[0], rows), BF16)],
        compiler_params=params(),
        cost_estimate=pl.CostEstimate(
            flops=2 * left.shape[0] * count * rows * width,
            bytes_accessed=4 * count * rows * width + 4 * left.shape[0] * left.shape[1],
            transcendentals=0,
        ),
    )(where, left, right, *(() if away else (came,)))


def mixed_back_kernel(count, parts_count, *refs):
    where, mixed, weight = refs[:3]
    parts = refs[3 : 3 + parts_count]
    d_attended, out_away, out_kept, out_sum = refs[3 + parts_count :]
    here, core = where[0], where[1]
    rows = parts[0].shape[0]
    for k, part in enumerate(parts):
        start = jnp.bitwise_xor(here, k // 2) * (2 * rows) + (k % 2) * rows
        at = pl.ds(pl.multiple_of(start, 32), rows)
        d_attended[at, :] = matmul_nt(part[...], weight[...]).astype(BF16)
        term = matmul_tn(mixed[at, :], part[...])
        if k == 0:
            out_sum[...] = term
        else:
            out_sum[...] += term
    half = out_kept.shape[0]
    out_kept[...] = out_sum[pl.ds(pl.multiple_of(core * half, 32), half), :]
    out_away[...] = out_sum[pl.ds(pl.multiple_of((1 - core) * half, 32), half), :].astype(BF16)


def mixed_back(count, where, mixed, weight, parts):
    length, val_width = mixed.shape
    width = weight.shape[1]
    vmem = pl.BlockSpec(memory_space=pltpu.VMEM)
    return pl.pallas_call(
        functools.partial(mixed_back_kernel, count, len(parts)),
        in_specs=[scalar_spec()] + [vmem] * (2 + len(parts)),
        out_specs=[vmem] * 3,
        out_shape=[
            shape((length, val_width), BF16),
            shape((val_width // 2, width), BF16),
            shape((val_width // 2, width), F32),
        ],
        scratch_shapes=[pltpu.VMEM((val_width, width), F32)],
        compiler_params=params(),
        cost_estimate=pl.CostEstimate(
            flops=4 * length * val_width * width,
            bytes_accessed=2 * length * (width + 2 * val_width),
            transcendentals=0,
        ),
    )(where, mixed, weight, *parts)


def rows_back_kernel(count, where, order, d_heads, window, weight, d_along, *refs):
    d_normed, first_sums = refs[:-1], refs[-1]
    here = where[0]
    step = pl.program_id(0)
    rows, width = window.shape
    length = order.shape[1]
    bins = lax.broadcasted_iota(jnp.int32, (rows, length), 0) + jnp.bitwise_xor(here, step) * rows
    picks = jnp.where(order[0:1, :] == bins, 1.0, 0.0).astype(BF16)
    along = matmul(picks, d_heads[...]).astype(BF16)
    d_along[...] = along
    unit, _ = norm_of(window[...].astype(F32))
    normed = matmul_nt(along, weight[...])

    @pl.when(step == 0)
    def _():
        first_sums[...] = jnp.zeros_like(first_sums)

    first_sums[0:1, :] += jnp.sum(normed * unit, axis=0, keepdims=True)
    first_sums[1:2, :] += jnp.sum(normed, axis=0, keepdims=True)
    half = width // 2
    for m in range(count):

        @pl.when(step == m)
        def _():
            d_normed[2 * m][...] = normed[:, :half].astype(BF16)
            d_normed[2 * m + 1][...] = normed[:, half:].astype(BF16)


def rows_back(count, where, order, d_heads, window, weight):
    length, width = window.shape
    rows = length // count
    heads_width = d_heads.shape[1]
    outs = [shape((length, heads_width), BF16)]
    outs += [shape((rows, width // 2), BF16) for _ in range(2 * count)]
    outs += [shape((8, width), F32)]
    return pl.pallas_call(
        functools.partial(rows_back_kernel, count),
        grid=(count,),
        in_specs=[
            scalar_spec(),
            whole_spec(order),
            whole_spec(d_heads),
            pl.BlockSpec((rows, width), lambda i: (i, 0)),
            whole_spec(weight),
        ],
        out_specs=[pl.BlockSpec((rows, heads_width), lambda i: (i, 0))]
        + [whole_spec(out) for out in outs[1:]],
        out_shape=outs,
        compiler_params=params(),
        cost_estimate=pl.CostEstimate(
            flops=2 * length * heads_width * (length + width),
            bytes_accessed=4 * length * (width + heads_width),
            transcendentals=0,
        ),
    )(where, order, d_heads, window, weight)


def pack_kernel(
    count, where, hidden, d_along, first_sums, sums, inner_sums, d_bias, d_rel, kept, away, grads
):
    here, core = where[0], where[1]
    step = pl.program_id(0)
    row_count = hidden.shape[1] // count
    key_width = d_rel.shape[1]
    terms = matmul_tn(hidden[...], d_along[...])

    @pl.when(step == 0)
    def _():
        for s in range(count):
            grads[s, :row_count, :] = terms[s * row_count : (s + 1) * row_count, :]

    @pl.when(step > 0)
    def _():
        for s in range(count):
            grads[s, :row_count, :] += terms[s * row_count : (s + 1) * row_count, :]

    @pl.when(step == pl.num_programs(0) - 1)
    def _():
        rel_rows = d_rel.shape[0] // count
        for s in range(count):
            at = slice(s * row_count, (s + 1) * row_count)
            grads[s, row_count:, :] = jnp.zeros((EXTRA, grads.shape[2]), F32)
            grads[s, row_count : row_count + 2, :row_count] = first_sums[0:2, at]
            grads[s, row_count + 2 : row_count + 6, :row_count] = sums[2:6, at]
            for j in range(2):
                part = slice((2 * s + j) * row_count, (2 * s + j + 1) * row_count)
                grads[s, row_count + 6 + j : row_count + 7 + j, :row_count] = inner_sums[0:1, part]
            for j in range(-(-rel_rows // EXTRA)):
                some = d_rel[s * rel_rows + j * EXTRA : s * rel_rows + min(rel_rows, (j + 1) * EXTRA), :]
                lane = row_count + j * key_width
                grads[s, row_count : row_count + some.shape[0], lane : lane + key_width] = some
        for s in range(count):

            @pl.when(here == s)
            def _():
                grads[s, row_count + 8 : row_count + 10, :key_width] = d_bias[0:2, :]

        half = kept.shape[1]
        kept[...] = grads[:, pl.ds(pl.multiple_of(core * half, 16), half), :].astype(BF16)
        away[...] = grads[:, pl.ds(pl.multiple_of((1 - core) * half, 16), half), :].astype(BF16)


def pack(count, where, hidden, d_along, *small):
    length, width = hidden.shape
    heads_width = d_along.shape[1]
    rows = math.gcd(768, length)
    packed = (count, width // count + EXTRA, heads_width)
    outs = [shape((count, packed[1] // 2, heads_width), BF16) for _ in range(2)]
    return pl.pallas_call(
        functools.partial(pack_kernel, count),
        grid=(length // rows,),
        in_specs=[
            scalar_spec(),
            pl.BlockSpec((rows, width), lambda i: (i, 0)),
            pl.BlockSpec((rows, heads_width), lambda i: (i, 0)),
        ]
        + [whole_spec(a) for a in small],
        out_specs=[whole_spec(out) for out in outs],
        out_shape=outs,
        scratch_shapes=[pltpu.VMEM(packed, F32)],
        compiler_params=params(),
        cost_estimate=pl.CostEstimate(
            flops=2 * length * heads_width * width,
            bytes_accessed=2 * length * (width + heads_width) + 8 * width * heads_width,
            transcendentals=0,
        ),
    )(where, hidden, d_along, *small)


def swap(array, mask, count):
    return lax.ppermute(array, "seq", [(i, i ^ mask) for i in range(count)])


def bit_orders(count):
    bits = [1 << k for k in range(count.bit_length() - 1)]
    return bits, bits[::-1]


def pin(*arrays):
    return lax.optimization_barrier(arrays)


def returned_kernel(count, where, order, *refs):
    parts, returned = refs[:-1], refs[-1]
    here = where[0]
    rows = parts[0].shape[0]
    bins = lax.broadcasted_iota(jnp.int32, (returned.shape[0], rows), 0)
    bins = bins + here * returned.shape[0]
    for k, part in enumerate(parts):
        shard = jnp.bitwise_xor(here, k // 2)
        picks = jnp.where(order[pl.ds(2 * shard + k % 2, 1), :] == bins, 1.0, 0.0).astype(BF16)
        term = matmul(picks, part[...])
        if k == 0:
            returned[...] = term
        else:
            returned[...] += term


def returned_rows(count, where, order, parts):
    rows, width = parts[0].shape
    vmem = pl.BlockSpec(memory_space=pltpu.VMEM)
    return pl.pallas_call(
        functools.partial(returned_kernel, count),
        in_specs=[scalar_spec()] + [vmem] * (1 + len(parts)),
        out_specs=vmem,
        out_shape=shape((2 * rows, width), F32),
        compiler_params=params(),
        cost_estimate=pl.CostEstimate(
            flops=4 * rows * rows * len(parts) * width,
            bytes_accessed=2 * rows * width * len(parts) + 8 * rows * width,
            transcendentals=0,
        ),
    )(where, order, *parts)


def unpack_kernel(count, row_count, key_width, *refs):
    where, mine, theirs, query, key, value, extra, whole = refs
    half = mine.shape[1]
    core = where[1]
    for c in range(2):

        @pl.when(core == c)
        def _():
            whole[:, c * half : (c + 1) * half, :] = mine[...]
            whole[:, (1 - c) * half : (2 - c) * half, :] = theirs[...]

    for out, at in ((query, 0), (key, key_width), (value, 2 * key_width)):
        size = out.shape[1] // count
        for s in range(count):
            rows = whole[s, :row_count, at : at + size]
            out[:, s * size : (s + 1) * size] = rows.astype(F32)
    extra[...] = whole[:, row_count:, :].astype(F32)


def unpack(where, parts, row_count, key_width, val_width):
    count, half, width = parts[0].shape
    vmem = pl.BlockSpec(memory_space=pltpu.VMEM)
    return pl.pallas_call(
        functools.partial(unpack_kernel, count, row_count, key_width),
        in_specs=[scalar_spec()] + [vmem] * 2,
        out_specs=[vmem] * 4,
        out_shape=[
            shape((row_count, count * key_width), F32),
            shape((row_count, count * key_width), F32),
            shape((row_count, count * val_width), F32),
            shape((count, EXTRA, width), F32),
        ],
        scratch_shapes=[pltpu.VMEM((count, 2 * half, width), BF16)],
        compiler_params=params(),
    )(where, *parts)


class Exchange:
    def __init__(self):
        self.new = {}


def pin_all(exchanges, *arrays):
    keys = [sorted(e.new) for e in exchanges]
    out = pin(*arrays, *[e.new[k] for e, ks in zip(exchanges, keys) for k in ks])
    at = len(arrays)
    for e, ks in zip(exchanges, keys):
        e.new = dict(zip(ks, out[at : at + len(ks)]))
        at += len(ks)
    return out[: len(arrays)]


def take_after(exchanges, array):
    pin_all(exchanges, array)


def pin_some(exchanges, *arrays, firsts=None):
    firsts = firsts or [max(e.new) for e in exchanges]
    out = pin(*arrays, *[e.new[k] for e, k in zip(exchanges, firsts)])
    for e, k, block in zip(exchanges, firsts, out[len(arrays) :]):
        e.new[k] = block
    return out[: len(arrays)]


class Gather(Exchange):
    def __init__(self, part, order, count):
        super().__init__()
        self.have, self.order, self.count, self.last = {0: part}, order, count, [0]

    def take(self):
        self.have.update(self.new)
        self.new = {}

    def send(self):
        self.take()
        new = {}
        for m in self.last:
            used = [k for k, bit in enumerate(self.order) if m & bit]
            for bit in self.order[max(used, default=-1) + 1 :]:
                new[m | bit] = swap(self.have[m], bit, self.count)
        self.new, self.last = new, sorted(new)


class Scatter(Exchange):
    def __init__(self, blocks, order, count):
        super().__init__()
        self.have, self.order, self.count, self.step = dict(enumerate(blocks)), order, count, 0

    def take(self):
        if self.new:
            bit = self.order[self.step - 1]
            self.have = {
                m: self.have[m].astype(F32) + self.new[m | bit].astype(F32)
                for m in self.have
                if not m & bit
            }
            self.new = {}

    def send(self):
        self.take()
        bit = self.order[self.step]
        self.new = {
            m: swap(self.have[m].astype(BF16), bit, self.count)
            for m in sorted(self.have, reverse=True)
            if m & bit
        }
        self.step += 1

    def rest(self):
        while self.step < len(self.order):
            self.send()
        self.take()
        return self.have[0]


class CubeSum(Exchange):
    def __init__(self, piece, count):
        super().__init__()
        self.total, self.step = piece, 0
        self.count, self.bits = count, count.bit_length() - 1

    def swap(self, array, bit):
        return lax.ppermute(array, "wz", [(i, i ^ bit) for i in range(self.count)])

    def mine(self, bit):
        return jnp.where(lax.axis_index("wz") & bit, 1, 0)

    def take(self):
        if self.new:
            came, at = self.new[0], self.step - 1
            if at < self.bits:
                half = came.shape[0]
                kept = lax.dynamic_slice_in_dim(self.total, self.mine(1 << at) * half, half, 0)
                self.total = (kept.astype(F32) + came.astype(F32)).astype(BF16)
            else:
                upper = self.mine(1 << (2 * self.bits - 1 - at)) == 1
                self.total = jnp.concatenate(
                    [jnp.where(upper, came, self.total), jnp.where(upper, self.total, came)], axis=0
                )
            self.new = {}

    def send(self):
        self.take()
        if self.step >= 2 * self.bits:
            return
        if self.step < self.bits:
            bit = 1 << self.step
            half = self.total.shape[0] // 2
            away = lax.dynamic_slice_in_dim(self.total, (1 - self.mine(bit)) * half, half, 0)
            self.new = {0: self.swap(away.astype(BF16), bit)}
        else:
            self.new = {0: self.swap(self.total, 1 << (2 * self.bits - 1 - self.step))}
        self.step += 1

    def rest(self):
        while self.step < 2 * self.bits:
            self.send()
        self.take()
        return self.total.astype(BF16)


class OtherPlane(Exchange):
    def __init__(self, blocks, count):
        super().__init__()
        pairs = [(i, i ^ 1) for i in range(count)]
        self.new = {m: lax.ppermute(block, "wz", pairs) for m, block in sorted(blocks.items())}


class OtherCore(Exchange):
    def __init__(self, array):
        super().__init__()
        self.new = {0: other_core(array)}


def split_columns(blocks, count):
    half = blocks[0].shape[1] // 2
    return [
        Scatter([block[:, k * half : (k + 1) * half] for block in blocks], order, count)
        for k, order in enumerate(bit_orders(count))
    ]


def other_core(array):
    return lax.ppermute(array, "core", [(0, 1), (1, 0)])


def shards(
    seq_count,
    wz_count,
    inputs,
    bin_order,
    first_gain,
    first_shift,
    query_weight,
    key_weight,
    value_weight,
    bias_content,
    bias_position,
    relative_weight,
    out_weight,
    bias_out,
    second_gain,
    second_shift,
    inner_weight,
    bias_inner,
    outer_weight,
    bias_outer,
    grad_output,
):
    row_count, width = inputs.shape[1:]
    length = bin_order.shape[1]
    here = lax.axis_index("seq")
    core = lax.axis_index("core")
    plane = lax.axis_index("wz") & 1
    where = jnp.stack([here, core, plane]).astype(jnp.int32)
    row_start = here * row_count
    key_width = query_weight.shape[1] // seq_count
    val_width = value_weight.shape[1] // seq_count
    heads_width = 2 * key_width + val_width
    up, down = bit_orders(seq_count)

    others = [jnp.bitwise_xor(here, m) for m in range(seq_count)]
    along = jnp.concatenate(
        [other * row_count + jnp.arange(row_count, dtype=jnp.int32) for other in others]
    )

    def natural(rows):
        parts = rows.reshape(seq_count, row_count, -1)
        parts = [lax.dynamic_index_in_dim(parts, other, 0) for other in others]
        return jnp.concatenate(parts, axis=0).reshape(rows.shape)

    def halves(rows):
        half = rows.shape[0] // 2
        return [Gather(rows[:half], up, seq_count), Gather(rows[half:], down, seq_count)]

    def blocks_of(gathers):
        for g in gathers:
            g.take()
        return [g.have[m] for m in range(seq_count) for g in gathers]

    window_gathers = halves(inputs[0])
    for g in window_gathers:
        g.send()

    def by_head(weight):
        return weight.reshape(weight.shape[0], seq_count, -1)

    vectors = jnp.stack([first_gain, first_shift, bias_out, second_gain, second_shift, bias_outer])
    vectors = jnp.concatenate([vectors, bias_inner.reshape(2, row_count)], axis=0)
    vectors = jnp.pad(vectors, ((0, EXTRA - 8), (0, 0)))
    rel_rows = relative_weight.shape[0]
    rel_blocks = -(-rel_rows // EXTRA)
    rel_part = jnp.pad(by_head(relative_weight), ((0, rel_blocks * EXTRA - rel_rows), (0, 0), (0, 0)))
    rel_part = rel_part.reshape(rel_blocks, EXTRA, seq_count, key_width).transpose(2, 1, 0, 3)
    rel_part = rel_part.reshape(seq_count, EXTRA, -1)
    spare = heads_width - row_count - rel_part.shape[2]
    extra = jnp.concatenate(
        [
            jnp.broadcast_to(vectors[None], (seq_count,) + vectors.shape),
            jnp.pad(rel_part, ((0, 0), (0, 0), (0, spare))),
        ],
        axis=2,
    )
    mine = jnp.concatenate(
        [by_head(query_weight), by_head(key_weight), by_head(value_weight)], axis=2
    ).transpose(1, 0, 2)
    mine = jnp.concatenate([mine, extra], axis=1)
    half = mine.shape[1] // 2
    mine = lax.dynamic_slice_in_dim(mine, core * half, half, 1)

    def own_quarter(weight):
        quarter = weight.shape[0] // 4
        return lax.dynamic_slice_in_dim(weight, (2 * core + plane) * quarter, quarter, 0)

    inner_part, outer_part = own_quarter(inner_weight), own_quarter(outer_weight)
    mine, inner_part, outer_part = pin_all(window_gathers, mine, inner_part, outer_part)
    for step in range(1, len(up)):
        for g in window_gathers:
            g.send()
    weight_gathers = [
        Gather(inner_part, up, seq_count),
        Gather(outer_part, down, seq_count),
    ]
    for g in weight_gathers:
        g.send()
    mine = lax.all_to_all(mine, "seq", 0, 0, tiled=True)
    (mine,) = pin_all(window_gathers, mine)
    first = core == 0
    theirs = other_core(mine)
    attention_weight = jnp.concatenate(
        [jnp.where(first, mine, theirs), jnp.where(first, theirs, mine)], axis=1
    )
    table, table_back = basis_tables(jnp.asarray(basis_constants(length)), length)
    flat = attention_weight[:, row_count:]
    vectors = flat[:, :8, :row_count].astype(F32)
    inner_bias = vectors[:, 6:8].reshape(1, -1)
    vectors = vectors.transpose(1, 0, 2).reshape(8, width)
    rel = flat[:, :, row_count : row_count + rel_blocks * key_width]
    rel = rel.reshape(seq_count, EXTRA, rel_blocks, key_width).transpose(0, 2, 1, 3)
    rel = rel.reshape(seq_count, rel_blocks * EXTRA, key_width)[:, :rel_rows].reshape(REL, key_width)

    window_blocks = blocks_of(window_gathers)

    order = bin_order[0]
    placing = (order[:, None] == along[None, :]).astype(BF16)
    bias = jnp.concatenate([bias_content, bias_position])[None].astype(F32)
    window, hidden_one, in_bins, weight_whole = project(
        window_blocks, attention_weight, vectors, bias, row_count
    )
    placed_heads = matmul(placing, in_bins).astype(BF16)
    (placed_heads,) = pin_all(weight_gathers, placed_heads)
    for g in weight_gathers:
        g.take()
    early = [{m: block for m, block in g.have.items() if m > 0} for g in weight_gathers]
    planes = [[OtherPlane(blocks, wz_count)] for blocks in early]
    for step in range(1, len(up)):
        for g in weight_gathers:
            g.send()
    mixed, probs = attend(placed_heads, rel, table)
    (mixed,) = pin_all(weight_gathers, mixed)
    for g, p, blocks in zip(weight_gathers, planes, early):
        g.take()
        last = {m: block for m, block in g.have.items() if m > 0 and m not in blocks}
        p.append(OtherPlane(last, wz_count))
    mixed_along = natural(mixed).reshape(seq_count, row_count, val_width)
    attended = [matmul(mixed_along[m], out_weight).astype(BF16) for m in range(seq_count)]
    attended = split_columns(attended, seq_count)
    for g in attended:
        g.send()
    own_order = lax.dynamic_slice_in_dim(order, row_start, row_count, 0)
    placed = matmul((own_order[:, None] == along[None, :]).astype(BF16), window)
    (placed,) = pin_all(attended, placed)
    attended = [g.rest() for g in attended]
    weight_parts = []
    for g, p, own in zip(weight_gathers, planes, (inner_weight, outer_weight)):
        across = {m: block for exchange in p for m, block in exchange.new.items()}
        parts = [own]
        for m in range(1, seq_count):
            pair = [g.have[m], across[m]]
            parts += pair + [other_core(block) for block in pair]
        weight_parts.append(parts)

    grad_rows = grad_output[0]
    layer_output, d_mixed_in, hidden_two, activated, d_inner, sums, inner_sums = feed_forward(
        where, placed, attended, grad_rows, vectors, inner_bias, *weight_parts
    )

    d_mixed_gathers = halves(d_mixed_in)
    for g in d_mixed_gathers:
        g.send()
    came_inner = other_core(half_gradient(seq_count, True, where, hidden_two, d_inner))
    outer_away = half_gradient(seq_count, False, where, activated, grad_rows)
    (outer_away,) = pin_some(d_mixed_gathers, outer_away, firsts=[up[0], down[0]])
    came_outer = other_core(outer_away)
    kept_inner = half_gradient(seq_count, True, where, hidden_two, d_inner, came_inner)
    kept_inner = pin_all(d_mixed_gathers, *kept_inner)
    for step in range(1, len(up)):
        for g in d_mixed_gathers:
            g.send()
    kept_outer = half_gradient(seq_count, False, where, activated, grad_rows, came_outer)
    kept = pin_all(d_mixed_gathers, *kept_inner, *kept_outer)
    d_mixed_blocks = blocks_of(d_mixed_gathers)
    count = seq_count
    inner_sums_of, outer_sums_of = [
        [
            Scatter([kept[2 * (k * count + m) + side] for m in range(count)], bits, count)
            for side, bits in enumerate((up, down))
        ]
        for k in range(2)
    ]
    for g in inner_sums_of:
        g.send()

    d_attended, out_away, grad_out_w = mixed_back(
        seq_count, where, mixed, out_weight, d_mixed_blocks
    )
    (d_attended,) = pin_some(inner_sums_of, d_attended)
    out_core = OtherCore(out_away)

    def send_all(exchanges):
        for exchange in exchanges:
            exchange.send()

    def scatter_windows(piece):
        return lax.psum_scatter(piece.astype(BF16), "wz", scatter_dimension=0, tiled=True)

    def gather_windows(piece):
        return lax.all_gather(piece, ("core", "wz"), axis=0, tiled=True)

    def joined_sum(scatters):
        return jnp.concatenate([g.rest().astype(BF16) for g in scatters], axis=1)

    (d_attended,) = pin_all([out_core], d_attended)
    out_sum = scatter_windows(grad_out_w + out_core.new[0].astype(F32))
    back = attend_back(0, placed_heads, rel, table_back, mixed, d_attended, probs)
    *back, out_sum = pin_all(inner_sums_of, *back, out_sum)
    out_sum = gather_windows(out_sum)
    for step in range(1, len(up)):
        send_all(inner_sums_of)
    send_all(outer_sums_of)
    for head in range(1, key_width // KEY):
        back = attend_back(head, placed_heads, rel, table_back, mixed, d_attended, probs, back)
    *back, out_sum = pin_all(inner_sums_of, *back, out_sum)
    d_heads, d_rel, d_bias = back
    inner_sum = scatter_windows(joined_sum(inner_sums_of))
    d_along, *d_normed, first_sums = rows_back(
        seq_count, where, order[None], d_heads, window, weight_whole
    )
    out = pin_all(outer_sums_of, d_along, inner_sum, *d_normed)
    d_along, inner_sum, d_normed = out[0], out[1], out[2:]
    inner_sum = gather_windows(inner_sum)
    for step in range(1, len(up)):
        send_all(outer_sums_of)
    arrived = [
        Scatter([d_normed[2 * m + side] for m in range(count)], bits, count)
        for side, bits in enumerate((up, down))
    ]
    results = pack(
        seq_count, where, hidden_one, d_along, first_sums, sums, inner_sums, d_bias, d_rel
    )
    results = pin_all(outer_sums_of, *results)
    packed_core = OtherCore(results[1])
    outer_sum = scatter_windows(joined_sum(outer_sums_of))
    (packed,) = pin_all([packed_core], results[0])
    packed = (packed.astype(F32) + packed_core.new[0].astype(F32)).astype(BF16)
    packed_shape = packed.shape
    packed = lax.all_to_all(packed, "seq", 0, 0, tiled=True)
    send_all(arrived)
    take_after(arrived, packed)
    packed_cube = CubeSum(packed.reshape(-1, packed_shape[2]), wz_count)
    packed_cube.send()
    take_after(arrived, packed_cube.new[0])
    packed_cube.send()
    (outer_sum,) = pin_all(arrived, outer_sum)
    outer_sum = gather_windows(outer_sum)
    for step in range(1, len(up)):
        send_all(arrived)
    take_after(arrived, packed_cube.new[0])
    d_mixed_blocks = pin(packed_cube.new[0], *d_mixed_blocks)[1:]
    packed_cube.send()
    returned = returned_rows(
        seq_count, where, order.reshape(2 * seq_count, row_count // 2), d_mixed_blocks
    )
    own_unit, own_scale = norm_of(inputs[0].astype(F32))
    arrived = jnp.concatenate([g.rest() for g in arrived], axis=1)
    grad_inputs = norm_back(own_unit, own_scale, vectors[0:1], arrived) + returned

    def both_halves(pieces, axis):
        half = pieces.shape[0] // 2
        return jnp.concatenate([pieces[:half], pieces[half:]], axis=axis).astype(F32)

    grad_out_w = both_halves(out_sum, 0)
    (grad_inputs,) = pin_all([packed_cube], grad_inputs)
    packed_cube.send()
    grad_inner_w = both_halves(inner_sum, 1)
    grad_outer_w = both_halves(outer_sum, 0)
    packed = packed_cube.rest().reshape(packed_shape)
    grad_query_w, grad_key_w, grad_value_w, flat = unpack(
        where, (packed, other_core(packed)), row_count, key_width, val_width
    )
    small = jnp.sum(flat[:, :16, :row_count], axis=0)
    g_gain_one, g_shift_one, g_out_b, g_gain_two, g_shift_two, g_outer_b = small[:6]
    g_inner_b = small[6:8].reshape(-1)
    grad_rel = flat[:, :, row_count : row_count + rel_blocks * key_width]
    grad_rel = grad_rel.reshape(seq_count, EXTRA, rel_blocks, key_width).transpose(2, 1, 0, 3)
    grad_rel = grad_rel.reshape(rel_blocks * EXTRA, -1)[:rel_rows]
    return (
        layer_output[None],
        grad_inputs[None],
        g_gain_one,
        g_shift_one,
        grad_query_w,
        grad_key_w,
        grad_value_w,
        small[8, :key_width],
        small[9, :key_width],
        grad_rel,
        grad_out_w,
        g_out_b,
        g_gain_two,
        g_shift_two,
        grad_inner_w,
        g_inner_b,
        grad_outer_w,
        g_outer_b,
    )


def solution(mesh):
    seq_count = mesh.shape["seq"]
    devices = mesh.devices.reshape(seq_count, -1, 2)
    split_mesh = Mesh(devices, ("seq", "wz", "core"))
    rows = P(("wz", "core"), "seq", None)
    vector = P("seq")
    matrix = P("seq", None)
    weights = (
        vector,
        vector,
        matrix,
        matrix,
        matrix,
        vector,
        vector,
        matrix,
        matrix,
        vector,
        vector,
        vector,
        matrix,
        vector,
        matrix,
        vector,
    )
    return jax.shard_map(
        functools.partial(shards, seq_count, mesh.shape["win"] // 2),
        mesh=split_mesh,
        in_specs=(rows, P(("wz", "core"), None)) + weights + (rows,),
        out_specs=(rows, rows) + weights,
        check_vma=False,
    )
```
